128 devices in a mesh: section: 8 (over x, y_hi), head: 8 (over z, y_lo), batch: 2 (over core).
Axes of the slice: x: 4, y: 4 (y_hi: 2, y_lo: 2; y = y_hi * 2 + y_lo), z: 4, core: 2. Of those that a mesh axis runs over, the one named last changes fastest.
Arguments:
- keys_prefill: bfloat16 [8, 32, 512, 1024], P('section', 'batch', None, 'head'), may hold values from -6 to 6
- values_prefill: bfloat16 [8, 32, 512, 1024], P('section', 'batch', None, 'head'), may hold values from -6 to 6
- lengths: int32 [32], replicated, may hold values from 1 to 510, 8192 in all
- slot_order: int32 [32], replicated, may hold values from 0 to 31, each once
- queries: bfloat16 [2, 8, 32, 8192], P(None, None, 'section'), may hold values from -51 to 51
- new_keys: bfloat16 [2, 8, 32, 1024], P(None, None, 'section'), may hold values from -5 to 5
- new_values: bfloat16 [2, 8, 32, 1024], P(None, None, 'section'), may hold values from -6 to 6
Outputs:
- attention: bfloat16 [2, 8, 32, 8192], P(None, None, 'section', ('head', 'batch'))
- keys_cache: bfloat16 [8, 32, 512, 1024], P(None, 'section', ('head', 'batch'))
- values_cache: bfloat16 [8, 32, 512, 1024], P(None, 'section', ('head', 'batch'))
The draws below stay inside these ranges and needn't reach their ends.
Inputs may be any that keep to these rules, and one draw needn't show every extreme that they name: lengths[p] is the number of cached tokens of prompt p; the prefill cache holds stale values from position lengths[p] on, which are not part of the cache (zero in keys_cache and values_cache unless a new row is placed there, and never visible to attention). `slot_order`: each prompt appears in exactly one decode slot.
All inputs are finite; a program needn't handle non-finite values.
Results may differ from the reference program's by a relative error of at most 0.0044.
Values may be sent and summed in bfloat16 or wider, within the bound.
A program may use at most 128 MiB of HBM per device.

```python
import math
import jax
import jax.numpy as jnp
import numpy as np
from jax import lax

KVH = 8
HD = 128
GROUP = 8
CAP = 512
STEPS = 2
LAYERS = 8
PROMPTS = 32


def shared_uniform(key):
    return jax.random.uniform(key, (STEPS, LAYERS, PROMPTS, KVH * HD), jnp.float32, 1e-06, 1.0 - 1e-06)


def spread_normal(uniform_draw):
    return jnp.clip(0.5513 * jnp.log(uniform_draw / (1.0 - uniform_draw)), -5.0, 5.0)


def draw_new_keys(key, part):
    common = shared_uniform(key)
    return spread_normal(common).astype(jnp.bfloat16)


def draw_queries(key, part):
    key = jax.random.fold_in(key, 5)
    noise_key = jax.random.fold_in(key, 0)
    full_shape = (STEPS, LAYERS, PROMPTS, KVH * GROUP * HD)
    return jnp.clip(jax.random.normal(noise_key, full_shape, jnp.float32), -5.0, 5.0).astype(jnp.bfloat16)


def block_scale(rng, extent, cuts, smallest, high):
    loudness, own = 1.0, jax.random.fold_in(rng, 6)
    for axis_at, parts in cuts:
        draws = jnp.exp(jax.random.uniform(jax.random.fold_in(own, axis_at), (parts,), jnp.float32, smallest / len(cuts), high / len(cuts)))
        loudness = loudness * jnp.repeat(draws, extent[axis_at] // parts).reshape([-1 if axis == axis_at else 1 for axis in range(len(extent))])
    return loudness


def profile(amount, total, limit, slope):
    loads = [(1 << 20) // math.isqrt(standing ** slope) + 1 for standing in range(2, amount + 1)]
    surplus, given = total - limit - (amount - 1), [1] * (amount - 1)
    while surplus > 0:
        candidates = [i for i in range(amount - 1) if given[i] < limit]
        whole, remaining = sum([loads[i] for i in candidates]), surplus
        for i in candidates:
            more = min(limit - given[i], max(1, remaining * loads[i] // whole), surplus)
            given[i] = given[i] + more
            surplus = surplus - more
    return np.array([limit] + given)


def ragged(own_key, number_of, total, limit, slope):
    if number_of == 2:
        one = jax.random.randint(own_key, (), max(1, total - limit), min(limit, total - 1) + 1)
        return jnp.stack([one, total - one])
    sizes = jnp.asarray(profile(number_of, total, limit, slope), jnp.int32)
    couples = (number_of - 1) // 2
    donor, taker = sizes[1:1 + 2 * couples:2], sizes[2:2 + 2 * couples:2]
    room = jnp.minimum(donor - 1, limit - taker)
    shifted = jax.random.randint(jax.random.fold_in(own_key, 1), (couples,), 0, 1 << 20) % (room + 1)
    sizes = sizes.at[1:1 + 2 * couples:2].set(donor - shifted).at[2:2 + 2 * couples:2].set(taker + shifted)
    return sizes[jax.random.permutation(jax.random.fold_in(own_key, 2), number_of)]


def bell_draw(key, shape, deviation, bound, cuts=(), kind=jnp.bfloat16):
    entries = jax.random.normal(key, shape, jnp.float32) * deviation
    if len(cuts) > 0:
        entries = block_scale(key, shape, cuts, -0.22, 0.18) * entries
    return jnp.clip(entries, min=-bound, max=bound).astype(kind)


def setup_inputs(seed: int = 0) -> dict:
    streams_of = jax.random.split(jax.random.key(seed), 8)
    return {
        "keys_prefill": bell_draw(streams_of[0], (LAYERS, PROMPTS, CAP, KVH * HD), 1.0, 6.0, ((0, 8), (1, 2), (3, 8))),
        "values_prefill": bell_draw(streams_of[1], (LAYERS, PROMPTS, CAP, KVH * HD), 1.0, 6.0, ((0, 8), (1, 2), (3, 8))),
        "lengths": ragged(streams_of[2], PROMPTS, PROMPTS * CAP // 2, CAP - STEPS, 2).astype(jnp.int32),
        "slot_order": jax.random.permutation(streams_of[3], PROMPTS).astype(jnp.int32),
        "queries": draw_queries(jax.random.fold_in(streams_of[7], 71), 0),
        "new_keys": draw_new_keys(jax.random.fold_in(streams_of[7], 71), 0),
        "new_values": bell_draw(streams_of[6], (STEPS, LAYERS, PROMPTS, KVH * HD), 1.0, 6.0, ((2, 8),)),
    }


def place_new(layer_cache, fresh_rows, slot_order, live_len):
    positions = jnp.arange(layer_cache.shape[1], dtype=jnp.int32)
    picked = jnp.take(layer_cache, slot_order, axis=0)
    kept_mask = positions[None, :] < live_len[:, None]
    picked = jnp.where(kept_mask[:, :, None], picked, jnp.zeros((), picked.dtype))
    for step_num in range(fresh_rows.shape[0]):
        hit_mask = positions[None, :] == (live_len + step_num)[:, None]
        picked = jnp.where(hit_mask[:, :, None], fresh_rows[step_num][:, None, :], picked)
    return picked


def reference(keys_prefill, values_prefill, lengths, slot_order, queries, new_keys, new_values):
    live_len = jnp.take(lengths, slot_order).astype(jnp.int32)
    positions = jnp.arange(CAP, dtype=jnp.int32)
    offsets = jnp.arange(STEPS, dtype=jnp.int32)
    visible = positions[None, None, :] <= (live_len[None, :, None] + offsets[:, None, None])
    shown_mask = visible[:, :, None, None, :]

    def one_layer(pieces):
        layer_keys, layer_values, layer_queries, fresh_keys, fresh_values = pieces
        keys_now = place_new(layer_keys, fresh_keys, slot_order, live_len)
        values_now = place_new(layer_values, fresh_values, slot_order, live_len)
        query_heads = layer_queries.reshape(STEPS, PROMPTS, KVH, GROUP, HD).astype(jnp.float32)
        key_heads = keys_now.reshape(PROMPTS, CAP, KVH, HD).astype(jnp.float32)
        scores = jnp.einsum("tpkgd,pckd->tpkgc", query_heads, key_heads) * (HD ** -0.5)
        row_peak = jnp.max(jnp.where(shown_mask, scores, -1e30), axis=-1, keepdims=True)
        exp_mass = jnp.where(shown_mask, jnp.exp(scores - row_peak), 0.0)
        row_total = jnp.sum(exp_mass, axis=-1)
        weights = lax.optimization_barrier(exp_mass.astype(jnp.bfloat16)).astype(jnp.float32)
        value_heads = values_now.reshape(PROMPTS, CAP, KVH, HD).astype(jnp.float32)
        weighted = jnp.einsum("tpkgc,pckd->tpkgd", weights, value_heads)
        attention = (weighted / row_total[..., None]).astype(jnp.bfloat16)
        return attention.reshape(STEPS, PROMPTS, KVH * GROUP * HD), keys_now, values_now

    attention, keys_cache, values_cache = lax.map(one_layer, (keys_prefill, values_prefill, jnp.moveaxis(queries, 1, 0), jnp.moveaxis(new_keys, 1, 0), jnp.moveaxis(new_values, 1, 0)))
    return jnp.moveaxis(attention, 0, 1), keys_cache, values_cache
```

```python
import jax
import jax.numpy as jnp
from jax import lax
from jax.experimental import pallas as pl
from jax.experimental.pallas import tpu as pltpu
from jax.sharding import PartitionSpec as P

KVH = 8
HD = 128
GROUP = 8
BLOCK = 32
MESH = pl.DeviceIdType.MESH
HIDDEN = -1e30


def place(offset, s, h):
    dx, dy, dz = lax.rem(offset, 4), lax.rem(lax.div(offset, 4), 4), lax.div(offset, 16)
    x = lax.rem(lax.div(s, 2) + dx, 4)
    y = lax.rem(lax.rem(s, 2) * 2 + lax.rem(h, 2) + dy, 4)
    z = lax.rem(lax.div(h, 2) + dz, 4)
    return x * 2 + lax.div(y, 2), z * 2 + lax.rem(y, 2)


def order(step, b):
    forward = lax.rem(step * 27, 64)
    return b * (64 - forward) + (1 - b) * forward


def relay(
    slot_order, keys, values, small,
    keys_out, values_out, rows_out,
    keys_all, values_all, keys_full, values_full, keys_send, values_send, small_all, rows_send,
    own_sem, swap_send, swap_recv, full_sem, small_send_sem, small_recv_sem,
    bulk_send, bulk_recv, rows_send_sem, rows_recv_sem,
):
    s, h, b = lax.axis_index("section"), lax.axis_index("head"), lax.axis_index("batch")
    other = 1 - b
    mine = pl.ds(b * 16, 16)

    full = (
        pltpu.make_async_copy(keys, keys_full, full_sem.at[0]),
        pltpu.make_async_copy(values, values_full, full_sem.at[1]),
    )
    own = tuple(
        pltpu.make_async_copy(src.at[:, :, b], dst.at[mine], own_sem.at[n])
        for n, (src, dst) in enumerate(((keys, keys_all), (values, values_all)))
    )
    swap = tuple(
        pltpu.make_async_remote_copy(
            src_ref=src.at[:, :, other],
            dst_ref=dst.at[mine],
            send_sem=swap_send.at[n],
            recv_sem=swap_recv.at[n],
            device_id=(s, h, other),
            device_id_type=MESH,
        )
        for n, (src, dst) in enumerate(((keys, keys_all), (values, values_all)))
    )
    own[0].start()
    own[1].start()

    barrier = pltpu.get_barrier_semaphore()

    def greet(step, carry):
        to_s, to_h = place(order(step, b), s, h)
        pl.semaphore_signal(barrier, inc=1, device_id=(to_s, to_h, b), device_id_type=MESH)
        return carry

    def greet_other(step, carry):
        pl.semaphore_signal(
            barrier, inc=1, device_id=(lax.rem(s + step, 8), h, other), device_id_type=MESH
        )
        return carry

    lax.fori_loop(0, 8, greet_other, 0)
    lax.fori_loop(1, 64, greet, 0)
    pl.semaphore_wait(barrier, 71)

    swap[0].start()
    swap[1].start()

    def send_small(step, carry):
        to_s = lax.rem(s + step, 8)
        pltpu.make_async_remote_copy(
            src_ref=small.at[to_s],
            dst_ref=small_all.at[s],
            send_sem=small_send_sem,
            recv_sem=small_recv_sem,
            device_id=(to_s, h, b),
            device_id_type=MESH,
        ).start()
        return carry

    lax.fori_loop(1, 8, send_small, 0)
    pltpu.make_async_copy(small.at[s], small_all.at[s], small_recv_sem).start()

    for n, (gathered, packed, landed) in enumerate(
        ((keys_all, keys_send, keys_out), (values_all, values_send, values_out))
    ):
        own[n].wait()
        swap[n].wait_recv()

        def pack(slot, carry):
            packed[lax.div(slot, 4), :, lax.rem(slot, 4)] = gathered[slot_order[slot]]
            return carry

        lax.fori_loop(0, 32, pack, 0)

        def send(step, carry):
            to_s, to_h = place(order(step, b), s, h)
            pltpu.make_async_remote_copy(
                src_ref=packed.at[to_s, to_h],
                dst_ref=landed.at[s, h],
                send_sem=bulk_send.at[n],
                recv_sem=bulk_recv.at[n],
                device_id=(to_s, to_h, b),
                device_id_type=MESH,
            ).start()
            return carry

        lax.fori_loop(1, 64, send, 0)
        pltpu.make_async_copy(packed.at[s, h], landed.at[s, h], bulk_recv.at[n]).start()
        full[n].start()

    pltpu.make_async_copy(small_all, small_all, small_recv_sem).wait()
    full[0].wait()
    full[1].wait()

    def attend(slot):
        prompt = slot_order[slot] - b * 16
        inside = jnp.logical_and(prompt >= 0, prompt < 16)
        prompt = jnp.clip(prompt, 0, 15)
        live = slot_order[32 + slot]
        at_s, at_k = lax.div(slot, 4), lax.rem(slot, 4)
        q = small_all[at_s, pl.ds(pl.multiple_of(at_k * 16, 16), 16)]
        fresh = small_all[at_s, pl.ds(64, 16)].astype(jnp.float32)
        row16 = lax.broadcasted_iota(jnp.int32, (16, HD), 0)

        def fresh_row(at):
            return jnp.sum(jnp.where(row16 == at, fresh, 0.0), axis=0, keepdims=True)

        k0, k1 = fresh_row(at_k * 2), fresh_row(at_k * 2 + 1)
        v0, v1 = fresh_row(8 + at_k * 2), fresh_row(8 + at_k * 2 + 1)
        k = keys_full[prompt].reshape(512, HD)
        v = values_full[prompt].reshape(512, HD)
        scale = HD ** -0.5
        scores = lax.dot_general(
            q, k, (((1,), (1,)), ((), ())), preferred_element_type=jnp.float32
        ) * scale
        qf = q.astype(jnp.float32)
        n0 = jnp.sum(qf * k0, axis=1, keepdims=True) * scale
        n1 = jnp.sum(qf * k1, axis=1, keepdims=True) * scale
        later = lax.rem(lax.div(lax.broadcasted_iota(jnp.int32, (16, 1), 0), 4), 2) == 1
        kept = lax.broadcasted_iota(jnp.int32, (16, 512), 1) < live
        scores = jnp.where(kept, scores, HIDDEN)
        n1 = jnp.where(later, n1, HIDDEN)
        peak = jnp.maximum(jnp.max(scores, axis=1, keepdims=True), jnp.maximum(n0, n1))
        mass = jnp.where(kept, jnp.exp(scores - peak), 0.0)
        m0 = jnp.exp(n0 - peak)
        m1 = jnp.where(later, jnp.exp(n1 - peak), 0.0)
        total = jnp.sum(mass, axis=1, keepdims=True) + m0 + m1
        weighted = jnp.dot(mass.astype(jnp.bfloat16), v, preferred_element_type=jnp.float32)
        weighted += m0.astype(jnp.bfloat16).astype(jnp.float32) * v0
        weighted += m1.astype(jnp.bfloat16).astype(jnp.float32) * v1
        return jnp.where(inside, weighted / total, 0.0)

    def attend_pair(pair, carry):
        first, second = attend(pair * 2), attend(pair * 2 + 1)
        for to_b in range(2):
            cut = slice(to_b * 8, to_b * 8 + 8)
            rows_send[lax.div(pair, 2), to_b, lax.rem(pair, 2)] = jnp.concatenate(
                (first[cut], second[cut]), axis=0
            ).astype(jnp.bfloat16)
        return carry

    lax.fori_loop(0, 16, attend_pair, 0)

    def send_rows(step, carry):
        to_s = lax.rem(s + step, 8)
        for to_b in (b, other):
            pltpu.make_async_remote_copy(
                src_ref=rows_send.at[to_s, to_b],
                dst_ref=rows_out.at[s, b],
                send_sem=rows_send_sem,
                recv_sem=rows_recv_sem,
                device_id=(to_s, h, to_b),
                device_id_type=MESH,
            ).start()
        return carry

    lax.fori_loop(1, 8, send_rows, 0)
    pltpu.make_async_remote_copy(
        src_ref=rows_send.at[s, other],
        dst_ref=rows_out.at[s, b],
        send_sem=rows_send_sem,
        recv_sem=rows_recv_sem,
        device_id=(s, h, other),
        device_id_type=MESH,
    ).start()
    pltpu.make_async_copy(rows_send.at[s, b], rows_out.at[s, b], rows_recv_sem).start()

    swap[0].wait_send()
    swap[1].wait_send()

    pltpu.make_async_copy(small.at[pl.ds(0, 7)], small.at[pl.ds(0, 7)], small_send_sem).wait()
    for n, (packed, landed) in enumerate(((keys_send, keys_out), (values_send, values_out))):
        pltpu.make_async_copy(packed.at[pl.ds(0, 7)], packed.at[pl.ds(0, 7)], bulk_send.at[n]).wait()
        pltpu.make_async_copy(
            packed.at[0, pl.ds(0, 7)], packed.at[0, pl.ds(0, 7)], bulk_send.at[n]
        ).wait()
        pltpu.make_async_copy(landed, landed, bulk_recv.at[n]).wait()
    pltpu.make_async_copy(
        rows_send.at[pl.ds(0, 7)], rows_send.at[pl.ds(0, 7)], rows_send_sem
    ).wait()
    pltpu.make_async_copy(rows_send.at[0, 0], rows_send.at[0, 0], rows_send_sem).wait()
    pltpu.make_async_copy(rows_out, rows_out, rows_recv_sem).wait()


def settle(slot_order, keys, values, new_keys, new_values, keys_out, values_out):
    s, h, b = lax.axis_index("section"), lax.axis_index("head"), lax.axis_index("batch")
    position = (h * 2 + b) * BLOCK + lax.broadcasted_iota(jnp.int32, (BLOCK, HD), 0)
    for slot in range(4):
        live = slot_order[32 + s * 4 + slot]
        kept, hits = position < live, (position == live, position == live + 1)
        for src, fresh, dst in ((keys, new_keys, keys_out), (values, new_values, values_out)):
            for head in range(KVH):
                cut = slice(head * HD, head * HD + HD)
                rows = jnp.where(kept, src[0, head, slot].astype(jnp.float32), 0.0)
                for step in range(2):
                    row = fresh[step, 0, slot : slot + 1, cut].astype(jnp.float32)
                    rows = jnp.where(hits[step], row, rows)
                dst[0, slot, :, cut] = rows.astype(jnp.bfloat16)


def body(keys_prefill, values_prefill, lengths, slot_order, queries, new_keys, new_values):
    h, b = lax.axis_index("head"), lax.axis_index("batch")
    s = lax.axis_index("section")
    scalars = jnp.concatenate((slot_order, jnp.take(lengths, slot_order)))

    def of_head(array, width):
        return lax.dynamic_slice_in_dim(array, h * width, width, axis=3)

    q = of_head(queries, GROUP * HD).reshape(2, 8, 4, 2, 4, HD)
    q = q.transpose(1, 2, 3, 0, 4, 5).reshape(8, 64, HD)
    fresh = [
        of_head(array, HD).transpose(1, 2, 0, 3).reshape(8, 8, HD) for array in (new_keys, new_values)
    ]
    small = jnp.concatenate((q, *fresh), axis=1)
    keys = keys_prefill.reshape(16, 8, 2, BLOCK, HD)
    values = values_prefill.reshape(16, 8, 2, BLOCK, HD)

    any_spec = pl.BlockSpec(memory_space=pl.ANY)
    smem_spec = pl.BlockSpec(memory_space=pltpu.SMEM)
    bf16 = jnp.bfloat16
    landed = jax.ShapeDtypeStruct((8, 8, 4, BLOCK, HD), bf16)
    dma = pltpu.SemaphoreType.DMA
    keys_raw, values_raw, rows = pl.pallas_call(
        relay,
        out_shape=(landed, landed, jax.ShapeDtypeStruct((8, 2, 2, 16, HD), bf16)),
        in_specs=[smem_spec, any_spec, any_spec, any_spec],
        out_specs=(any_spec, any_spec, any_spec),
        scratch_shapes=[
            pltpu.VMEM((32, 8, BLOCK, HD), bf16),
            pltpu.VMEM((32, 8, BLOCK, HD), bf16),
            pltpu.VMEM((16, 8, 2, BLOCK, HD), bf16),
            pltpu.VMEM((16, 8, 2, BLOCK, HD), bf16),
            pltpu.VMEM((8, 8, 4, BLOCK, HD), bf16),
            pltpu.VMEM((8, 8, 4, BLOCK, HD), bf16),
            pltpu.VMEM((8, 80, HD), bf16),
            pltpu.VMEM((8, 2, 2, 16, HD), bf16),
            dma((2,)), dma((2,)), dma((2,)), dma((2,)), dma, dma,
            dma((2,)), dma((2,)), dma, dma,
        ],
        compiler_params=pltpu.CompilerParams(
            collective_id=0, has_side_effects=True, vmem_limit_bytes=32 * 2**20
        ),
        name="relay",
    )(scalars, keys, values, small)

    taken = pl.BlockSpec((1, 8, 4, BLOCK, HD), lambda l: (l, 0, 0, 0, 0))
    fresh_spec = pl.BlockSpec((2, 1, 4, KVH * HD), lambda l: (0, l, 0, 0))
    given = pl.BlockSpec((1, 4, BLOCK, KVH * HD), lambda l: (l, 0, 0, 0))
    cache = jax.ShapeDtypeStruct((8, 4, BLOCK, KVH * HD), bf16)
    keys_cache, values_cache = pl.pallas_call(
        settle,
        out_shape=(cache, cache),
        grid=(8,),
        in_specs=[smem_spec, taken, taken, fresh_spec, fresh_spec],
        out_specs=(given, given),
        compiler_params=pltpu.CompilerParams(vmem_limit_bytes=16 * 2**20),
        name="settle",
    )(scalars, keys_raw, values_raw, new_keys, new_values)

    owner = lax.dynamic_slice_in_dim(slot_order, s * 4, 4) // 16
    rows = rows.reshape(8, 2, 4, 2, 4, HD)
    first = (owner == 0)[None, :, None, None, None]
    attention = jnp.where(first, rows[:, 0], rows[:, 1])
    attention = attention.transpose(2, 0, 1, 3, 4).reshape(2, 8, 4, 4 * HD)
    return attention, keys_cache, values_cache


def solution(mesh):
    in_specs = (
        P("section", "batch", None, "head"),
        P("section", "batch", None, "head"),
        P(),
        P(),
        P(None, None, "section", None),
        P(None, None, "section", None),
        P(None, None, "section", None),
    )
    out_specs = (
        P(None, None, "section", ("head", "batch")),
        P(None, "section", ("head", "batch"), None),
        P(None, "section", ("head", "batch"), None),
    )
    return jax.shard_map(body, mesh=mesh, in_specs=in_specs, out_specs=out_specs, check_vma=False)
```

```python
import jax
import jax.numpy as jnp
from jax import lax
from jax.experimental import pallas as pl
from jax.experimental.pallas import tpu as pltpu
from jax.sharding import PartitionSpec as P

KVH = 8
HD = 128
GROUP = 8
BLOCK = 32
MESH = pl.DeviceIdType.MESH
HIDDEN = -1e30
BF16, F32 = jnp.bfloat16, jnp.float32


def turn(offset):
    return lax.rem(offset * 4 - 1, 63) + 1


def static_turn(offset):
    return (offset * 4 - 1) % 63 + 1


def hops(offset):
    return sum(min(d, 4 - d) for d in (offset % 4, offset // 4 % 4, offset // 16))


def orbits():
    seen, out, fixed = set(), [], []
    for offset in range(1, 64):
        if offset in seen:
            continue
        ring = {offset, static_turn(offset), static_turn(static_turn(offset))}
        seen |= ring
        (out if len(ring) == 3 else fixed).append(offset)
    return out, fixed


REPS, FIXED = orbits()
REPS = sorted(REPS, key=lambda o: -hops(o))
GROUPS = [[REPS[g], REPS[g + 7], REPS[g + 14]] if g + 14 < len(REPS) else [REPS[g], REPS[g + 7]] for g in range(7)]


def coordinates(offset, sign, s, h):
    dx, dy, dz = lax.rem(offset, 4), lax.rem(lax.div(offset, 4), 4), lax.div(offset, 16)
    x = lax.rem(lax.div(s, 2) + sign * dx + 4, 4)
    y = lax.rem(lax.rem(s, 2) * 2 + lax.rem(h, 2) + sign * dy + 4, 4)
    z = lax.rem(lax.div(h, 2) + sign * dz + 4, 4)
    return x * 2 + lax.div(y, 2), z * 2 + lax.rem(y, 2)


def each_of(group, do):
    reps = GROUPS[group]
    word = sum(rep * 64**n for n, rep in enumerate(reps))

    def rep_step(_, word):
        def turn_step(_, offset):
            do(offset)
            return turn(offset)

        lax.fori_loop(0, 3, turn_step, lax.rem(word, 64))
        return lax.div(word, 64)

    lax.fori_loop(0, len(reps), rep_step, jnp.int32(word))
    if len(reps) == 2:
        for offset in FIXED:
            do(jnp.int32(offset))


def relay(
    slot_order, lengths, keys, values, queries, new_keys, new_values,
    attention, keys_cache, values_cache,
    keys_all, values_all, keys_full, values_full, keys_send, values_send, keys_land, values_land,
    fresh_keys, fresh_values, query_all, query_rows, fresh_key_all, fresh_value_all, rows_send, rows_land,
    own_sem, swap_send, swap_recv, full_sem, fresh_sem, small_send, small_recv,
    bulk_send, bulk_recv, rows_send_sem, rows_recv_sem,
):
    s, h, b = lax.axis_index("section"), lax.axis_index("head"), lax.axis_index("batch")
    other = 1 - b
    sign = 1 - 2 * b
    mine = pl.ds(b * 16, 16)
    inputs = ((keys, keys_all, keys_full), (values, values_all, values_full))

    full = [pltpu.make_async_copy(src, dst, full_sem.at[n]) for n, (src, _, dst) in enumerate(inputs)]
    own = [
        pltpu.make_async_copy(src.at[:, :, b], dst.at[mine], own_sem.at[n])
        for n, (src, dst, _) in enumerate(inputs)
    ]
    fresh = [
        pltpu.make_async_copy(new_keys, fresh_keys, fresh_sem.at[0]),
        pltpu.make_async_copy(new_values, fresh_values, fresh_sem.at[1]),
    ]
    swap = [
        pltpu.make_async_remote_copy(
            src_ref=src.at[:, :, other],
            dst_ref=dst.at[mine],
            send_sem=swap_send.at[n],
            recv_sem=swap_recv.at[n],
            device_id=(s, h, other),
            device_id_type=MESH,
        )
        for n, (src, dst, _) in enumerate(inputs)
    ]
    for copy in own + fresh:
        copy.start()

    barrier = pltpu.get_barrier_semaphore()

    def greet_other(step, carry):
        pl.semaphore_signal(
            barrier, inc=1, device_id=(lax.rem(s + step, 8), h, other), device_id_type=MESH
        )
        return carry

    def greet(step, carry):
        to_s, to_h = lax.rem(s + lax.div(step, 8), 8), lax.rem(h + lax.rem(step, 8), 8)
        pl.semaphore_signal(barrier, inc=1, device_id=(to_s, to_h, b), device_id_type=MESH)
        return carry

    lax.fori_loop(0, 8, greet_other, 0)
    lax.fori_loop(1, 64, greet, 0)
    pl.semaphore_wait(barrier, 71)

    swap[0].start()
    swap[1].start()

    head_rows = pl.ds(pl.multiple_of(h * GROUP * HD, GROUP * HD), GROUP * HD)
    head_cols = pl.ds(pl.multiple_of(h * HD, HD), HD)

    def small_pieces(to_s):
        return (
            (queries.at[:, to_s, :, head_rows], query_all.at[s]),
            (new_keys.at[:, to_s, :, head_cols], fresh_key_all.at[s]),
            (new_values.at[:, to_s, :, head_cols], fresh_value_all.at[s]),
        )

    def send_small(step, carry):
        to_s = lax.rem(s + step, 8)
        for n, (src, dst) in enumerate(small_pieces(to_s)):
            pltpu.make_async_remote_copy(
                src_ref=src,
                dst_ref=dst,
                send_sem=small_send.at[n],
                recv_sem=small_recv.at[n],
                device_id=(to_s, h, b),
                device_id_type=MESH,
            ).start()
        return carry

    lax.fori_loop(1, 8, send_small, 0)
    for n, (src, dst) in enumerate(small_pieces(s)):
        pltpu.make_async_copy(src, dst, small_recv.at[n]).start()

    bulk = ((keys_all, keys_send, keys_land), (values_all, values_send, values_land))
    for n, (gathered, packed, landed) in enumerate(bulk):
        own[n].wait()
        swap[n].wait_recv()

        def pack(slot, carry):
            at_s, at_k = lax.div(slot, 4), lax.rem(slot, 4)
            packed[pl.ds(at_s * 8, 8), at_k] = gathered[slot_order[slot]]
            return carry

        lax.fori_loop(0, 32, pack, 0)
        for group in range(7):

            def send(offset):
                to_s, to_h = coordinates(offset, sign, s, h)
                pltpu.make_async_remote_copy(
                    src_ref=packed.at[to_s * 8 + to_h],
                    dst_ref=landed.at[s * 8 + h],
                    send_sem=bulk_send.at[n],
                    recv_sem=bulk_recv.at[n, group],
                    device_id=(to_s, to_h, b),
                    device_id_type=MESH,
                ).start()

            each_of(group, send)
        full[n].start()

    for n, whole in enumerate((query_all, fresh_key_all, fresh_value_all)):
        pltpu.make_async_copy(whole, whole, small_recv.at[n]).wait()
    full[0].wait()
    full[1].wait()

    later = lax.rem(lax.div(lax.broadcasted_iota(jnp.int32, (16, 1), 0), 4), 2) == 1
    column = lax.broadcasted_iota(jnp.int32, (16, 512), 1)
    scale = HD ** -0.5

    def attend(at_s, at_k):
        slot = slot_order[at_s * 4 + at_k]
        prompt = slot - b * 16
        inside = jnp.logical_and(prompt >= 0, prompt < 16)
        prompt = jnp.clip(prompt, 0, 15)
        live = lengths[slot]
        qf = query_rows[at_k]
        k0, k1 = (fresh_key_all[at_s, t].astype(F32)[at_k : at_k + 1] for t in range(2))
        v0, v1 = (fresh_value_all[at_s, t].astype(F32)[at_k : at_k + 1] for t in range(2))
        k = keys_full[prompt].reshape(512, HD)
        v = values_full[prompt].reshape(512, HD)
        scores = lax.dot_general(
            qf.astype(BF16), k, (((1,), (1,)), ((), ())), preferred_element_type=F32
        ) * scale
        n0 = jnp.sum(qf * k0, axis=1, keepdims=True) * scale
        n1 = jnp.sum(qf * k1, axis=1, keepdims=True) * scale
        kept = column < live
        scores = jnp.where(kept, scores, HIDDEN)
        n1 = jnp.where(later, n1, HIDDEN)
        peak = jnp.maximum(jnp.max(scores, axis=1, keepdims=True), jnp.maximum(n0, n1))
        mass = jnp.where(kept, jnp.exp(scores - peak), 0.0)
        m0 = jnp.exp(n0 - peak)
        m1 = jnp.where(later, jnp.exp(n1 - peak), 0.0)
        total = jnp.sum(mass, axis=1, keepdims=True) + m0 + m1
        weighted = jnp.dot(mass.astype(BF16), v, preferred_element_type=F32)
        weighted += m0.astype(BF16).astype(F32) * v0
        weighted += m1.astype(BF16).astype(F32) * v1
        return jnp.where(inside, weighted / total, 0.0)

    def attend_section(at_s, carry):
        for t in range(2):
            x = query_all[at_s, t].astype(F32)
            for g in range(GROUP):
                row = (g // 4) * 8 + t * 4 + g % 4
                for k in range(4):
                    query_rows[k, row : row + 1, :] = x[k : k + 1, g * HD : g * HD + HD]
        for pair in range(2):
            first, second = attend(at_s, pair * 2), attend(at_s, pair * 2 + 1)
            for to_b in range(2):
                cut = slice(to_b * 8, to_b * 8 + 8)
                rows_send[at_s, to_b, pair] = jnp.concatenate(
                    (first[cut], second[cut]), axis=0
                ).astype(BF16)
        return carry

    lax.fori_loop(0, 8, attend_section, 0)

    def send_rows(to_s, to_b):
        pltpu.make_async_remote_copy(
            src_ref=rows_send.at[to_s, to_b],
            dst_ref=rows_land.at[s, b],
            send_sem=rows_send_sem,
            recv_sem=rows_recv_sem,
            device_id=(to_s, h, to_b),
            device_id_type=MESH,
        ).start()

    def send_rows_step(step, carry):
        to_s = lax.rem(s + step, 8)
        send_rows(to_s, b)
        send_rows(to_s, other)
        return carry

    lax.fori_loop(1, 8, send_rows_step, 0)
    send_rows(s, other)
    pltpu.make_async_copy(rows_send.at[s, b], rows_land.at[s, b], rows_recv_sem).start()

    slots = [slot_order[s * 4 + k] for k in range(4)]
    lives = [lengths[slot] for slot in slots]
    position = (h * 2 + b) * BLOCK + lax.broadcasted_iota(jnp.int32, (BLOCK, HD), 0)
    fresh[0].wait()
    fresh[1].wait()

    def settle(block, n, from_s, from_h):
        new, out = ((fresh_keys, keys_cache), (fresh_values, values_cache))[n]
        cut = pl.ds(pl.multiple_of(from_h * HD, HD), HD)
        placed = [new[t, from_s, :, cut].astype(F32) for t in range(2)]
        for k in range(4):
            rows = jnp.where(position < lives[k], block[k].astype(F32), 0.0)
            for t in range(2):
                rows = jnp.where(position == lives[k] + t, placed[t][k : k + 1], rows)
            out[from_s, k, :, cut] = rows.astype(BF16)

    for n, (_, packed, landed) in enumerate(bulk):
        settle(packed.at[s * 8 + h], n, s, h)
        for group in range(7):
            nine = landed.at[pl.ds(0, 9)]
            pltpu.make_async_copy(nine, nine, bulk_recv.at[n, group]).wait()

            def settle_one(offset):
                from_s, from_h = coordinates(offset, -sign, s, h)
                settle(landed.at[from_s * 8 + from_h], n, from_s, from_h)

            each_of(group, settle_one)

    pltpu.make_async_copy(rows_land, rows_land, rows_recv_sem).wait()
    owners = [lax.div(slot, 16) for slot in slots]

    def assemble(l, carry):
        picked = []
        for k in range(4):
            part = slice((k % 2) * 8, (k % 2) * 8 + 8)
            first, second = (rows_land[l, n, k // 2].astype(F32)[part] for n in range(2))
            picked.append(jnp.where(owners[k] == 0, first, second))
        for t in range(2):
            attention[t, l] = jnp.concatenate(
                [
                    jnp.concatenate([rows[t * 4 + g : t * 4 + g + 1] for rows in picked], axis=0)
                    for g in range(4)
                ],
                axis=1,
            ).astype(BF16)
        return carry

    lax.fori_loop(0, 8, assemble, 0)

    swap[0].wait_send()
    swap[1].wait_send()
    for n, whole in enumerate((query_all, fresh_key_all, fresh_value_all)):
        seven = whole.at[pl.ds(0, 7)]
        pltpu.make_async_copy(seven, seven, small_send.at[n]).wait()
    for n, (_, packed, _) in enumerate(bulk):
        sent = packed.at[pl.ds(0, 63)]
        pltpu.make_async_copy(sent, sent, bulk_send.at[n]).wait()
    seven, one = rows_send.at[pl.ds(0, 7)], rows_send.at[0, 0]
    pltpu.make_async_copy(seven, seven, rows_send_sem).wait()
    pltpu.make_async_copy(one, one, rows_send_sem).wait()


def hand_out(attention, keys, values, attention_out, keys_out, values_out, sem):
    copies = [pltpu.make_async_copy(attention, attention_out, sem.at[16])]
    for n, (src, dst) in enumerate(((keys, keys_out), (values, values_out))):
        copies += [pltpu.make_async_copy(src.at[l], dst.at[l], sem.at[n * 8 + l]) for l in range(8)]
    for copy in copies:
        copy.start()
    for copy in copies:
        copy.wait()


def body(keys_prefill, values_prefill, lengths, slot_order, queries, new_keys, new_values):
    keys = keys_prefill.reshape(16, 8, 2, BLOCK, HD)
    values = values_prefill.reshape(16, 8, 2, BLOCK, HD)
    any_spec = pl.BlockSpec(memory_space=pl.ANY)
    smem_spec = pl.BlockSpec(memory_space=pltpu.SMEM)
    vmem_spec = pl.BlockSpec(memory_space=pltpu.VMEM)
    dma, vmem = pltpu.SemaphoreType.DMA, pltpu.VMEM
    rows_shape, cache_shape = (2, 8, 4, 4 * HD), (8, 4, BLOCK, KVH * HD)
    blocks = (64, 4, BLOCK, HD)
    held = pl.pallas_call(
        relay,
        out_shape=(vmem(rows_shape, BF16), vmem(cache_shape, BF16), vmem(cache_shape, BF16)),
        in_specs=[smem_spec] * 2 + [any_spec] * 5,
        out_specs=(vmem_spec,) * 3,
        scratch_shapes=[
            vmem((32, 8, BLOCK, HD), BF16), vmem((32, 8, BLOCK, HD), BF16),
            vmem((16, 8, 2, BLOCK, HD), BF16), vmem((16, 8, 2, BLOCK, HD), BF16),
            vmem(blocks, BF16), vmem(blocks, BF16), vmem(blocks, BF16), vmem(blocks, BF16),
            vmem((2, 8, 4, KVH * HD), BF16), vmem((2, 8, 4, KVH * HD), BF16),
            vmem((8, 2, 4, GROUP * HD), BF16), vmem((4, 16, HD), F32),
            vmem((8, 2, 4, HD), BF16), vmem((8, 2, 4, HD), BF16),
            vmem((8, 2, 2, 16, HD), BF16), vmem((8, 2, 2, 16, HD), BF16),
            dma((2,)), dma((2,)), dma((2,)), dma((2,)), dma((2,)), dma((3,)), dma((3,)),
            dma((2,)), dma((2, 7)), dma, dma,
        ],
        compiler_params=pltpu.CompilerParams(
            collective_id=0, has_side_effects=True, vmem_limit_bytes=48 * 2**20
        ),
        name="relay",
    )(slot_order, lengths, keys, values, queries, new_keys, new_values)
    return pl.pallas_call(
        hand_out,
        out_shape=tuple(jax.ShapeDtypeStruct(shape, BF16) for shape in (rows_shape, cache_shape, cache_shape)),
        in_specs=[any_spec] * 3,
        out_specs=(any_spec,) * 3,
        scratch_shapes=[dma((17,))],
        name="hand_out",
    )(*held)


def solution(mesh):
    in_specs = (
        P("section", "batch", None, "head"),
        P("section", "batch", None, "head"),
        P(),
        P(),
        P(None, None, "section", None),
        P(None, None, "section", None),
        P(None, None, "section", None),
    )
    out_specs = (
        P(None, None, "section", ("head", "batch")),
        P(None, "section", ("head", "batch"), None),
        P(None, "section", ("head", "batch"), None),
    )
    return jax.shard_map(body, mesh=mesh, in_specs=in_specs, out_specs=out_specs, check_vma=False)
```

```python
import jax
import jax.numpy as jnp
from jax import lax
from jax.experimental import pallas as pl
from jax.experimental.pallas import tpu as pltpu
from jax.sharding import PartitionSpec as P

KVH = 8
HD = 128
GROUP = 8
BLOCK = 32
MESH = pl.DeviceIdType.MESH
HIDDEN = -1e30
BF16, F32 = jnp.bfloat16, jnp.float32


PIECES = ((1, 1), (3, 1), (2, 1), (0, 1), (1, 0), (3, 0), (2, 0), (0, 0))


def head_at(piece, sign, h):
    dz, dy = PIECES[piece]
    z = lax.rem(lax.div(h, 2) + sign * dz + 4, 4)
    return z * 2 + lax.rem(lax.rem(h, 2) + dy, 2)


def section_at(step, sign, s):
    x = lax.rem(lax.div(s, 2) + sign * lax.rem(step, 4) + 4, 4)
    return x * 2 + lax.rem(lax.rem(s, 2) + lax.div(step, 4), 2)


def relay(
    slot_order_hbm, lengths_hbm, keys, values, queries, new_keys, new_values,
    attention, keys_cache, values_cache,
    keys_all, values_all, keys_full, values_full, keys_send, values_send, keys_land, values_land,
    fresh_keys, fresh_values, query_all, query_rows, fresh_key_all, fresh_value_all, rows_send, rows_land,
    slot_order, lengths,
    own_sem, swap_send, swap_recv, full_sem, fresh_sem, small_send, small_recv,
    bulk_send, bulk_recv, rows_send_sem, rows_recv_sem, scalar_sem,
):
    s, h, b = lax.axis_index("section"), lax.axis_index("head"), lax.axis_index("batch")
    other = 1 - b
    sign = 1 - 2 * b
    mine = pl.ds(b * 16, 16)
    inputs = ((keys, keys_all, keys_full), (values, values_all, values_full))

    full = [pltpu.make_async_copy(src, dst, full_sem.at[n]) for n, (src, _, dst) in enumerate(inputs)]
    own = [
        [
            pltpu.make_async_copy(
                src.at[:, head_at(piece, sign, h), b], dst[piece].at[mine], own_sem.at[n, piece]
            )
            for piece in range(8)
        ]
        for n, (src, dst, _) in enumerate(inputs)
    ]
    fresh = [
        pltpu.make_async_copy(new_keys, fresh_keys, fresh_sem.at[0]),
        pltpu.make_async_copy(new_values, fresh_values, fresh_sem.at[1]),
    ]
    scalars = [
        pltpu.make_async_copy(slot_order_hbm, slot_order, scalar_sem.at[0]),
        pltpu.make_async_copy(lengths_hbm, lengths, scalar_sem.at[1]),
    ]

    def swap(n, piece, receiver_sign):
        src, dst, _ = inputs[n]
        at_h = head_at(piece, receiver_sign, h)
        return pltpu.make_async_remote_copy(
            src_ref=src.at[:, at_h, other],
            dst_ref=dst[piece].at[mine],
            send_sem=swap_send,
            recv_sem=swap_recv.at[n, piece],
            device_id=(s, h, other),
            device_id_type=MESH,
        )

    for copy in scalars + own[0] + own[1] + fresh:
        copy.start()

    barrier = pltpu.get_barrier_semaphore()

    def greet_other(step, carry):
        pl.semaphore_signal(
            barrier, inc=1, device_id=(lax.rem(s + step, 8), h, other), device_id_type=MESH
        )
        return carry

    def greet(step, carry):
        to_s, to_h = lax.rem(s + lax.div(step, 8), 8), lax.rem(h + lax.rem(step, 8), 8)
        pl.semaphore_signal(barrier, inc=1, device_id=(to_s, to_h, b), device_id_type=MESH)
        return carry

    lax.fori_loop(0, 8, greet_other, 0)
    lax.fori_loop(1, 64, greet, 0)
    pl.semaphore_wait(barrier, 71)

    for n in range(2):
        for piece in range(8):
            swap(n, piece, -sign).start()

    head_rows = pl.ds(pl.multiple_of(h * GROUP * HD, GROUP * HD), GROUP * HD)
    head_cols = pl.ds(pl.multiple_of(h * HD, HD), HD)

    def small_pieces(to_s):
        return (
            (queries.at[:, to_s, :, head_rows], query_all.at[s]),
            (new_keys.at[:, to_s, :, head_cols], fresh_key_all.at[s]),
            (new_values.at[:, to_s, :, head_cols], fresh_value_all.at[s]),
        )

    def send_small(step, carry):
        to_s = lax.rem(s + step, 8)
        for n, (src, dst) in enumerate(small_pieces(to_s)):
            pltpu.make_async_remote_copy(
                src_ref=src,
                dst_ref=dst,
                send_sem=small_send.at[n],
                recv_sem=small_recv.at[n],
                device_id=(to_s, h, b),
                device_id_type=MESH,
            ).start()
        return carry

    lax.fori_loop(1, 8, send_small, 0)
    for n, (src, dst) in enumerate(small_pieces(s)):
        pltpu.make_async_copy(src, dst, small_recv.at[n]).start()

    bulk = ((keys_all, keys_send, keys_land), (values_all, values_send, values_land))
    scalars[0].wait()
    scalars[1].wait()
    for n, (gathered, packed, landed) in enumerate(bulk):
        for piece in range(8):
            own[n][piece].wait()
            swap(n, piece, sign).wait_recv()
            at_h = head_at(piece, sign, h)

            def pack(at_s, carry):
                for k in range(4):
                    packed[at_s * 8 + at_h, k] = gathered[piece][slot_order[at_s * 4 + k]]
                return carry

            lax.fori_loop(0, 8, pack, 0)

            def send(step, carry):
                to_s = section_at(step, sign, s)
                pltpu.make_async_remote_copy(
                    src_ref=packed.at[to_s * 8 + at_h],
                    dst_ref=landed.at[s * 8 + h],
                    send_sem=bulk_send.at[n],
                    recv_sem=bulk_recv.at[n, piece],
                    device_id=(to_s, at_h, b),
                    device_id_type=MESH,
                ).start()
                return carry

            lax.fori_loop(1 if piece == 7 else 0, 8, send, 0)
        full[n].start()

    for n, whole in enumerate((query_all, fresh_key_all, fresh_value_all)):
        pltpu.make_async_copy(whole, whole, small_recv.at[n]).wait()
    full[0].wait()
    full[1].wait()

    later = lax.rem(lax.div(lax.broadcasted_iota(jnp.int32, (16, 1), 0), 4), 2) == 1
    column = lax.broadcasted_iota(jnp.int32, (16, 512), 1)
    scale = HD ** -0.5

    def attend(at_s, at_k):
        slot = slot_order[at_s * 4 + at_k]
        prompt = slot - b * 16
        inside = jnp.logical_and(prompt >= 0, prompt < 16)
        prompt = jnp.clip(prompt, 0, 15)
        live = lengths[slot]
        qf = query_rows[at_k]
        k0, k1 = (fresh_key_all[at_s, t].astype(F32)[at_k : at_k + 1] for t in range(2))
        v0, v1 = (fresh_value_all[at_s, t].astype(F32)[at_k : at_k + 1] for t in range(2))
        k = keys_full[prompt].reshape(512, HD)
        v = values_full[prompt].reshape(512, HD)
        scores = lax.dot_general(
            qf.astype(BF16), k, (((1,), (1,)), ((), ())), preferred_element_type=F32
        ) * scale
        n0 = jnp.sum(qf * k0, axis=1, keepdims=True) * scale
        n1 = jnp.sum(qf * k1, axis=1, keepdims=True) * scale
        kept = column < live
        scores = jnp.where(kept, scores, HIDDEN)
        n1 = jnp.where(later, n1, HIDDEN)
        peak = jnp.maximum(jnp.max(scores, axis=1, keepdims=True), jnp.maximum(n0, n1))
        mass = jnp.where(kept, jnp.exp(scores - peak), 0.0)
        m0 = jnp.exp(n0 - peak)
        m1 = jnp.where(later, jnp.exp(n1 - peak), 0.0)
        total = jnp.sum(mass, axis=1, keepdims=True) + m0 + m1
        weighted = jnp.dot(mass.astype(BF16), v, preferred_element_type=F32)
        weighted += m0.astype(BF16).astype(F32) * v0
        weighted += m1.astype(BF16).astype(F32) * v1
        return jnp.where(inside, weighted / total, 0.0)

    def attend_section(at_s, carry):
        for t in range(2):
            x = query_all[at_s, t].astype(F32)
            for g in range(GROUP):
                row = (g // 4) * 8 + t * 4 + g % 4
                for k in range(4):
                    query_rows[k, row : row + 1, :] = x[k : k + 1, g * HD : g * HD + HD]
        for pair in range(2):
            first, second = attend(at_s, pair * 2), attend(at_s, pair * 2 + 1)
            for to_b in range(2):
                cut = slice(to_b * 8, to_b * 8 + 8)
                rows_send[at_s, to_b, pair] = jnp.concatenate(
                    (first[cut], second[cut]), axis=0
                ).astype(BF16)
        return carry

    lax.fori_loop(0, 8, attend_section, 0)

    def send_rows(to_s, to_b):
        pltpu.make_async_remote_copy(
            src_ref=rows_send.at[to_s, to_b],
            dst_ref=rows_land.at[s, b],
            send_sem=rows_send_sem,
            recv_sem=rows_recv_sem,
            device_id=(to_s, h, to_b),
            device_id_type=MESH,
        ).start()

    def send_rows_step(step, carry):
        to_s = lax.rem(s + step, 8)
        send_rows(to_s, b)
        send_rows(to_s, other)
        return carry

    lax.fori_loop(1, 8, send_rows_step, 0)
    send_rows(s, other)
    pltpu.make_async_copy(rows_send.at[s, b], rows_land.at[s, b], rows_recv_sem).start()

    slots = [slot_order[s * 4 + k] for k in range(4)]
    lives = [lengths[slot] for slot in slots]
    position = (h * 2 + b) * BLOCK + lax.broadcasted_iota(jnp.int32, (BLOCK, HD), 0)
    fresh[0].wait()
    fresh[1].wait()

    def settle(block, n, from_s, from_h):
        new, out = ((fresh_keys, keys_cache), (fresh_values, values_cache))[n]
        cut = pl.ds(pl.multiple_of(from_h * HD, HD), HD)
        placed = [new[t, from_s, :, cut].astype(F32) for t in range(2)]
        for k in range(4):
            rows = jnp.where(position < lives[k], block[k].astype(F32), 0.0)
            for t in range(2):
                rows = jnp.where(position == lives[k] + t, placed[t][k : k + 1], rows)
            out[from_s, k, :, cut] = rows.astype(BF16)

    def assemble_rows():
        pltpu.make_async_copy(rows_land, rows_land, rows_recv_sem).wait()
        owners = [lax.div(slot, 16) for slot in slots]

        def assemble(l, carry):
            picked = []
            for k in range(4):
                part = slice((k % 2) * 8, (k % 2) * 8 + 8)
                first, second = (rows_land[l, n, k // 2].astype(F32)[part] for n in range(2))
                picked.append(jnp.where(owners[k] == 0, first, second))
            for t in range(2):
                attention[t, l] = jnp.concatenate(
                    [
                        jnp.concatenate([rows[t * 4 + g : t * 4 + g + 1] for rows in picked], axis=0)
                        for g in range(4)
                    ],
                    axis=1,
                ).astype(BF16)
            return carry

        lax.fori_loop(0, 8, assemble, 0)

    for n, (_, packed, landed) in enumerate(bulk):
        settle(packed.at[s * 8 + h], n, s, h)
        for piece in range(8):
            if n == 1 and piece == 6:
                assemble_rows()
            blocks = landed.at[pl.ds(0, 7 if piece == 7 else 8)]
            pltpu.make_async_copy(blocks, blocks, bulk_recv.at[n, piece]).wait()
            from_h = head_at(piece, -sign, h)

            def settle_one(step, carry):
                from_s = section_at(step, -sign, s)
                settle(landed.at[from_s * 8 + from_h], n, from_s, from_h)
                return carry

            lax.fori_loop(1 if piece == 7 else 0, 8, settle_one, 0)

    pltpu.make_async_copy(keys_full, keys_full, swap_send).wait()
    for n, whole in enumerate((query_all, fresh_key_all, fresh_value_all)):
        seven = whole.at[pl.ds(0, 7)]
        pltpu.make_async_copy(seven, seven, small_send.at[n]).wait()
    for n, (_, packed, _) in enumerate(bulk):
        sent = packed.at[pl.ds(0, 63)]
        pltpu.make_async_copy(sent, sent, bulk_send.at[n]).wait()
    seven, one = rows_send.at[pl.ds(0, 7)], rows_send.at[0, 0]
    pltpu.make_async_copy(seven, seven, rows_send_sem).wait()
    pltpu.make_async_copy(one, one, rows_send_sem).wait()


def hand_out(attention, keys, values, attention_out, keys_out, values_out, sem):
    copies = [pltpu.make_async_copy(attention, attention_out, sem.at[16])]
    for n, (src, dst) in enumerate(((keys, keys_out), (values, values_out))):
        copies += [pltpu.make_async_copy(src.at[l], dst.at[l], sem.at[n * 8 + l]) for l in range(8)]
    for copy in copies:
        copy.start()
    for copy in copies:
        copy.wait()


def body(keys_prefill, values_prefill, lengths, slot_order, queries, new_keys, new_values):
    keys = keys_prefill.reshape(16, 8, 2, BLOCK, HD)
    values = values_prefill.reshape(16, 8, 2, BLOCK, HD)
    any_spec = pl.BlockSpec(memory_space=pl.ANY)
    hbm_spec = pl.BlockSpec(memory_space=pltpu.HBM)
    vmem_spec = pl.BlockSpec(memory_space=pltpu.VMEM)
    dma, vmem = pltpu.SemaphoreType.DMA, pltpu.VMEM
    rows_shape, cache_shape = (2, 8, 4, 4 * HD), (8, 4, BLOCK, KVH * HD)
    blocks = (64, 4, BLOCK, HD)

    def in_hbm(array):
        return pltpu.with_memory_space_constraint(array, pltpu.HBM)

    held = pl.pallas_call(
        relay,
        out_shape=(vmem(rows_shape, BF16), vmem(cache_shape, BF16), vmem(cache_shape, BF16)),
        in_specs=[hbm_spec] * 7,
        out_specs=(vmem_spec,) * 3,
        scratch_shapes=[
            [vmem((32, BLOCK, HD), BF16)] * 8, [vmem((32, BLOCK, HD), BF16)] * 8,
            vmem((16, 8, 2, BLOCK, HD), BF16), vmem((16, 8, 2, BLOCK, HD), BF16),
            vmem(blocks, BF16), vmem(blocks, BF16), vmem(blocks, BF16), vmem(blocks, BF16),
            vmem((2, 8, 4, KVH * HD), BF16), vmem((2, 8, 4, KVH * HD), BF16),
            vmem((8, 2, 4, GROUP * HD), BF16), vmem((4, 16, HD), F32),
            vmem((8, 2, 4, HD), BF16), vmem((8, 2, 4, HD), BF16),
            vmem((8, 2, 2, 16, HD), BF16), vmem((8, 2, 2, 16, HD), BF16),
            pltpu.SMEM((32,), jnp.int32), pltpu.SMEM((32,), jnp.int32),
            dma((2, 8)), dma, dma((2, 8)), dma((2,)), dma((2,)), dma((3,)), dma((3,)),
            dma((2,)), dma((2, 8)), dma, dma, dma((2,)),
        ],
        compiler_params=pltpu.CompilerParams(
            collective_id=0, has_side_effects=True, vmem_limit_bytes=48 * 2**20
        ),
        name="relay",
    )(*(in_hbm(x) for x in (slot_order, lengths, keys, values, queries, new_keys, new_values)))
    return pl.pallas_call(
        hand_out,
        out_shape=tuple(jax.ShapeDtypeStruct(shape, BF16) for shape in (rows_shape, cache_shape, cache_shape)),
        in_specs=[vmem_spec] * 3,
        out_specs=(any_spec,) * 3,
        scratch_shapes=[dma((17,))],
        compiler_params=pltpu.CompilerParams(vmem_limit_bytes=8 * 2**20),
        name="hand_out",
    )(*(pltpu.with_memory_space_constraint(x, pltpu.VMEM) for x in held))


def solution(mesh):
    in_specs = (
        P("section", "batch", None, "head"),
        P("section", "batch", None, "head"),
        P(),
        P(),
        P(None, None, "section", None),
        P(None, None, "section", None),
        P(None, None, "section", None),
    )
    out_specs = (
        P(None, None, "section", ("head", "batch")),
        P(None, "section", ("head", "batch"), None),
        P(None, "section", ("head", "batch"), None),
    )
    return jax.shard_map(body, mesh=mesh, in_specs=in_specs, out_specs=out_specs, check_vma=False)
```

```python
import jax
import jax.numpy as jnp
from jax import lax
from jax.experimental import pallas as pl
from jax.experimental.pallas import tpu as pltpu
from jax.sharding import PartitionSpec as P

KVH = 8
HD = 128
GROUP = 8
BLOCK = 32
MESH = pl.DeviceIdType.MESH
HIDDEN = -1e30
BF16, F32 = jnp.bfloat16, jnp.float32


PIECES = ((2, 1), (2, 0), (1, 0), (3, 0), (1, 1), (3, 1), (0, 1), (0, 0))


def has_tie(offset):
    return 2 in offset


OFFSETS = [(dx, dy, dz) for dz, low in PIECES for dy in (low, low + 2) for dx in (1, 3, 2, 0)]
STOPS = [o for o in OFFSETS if has_tie(o)]
DIRECT = [o for o in OFFSETS if not has_tie(o) and any(o)]
PER_SECTION = -(-len(STOPS) // 8)
DIRECT_EARLY = 10


def coordinates(offset, sign, s, h):
    dx, dy, dz = offset
    x = lax.rem(lax.div(s, 2) + sign * dx + 4, 4)
    y = lax.rem(lax.rem(s, 2) * 2 + lax.rem(h, 2) + sign * dy + 4, 4)
    z = lax.rem(lax.div(h, 2) + sign * dz + 4, 4)
    return x * 2 + lax.div(y, 2), z * 2 + lax.rem(y, 2)


def first_leg(offset):
    return tuple(d // 2 * (1 - d % 2) if isinstance(d, int) else lax.div(d, 2) * (1 - lax.rem(d, 2)) for d in offset)


def pack_word(offsets):
    return sum((dx + 4 * dy + 16 * dz) * 64**n for n, (dx, dy, dz) in enumerate(offsets))


def from_word(word):
    return lax.rem(word, 4), lax.rem(lax.div(word, 4), 4), lax.rem(lax.div(word, 16), 4)


def relay(
    slot_order_hbm, lengths_hbm, keys, values, queries, new_keys, new_values,
    attention, keys_cache, values_cache,
    gathered, full, packed, landed, stopped,
    fresh_rows, query_all, query_rows, fresh_all, slot_rows, rows_send, rows_land,
    slot_order, lengths,
    piece_sem, swap_send, full_sem, fresh_sem, small_send, small_recv,
    bulk_send, bulk_recv, stop_send, stop_recv, rows_send_sem, rows_recv_sem, scalar_sem,
):
    s, h, b = lax.axis_index("section"), lax.axis_index("head"), lax.axis_index("batch")
    other = 1 - b
    sign = 1 - 2 * b
    mine = pl.ds(b * 16, 16)
    caches = (keys, values)

    def remote(src, dst, send_sem, recv_sem, to):
        return pltpu.make_async_remote_copy(
            src_ref=src, dst_ref=dst, send_sem=send_sem, recv_sem=recv_sem,
            device_id=to, device_id_type=MESH,
        )

    def wait_for(ref, sem):
        pltpu.make_async_copy(ref, ref, sem).wait()

    def head_at(piece, sign):
        dz, dy = PIECES[piece]
        return coordinates((0, dy, dz), sign, s, h)[1]

    scalars = [
        pltpu.make_async_copy(slot_order_hbm, slot_order, scalar_sem.at[0]),
        pltpu.make_async_copy(lengths_hbm, lengths, scalar_sem.at[1]),
    ]
    for copy in scalars:
        copy.start()
    for piece in range(8):
        for n in range(2):
            pltpu.make_async_copy(
                caches[n].at[:, head_at(piece, sign), b], gathered[piece].at[n, mine], piece_sem.at[piece]
            ).start()
    whole = [pltpu.make_async_copy(caches[n], full.at[n], full_sem.at[n]) for n in range(2)]
    fresh = [
        pltpu.make_async_copy(src, fresh_rows.at[n], fresh_sem.at[n])
        for n, src in enumerate((new_keys, new_values))
    ]
    for copy in whole + fresh:
        copy.start()

    barrier = pltpu.get_barrier_semaphore()

    def greet_other(step, carry):
        pl.semaphore_signal(
            barrier, inc=1, device_id=(lax.rem(s + step, 8), h, other), device_id_type=MESH
        )
        return carry

    def greet(step, carry):
        to_s, to_h = lax.rem(s + lax.div(step, 8), 8), lax.rem(h + lax.rem(step, 8), 8)
        pl.semaphore_signal(barrier, inc=1, device_id=(to_s, to_h, b), device_id_type=MESH)
        return carry

    lax.fori_loop(0, 8, greet_other, 0)
    lax.fori_loop(1, 64, greet, 0)
    pl.semaphore_wait(barrier, 71)

    for piece in range(8):
        for n in range(2):
            remote(
                caches[n].at[:, head_at(piece, -sign), other], gathered[piece].at[n, mine],
                swap_send, piece_sem.at[piece], (s, h, other),
            ).start()

    head_rows = pl.ds(pl.multiple_of(h * GROUP * HD, GROUP * HD), GROUP * HD)
    head_cols = pl.ds(pl.multiple_of(h * HD, HD), HD)

    def small_pieces(to_s):
        return (
            (queries.at[:, to_s, :, head_rows], query_all.at[s]),
            (new_keys.at[:, to_s, :, head_cols], fresh_all.at[0, s]),
            (new_values.at[:, to_s, :, head_cols], fresh_all.at[1, s]),
        )

    def send_small(step, carry):
        to_s = lax.rem(s + step, 8)
        for n, (src, dst) in enumerate(small_pieces(to_s)):
            remote(src, dst, small_send.at[n], small_recv.at[n], (to_s, h, b)).start()
        return carry

    lax.fori_loop(1, 8, send_small, 0)
    for n, (src, dst) in enumerate(small_pieces(s)):
        pltpu.make_async_copy(src, dst, small_recv.at[n]).start()

    def deliver(src, offset, legs_left, send_sem, from_place):
        to_s, to_h = coordinates(legs_left, sign, s, h)
        _, dy, dz = offset
        remote(
            src(to_s * 8 + to_h), landed.at[from_place], send_sem,
            bulk_recv.at[dz * 2 + lax.rem(dy, 2)], (to_s, to_h, b),
        ).start()

    def send_direct(offset):
        offset = tuple(jnp.int32(d) if isinstance(d, int) else d for d in offset)
        deliver(lambda place: packed.at[place], offset, offset, bulk_send, s * 8 + h)

    scalars[0].wait()
    scalars[1].wait()
    for piece, (dz, low) in enumerate(PIECES):
        at_h = head_at(piece, sign)
        wait_for(gathered[piece], piece_sem.at[piece])

        def pack(at_s, carry):
            for k in range(4):
                slot = slot_order[at_s * 4 + k]
                for n in range(2):
                    packed[at_s * 8 + at_h, n, k] = gathered[piece][n, slot]
            return carry

        lax.fori_loop(0, 8, pack, 0)
        for at, offset in enumerate(STOPS):
            if offset[2] == dz and offset[1] % 2 == low:
                owner_s, owner_h = coordinates(offset, sign, s, h)
                to_s, to_h = coordinates(first_leg(offset), sign, s, h)
                remote(
                    packed.at[owner_s * 8 + owner_h], stopped.at[at], bulk_send, stop_recv.at[at],
                    (to_s, to_h, b),
                ).start()
    for offset in DIRECT[:DIRECT_EARLY]:
        send_direct(offset)

    for n, part in enumerate((query_all, fresh_all.at[0], fresh_all.at[1])):
        wait_for(part, small_recv.at[n])
    whole[0].wait()
    whole[1].wait()

    later = lax.rem(lax.div(lax.broadcasted_iota(jnp.int32, (16, 1), 0), 4), 2) == 1
    column = lax.broadcasted_iota(jnp.int32, (16, 512), 1)
    row4 = lax.broadcasted_iota(jnp.int32, (4, HD), 0)
    scale = HD ** -0.5

    def attend(at_s, at_k):
        slot = slot_order[at_s * 4 + at_k]
        prompt = slot - b * 16
        inside = jnp.logical_and(prompt >= 0, prompt < 16)
        prompt = jnp.clip(prompt, 0, 15)
        live = lengths[slot]
        qf = query_rows[at_k]

        def fresh_row(n, t):
            return jnp.sum(
                jnp.where(row4 == at_k, fresh_all[n, at_s, t].astype(F32), 0.0), axis=0, keepdims=True
            )

        k0, k1, v0, v1 = (fresh_row(n, t) for n in range(2) for t in range(2))
        k = full[0, prompt].reshape(512, HD)
        v = full[1, prompt].reshape(512, HD)
        scores = lax.dot_general(
            qf.astype(BF16), k, (((1,), (1,)), ((), ())), preferred_element_type=F32
        ) * scale
        n0 = jnp.sum(qf * k0, axis=1, keepdims=True) * scale
        n1 = jnp.sum(qf * k1, axis=1, keepdims=True) * scale
        kept = column < live
        scores = jnp.where(kept, scores, HIDDEN)
        n1 = jnp.where(later, n1, HIDDEN)
        peak = jnp.maximum(jnp.max(scores, axis=1, keepdims=True), jnp.maximum(n0, n1))
        mass = jnp.where(kept, jnp.exp(scores - peak), 0.0)
        m0 = jnp.exp(n0 - peak)
        m1 = jnp.where(later, jnp.exp(n1 - peak), 0.0)
        total = jnp.sum(mass, axis=1, keepdims=True) + m0 + m1
        weighted = jnp.dot(mass.astype(BF16), v, preferred_element_type=F32)
        weighted += m0.astype(BF16).astype(F32) * v0
        weighted += m1.astype(BF16).astype(F32) * v1
        return jnp.where(inside, weighted / total, 0.0)

    def pass_on(at, word):
        offset = from_word(word)
        leg = first_leg(offset)
        rest = tuple(d - m for d, m in zip(offset, leg))
        from_s, from_h = coordinates(leg, -sign, s, h)
        wait_for(stopped.at[at], stop_recv.at[at])
        deliver(lambda _: stopped.at[at], offset, rest, stop_send, from_s * 8 + from_h)

    late = DIRECT[DIRECT_EARLY:]
    for at_s in range(8):
        for t in range(2):
            x = query_all[at_s, t].astype(F32)
            for g in range(GROUP):
                row = (g // 4) * 8 + t * 4 + g % 4
                for k in range(4):
                    query_rows[k, row : row + 1, :] = x[k : k + 1, g * HD : g * HD + HD]
        stops = STOPS[at_s * PER_SECTION : (at_s + 1) * PER_SECTION]
        beside = min(4, len(stops))

        def slot_step(k, word):
            pass_on(at_s * PER_SECTION + k, word)
            slot_rows[k] = attend(at_s, k)
            return lax.div(word, 64)

        lax.fori_loop(0, beside, slot_step, jnp.int32(pack_word(stops[:beside])))
        for k in range(beside, 4):
            slot_rows[k] = attend(at_s, k)
        for n in range(beside, len(stops)):
            pass_on(at_s * PER_SECTION + n, jnp.int32(pack_word(stops[n : n + 1])))
        for offset in late[at_s::8]:
            send_direct(offset)
        for pair in range(2):
            first, second = slot_rows[pair * 2], slot_rows[pair * 2 + 1]
            for to_b in range(2):
                cut = slice(to_b * 8, to_b * 8 + 8)
                rows_send[at_s, to_b, pair] = jnp.concatenate(
                    (first[cut], second[cut]), axis=0
                ).astype(BF16)

    def send_rows(to_s, to_b):
        remote(
            rows_send.at[to_s, to_b], rows_land.at[s, b], rows_send_sem, rows_recv_sem, (to_s, h, to_b)
        ).start()

    def send_rows_step(step, carry):
        to_s = lax.rem(s + step, 8)
        send_rows(to_s, b)
        send_rows(to_s, other)
        return carry

    lax.fori_loop(1, 8, send_rows_step, 0)
    send_rows(s, other)
    pltpu.make_async_copy(rows_send.at[s, b], rows_land.at[s, b], rows_recv_sem).start()

    slots = [slot_order[s * 4 + k] for k in range(4)]
    lives = [lengths[slot] for slot in slots]
    position = (h * 2 + b) * BLOCK + lax.broadcasted_iota(jnp.int32, (BLOCK, HD), 0)
    fresh[0].wait()
    fresh[1].wait()

    def settle(block, from_s, from_h):
        cut = pl.ds(pl.multiple_of(from_h * HD, HD), HD)
        for n, out in enumerate((keys_cache, values_cache)):
            placed = [fresh_rows[n, t, from_s, :, cut].astype(F32) for t in range(2)]
            for k in range(4):
                rows = jnp.where(position < lives[k], block[n, k].astype(F32), 0.0)
                for t in range(2):
                    rows = jnp.where(position == lives[k] + t, placed[t][k : k + 1], rows)
                out[from_s, k, :, cut] = rows.astype(BF16)

    owners = [lax.div(slot, 16) for slot in slots]

    def assemble(l, carry):
        picked = []
        for k in range(4):
            part = slice((k % 2) * 8, (k % 2) * 8 + 8)
            first, second = (rows_land[l, n, k // 2].astype(F32)[part] for n in range(2))
            picked.append(jnp.where(owners[k] == 0, first, second))
        for t in range(2):
            attention[t, l] = jnp.concatenate(
                [
                    jnp.concatenate([rows[t * 4 + g : t * 4 + g + 1] for rows in picked], axis=0)
                    for g in range(4)
                ],
                axis=1,
            ).astype(BF16)
        return carry

    settle(packed.at[s * 8 + h], s, h)
    for piece, (dz, low) in enumerate(PIECES):
        if piece == 7:
            wait_for(rows_land, rows_recv_sem)
            lax.fori_loop(0, 8, assemble, 0)
        blocks = 7 if piece == 7 else 8
        wait_for(landed.at[pl.ds(0, blocks)], bulk_recv.at[dz * 2 + low])

        def settle_one(step, carry):
            offset = (lax.rem(step, 4), low + 2 * lax.div(step, 4), dz)
            from_s, from_h = coordinates(offset, -sign, s, h)
            settle(landed.at[from_s * 8 + from_h], from_s, from_h)
            return carry

        lax.fori_loop(8 - blocks, 8, settle_one, 0)

    wait_for(full.at[0], swap_send)
    for n, part in enumerate((query_all, fresh_all.at[0], fresh_all.at[1])):
        wait_for(part.at[pl.ds(0, 7)], small_send.at[n])
    wait_for(packed.at[pl.ds(0, 63)], bulk_send)
    wait_for(stopped, stop_send)
    wait_for(rows_send.at[pl.ds(0, 7)], rows_send_sem)
    wait_for(rows_send.at[0, 0], rows_send_sem)


def hand_out(attention, keys, values, attention_out, keys_out, values_out, sem):
    copies = [pltpu.make_async_copy(attention, attention_out, sem.at[16])]
    for n, (src, dst) in enumerate(((keys, keys_out), (values, values_out))):
        copies += [pltpu.make_async_copy(src.at[l], dst.at[l], sem.at[n * 8 + l]) for l in range(8)]
    for copy in copies:
        copy.start()
    for copy in copies:
        copy.wait()


def body(keys_prefill, values_prefill, lengths, slot_order, queries, new_keys, new_values):
    keys = keys_prefill.reshape(16, 8, 2, BLOCK, HD)
    values = values_prefill.reshape(16, 8, 2, BLOCK, HD)
    any_spec = pl.BlockSpec(memory_space=pl.ANY)
    hbm_spec = pl.BlockSpec(memory_space=pltpu.HBM)
    vmem_spec = pl.BlockSpec(memory_space=pltpu.VMEM)
    dma, vmem = pltpu.SemaphoreType.DMA, pltpu.VMEM
    rows_shape, cache_shape = (2, 8, 4, 4 * HD), (8, 4, BLOCK, KVH * HD)

    def in_hbm(array):
        return pltpu.with_memory_space_constraint(array, pltpu.HBM)

    held = pl.pallas_call(
        relay,
        out_shape=(vmem(rows_shape, BF16), vmem(cache_shape, BF16), vmem(cache_shape, BF16)),
        in_specs=[hbm_spec] * 7,
        out_specs=(vmem_spec,) * 3,
        scratch_shapes=[
            [vmem((2, 32, BLOCK, HD), BF16)] * 8, vmem((2, 16, 8, 2, BLOCK, HD), BF16),
            vmem((64, 2, 4, BLOCK, HD), BF16), vmem((64, 2, 4, BLOCK, HD), BF16),
            vmem((len(STOPS), 2, 4, BLOCK, HD), BF16),
            vmem((2, 2, 8, 4, KVH * HD), BF16), vmem((8, 2, 4, GROUP * HD), BF16), vmem((4, 16, HD), F32),
            vmem((2, 8, 2, 4, HD), BF16), vmem((4, 16, HD), F32),
            vmem((8, 2, 2, 16, HD), BF16), vmem((8, 2, 2, 16, HD), BF16),
            pltpu.SMEM((32,), jnp.int32), pltpu.SMEM((32,), jnp.int32),
            dma((8,)), dma, dma((2,)), dma((2,)), dma((3,)), dma((3,)),
            dma, dma((8,)), dma, dma((len(STOPS),)), dma, dma, dma((2,)),
        ],
        compiler_params=pltpu.CompilerParams(
            collective_id=0, has_side_effects=True, vmem_limit_bytes=48 * 2**20
        ),
        name="relay",
    )(*(in_hbm(x) for x in (slot_order, lengths, keys, values, queries, new_keys, new_values)))
    return pl.pallas_call(
        hand_out,
        out_shape=tuple(jax.ShapeDtypeStruct(shape, BF16) for shape in (rows_shape, cache_shape, cache_shape)),
        in_specs=[vmem_spec] * 3,
        out_specs=(any_spec,) * 3,
        scratch_shapes=[dma((17,))],
        compiler_params=pltpu.CompilerParams(vmem_limit_bytes=8 * 2**20),
        name="hand_out",
    )(*(pltpu.with_memory_space_constraint(x, pltpu.VMEM) for x in held))


def solution(mesh):
    in_specs = (
        P("section", "batch", None, "head"),
        P("section", "batch", None, "head"),
        P(),
        P(),
        P(None, None, "section", None),
        P(None, None, "section", None),
        P(None, None, "section", None),
    )
    out_specs = (
        P(None, None, "section", ("head", "batch")),
        P(None, "section", ("head", "batch"), None),
        P(None, "section", ("head", "batch"), None),
    )
    return jax.shard_map(body, mesh=mesh, in_specs=in_specs, out_specs=out_specs, check_vma=False)
```

```python
import jax
import jax.numpy as jnp
from jax import lax
from jax.experimental import pallas as pl
from jax.experimental.pallas import tpu as pltpu
from jax.sharding import PartitionSpec as P

KVH = 8
HD = 128
GROUP = 8
BLOCK = 32
MESH = pl.DeviceIdType.MESH
HIDDEN = -1e30
BF16, F32 = jnp.bfloat16, jnp.float32


def turn(offset):
    return lax.rem(offset * 4 - 1, 63) + 1


def static_turn(offset):
    return (offset * 4 - 1) % 63 + 1


def digits(offset):
    return offset % 4, offset // 4 % 4, offset // 16


def hops(offset):
    return sum(min(d, 4 - d) for d in digits(offset))


def orbits():
    seen, out, fixed = set(), [], []
    for offset in range(1, 64):
        if offset not in seen:
            ring = {offset, static_turn(offset), static_turn(static_turn(offset))}
            seen |= ring
            (out if len(ring) == 3 else fixed).append(offset)
    return out, fixed


def grouped():
    reps, fixed = orbits()
    odd = [o for o in reps if all(d % 2 for d in digits(o))]
    rest = sorted((o for o in reps if o not in odd), key=lambda o: -hops(o))
    groups = [(odd, [o for o in fixed if all(d % 2 for d in digits(o))])]
    groups += [([rest[g], rest[11 - g], rest[12 + g]], []) for g in range(6)]
    groups[3][1].append(42)
    return groups


GROUPS = grouped()
SIZES = [3 * len(reps) + len(lone) for reps, lone in GROUPS]
PIECES = ((1, 1), (3, 1), (2, 1), (0, 1), (1, 0), (3, 0), (2, 0), (0, 0))


def coordinates(offset, sign, s, h):
    dx, dy, dz = lax.rem(offset, 4), lax.rem(lax.div(offset, 4), 4), lax.div(offset, 16)
    x = lax.rem(lax.div(s, 2) + sign * dx + 4, 4)
    y = lax.rem(lax.rem(s, 2) * 2 + lax.rem(h, 2) + sign * dy + 4, 4)
    z = lax.rem(lax.div(h, 2) + sign * dz + 4, 4)
    return x * 2 + lax.div(y, 2), z * 2 + lax.rem(y, 2)


def head_at(piece, sign, h):
    dz, dy = PIECES[piece]
    z = lax.rem(lax.div(h, 2) + sign * dz + 4, 4)
    return z * 2 + lax.rem(lax.rem(h, 2) + dy, 2)


def each_of(group, do):
    reps, lone = GROUPS[group]
    for offset in lone:
        do(jnp.int32(offset))

    def rep_step(_, word):
        def turn_step(_, offset):
            do(offset)
            return turn(offset)

        lax.fori_loop(0, 3, turn_step, lax.rem(word, 64))
        return lax.div(word, 64)

    lax.fori_loop(0, len(reps), rep_step, jnp.int32(sum(rep * 64**n for n, rep in enumerate(reps))))


def relay(
    slot_order_hbm, lengths_hbm, keys, values, queries, new_keys, new_values,
    attention, keys_cache, values_cache,
    keys_all, values_all, keys_full, values_full, keys_send, values_send, keys_land, values_land,
    fresh_keys, fresh_values, query_all, query_rows, fresh_key_all, fresh_value_all, rows_send, rows_land,
    slot_order, lengths,
    own_sem, swap_send, swap_recv, full_sem, fresh_sem, small_send, small_recv,
    bulk_send, bulk_recv, rows_send_sem, rows_recv_sem, scalar_sem,
):
    s, h, b = lax.axis_index("section"), lax.axis_index("head"), lax.axis_index("batch")
    other = 1 - b
    sign = 1 - 2 * b
    mine = pl.ds(b * 16, 16)
    inputs = ((keys, keys_all, keys_full), (values, values_all, values_full))

    full = [pltpu.make_async_copy(src, dst, full_sem.at[n]) for n, (src, _, dst) in enumerate(inputs)]
    own = [
        [
            pltpu.make_async_copy(
                src.at[:, head_at(piece, sign, h), b], dst[piece].at[mine], own_sem.at[n, piece]
            )
            for piece in range(8)
        ]
        for n, (src, dst, _) in enumerate(inputs)
    ]
    fresh = [
        pltpu.make_async_copy(new_keys, fresh_keys, fresh_sem.at[0]),
        pltpu.make_async_copy(new_values, fresh_values, fresh_sem.at[1]),
    ]
    scalars = [
        pltpu.make_async_copy(slot_order_hbm, slot_order, scalar_sem.at[0]),
        pltpu.make_async_copy(lengths_hbm, lengths, scalar_sem.at[1]),
    ]

    def swap(n, piece, receiver_sign):
        src, dst, _ = inputs[n]
        at_h = head_at(piece, receiver_sign, h)
        return pltpu.make_async_remote_copy(
            src_ref=src.at[:, at_h, other],
            dst_ref=dst[piece].at[mine],
            send_sem=swap_send,
            recv_sem=swap_recv.at[n, piece],
            device_id=(s, h, other),
            device_id_type=MESH,
        )

    barrier = pltpu.get_barrier_semaphore()

    def greet(to_s, to_h, to_b):
        pl.semaphore_signal(barrier, inc=1, device_id=(to_s, to_h, to_b), device_id_type=MESH)

    def greet_section(step, carry):
        to_s = lax.rem(s + step, 8)
        greet(to_s, h, other)
        for at in range(8):
            greet(to_s, lax.rem(h + at, 8), b)
        return carry

    greet(s, h, other)
    for at in range(1, 8):
        greet(s, lax.rem(h + at, 8), b)
    lax.fori_loop(1, 8, greet_section, 0)
    for copy in scalars + own[0] + own[1] + fresh + full:
        copy.start()
    pl.semaphore_wait(barrier, 71)

    for n in range(2):
        for piece in range(8):
            swap(n, piece, -sign).start()

    head_rows = pl.ds(pl.multiple_of(h * GROUP * HD, GROUP * HD), GROUP * HD)
    head_cols = pl.ds(pl.multiple_of(h * HD, HD), HD)

    def small_pieces(to_s):
        return (
            (queries.at[:, to_s, :, head_rows], query_all.at[s]),
            (new_keys.at[:, to_s, :, head_cols], fresh_key_all.at[s]),
            (new_values.at[:, to_s, :, head_cols], fresh_value_all.at[s]),
        )

    def send_small(step, carry):
        to_s = lax.rem(s + step, 8)
        for n, (src, dst) in enumerate(small_pieces(to_s)):
            pltpu.make_async_remote_copy(
                src_ref=src,
                dst_ref=dst,
                send_sem=small_send.at[n],
                recv_sem=small_recv.at[n],
                device_id=(to_s, h, b),
                device_id_type=MESH,
            ).start()
        return carry

    lax.fori_loop(1, 8, send_small, 0)
    for n, (src, dst) in enumerate(small_pieces(s)):
        pltpu.make_async_copy(src, dst, small_recv.at[n]).start()

    bulk = ((keys_all, keys_send, keys_land), (values_all, values_send, values_land))
    scalars[0].wait()
    scalars[1].wait()
    for n, (gathered, packed, landed) in enumerate(bulk):

        def send(group):
            def send_one(offset):
                to_s, to_h = coordinates(offset, sign, s, h)
                pltpu.make_async_remote_copy(
                    src_ref=packed.at[to_s * 8 + to_h],
                    dst_ref=landed.at[s * 8 + h],
                    send_sem=bulk_send.at[n],
                    recv_sem=bulk_recv.at[n, group],
                    device_id=(to_s, to_h, b),
                    device_id_type=MESH,
                ).start()

            each_of(group, send_one)

        for piece in range(8):
            own[n][piece].wait()
            swap(n, piece, sign).wait_recv()
            at_h = head_at(piece, sign, h)

            def pack(at_s, carry):
                for k in range(4):
                    packed[at_s * 8 + at_h, k] = gathered[piece][slot_order[at_s * 4 + k]]
                return carry

            lax.fori_loop(0, 8, pack, 0)
            if piece == 1:
                send(0)
        for group in range(1, 7):
            send(group)

    for n, whole in enumerate((query_all, fresh_key_all, fresh_value_all)):
        pltpu.make_async_copy(whole, whole, small_recv.at[n]).wait()
    full[0].wait()
    full[1].wait()

    later = lax.rem(lax.div(lax.broadcasted_iota(jnp.int32, (16, 1), 0), 4), 2) == 1
    column = lax.broadcasted_iota(jnp.int32, (16, 512), 1)
    scale = HD ** -0.5

    def attend(at_s, at_k):
        slot = slot_order[at_s * 4 + at_k]
        prompt = slot - b * 16
        inside = jnp.logical_and(prompt >= 0, prompt < 16)
        prompt = jnp.clip(prompt, 0, 15)
        live = lengths[slot]
        qf = query_rows[at_k]
        k0, k1 = (fresh_key_all[at_s, t].astype(F32)[at_k : at_k + 1] for t in range(2))
        v0, v1 = (fresh_value_all[at_s, t].astype(F32)[at_k : at_k + 1] for t in range(2))
        k = keys_full[prompt].reshape(512, HD)
        v = values_full[prompt].reshape(512, HD)
        scores = lax.dot_general(
            qf.astype(BF16), k, (((1,), (1,)), ((), ())), preferred_element_type=F32
        ) * scale
        n0 = jnp.sum(qf * k0, axis=1, keepdims=True) * scale
        n1 = jnp.sum(qf * k1, axis=1, keepdims=True) * scale
        kept = column < live
        scores = jnp.where(kept, scores, HIDDEN)
        n1 = jnp.where(later, n1, HIDDEN)
        peak = jnp.maximum(jnp.max(scores, axis=1, keepdims=True), jnp.maximum(n0, n1))
        mass = jnp.where(kept, jnp.exp(scores - peak), 0.0)
        m0 = jnp.exp(n0 - peak)
        m1 = jnp.where(later, jnp.exp(n1 - peak), 0.0)
        total = jnp.sum(mass, axis=1, keepdims=True) + m0 + m1
        weighted = jnp.dot(mass.astype(BF16), v, preferred_element_type=F32)
        weighted += m0.astype(BF16).astype(F32) * v0
        weighted += m1.astype(BF16).astype(F32) * v1
        return jnp.where(inside, weighted / total, 0.0)

    def attend_section(at_s, carry):
        for t in range(2):
            x = query_all[at_s, t].astype(F32)
            for g in range(GROUP):
                row = (g // 4) * 8 + t * 4 + g % 4
                for k in range(4):
                    query_rows[k, row : row + 1, :] = x[k : k + 1, g * HD : g * HD + HD]
        for pair in range(2):
            first, second = attend(at_s, pair * 2), attend(at_s, pair * 2 + 1)
            for to_b in range(2):
                cut = slice(to_b * 8, to_b * 8 + 8)
                rows_send[at_s, to_b, pair] = jnp.concatenate(
                    (first[cut], second[cut]), axis=0
                ).astype(BF16)
        return carry

    lax.fori_loop(0, 8, attend_section, 0)

    def send_rows(to_s, to_b):
        pltpu.make_async_remote_copy(
            src_ref=rows_send.at[to_s, to_b],
            dst_ref=rows_land.at[s, b],
            send_sem=rows_send_sem,
            recv_sem=rows_recv_sem,
            device_id=(to_s, h, to_b),
            device_id_type=MESH,
        ).start()

    def send_rows_step(step, carry):
        to_s = lax.rem(s + step, 8)
        send_rows(to_s, b)
        send_rows(to_s, other)
        return carry

    lax.fori_loop(1, 8, send_rows_step, 0)
    send_rows(s, other)
    pltpu.make_async_copy(rows_send.at[s, b], rows_land.at[s, b], rows_recv_sem).start()

    slots = [slot_order[s * 4 + k] for k in range(4)]
    lives = [lengths[slot] for slot in slots]
    position = (h * 2 + b) * BLOCK + lax.broadcasted_iota(jnp.int32, (BLOCK, HD), 0)
    fresh[0].wait()
    fresh[1].wait()

    def settle(block, n, from_s, from_h):
        new, out = ((fresh_keys, keys_cache), (fresh_values, values_cache))[n]
        cut = pl.ds(pl.multiple_of(from_h * HD, HD), HD)
        placed = [new[t, from_s, :, cut].astype(F32) for t in range(2)]
        for k in range(4):
            rows = jnp.where(position < lives[k], block[k].astype(F32), 0.0)
            for t in range(2):
                rows = jnp.where(position == lives[k] + t, placed[t][k : k + 1], rows)
            out[from_s, k, :, cut] = rows.astype(BF16)

    def assemble_rows():
        pltpu.make_async_copy(rows_land, rows_land, rows_recv_sem).wait()
        owners = [lax.div(slot, 16) for slot in slots]

        def assemble(l, carry):
            picked = []
            for k in range(4):
                part = slice((k % 2) * 8, (k % 2) * 8 + 8)
                first, second = (rows_land[l, n, k // 2].astype(F32)[part] for n in range(2))
                picked.append(jnp.where(owners[k] == 0, first, second))
            for t in range(2):
                attention[t, l] = jnp.concatenate(
                    [
                        jnp.concatenate([rows[t * 4 + g : t * 4 + g + 1] for rows in picked], axis=0)
                        for g in range(4)
                    ],
                    axis=1,
                ).astype(BF16)
            return carry

        lax.fori_loop(0, 8, assemble, 0)

    for n, (_, packed, landed) in enumerate(bulk):
        settle(packed.at[s * 8 + h], n, s, h)
        for group in range(7):
            if n == 1 and group == 6:
                assemble_rows()
            blocks = landed.at[pl.ds(0, SIZES[group])]
            pltpu.make_async_copy(blocks, blocks, bulk_recv.at[n, group]).wait()

            def settle_one(offset):
                from_s, from_h = coordinates(offset, -sign, s, h)
                settle(landed.at[from_s * 8 + from_h], n, from_s, from_h)

            each_of(group, settle_one)

    pltpu.make_async_copy(keys_full, keys_full, swap_send).wait()
    for n, whole in enumerate((query_all, fresh_key_all, fresh_value_all)):
        seven = whole.at[pl.ds(0, 7)]
        pltpu.make_async_copy(seven, seven, small_send.at[n]).wait()
    for n, (_, packed, _) in enumerate(bulk):
        sent = packed.at[pl.ds(0, 63)]
        pltpu.make_async_copy(sent, sent, bulk_send.at[n]).wait()
    seven, one = rows_send.at[pl.ds(0, 7)], rows_send.at[0, 0]
    pltpu.make_async_copy(seven, seven, rows_send_sem).wait()
    pltpu.make_async_copy(one, one, rows_send_sem).wait()


def hand_out(attention, keys, values, attention_out, keys_out, values_out, sem):
    copies = [pltpu.make_async_copy(attention, attention_out, sem.at[16])]
    for n, (src, dst) in enumerate(((keys, keys_out), (values, values_out))):
        copies += [pltpu.make_async_copy(src.at[l], dst.at[l], sem.at[n * 8 + l]) for l in range(8)]
    for copy in copies:
        copy.start()
    for copy in copies:
        copy.wait()


def body(keys_prefill, values_prefill, lengths, slot_order, queries, new_keys, new_values):
    keys = keys_prefill.reshape(16, 8, 2, BLOCK, HD)
    values = values_prefill.reshape(16, 8, 2, BLOCK, HD)
    any_spec = pl.BlockSpec(memory_space=pl.ANY)
    hbm_spec = pl.BlockSpec(memory_space=pltpu.HBM)
    vmem_spec = pl.BlockSpec(memory_space=pltpu.VMEM)
    dma, vmem = pltpu.SemaphoreType.DMA, pltpu.VMEM
    rows_shape, cache_shape = (2, 8, 4, 4 * HD), (8, 4, BLOCK, KVH * HD)
    blocks = (64, 4, BLOCK, HD)

    def in_hbm(array):
        return pltpu.with_memory_space_constraint(array, pltpu.HBM)

    held = pl.pallas_call(
        relay,
        out_shape=(vmem(rows_shape, BF16), vmem(cache_shape, BF16), vmem(cache_shape, BF16)),
        in_specs=[hbm_spec] * 7,
        out_specs=(vmem_spec,) * 3,
        scratch_shapes=[
            [vmem((32, BLOCK, HD), BF16)] * 8, [vmem((32, BLOCK, HD), BF16)] * 8,
            vmem((16, 8, 2, BLOCK, HD), BF16), vmem((16, 8, 2, BLOCK, HD), BF16),
            vmem(blocks, BF16), vmem(blocks, BF16), vmem(blocks, BF16), vmem(blocks, BF16),
            vmem((2, 8, 4, KVH * HD), BF16), vmem((2, 8, 4, KVH * HD), BF16),
            vmem((8, 2, 4, GROUP * HD), BF16), vmem((4, 16, HD), F32),
            vmem((8, 2, 4, HD), BF16), vmem((8, 2, 4, HD), BF16),
            vmem((8, 2, 2, 16, HD), BF16), vmem((8, 2, 2, 16, HD), BF16),
            pltpu.SMEM((32,), jnp.int32), pltpu.SMEM((32,), jnp.int32),
            dma((2, 8)), dma, dma((2, 8)), dma((2,)), dma((2,)), dma((3,)), dma((3,)),
            dma((2,)), dma((2, 8)), dma, dma, dma((2,)),
        ],
        compiler_params=pltpu.CompilerParams(
            collective_id=0, has_side_effects=True, vmem_limit_bytes=48 * 2**20
        ),
        name="relay",
    )(*(in_hbm(x) for x in (slot_order, lengths, keys, values, queries, new_keys, new_values)))
    return pl.pallas_call(
        hand_out,
        out_shape=tuple(jax.ShapeDtypeStruct(shape, BF16) for shape in (rows_shape, cache_shape, cache_shape)),
        in_specs=[vmem_spec] * 3,
        out_specs=(any_spec,) * 3,
        scratch_shapes=[dma((17,))],
        compiler_params=pltpu.CompilerParams(vmem_limit_bytes=8 * 2**20),
        name="hand_out",
    )(*(pltpu.with_memory_space_constraint(x, pltpu.VMEM) for x in held))


def solution(mesh):
    in_specs = (
        P("section", "batch", None, "head"),
        P("section", "batch", None, "head"),
        P(),
        P(),
        P(None, None, "section", None),
        P(None, None, "section", None),
        P(None, None, "section", None),
    )
    out_specs = (
        P(None, None, "section", ("head", "batch")),
        P(None, "section", ("head", "batch"), None),
        P(None, "section", ("head", "batch"), None),
    )
    return jax.shard_map(body, mesh=mesh, in_specs=in_specs, out_specs=out_specs, check_vma=False)
```

```python
import jax
import jax.numpy as jnp
from jax import lax
from jax.experimental import pallas as pl
from jax.experimental.pallas import tpu as pltpu
from jax.sharding import PartitionSpec as P

KVH = 8
HD = 128
GROUP = 8
BLOCK = 32
MESH = pl.DeviceIdType.MESH
HIDDEN = -1e30
BF16, F32 = jnp.bfloat16, jnp.float32


PLANE = {
    1: ((1, 1), (3, 3), (1, 3), (3, 1), (2, 1), (0, 3), (2, 3), (0, 1)),
    0: ((1, 0), (0, 2), (3, 2), (1, 2), (3, 0), (2, 2), (2, 0)),
}
ARRIVALS = {low: tuple((dx, low) for dx in (1, 3, 2, 0)) for low in (1, 0)}


def group_of(dx, low):
    return low * 4 + dx


def relay(
    slot_order_hbm, lengths_hbm, keys, values, queries, new_keys, new_values,
    attention, keys_cache, values_cache,
    full, keys_line, values_chip, keys_packed, values_packed, keys_land, values_mid, values_land,
    fresh_rows, query_all, query_rows, fresh_all, rows_send, rows_land,
    slot_order, lengths,
    scalar_sem, full_sem, fresh_sem, line_send, line_recv, chip_send, chip_recv,
    keys_send, keys_recv, mid_send, mid_recv, values_send, values_recv,
    small_send, small_recv, rows_send_sem, rows_recv_sem,
):
    s, h, b = lax.axis_index("section"), lax.axis_index("head"), lax.axis_index("batch")
    x, z = lax.div(s, 2), lax.div(h, 2)
    y_low = lax.rem(h, 2)
    y = lax.rem(s, 2) * 2 + y_low
    other = 1 - b
    sign = 1 - 2 * b
    mine = pl.ds(b * 16, 16)
    here = x * 4 + y
    here_mid = x * 4 + y_low * 2 + lax.div(y, 2)

    def remote(src, dst, send_sem, recv_sem, to):
        return pltpu.make_async_remote_copy(
            src_ref=src, dst_ref=dst, send_sem=send_sem, recv_sem=recv_sem,
            device_id=to, device_id_type=MESH,
        )

    def wait_for(ref, sem):
        pltpu.make_async_copy(ref, ref, sem).wait()

    def away(d, at, way):
        return lax.rem(at + way * d + 4, 4)

    def in_plane(at_x, at_y):
        return at_x * 2 + lax.div(at_y, 2), z * 2 + lax.rem(at_y, 2)

    def in_line(at_z):
        return at_z * 2 + y_low

    def owner_low(low):
        return lax.rem(y_low + low, 2)

    barrier = pltpu.get_barrier_semaphore()

    def greet(to):
        pl.semaphore_signal(barrier, inc=1, device_id=to, device_id_type=MESH)

    for dz in range(4):
        at_h = in_line(away(dz, z, 1))
        greet((s, at_h, other))
        if dz:
            greet((s, at_h, b))
    for low in (1, 0):
        for dx, dy in PLANE[low]:
            at_s, at_h = in_plane(away(dx, x, 1), away(dy, y, 1))
            greet((at_s, at_h, b))
            if low == 0:
                greet((at_s, at_h, other))

    scalars = [
        pltpu.make_async_copy(slot_order_hbm, slot_order, scalar_sem.at[0]),
        pltpu.make_async_copy(lengths_hbm, lengths, scalar_sem.at[1]),
    ]
    whole = [pltpu.make_async_copy(src, full.at[n], full_sem.at[n]) for n, src in enumerate((keys, values))]
    fresh = [
        pltpu.make_async_copy(src, fresh_rows.at[n], fresh_sem.at[n])
        for n, src in enumerate((new_keys, new_values))
    ]
    for copy in scalars:
        copy.start()
    for low in (1, 0):
        pltpu.make_async_copy(
            values.at[:, :, owner_low(low), b], values_chip[low].at[mine], chip_recv.at[low]
        ).start()
    for low in (1, 0):
        pltpu.make_async_copy(
            keys.at[:, z, owner_low(low), b], keys_line[low].at[z, mine], line_recv.at[low]
        ).start()
    for copy in whole + fresh:
        copy.start()
    pl.semaphore_wait(barrier, 29)

    for low in (1, 0):
        remote(
            values.at[:, :, owner_low(low), other], values_chip[low].at[mine],
            chip_send, chip_recv.at[low], (s, h, other),
        ).start()

    def send_line(low, dz, to_b):
        to_z = away(dz, z, sign)
        remote(
            keys.at[:, to_z, owner_low(low), to_b], keys_line[low].at[z, mine],
            line_send, line_recv.at[low], (s, in_line(to_z), to_b),
        ).start()

    lines = [
        (low, dz, to_b)
        for low in (1, 0)
        for dz, to_b in ((1, b), (3, other), (2, b), (1, other), (3, b), (2, other), (0, other))
    ]
    for line in lines[:3]:
        send_line(*line)

    head_rows = pl.ds(pl.multiple_of(h * GROUP * HD, GROUP * HD), GROUP * HD)
    head_cols = pl.ds(pl.multiple_of(h * HD, HD), HD)

    def small_pieces(to_s):
        return (
            (queries.at[:, to_s, :, head_rows], query_all.at[s]),
            (new_keys.at[:, to_s, :, head_cols], fresh_all.at[0, s]),
            (new_values.at[:, to_s, :, head_cols], fresh_all.at[1, s]),
        )

    def send_small(step, carry):
        to_s = lax.rem(s + step, 8)
        for n, (src, dst) in enumerate(small_pieces(to_s)):
            remote(src, dst, small_send.at[n], small_recv.at[n], (to_s, h, b)).start()
        return carry

    lax.fori_loop(1, 8, send_small, 0)
    for n, (src, dst) in enumerate(small_pieces(s)):
        pltpu.make_async_copy(src, dst, small_recv.at[n]).start()

    scalars[0].wait()
    scalars[1].wait()

    def pack_values(low):
        def step(at_s, carry):
            for k in range(4):
                values_packed[at_s * 2 + owner_low(low), :, k] = values_chip[low][slot_order[at_s * 4 + k]]
            return carry

        lax.fori_loop(0, 8, step, 0)

    def pack_keys(low):
        def step(at_s, carry):
            for k in range(4):
                slot = slot_order[at_s * 4 + k]
                for from_z in range(4):
                    keys_packed[at_s * 2 + owner_low(low), from_z, k] = keys_line[low][from_z, slot]
            return carry

        lax.fori_loop(0, 8, step, 0)

    def send_plane(packed, dx, dy, dst, send_sem, recv_sem):
        to_x, to_y = away(dx, x, sign), away(dy, y, sign)
        to_s, to_h = in_plane(to_x, to_y)
        remote(
            packed.at[to_x * 4 + to_y], dst, send_sem, recv_sem.at[group_of(dx, dy % 2)], (to_s, to_h, b)
        ).start()

    lines = lines[3:]
    for low in (1, 0):
        wait_for(values_chip[low], chip_recv.at[low])
        pack_values(low)
        for dx, dy in PLANE[low]:
            send_plane(values_packed, dx, dy, values_mid.at[:, here_mid], mid_send, mid_recv)
            if lines:
                send_line(*lines.pop(0))
    assert not lines
    pltpu.make_async_copy(
        values_packed.at[here], values_mid.at[:, here_mid], mid_recv.at[group_of(0, 0)]
    ).start()

    def start_of(dx, low):
        return away(dx, x, -sign) * 4 + owner_low(low) * 2

    def turn_keys(low):
        wait_for(keys_line[low], line_recv.at[low])
        pack_keys(low)
        for dx, dy in PLANE[low]:
            send_plane(keys_packed, dx, dy, keys_land.at[here], keys_send, keys_recv)

    def turn_values(low):
        for dx, low in ARRIVALS[low]:
            group = group_of(dx, low)
            wait_for(values_mid.at[:, pl.ds(0, 2)], mid_recv.at[group])
            pair = pl.ds(start_of(dx, low), 2)
            for dz in (1, 3, 2):
                to_z = away(dz, z, sign)
                remote(
                    values_mid.at[to_z, pair], values_land.at[z, pair],
                    values_send, values_recv.at[group], (s, in_line(to_z), b),
                ).start()

    for n, part in enumerate((query_all, fresh_all.at[0], fresh_all.at[1])):
        wait_for(part, small_recv.at[n])
    whole[0].wait()
    whole[1].wait()

    later = lax.rem(lax.div(lax.broadcasted_iota(jnp.int32, (16, 1), 0), 4), 2) == 1
    column = lax.broadcasted_iota(jnp.int32, (16, 512), 1)
    scale = HD ** -0.5

    def attend(at_s, at_k):
        slot = slot_order[at_s * 4 + at_k]
        prompt = slot - b * 16
        inside = jnp.logical_and(prompt >= 0, prompt < 16)
        prompt = jnp.clip(prompt, 0, 15)
        live = lengths[slot]
        qf = query_rows[at_k]
        k0, k1, v0, v1 = (
            fresh_all[n, at_s, t].astype(F32)[at_k : at_k + 1] for n in range(2) for t in range(2)
        )
        k = full[0, prompt].reshape(512, HD)
        v = full[1, prompt].reshape(512, HD)
        scores = lax.dot_general(
            qf.astype(BF16), k, (((1,), (1,)), ((), ())), preferred_element_type=F32
        ) * scale
        n0 = jnp.sum(qf * k0, axis=1, keepdims=True) * scale
        n1 = jnp.sum(qf * k1, axis=1, keepdims=True) * scale
        kept = column < live
        scores = jnp.where(kept, scores, HIDDEN)
        n1 = jnp.where(later, n1, HIDDEN)
        peak = jnp.maximum(jnp.max(scores, axis=1, keepdims=True), jnp.maximum(n0, n1))
        mass = jnp.where(kept, jnp.exp(scores - peak), 0.0)
        m0 = jnp.exp(n0 - peak)
        m1 = jnp.where(later, jnp.exp(n1 - peak), 0.0)
        total = jnp.sum(mass, axis=1, keepdims=True) + m0 + m1
        weighted = jnp.dot(mass.astype(BF16), v, preferred_element_type=F32)
        weighted += m0.astype(BF16).astype(F32) * v0
        weighted += m1.astype(BF16).astype(F32) * v1
        return jnp.where(inside, weighted / total, 0.0)

    def attend_section(at_s, carry):
        for t in range(2):
            rows = query_all[at_s, t].astype(F32)
            for g in range(GROUP):
                row = (g // 4) * 8 + t * 4 + g % 4
                for k in range(4):
                    query_rows[k, row : row + 1, :] = rows[k : k + 1, g * HD : g * HD + HD]
        for pair in range(2):
            first, second = attend(at_s, pair * 2), attend(at_s, pair * 2 + 1)
            for to_b in range(2):
                cut = slice(to_b * 8, to_b * 8 + 8)
                rows_send[at_s, to_b, pair] = jnp.concatenate(
                    (first[cut], second[cut]), axis=0
                ).astype(BF16)
        return carry

    lax.fori_loop(0, 4, attend_section, 0)
    turn_keys(1)
    turn_values(1)
    lax.fori_loop(4, 8, attend_section, 0)

    def send_rows(to_s, to_b):
        remote(
            rows_send.at[to_s, to_b], rows_land.at[s, b], rows_send_sem, rows_recv_sem, (to_s, h, to_b)
        ).start()

    def send_rows_step(step, carry):
        to_s = lax.rem(s + step, 8)
        send_rows(to_s, b)
        send_rows(to_s, other)
        return carry

    lax.fori_loop(1, 8, send_rows_step, 0)
    send_rows(s, other)
    pltpu.make_async_copy(rows_send.at[s, b], rows_land.at[s, b], rows_recv_sem).start()
    turn_keys(0)
    turn_values(0)

    slots = [slot_order[s * 4 + k] for k in range(4)]
    lives = [lengths[slot] for slot in slots]
    position = (h * 2 + b) * BLOCK + lax.broadcasted_iota(jnp.int32, (BLOCK, HD), 0)
    fresh[0].wait()
    fresh[1].wait()

    def settle(block, n, from_x, from_y, from_z):
        layer = from_x * 2 + lax.div(from_y, 2)
        cut = pl.ds(pl.multiple_of((from_z * 2 + lax.rem(from_y, 2)) * HD, HD), HD)
        out = (keys_cache, values_cache)[n]
        placed = [fresh_rows[n, t, layer, :, cut].astype(F32) for t in range(2)]
        for k in range(4):
            rows = jnp.where(position < lives[k], block[k].astype(F32), 0.0)
            for t in range(2):
                rows = jnp.where(position == lives[k] + t, placed[t][k : k + 1], rows)
            out[layer, k, :, cut] = rows.astype(BF16)

    def settle_keys(src, from_x, from_y):
        def step(from_z, carry):
            settle(src.at[from_x * 4 + from_y, from_z], 0, from_x, from_y, from_z)
            return carry

        lax.fori_loop(0, 4, step, 0)

    def settle_values(src, from_x, low, from_z):
        def step(half, carry):
            from_low = owner_low(low)
            block = src.at[from_z, from_x * 4 + from_low * 2 + half]
            settle(block, 1, from_x, half * 2 + from_low, from_z)
            return carry

        lax.fori_loop(0, 2, step, 0)

    owners = [lax.div(slot, 16) for slot in slots]

    def assemble(l, carry):
        picked = []
        for k in range(4):
            part = slice((k % 2) * 8, (k % 2) * 8 + 8)
            first, second = (rows_land[l, n, k // 2].astype(F32)[part] for n in range(2))
            picked.append(jnp.where(owners[k] == 0, first, second))
        for t in range(2):
            attention[t, l] = jnp.concatenate(
                [
                    jnp.concatenate([rows[t * 4 + g : t * 4 + g + 1] for rows in picked], axis=0)
                    for g in range(4)
                ],
                axis=1,
            ).astype(BF16)
        return carry

    settle_keys(keys_packed, x, y)
    for low in (1, 0):
        for dx, _ in ARRIVALS[low]:
            settle_values(values_mid, away(dx, x, -sign), low, z)
    for low in (1, 0):
        if low == 0:
            wait_for(rows_land, rows_recv_sem)
            lax.fori_loop(0, 8, assemble, 0)
        for dx, _ in ARRIVALS[low]:
            group = group_of(dx, low)
            from_x = away(dx, x, -sign)
            chips = [dy for to_x, dy in PLANE[low] if to_x == dx]
            wait_for(keys_land.at[pl.ds(0, len(chips))], keys_recv.at[group])
            for dy in chips:
                settle_keys(keys_land, from_x, away(dy, y, -sign))
            wait_for(values_land.at[pl.ds(0, 3), pl.ds(0, 2)], values_recv.at[group])
            for dz in (1, 3, 2):
                settle_values(values_land, from_x, low, away(dz, z, -sign))

    half = full.at[0, :, pl.ds(0, 2)]
    wait_for(half, chip_send)
    wait_for(half, line_send)
    wait_for(full.at[0, :, pl.ds(2, 1)], line_send)
    wait_for(full.at[0, :, pl.ds(3, 1), pl.ds(0, 1)], line_send)
    for n, part in enumerate((query_all, fresh_all.at[0], fresh_all.at[1])):
        wait_for(part.at[pl.ds(0, 7)], small_send.at[n])
    wait_for(values_packed.at[pl.ds(0, 15)], mid_send)
    wait_for(keys_packed.at[pl.ds(0, 15)], keys_send)
    wait_for(values_land.at[pl.ds(0, 3)], values_send)
    wait_for(rows_send.at[pl.ds(0, 7)], rows_send_sem)
    wait_for(rows_send.at[0, 0], rows_send_sem)


def hand_out(attention, keys, values, attention_out, keys_out, values_out, sem):
    copies = [pltpu.make_async_copy(attention, attention_out, sem.at[16])]
    for n, (src, dst) in enumerate(((keys, keys_out), (values, values_out))):
        copies += [pltpu.make_async_copy(src.at[l], dst.at[l], sem.at[n * 8 + l]) for l in range(8)]
    for copy in copies:
        copy.start()
    for copy in copies:
        copy.wait()


def body(keys_prefill, values_prefill, lengths, slot_order, queries, new_keys, new_values):
    keys = keys_prefill.reshape(16, 4, 2, 2, BLOCK, HD)
    values = values_prefill.reshape(16, 4, 2, 2, BLOCK, HD)
    any_spec = pl.BlockSpec(memory_space=pl.ANY)
    hbm_spec = pl.BlockSpec(memory_space=pltpu.HBM)
    vmem_spec = pl.BlockSpec(memory_space=pltpu.VMEM)
    dma, vmem = pltpu.SemaphoreType.DMA, pltpu.VMEM
    rows_shape, cache_shape = (2, 8, 4, 4 * HD), (8, 4, BLOCK, KVH * HD)
    plane, line = vmem((16, 4, 4, BLOCK, HD), BF16), vmem((4, 16, 4, BLOCK, HD), BF16)

    def in_hbm(array):
        return pltpu.with_memory_space_constraint(array, pltpu.HBM)

    held = pl.pallas_call(
        relay,
        out_shape=(vmem(rows_shape, BF16), vmem(cache_shape, BF16), vmem(cache_shape, BF16)),
        in_specs=[hbm_spec] * 7,
        out_specs=(vmem_spec,) * 3,
        scratch_shapes=[
            vmem((2, 16, 4, 2, 2, BLOCK, HD), BF16),
            [vmem((4, 32, BLOCK, HD), BF16)] * 2, [vmem((32, 4, BLOCK, HD), BF16)] * 2,
            plane, plane, plane, line, line,
            vmem((2, 2, 8, 4, KVH * HD), BF16), vmem((8, 2, 4, GROUP * HD), BF16), vmem((4, 16, HD), F32),
            vmem((2, 8, 2, 4, HD), BF16),
            vmem((8, 2, 2, 16, HD), BF16), vmem((8, 2, 2, 16, HD), BF16),
            pltpu.SMEM((32,), jnp.int32), pltpu.SMEM((32,), jnp.int32),
            dma((2,)), dma((2,)), dma((2,)), dma, dma((2,)), dma, dma((2,)),
            dma, dma((8,)), dma, dma((8,)), dma, dma((8,)),
            dma((3,)), dma((3,)), dma, dma,
        ],
        compiler_params=pltpu.CompilerParams(
            collective_id=0, has_side_effects=True, vmem_limit_bytes=48 * 2**20
        ),
        name="relay",
    )(*(in_hbm(x) for x in (slot_order, lengths, keys, values, queries, new_keys, new_values)))
    return pl.pallas_call(
        hand_out,
        out_shape=tuple(jax.ShapeDtypeStruct(shape, BF16) for shape in (rows_shape, cache_shape, cache_shape)),
        in_specs=[vmem_spec] * 3,
        out_specs=(any_spec,) * 3,
        scratch_shapes=[dma((17,))],
        compiler_params=pltpu.CompilerParams(vmem_limit_bytes=8 * 2**20),
        name="hand_out",
    )(*(pltpu.with_memory_space_constraint(x, pltpu.VMEM) for x in held))


def solution(mesh):
    in_specs = (
        P("section", "batch", None, "head"),
        P("section", "batch", None, "head"),
        P(),
        P(),
        P(None, None, "section", None),
        P(None, None, "section", None),
        P(None, None, "section", None),
    )
    out_specs = (
        P(None, None, "section", ("head", "batch")),
        P(None, "section", ("head", "batch"), None),
        P(None, "section", ("head", "batch"), None),
    )
    return jax.shard_map(body, mesh=mesh, in_specs=in_specs, out_specs=out_specs, check_vma=False)
```

```python
import jax
import jax.numpy as jnp
from jax import lax
from jax.experimental import pallas as pl
from jax.experimental.pallas import tpu as pltpu
from jax.sharding import PartitionSpec as P

KVH = 8
HD = 128
GROUP = 8
BLOCK = 32
MESH = pl.DeviceIdType.MESH
HIDDEN = -1e30
BF16, F32 = jnp.bfloat16, jnp.float32


PLANE = {
    1: ((1, 1), (3, 3), (1, 3), (3, 1), (2, 1), (0, 3), (2, 3), (0, 1)),
    0: ((1, 0), (0, 2), (3, 2), (1, 2), (3, 0), (2, 2), (2, 0)),
}
ARRIVALS = {low: tuple((dx, low) for dx in (1, 3, 2, 0)) for low in (1, 0)}


def group_of(dx, low):
    return low * 4 + dx


def relay(
    slot_order_hbm, lengths_hbm, keys, values, queries, new_keys, new_values,
    attention, keys_cache, values_cache,
    full, keys_line, values_chip, keys_packed, values_packed, keys_land, values_mid, values_land,
    fresh_rows, query_all, query_rows, fresh_all, rows_send, rows_land,
    slot_order, lengths,
    scalar_sem, full_sem, fresh_sem, line_send, line_recv, chip_send, chip_recv,
    keys_send, keys_recv, mid_send, mid_recv, values_send, values_recv,
    small_send, small_recv, rows_send_sem, rows_recv_sem,
):
    s, h, b = lax.axis_index("section"), lax.axis_index("head"), lax.axis_index("batch")
    x, z = lax.div(s, 2), lax.div(h, 2)
    y_low = lax.rem(h, 2)
    y = lax.rem(s, 2) * 2 + y_low
    other = 1 - b
    sign = 1 - 2 * b
    mine = pl.ds(b * 16, 16)
    here = x * 4 + y
    here_mid = x * 4 + y_low * 2 + lax.div(y, 2)

    def remote(src, dst, send_sem, recv_sem, to):
        return pltpu.make_async_remote_copy(
            src_ref=src, dst_ref=dst, send_sem=send_sem, recv_sem=recv_sem,
            device_id=to, device_id_type=MESH,
        )

    def wait_for(ref, sem):
        pltpu.make_async_copy(ref, ref, sem).wait()

    def away(d, at, way):
        return lax.rem(at + way * d + 4, 4)

    def in_plane(at_x, at_y):
        return at_x * 2 + lax.div(at_y, 2), z * 2 + lax.rem(at_y, 2)

    def in_line(at_z):
        return at_z * 2 + y_low

    def owner_low(low):
        return lax.rem(y_low + low, 2)

    barrier = pltpu.get_barrier_semaphore()

    def greet(to):
        pl.semaphore_signal(barrier, inc=1, device_id=to, device_id_type=MESH)

    for dz in range(4):
        at_h = in_line(away(dz, z, 1))
        greet((s, at_h, other))
        if dz:
            greet((s, at_h, b))
    for low in (1, 0):
        for dx, dy in PLANE[low]:
            at_s, at_h = in_plane(away(dx, x, 1), away(dy, y, 1))
            greet((at_s, at_h, b))
            if low == 0:
                greet((at_s, at_h, other))

    scalars = [
        pltpu.make_async_copy(slot_order_hbm, slot_order, scalar_sem.at[0]),
        pltpu.make_async_copy(lengths_hbm, lengths, scalar_sem.at[1]),
    ]
    whole = [pltpu.make_async_copy(src, full.at[n], full_sem.at[n]) for n, src in enumerate((keys, values))]
    fresh = [
        pltpu.make_async_copy(src, fresh_rows.at[n], fresh_sem.at[n])
        for n, src in enumerate((new_keys, new_values))
    ]
    for copy in scalars:
        copy.start()
    for low in (1, 0):
        pltpu.make_async_copy(
            values.at[:, :, owner_low(low), b], values_chip[low].at[mine], chip_recv.at[low]
        ).start()
    for low in (1, 0):
        pltpu.make_async_copy(
            keys.at[:, z, owner_low(low), b], keys_line[low].at[z, mine], line_recv.at[low]
        ).start()
    for copy in whole + fresh:
        copy.start()
    pl.semaphore_wait(barrier, 29)

    for low in (1, 0):
        remote(
            values.at[:, :, owner_low(low), other], values_chip[low].at[mine],
            chip_send, chip_recv.at[low], (s, h, other),
        ).start()

    def send_line(low, dz, to_b):
        to_z = away(dz, z, sign)
        remote(
            keys.at[:, to_z, owner_low(low), to_b], keys_line[low].at[z, mine],
            line_send, line_recv.at[low], (s, in_line(to_z), to_b),
        ).start()

    lines = [
        (low, dz, to_b)
        for low in (1, 0)
        for dz, to_b in ((1, b), (3, other), (2, b), (1, other), (3, b), (2, other), (0, other))
    ]
    for line in lines[:3]:
        send_line(*line)

    head_rows = pl.ds(pl.multiple_of(h * GROUP * HD, GROUP * HD), GROUP * HD)
    head_cols = pl.ds(pl.multiple_of(h * HD, HD), HD)

    def small_pieces(to_s):
        return (
            (queries.at[:, to_s, :, head_rows], query_all.at[s]),
            (new_keys.at[:, to_s, :, head_cols], fresh_all.at[0, s]),
            (new_values.at[:, to_s, :, head_cols], fresh_all.at[1, s]),
        )

    def send_small(step, carry):
        to_s = lax.rem(s + step, 8)
        for n, (src, dst) in enumerate(small_pieces(to_s)):
            remote(src, dst, small_send.at[n], small_recv.at[n], (to_s, h, b)).start()
        return carry

    lax.fori_loop(1, 8, send_small, 0)
    for n, (src, dst) in enumerate(small_pieces(s)):
        pltpu.make_async_copy(src, dst, small_recv.at[n]).start()

    scalars[0].wait()
    scalars[1].wait()

    def pack_values(low):
        def step(at_s, carry):
            for k in range(4):
                values_packed[at_s * 2 + owner_low(low), :, k] = values_chip[low][slot_order[at_s * 4 + k]]
            return carry

        lax.fori_loop(0, 8, step, 0)

    def pack_keys(low):
        def step(at_s, carry):
            for k in range(4):
                slot = slot_order[at_s * 4 + k]
                for from_z in range(4):
                    keys_packed[at_s * 2 + owner_low(low), from_z, k] = keys_line[low][from_z, slot]
            return carry

        lax.fori_loop(0, 8, step, 0)

    def send_plane(packed, dx, dy, dst, send_sem, recv_sem):
        to_x, to_y = away(dx, x, sign), away(dy, y, sign)
        to_s, to_h = in_plane(to_x, to_y)
        remote(
            packed.at[to_x * 4 + to_y], dst, send_sem, recv_sem.at[group_of(dx, dy % 2)], (to_s, to_h, b)
        ).start()

    lines = lines[3:]
    for low in (1, 0):
        wait_for(values_chip[low], chip_recv.at[low])
        pack_values(low)
        for dx, dy in PLANE[low]:
            send_plane(values_packed, dx, dy, values_mid.at[:, here_mid], mid_send, mid_recv)
            if lines:
                send_line(*lines.pop(0))
    assert not lines
    pltpu.make_async_copy(
        values_packed.at[here], values_mid.at[:, here_mid], mid_recv.at[group_of(0, 0)]
    ).start()

    def start_of(dx, low):
        return away(dx, x, -sign) * 4 + owner_low(low) * 2

    def turn(low):
        wait_for(keys_line[low], line_recv.at[low])
        pack_keys(low)
        chips = list(PLANE[low])
        for dx, _ in ARRIVALS[low]:
            group = group_of(dx, low)
            wait_for(values_mid.at[:, pl.ds(0, 2)], mid_recv.at[group])
            pair = pl.ds(away(dx, x, -sign) * 4 + owner_low(low) * 2, 2)
            for dz in (1, 3, 2):
                to_z = away(dz, z, sign)
                remote(
                    values_mid.at[to_z, pair], values_land.at[z, pair],
                    values_send, values_recv.at[group], (s, in_line(to_z), b),
                ).start()
                if dz != 3 and chips:
                    send_plane(keys_packed, *chips.pop(0), keys_land.at[here], keys_send, keys_recv)

    for n, part in enumerate((query_all, fresh_all.at[0], fresh_all.at[1])):
        wait_for(part, small_recv.at[n])
    whole[0].wait()
    whole[1].wait()

    later = lax.rem(lax.div(lax.broadcasted_iota(jnp.int32, (16, 1), 0), 4), 2) == 1
    column = lax.broadcasted_iota(jnp.int32, (16, 512), 1)
    scale = HD ** -0.5

    def attend(at_s, at_k):
        slot = slot_order[at_s * 4 + at_k]
        prompt = slot - b * 16
        inside = jnp.logical_and(prompt >= 0, prompt < 16)
        prompt = jnp.clip(prompt, 0, 15)
        live = lengths[slot]
        qf = query_rows[at_k]
        k0, k1, v0, v1 = (
            fresh_all[n, at_s, t].astype(F32)[at_k : at_k + 1] for n in range(2) for t in range(2)
        )
        k = full[0, prompt].reshape(512, HD)
        v = full[1, prompt].reshape(512, HD)
        scores = lax.dot_general(
            qf.astype(BF16), k, (((1,), (1,)), ((), ())), preferred_element_type=F32
        ) * scale
        n0 = jnp.sum(qf * k0, axis=1, keepdims=True) * scale
        n1 = jnp.sum(qf * k1, axis=1, keepdims=True) * scale
        kept = column < live
        scores = jnp.where(kept, scores, HIDDEN)
        n1 = jnp.where(later, n1, HIDDEN)
        peak = jnp.maximum(jnp.max(scores, axis=1, keepdims=True), jnp.maximum(n0, n1))
        mass = jnp.where(kept, jnp.exp(scores - peak), 0.0)
        m0 = jnp.exp(n0 - peak)
        m1 = jnp.where(later, jnp.exp(n1 - peak), 0.0)
        total = jnp.sum(mass, axis=1, keepdims=True) + m0 + m1
        weighted = jnp.dot(mass.astype(BF16), v, preferred_element_type=F32)
        weighted += m0.astype(BF16).astype(F32) * v0
        weighted += m1.astype(BF16).astype(F32) * v1
        return jnp.where(inside, weighted / total, 0.0)

    def attend_section(at_s, carry):
        for t in range(2):
            rows = query_all[at_s, t].astype(F32)
            for g in range(GROUP):
                row = (g // 4) * 8 + t * 4 + g % 4
                for k in range(4):
                    query_rows[k, row : row + 1, :] = rows[k : k + 1, g * HD : g * HD + HD]
        for pair in range(2):
            first, second = attend(at_s, pair * 2), attend(at_s, pair * 2 + 1)
            for to_b in range(2):
                cut = slice(to_b * 8, to_b * 8 + 8)
                rows_send[at_s, to_b, pair] = jnp.concatenate(
                    (first[cut], second[cut]), axis=0
                ).astype(BF16)
        return carry

    lax.fori_loop(0, 4, attend_section, 0)
    turn(1)
    lax.fori_loop(4, 8, attend_section, 0)

    def send_rows(to_s, to_b):
        remote(
            rows_send.at[to_s, to_b], rows_land.at[s, b], rows_send_sem, rows_recv_sem, (to_s, h, to_b)
        ).start()

    def send_rows_step(step, carry):
        to_s = lax.rem(s + step, 8)
        send_rows(to_s, b)
        send_rows(to_s, other)
        return carry

    lax.fori_loop(1, 8, send_rows_step, 0)
    send_rows(s, other)
    pltpu.make_async_copy(rows_send.at[s, b], rows_land.at[s, b], rows_recv_sem).start()
    turn(0)

    slots = [slot_order[s * 4 + k] for k in range(4)]
    lives = [lengths[slot] for slot in slots]
    position = (h * 2 + b) * BLOCK + lax.broadcasted_iota(jnp.int32, (BLOCK, HD), 0)
    fresh[0].wait()
    fresh[1].wait()

    def settle(block, n, from_x, from_y, from_z):
        layer = from_x * 2 + lax.div(from_y, 2)
        cut = pl.ds(pl.multiple_of((from_z * 2 + lax.rem(from_y, 2)) * HD, HD), HD)
        out = (keys_cache, values_cache)[n]
        placed = [fresh_rows[n, t, layer, :, cut].astype(F32) for t in range(2)]
        for k in range(4):
            rows = jnp.where(position < lives[k], block[k].astype(F32), 0.0)
            for t in range(2):
                rows = jnp.where(position == lives[k] + t, placed[t][k : k + 1], rows)
            out[layer, k, :, cut] = rows.astype(BF16)

    def settle_keys(src, from_x, from_y):
        def step(from_z, carry):
            settle(src.at[from_x * 4 + from_y, from_z], 0, from_x, from_y, from_z)
            return carry

        lax.fori_loop(0, 4, step, 0)

    def settle_values(src, from_x, low, from_z):
        def step(half, carry):
            from_low = owner_low(low)
            block = src.at[from_z, from_x * 4 + from_low * 2 + half]
            settle(block, 1, from_x, half * 2 + from_low, from_z)
            return carry

        lax.fori_loop(0, 2, step, 0)

    owners = [lax.div(slot, 16) for slot in slots]

    def assemble(l, carry):
        picked = []
        for k in range(4):
            part = slice((k % 2) * 8, (k % 2) * 8 + 8)
            first, second = (rows_land[l, n, k // 2].astype(F32)[part] for n in range(2))
            picked.append(jnp.where(owners[k] == 0, first, second))
        for t in range(2):
            attention[t, l] = jnp.concatenate(
                [
                    jnp.concatenate([rows[t * 4 + g : t * 4 + g + 1] for rows in picked], axis=0)
                    for g in range(4)
                ],
                axis=1,
            ).astype(BF16)
        return carry

    settle_keys(keys_packed, x, y)
    for low in (1, 0):
        for dx, _ in ARRIVALS[low]:
            settle_values(values_mid, away(dx, x, -sign), low, z)
    for low in (1, 0):
        if low == 0:
            wait_for(rows_land, rows_recv_sem)
            lax.fori_loop(0, 8, assemble, 0)
        for dx, _ in ARRIVALS[low]:
            group = group_of(dx, low)
            from_x = away(dx, x, -sign)
            chips = [dy for to_x, dy in PLANE[low] if to_x == dx]
            wait_for(keys_land.at[pl.ds(0, len(chips))], keys_recv.at[group])
            for dy in chips:
                settle_keys(keys_land, from_x, away(dy, y, -sign))
            wait_for(values_land.at[pl.ds(0, 3), pl.ds(0, 2)], values_recv.at[group])
            for dz in (1, 3, 2):
                settle_values(values_land, from_x, low, away(dz, z, -sign))

    half = full.at[0, :, pl.ds(0, 2)]
    wait_for(half, chip_send)
    wait_for(half, line_send)
    wait_for(full.at[0, :, pl.ds(2, 1)], line_send)
    wait_for(full.at[0, :, pl.ds(3, 1), pl.ds(0, 1)], line_send)
    for n, part in enumerate((query_all, fresh_all.at[0], fresh_all.at[1])):
        wait_for(part.at[pl.ds(0, 7)], small_send.at[n])
    wait_for(values_packed.at[pl.ds(0, 15)], mid_send)
    wait_for(keys_packed.at[pl.ds(0, 15)], keys_send)
    wait_for(values_land.at[pl.ds(0, 3)], values_send)
    wait_for(rows_send.at[pl.ds(0, 7)], rows_send_sem)
    wait_for(rows_send.at[0, 0], rows_send_sem)


def hand_out(attention, keys, values, attention_out, keys_out, values_out, sem):
    copies = [pltpu.make_async_copy(attention, attention_out, sem.at[16])]
    for n, (src, dst) in enumerate(((keys, keys_out), (values, values_out))):
        copies += [pltpu.make_async_copy(src.at[l], dst.at[l], sem.at[n * 8 + l]) for l in range(8)]
    for copy in copies:
        copy.start()
    for copy in copies:
        copy.wait()


def body(keys_prefill, values_prefill, lengths, slot_order, queries, new_keys, new_values):
    keys = keys_prefill.reshape(16, 4, 2, 2, BLOCK, HD)
    values = values_prefill.reshape(16, 4, 2, 2, BLOCK, HD)
    any_spec = pl.BlockSpec(memory_space=pl.ANY)
    hbm_spec = pl.BlockSpec(memory_space=pltpu.HBM)
    vmem_spec = pl.BlockSpec(memory_space=pltpu.VMEM)
    dma, vmem = pltpu.SemaphoreType.DMA, pltpu.VMEM
    rows_shape, cache_shape = (2, 8, 4, 4 * HD), (8, 4, BLOCK, KVH * HD)
    plane, line = vmem((16, 4, 4, BLOCK, HD), BF16), vmem((4, 16, 4, BLOCK, HD), BF16)

    def in_hbm(array):
        return pltpu.with_memory_space_constraint(array, pltpu.HBM)

    held = pl.pallas_call(
        relay,
        out_shape=(vmem(rows_shape, BF16), vmem(cache_shape, BF16), vmem(cache_shape, BF16)),
        in_specs=[hbm_spec] * 7,
        out_specs=(vmem_spec,) * 3,
        scratch_shapes=[
            vmem((2, 16, 4, 2, 2, BLOCK, HD), BF16),
            [vmem((4, 32, BLOCK, HD), BF16)] * 2, [vmem((32, 4, BLOCK, HD), BF16)] * 2,
            plane, plane, plane, line, line,
            vmem((2, 2, 8, 4, KVH * HD), BF16), vmem((8, 2, 4, GROUP * HD), BF16), vmem((4, 16, HD), F32),
            vmem((2, 8, 2, 4, HD), BF16),
            vmem((8, 2, 2, 16, HD), BF16), vmem((8, 2, 2, 16, HD), BF16),
            pltpu.SMEM((32,), jnp.int32), pltpu.SMEM((32,), jnp.int32),
            dma((2,)), dma((2,)), dma((2,)), dma, dma((2,)), dma, dma((2,)),
            dma, dma((8,)), dma, dma((8,)), dma, dma((8,)),
            dma((3,)), dma((3,)), dma, dma,
        ],
        compiler_params=pltpu.CompilerParams(
            collective_id=0, has_side_effects=True, vmem_limit_bytes=48 * 2**20
        ),
        name="relay",
    )(*(in_hbm(x) for x in (slot_order, lengths, keys, values, queries, new_keys, new_values)))
    return pl.pallas_call(
        hand_out,
        out_shape=tuple(jax.ShapeDtypeStruct(shape, BF16) for shape in (rows_shape, cache_shape, cache_shape)),
        in_specs=[vmem_spec] * 3,
        out_specs=(any_spec,) * 3,
        scratch_shapes=[dma((17,))],
        compiler_params=pltpu.CompilerParams(vmem_limit_bytes=8 * 2**20),
        name="hand_out",
    )(*(pltpu.with_memory_space_constraint(x, pltpu.VMEM) for x in held))


def solution(mesh):
    in_specs = (
        P("section", "batch", None, "head"),
        P("section", "batch", None, "head"),
        P(),
        P(),
        P(None, None, "section", None),
        P(None, None, "section", None),
        P(None, None, "section", None),
    )
    out_specs = (
        P(None, None, "section", ("head", "batch")),
        P(None, "section", ("head", "batch"), None),
        P(None, "section", ("head", "batch"), None),
    )
    return jax.shard_map(body, mesh=mesh, in_specs=in_specs, out_specs=out_specs, check_vma=False)
```

```python
import jax
import jax.numpy as jnp
from jax import lax
from jax.experimental import pallas as pl
from jax.experimental.pallas import tpu as pltpu
from jax.sharding import PartitionSpec as P

KVH = 8
HD = 128
GROUP = 8
BLOCK = 32
MESH = pl.DeviceIdType.MESH
HIDDEN = -1e30
BF16, F32 = jnp.bfloat16, jnp.float32


PLANE = {
    1: ((1, 1), (3, 3), (1, 3), (3, 1), (2, 1), (0, 3), (2, 3), (0, 1)),
    0: ((1, 0), (0, 2), (3, 2), (1, 2), (3, 0), (2, 2), (2, 0)),
}
ARRIVALS = {low: tuple((dx, low) for dx in (1, 3, 2, 0)) for low in (1, 0)}


def group_of(dx, low):
    return low * 4 + dx


def relay(
    slot_order_hbm, lengths_hbm, keys, values, queries, new_keys, new_values,
    attention, keys_cache, values_cache,
    full, keys_line, values_chip, keys_packed, values_packed, keys_land, values_mid, values_land,
    fresh_rows, query_all, query_rows, fresh_all, rows_send, rows_land,
    slot_order, lengths,
    scalar_sem, full_sem, fresh_sem, line_send, line_recv, chip_send, chip_recv,
    keys_send, keys_recv, mid_send, mid_recv, values_send, values_recv,
    small_send, small_recv, rows_send_sem, rows_recv_sem,
):
    s, h, b = lax.axis_index("section"), lax.axis_index("head"), lax.axis_index("batch")
    x, z = lax.div(s, 2), lax.div(h, 2)
    y_low = lax.rem(h, 2)
    y = lax.rem(s, 2) * 2 + y_low
    other = 1 - b
    sign = 1 - 2 * b
    mine = pl.ds(b * 16, 16)
    here = x * 4 + y
    here_mid = x * 4 + y_low * 2 + lax.div(y, 2)

    def remote(src, dst, send_sem, recv_sem, to):
        return pltpu.make_async_remote_copy(
            src_ref=src, dst_ref=dst, send_sem=send_sem, recv_sem=recv_sem,
            device_id=to, device_id_type=MESH,
        )

    def wait_for(ref, sem):
        pltpu.make_async_copy(ref, ref, sem).wait()

    def away(d, at, way):
        return lax.rem(at + way * d + 4, 4)

    def in_plane(at_x, at_y):
        return at_x * 2 + lax.div(at_y, 2), z * 2 + lax.rem(at_y, 2)

    def in_line(at_z):
        return at_z * 2 + y_low

    def owner_low(low):
        return lax.rem(y_low + low, 2)

    barrier = pltpu.get_barrier_semaphore()

    def greet(to):
        pl.semaphore_signal(barrier, inc=1, device_id=to, device_id_type=MESH)

    for dz in range(4):
        at_h = in_line(away(dz, z, 1))
        greet((s, at_h, other))
        if dz:
            greet((s, at_h, b))
    for low in (1, 0):
        for dx, dy in PLANE[low]:
            at_s, at_h = in_plane(away(dx, x, 1), away(dy, y, 1))
            greet((at_s, at_h, b))
            if low == 0:
                greet((at_s, at_h, other))

    scalars = [
        pltpu.make_async_copy(slot_order_hbm, slot_order, scalar_sem.at[0]),
        pltpu.make_async_copy(lengths_hbm, lengths, scalar_sem.at[1]),
    ]
    whole = [pltpu.make_async_copy(src, full.at[n], full_sem.at[n]) for n, src in enumerate((keys, values))]
    fresh = [
        pltpu.make_async_copy(src, fresh_rows.at[n], fresh_sem.at[n])
        for n, src in enumerate((new_keys, new_values))
    ]
    for copy in scalars:
        copy.start()
    for low in (1, 0):
        pltpu.make_async_copy(
            values.at[:, :, owner_low(low), b], values_chip[low].at[mine], chip_recv.at[low]
        ).start()
    for low in (1, 0):
        pltpu.make_async_copy(
            keys.at[:, z, owner_low(low), b], keys_line[low].at[z, mine], line_recv.at[low]
        ).start()
    for copy in whole + fresh:
        copy.start()
    pl.semaphore_wait(barrier, 29)

    for low in (1, 0):
        remote(
            values.at[:, :, owner_low(low), other], values_chip[low].at[mine],
            chip_send, chip_recv.at[low], (s, h, other),
        ).start()

    def send_line(low, dz, to_b):
        to_z = away(dz, z, sign)
        remote(
            keys.at[:, to_z, owner_low(low), to_b], keys_line[low].at[z, mine],
            line_send, line_recv.at[low], (s, in_line(to_z), to_b),
        ).start()

    lines = [
        (low, dz, to_b)
        for low in (1, 0)
        for dz, to_b in ((1, b), (3, other), (2, b), (1, other), (3, b), (2, other), (0, other))
    ]
    for line in lines[:3]:
        send_line(*line)

    head_rows = pl.ds(pl.multiple_of(h * GROUP * HD, GROUP * HD), GROUP * HD)
    head_cols = pl.ds(pl.multiple_of(h * HD, HD), HD)

    def small_pieces(to_s):
        return (
            (queries.at[:, to_s, :, head_rows], query_all.at[s]),
            (new_keys.at[:, to_s, :, head_cols], fresh_all.at[0, s]),
            (new_values.at[:, to_s, :, head_cols], fresh_all.at[1, s]),
        )

    def send_small(step, carry):
        to_s = lax.rem(s + step, 8)
        for n, (src, dst) in enumerate(small_pieces(to_s)):
            remote(src, dst, small_send.at[n], small_recv.at[n], (to_s, h, b)).start()
        return carry

    lax.fori_loop(1, 8, send_small, 0)
    for n, (src, dst) in enumerate(small_pieces(s)):
        pltpu.make_async_copy(src, dst, small_recv.at[n]).start()

    scalars[0].wait()
    scalars[1].wait()

    def pack_values(low):
        def step(at_s, carry):
            for k in range(4):
                values_packed[at_s * 2 + owner_low(low), :, k] = values_chip[low][slot_order[at_s * 4 + k]]
            return carry

        lax.fori_loop(0, 8, step, 0)

    def pack_keys(low):
        def step(at_s, carry):
            for k in range(4):
                slot = slot_order[at_s * 4 + k]
                for from_z in range(4):
                    keys_packed[at_s * 2 + owner_low(low), from_z, k] = keys_line[low][from_z, slot]
            return carry

        lax.fori_loop(0, 8, step, 0)

    def send_plane(packed, dx, dy, dst, send_sem, recv_sem):
        to_x, to_y = away(dx, x, sign), away(dy, y, sign)
        to_s, to_h = in_plane(to_x, to_y)
        remote(
            packed.at[to_x * 4 + to_y], dst, send_sem, recv_sem.at[group_of(dx, dy % 2)], (to_s, to_h, b)
        ).start()

    lines = lines[3:]
    for low in (1, 0):
        wait_for(values_chip[low], chip_recv.at[low])
        pack_values(low)
        for dx, dy in PLANE[low]:
            send_plane(values_packed, dx, dy, values_mid.at[:, here_mid], mid_send, mid_recv)
            if lines:
                send_line(*lines.pop(0))
    assert not lines
    pltpu.make_async_copy(
        values_packed.at[here], values_mid.at[:, here_mid], mid_recv.at[group_of(0, 0)]
    ).start()

    def start_of(dx, low):
        return away(dx, x, -sign) * 4 + owner_low(low) * 2

    def turn(low):
        wait_for(keys_line[low], line_recv.at[low])
        pack_keys(low)
        chips = list(PLANE[low])
        for dx, _ in ARRIVALS[low]:
            group = group_of(dx, low)
            wait_for(values_mid.at[:, pl.ds(0, 2)], mid_recv.at[group])
            pair = pl.ds(away(dx, x, -sign) * 4 + owner_low(low) * 2, 2)
            for dz in (1, 3, 2):
                to_z = away(dz, z, sign)
                remote(
                    values_mid.at[to_z, pair], values_land.at[z, pair],
                    values_send, values_recv.at[group], (s, in_line(to_z), b),
                ).start()
                if dz != 3 and chips:
                    send_plane(keys_packed, *chips.pop(0), keys_land.at[here], keys_send, keys_recv)

    for n, part in enumerate((query_all, fresh_all.at[0], fresh_all.at[1])):
        wait_for(part, small_recv.at[n])
    whole[0].wait()
    whole[1].wait()

    later = lax.rem(lax.div(lax.broadcasted_iota(jnp.int32, (16, 1), 0), 4), 2) == 1
    column = lax.broadcasted_iota(jnp.int32, (16, 512), 1)
    scale = HD ** -0.5

    def attend(at_s, at_k):
        slot = slot_order[at_s * 4 + at_k]
        prompt = slot - b * 16
        inside = jnp.logical_and(prompt >= 0, prompt < 16)
        prompt = jnp.clip(prompt, 0, 15)
        live = lengths[slot]
        qf = query_rows[at_k]
        k0, k1, v0, v1 = (
            fresh_all[n, at_s, t].astype(F32)[at_k : at_k + 1] for n in range(2) for t in range(2)
        )
        k = full[0, prompt].reshape(512, HD)
        v = full[1, prompt].reshape(512, HD)
        scores = lax.dot_general(
            qf.astype(BF16), k, (((1,), (1,)), ((), ())), preferred_element_type=F32
        ) * scale
        n0 = jnp.sum(qf * k0, axis=1, keepdims=True) * scale
        n1 = jnp.sum(qf * k1, axis=1, keepdims=True) * scale
        kept = column < live
        scores = jnp.where(kept, scores, HIDDEN)
        n1 = jnp.where(later, n1, HIDDEN)
        peak = jnp.maximum(jnp.max(scores, axis=1, keepdims=True), jnp.maximum(n0, n1))
        mass = jnp.where(kept, jnp.exp(scores - peak), 0.0)
        m0 = jnp.exp(n0 - peak)
        m1 = jnp.where(later, jnp.exp(n1 - peak), 0.0)
        total = jnp.sum(mass, axis=1, keepdims=True) + m0 + m1
        weighted = jnp.dot(mass.astype(BF16), v, preferred_element_type=F32)
        weighted += m0.astype(BF16).astype(F32) * v0
        weighted += m1.astype(BF16).astype(F32) * v1
        return jnp.where(inside, weighted / total, 0.0)

    def attend_section(at_s, carry):
        for t in range(2):
            rows = query_all[at_s, t].astype(F32)
            for g in range(GROUP):
                row = (g // 4) * 8 + t * 4 + g % 4
                for k in range(4):
                    query_rows[k, row : row + 1, :] = rows[k : k + 1, g * HD : g * HD + HD]
        for pair in range(2):
            first, second = attend(at_s, pair * 2), attend(at_s, pair * 2 + 1)
            for to_b in range(2):
                cut = slice(to_b * 8, to_b * 8 + 8)
                rows_send[at_s, to_b, pair] = jnp.concatenate(
                    (first[cut], second[cut]), axis=0
                ).astype(BF16)
        return carry

    lax.fori_loop(0, 2, attend_section, 0)
    turn(1)
    lax.fori_loop(2, 4, attend_section, 0)
    turn(0)
    lax.fori_loop(4, 8, attend_section, 0)

    def send_rows(to_s, to_b):
        remote(
            rows_send.at[to_s, to_b], rows_land.at[s, b], rows_send_sem, rows_recv_sem, (to_s, h, to_b)
        ).start()

    def send_rows_step(step, carry):
        to_s = lax.rem(s + step, 8)
        send_rows(to_s, b)
        send_rows(to_s, other)
        return carry

    lax.fori_loop(1, 8, send_rows_step, 0)
    send_rows(s, other)
    pltpu.make_async_copy(rows_send.at[s, b], rows_land.at[s, b], rows_recv_sem).start()

    slots = [slot_order[s * 4 + k] for k in range(4)]
    lives = [lengths[slot] for slot in slots]
    position = (h * 2 + b) * BLOCK + lax.broadcasted_iota(jnp.int32, (BLOCK, HD), 0)
    fresh[0].wait()
    fresh[1].wait()

    def settle(block, n, from_x, from_y, from_z):
        layer = from_x * 2 + lax.div(from_y, 2)
        cut = pl.ds(pl.multiple_of((from_z * 2 + lax.rem(from_y, 2)) * HD, HD), HD)
        out = (keys_cache, values_cache)[n]
        placed = [fresh_rows[n, t, layer, :, cut].astype(F32) for t in range(2)]
        for k in range(4):
            rows = jnp.where(position < lives[k], block[k].astype(F32), 0.0)
            for t in range(2):
                rows = jnp.where(position == lives[k] + t, placed[t][k : k + 1], rows)
            out[layer, k, :, cut] = rows.astype(BF16)

    def settle_keys(src, from_x, from_y):
        def step(from_z, carry):
            settle(src.at[from_x * 4 + from_y, from_z], 0, from_x, from_y, from_z)
            return carry

        lax.fori_loop(0, 4, step, 0)

    def settle_values(src, from_x, low, from_z):
        def step(half, carry):
            from_low = owner_low(low)
            block = src.at[from_z, from_x * 4 + from_low * 2 + half]
            settle(block, 1, from_x, half * 2 + from_low, from_z)
            return carry

        lax.fori_loop(0, 2, step, 0)

    owners = [lax.div(slot, 16) for slot in slots]

    def assemble(l, carry):
        picked = []
        for k in range(4):
            part = slice((k % 2) * 8, (k % 2) * 8 + 8)
            first, second = (rows_land[l, n, k // 2].astype(F32)[part] for n in range(2))
            picked.append(jnp.where(owners[k] == 0, first, second))
        for t in range(2):
            attention[t, l] = jnp.concatenate(
                [
                    jnp.concatenate([rows[t * 4 + g : t * 4 + g + 1] for rows in picked], axis=0)
                    for g in range(4)
                ],
                axis=1,
            ).astype(BF16)
        return carry

    settle_keys(keys_packed, x, y)
    for low in (1, 0):
        for dx, _ in ARRIVALS[low]:
            settle_values(values_mid, away(dx, x, -sign), low, z)
    for low in (1, 0):
        if low == 0:
            wait_for(rows_land, rows_recv_sem)
            lax.fori_loop(0, 8, assemble, 0)
        for dx, _ in ARRIVALS[low]:
            group = group_of(dx, low)
            from_x = away(dx, x, -sign)
            chips = [dy for to_x, dy in PLANE[low] if to_x == dx]
            wait_for(keys_land.at[pl.ds(0, len(chips))], keys_recv.at[group])
            for dy in chips:
                settle_keys(keys_land, from_x, away(dy, y, -sign))
            wait_for(values_land.at[pl.ds(0, 3), pl.ds(0, 2)], values_recv.at[group])
            for dz in (1, 3, 2):
                settle_values(values_land, from_x, low, away(dz, z, -sign))

    half = full.at[0, :, pl.ds(0, 2)]
    wait_for(half, chip_send)
    wait_for(half, line_send)
    wait_for(full.at[0, :, pl.ds(2, 1)], line_send)
    wait_for(full.at[0, :, pl.ds(3, 1), pl.ds(0, 1)], line_send)
    for n, part in enumerate((query_all, fresh_all.at[0], fresh_all.at[1])):
        wait_for(part.at[pl.ds(0, 7)], small_send.at[n])
    wait_for(values_packed.at[pl.ds(0, 15)], mid_send)
    wait_for(keys_packed.at[pl.ds(0, 15)], keys_send)
    wait_for(values_land.at[pl.ds(0, 3)], values_send)
    wait_for(rows_send.at[pl.ds(0, 7)], rows_send_sem)
    wait_for(rows_send.at[0, 0], rows_send_sem)


def hand_out(attention, keys, values, attention_out, keys_out, values_out, sem):
    copies = [pltpu.make_async_copy(attention, attention_out, sem.at[16])]
    for n, (src, dst) in enumerate(((keys, keys_out), (values, values_out))):
        copies += [pltpu.make_async_copy(src.at[l], dst.at[l], sem.at[n * 8 + l]) for l in range(8)]
    for copy in copies:
        copy.start()
    for copy in copies:
        copy.wait()


def body(keys_prefill, values_prefill, lengths, slot_order, queries, new_keys, new_values):
    keys = keys_prefill.reshape(16, 4, 2, 2, BLOCK, HD)
    values = values_prefill.reshape(16, 4, 2, 2, BLOCK, HD)
    any_spec = pl.BlockSpec(memory_space=pl.ANY)
    hbm_spec = pl.BlockSpec(memory_space=pltpu.HBM)
    vmem_spec = pl.BlockSpec(memory_space=pltpu.VMEM)
    dma, vmem = pltpu.SemaphoreType.DMA, pltpu.VMEM
    rows_shape, cache_shape = (2, 8, 4, 4 * HD), (8, 4, BLOCK, KVH * HD)
    plane, line = vmem((16, 4, 4, BLOCK, HD), BF16), vmem((4, 16, 4, BLOCK, HD), BF16)

    def in_hbm(array):
        return pltpu.with_memory_space_constraint(array, pltpu.HBM)

    held = pl.pallas_call(
        relay,
        out_shape=(vmem(rows_shape, BF16), vmem(cache_shape, BF16), vmem(cache_shape, BF16)),
        in_specs=[hbm_spec] * 7,
        out_specs=(vmem_spec,) * 3,
        scratch_shapes=[
            vmem((2, 16, 4, 2, 2, BLOCK, HD), BF16),
            [vmem((4, 32, BLOCK, HD), BF16)] * 2, [vmem((32, 4, BLOCK, HD), BF16)] * 2,
            plane, plane, plane, line, line,
            vmem((2, 2, 8, 4, KVH * HD), BF16), vmem((8, 2, 4, GROUP * HD), BF16), vmem((4, 16, HD), F32),
            vmem((2, 8, 2, 4, HD), BF16),
            vmem((8, 2, 2, 16, HD), BF16), vmem((8, 2, 2, 16, HD), BF16),
            pltpu.SMEM((32,), jnp.int32), pltpu.SMEM((32,), jnp.int32),
            dma((2,)), dma((2,)), dma((2,)), dma, dma((2,)), dma, dma((2,)),
            dma, dma((8,)), dma, dma((8,)), dma, dma((8,)),
            dma((3,)), dma((3,)), dma, dma,
        ],
        compiler_params=pltpu.CompilerParams(
            collective_id=0, has_side_effects=True, vmem_limit_bytes=48 * 2**20
        ),
        name="relay",
    )(*(in_hbm(x) for x in (slot_order, lengths, keys, values, queries, new_keys, new_values)))
    return pl.pallas_call(
        hand_out,
        out_shape=tuple(jax.ShapeDtypeStruct(shape, BF16) for shape in (rows_shape, cache_shape, cache_shape)),
        in_specs=[vmem_spec] * 3,
        out_specs=(any_spec,) * 3,
        scratch_shapes=[dma((17,))],
        compiler_params=pltpu.CompilerParams(vmem_limit_bytes=8 * 2**20),
        name="hand_out",
    )(*(pltpu.with_memory_space_constraint(x, pltpu.VMEM) for x in held))


def solution(mesh):
    in_specs = (
        P("section", "batch", None, "head"),
        P("section", "batch", None, "head"),
        P(),
        P(),
        P(None, None, "section", None),
        P(None, None, "section", None),
        P(None, None, "section", None),
    )
    out_specs = (
        P(None, None, "section", ("head", "batch")),
        P(None, "section", ("head", "batch"), None),
        P(None, "section", ("head", "batch"), None),
    )
    return jax.shard_map(body, mesh=mesh, in_specs=in_specs, out_specs=out_specs, check_vma=False)
```

```python
import jax
import jax.numpy as jnp
from jax import lax
from jax.experimental import pallas as pl
from jax.experimental.pallas import tpu as pltpu
from jax.sharding import PartitionSpec as P

KVH = 8
HD = 128
GROUP = 8
BLOCK = 32
MESH = pl.DeviceIdType.MESH
HIDDEN = -1e30
BF16, F32 = jnp.bfloat16, jnp.float32


PLANE = {
    1: ((1, 1), (3, 3), (1, 3), (3, 1), (2, 1), (0, 3), (2, 3), (0, 1)),
    0: ((1, 0), (0, 2), (3, 2), (1, 2), (3, 0), (2, 2), (2, 0)),
}
ARRIVALS = {low: tuple((dx, low) for dx in (1, 3, 2, 0)) for low in (1, 0)}


def group_of(dx, low):
    return low * 4 + dx


def relay(
    slot_order_hbm, lengths_hbm, keys, values, keys_flat, values_flat, queries, new_keys, new_values,
    attention, keys_cache, values_cache,
    key_columns, value_rows, keys_line, values_chip, keys_packed, values_packed, keys_land, values_mid, values_land,
    fresh_rows, query_all, query_rows, fresh_all, result, rows_send, rows_land,
    slot_order, lengths, slot_of,
    scalar_sem, full_sem, fresh_sem, line_send, line_recv, chip_send, chip_recv,
    keys_send, keys_recv, mid_send, mid_recv, values_send, values_recv,
    small_send, small_recv, rows_send_sem, rows_recv_sem,
):
    s, h, b = lax.axis_index("section"), lax.axis_index("head"), lax.axis_index("batch")
    x, z = lax.div(s, 2), lax.div(h, 2)
    y_low = lax.rem(h, 2)
    y = lax.rem(s, 2) * 2 + y_low
    other = 1 - b
    sign = 1 - 2 * b
    mine = pl.ds(b * 16, 16)
    here = x * 4 + y
    here_mid = x * 4 + y_low * 2 + lax.div(y, 2)

    def remote(src, dst, send_sem, recv_sem, to):
        return pltpu.make_async_remote_copy(
            src_ref=src, dst_ref=dst, send_sem=send_sem, recv_sem=recv_sem,
            device_id=to, device_id_type=MESH,
        )

    def wait_for(ref, sem):
        pltpu.make_async_copy(ref, ref, sem).wait()

    def away(d, at, way):
        return lax.rem(at + way * d + 4, 4)

    def in_plane(at_x, at_y):
        return at_x * 2 + lax.div(at_y, 2), z * 2 + lax.rem(at_y, 2)

    def in_line(at_z):
        return at_z * 2 + y_low

    def owner_low(low):
        return lax.rem(y_low + low, 2)

    barrier = pltpu.get_barrier_semaphore()

    def greet(to):
        pl.semaphore_signal(barrier, inc=1, device_id=to, device_id_type=MESH)

    for dz in range(4):
        at_h = in_line(away(dz, z, 1))
        greet((s, at_h, other))
        if dz:
            greet((s, at_h, b))
    for low in (1, 0):
        for dx, dy in PLANE[low]:
            at_s, at_h = in_plane(away(dx, x, 1), away(dy, y, 1))
            greet((at_s, at_h, b))
            if low == 0:
                greet((at_s, at_h, other))

    scalars = [
        pltpu.make_async_copy(slot_order_hbm, slot_order, scalar_sem.at[0]),
        pltpu.make_async_copy(lengths_hbm, lengths, scalar_sem.at[1]),
    ]
    whole = [
        pltpu.make_async_copy(keys_flat.at[at], key_columns.at[:, pl.ds(at * HD, HD)], full_sem.at[0])
        for at in range(16)
    ]
    whole.append(pltpu.make_async_copy(values_flat, value_rows, full_sem.at[1]))
    fresh = [
        pltpu.make_async_copy(src, fresh_rows.at[n], fresh_sem.at[n])
        for n, src in enumerate((new_keys, new_values))
    ]
    for copy in scalars:
        copy.start()
    for low in (1, 0):
        pltpu.make_async_copy(
            values.at[:, :, owner_low(low), b], values_chip[low].at[mine], chip_recv.at[low]
        ).start()
    for low in (1, 0):
        pltpu.make_async_copy(
            keys.at[:, z, owner_low(low), b], keys_line[low].at[z, mine], line_recv.at[low]
        ).start()
    for copy in whole + fresh:
        copy.start()
    pl.semaphore_wait(barrier, 29)

    for low in (1, 0):
        remote(
            values.at[:, :, owner_low(low), other], values_chip[low].at[mine],
            chip_send, chip_recv.at[low], (s, h, other),
        ).start()

    def send_line(low, dz, to_b):
        to_z = away(dz, z, sign)
        remote(
            keys.at[:, to_z, owner_low(low), to_b], keys_line[low].at[z, mine],
            line_send, line_recv.at[low], (s, in_line(to_z), to_b),
        ).start()

    lines = [
        (low, dz, to_b)
        for low in (1, 0)
        for dz, to_b in ((1, b), (3, other), (2, b), (1, other), (3, b), (2, other), (0, other))
    ]
    for line in lines[:3]:
        send_line(*line)

    head_rows = pl.ds(pl.multiple_of(h * GROUP * HD, GROUP * HD), GROUP * HD)
    head_cols = pl.ds(pl.multiple_of(h * HD, HD), HD)

    def small_pieces(to_s):
        return (
            (queries.at[:, to_s, :, head_rows], query_all.at[s]),
            (new_keys.at[:, to_s, :, head_cols], fresh_all.at[0, s]),
            (new_values.at[:, to_s, :, head_cols], fresh_all.at[1, s]),
        )

    def send_small(step, carry):
        to_s = lax.rem(s + step, 8)
        for n, (src, dst) in enumerate(small_pieces(to_s)):
            remote(src, dst, small_send.at[n], small_recv.at[n], (to_s, h, b)).start()
        return carry

    lax.fori_loop(1, 8, send_small, 0)
    for n, (src, dst) in enumerate(small_pieces(s)):
        pltpu.make_async_copy(src, dst, small_recv.at[n]).start()

    scalars[0].wait()
    scalars[1].wait()

    def pack_values(low):
        def step(at_s, carry):
            for k in range(4):
                values_packed[at_s * 2 + owner_low(low), :, k] = values_chip[low][slot_order[at_s * 4 + k]]
            return carry

        lax.fori_loop(0, 8, step, 0)

    def pack_keys(low):
        def step(at_s, carry):
            for k in range(4):
                slot = slot_order[at_s * 4 + k]
                for from_z in range(4):
                    keys_packed[at_s * 2 + owner_low(low), from_z, k] = keys_line[low][from_z, slot]
            return carry

        lax.fori_loop(0, 8, step, 0)

    def send_plane(packed, dx, dy, dst, send_sem, recv_sem):
        to_x, to_y = away(dx, x, sign), away(dy, y, sign)
        to_s, to_h = in_plane(to_x, to_y)
        remote(
            packed.at[to_x * 4 + to_y], dst, send_sem, recv_sem.at[group_of(dx, dy % 2)], (to_s, to_h, b)
        ).start()

    lines = lines[3:]
    for low in (1, 0):
        wait_for(values_chip[low], chip_recv.at[low])
        pack_values(low)
        for dx, dy in PLANE[low]:
            send_plane(values_packed, dx, dy, values_mid.at[:, here_mid], mid_send, mid_recv)
            if lines:
                send_line(*lines.pop(0))
    assert not lines
    pltpu.make_async_copy(
        values_packed.at[here], values_mid.at[:, here_mid], mid_recv.at[group_of(0, 0)]
    ).start()

    def start_of(dx, low):
        return away(dx, x, -sign) * 4 + owner_low(low) * 2

    def turn(low):
        wait_for(keys_line[low], line_recv.at[low])
        pack_keys(low)
        chips = list(PLANE[low])
        for dx, _ in ARRIVALS[low]:
            group = group_of(dx, low)
            wait_for(values_mid.at[:, pl.ds(0, 2)], mid_recv.at[group])
            pair = pl.ds(away(dx, x, -sign) * 4 + owner_low(low) * 2, 2)
            for dz in (1, 3, 2):
                to_z = away(dz, z, sign)
                remote(
                    values_mid.at[to_z, pair], values_land.at[z, pair],
                    values_send, values_recv.at[group], (s, in_line(to_z), b),
                ).start()
                if dz != 3 and chips:
                    send_plane(keys_packed, *chips.pop(0), keys_land.at[here], keys_send, keys_recv)

    for n, part in enumerate((query_all, fresh_all.at[0], fresh_all.at[1])):
        wait_for(part, small_recv.at[n])
    wait_for(key_columns, full_sem.at[0])
    wait_for(value_rows, full_sem.at[1])

    def spread_queries(at_s, carry):
        for t in range(2):
            rows = query_all[at_s, t].astype(F32)
            for g in range(GROUP):
                row = (g // 4) * 8 + t * 4 + g % 4
                for k in range(4):
                    query_rows[at_s * 4 + k, row : row + 1, :] = rows[k : k + 1, g * HD : g * HD + HD]
        return carry

    lax.fori_loop(0, 8, spread_queries, 0)

    def find_slot(at, carry):
        found = jnp.int32(0)
        for slot in range(32):
            found = jnp.where(slot_order[slot] == b * 16 + at, slot, found)
        slot_of[at] = found
        return carry

    lax.fori_loop(0, 16, find_slot, 0)

    lane = lax.broadcasted_iota(jnp.int32, (1, HD), 1)
    lane_prompt = lax.div(lane, 16)
    lane_later = lax.rem(lax.div(lane, 4), 2) == 1
    block_lane = lax.div(lax.broadcasted_iota(jnp.int32, (HD, HD), 1), 16)
    row4 = lax.broadcasted_iota(jnp.int32, (4, HD), 0)
    row512 = lax.broadcasted_iota(jnp.int32, (512, HD), 0)
    scale = HD ** -0.5

    def attend(first):
        slots = [slot_of[first + p] for p in range(8)]
        live = jnp.zeros((1, HD), jnp.int32)
        for p in range(8):
            live = jnp.where(lane_prompt == p, lengths[first + p + b * 16], live)

        def fresh_row(n, t, slot):
            rows = fresh_all[n, lax.div(slot, 4), t].astype(F32)
            return jnp.sum(jnp.where(row4 == lax.rem(slot, 4), rows, 0.0), axis=0, keepdims=True)

        questions = jnp.concatenate([query_rows[slot] for slot in slots], axis=0).T
        diagonal = jnp.concatenate(
            [jnp.where(block_lane == p, questions, 0.0) for p in range(8)], axis=0
        ).astype(BF16)
        fresh_keys = jnp.concatenate(
            [
                jnp.concatenate([fresh_row(0, 0, slot), fresh_row(0, 1, slot), jnp.zeros((14, HD), F32)], axis=0)
                for slot in slots
            ],
            axis=1,
        ).astype(BF16)
        scores = jnp.dot(
            key_columns[:, first * HD : (first + 8) * HD], diagonal, preferred_element_type=F32
        ) * scale
        fresh_scores = jnp.dot(fresh_keys, diagonal, preferred_element_type=F32) * scale
        kept = row512 < live
        scores = jnp.where(kept, scores, HIDDEN)
        n0 = fresh_scores[0:1]
        n1 = jnp.where(lane_later, fresh_scores[1:2], HIDDEN)
        peak = jnp.maximum(jnp.max(scores, axis=0, keepdims=True), jnp.maximum(n0, n1))
        mass = jnp.where(kept, jnp.exp(scores - peak), 0.0)
        m0 = jnp.exp(n0 - peak)
        m1 = jnp.where(lane_later, jnp.exp(n1 - peak), 0.0)
        total = jnp.sum(mass, axis=0, keepdims=True) + m0 + m1
        weights = mass.T.astype(BF16)
        m0, m1 = (m.astype(BF16).astype(F32) for m in (m0, m1))
        sides = jnp.concatenate([total, m0, m1, jnp.zeros((HD - 3, HD), F32)], axis=0).T
        for p, slot in enumerate(slots):
            cut = slice(p * 16, p * 16 + 16)
            weighted = jnp.dot(weights[cut], value_rows[first + p], preferred_element_type=F32)
            weighted += sides[cut, 1:2] * fresh_row(1, 0, slot)
            weighted += sides[cut, 2:3] * fresh_row(1, 1, slot)
            result[first + p] = weighted / sides[cut, 0:1]

    attend(0)
    attend(8)

    def hand_rows(at_s, carry):
        for pair in range(2):
            first, second = (
                result[jnp.clip(slot_order[at_s * 4 + pair * 2 + n] - b * 16, 0, 15)] for n in range(2)
            )
            for to_b in range(2):
                cut = slice(to_b * 8, to_b * 8 + 8)
                rows_send[at_s, to_b, pair] = jnp.concatenate((first[cut], second[cut]), axis=0).astype(BF16)
        return carry

    lax.fori_loop(0, 8, hand_rows, 0)

    def send_rows(to_s, to_b):
        remote(
            rows_send.at[to_s, to_b], rows_land.at[s, b], rows_send_sem, rows_recv_sem, (to_s, h, to_b)
        ).start()

    def send_rows_step(step, carry):
        to_s = lax.rem(s + step, 8)
        send_rows(to_s, b)
        send_rows(to_s, other)
        return carry

    lax.fori_loop(1, 8, send_rows_step, 0)
    send_rows(s, other)
    pltpu.make_async_copy(rows_send.at[s, b], rows_land.at[s, b], rows_recv_sem).start()
    turn(1)
    turn(0)

    slots = [slot_order[s * 4 + k] for k in range(4)]
    lives = [lengths[slot] for slot in slots]
    position = (h * 2 + b) * BLOCK + lax.broadcasted_iota(jnp.int32, (BLOCK, HD), 0)
    fresh[0].wait()
    fresh[1].wait()

    def settle(block, n, from_x, from_y, from_z):
        layer = from_x * 2 + lax.div(from_y, 2)
        cut = pl.ds(pl.multiple_of((from_z * 2 + lax.rem(from_y, 2)) * HD, HD), HD)
        out = (keys_cache, values_cache)[n]
        placed = [fresh_rows[n, t, layer, :, cut].astype(F32) for t in range(2)]
        for k in range(4):
            rows = jnp.where(position < lives[k], block[k].astype(F32), 0.0)
            for t in range(2):
                rows = jnp.where(position == lives[k] + t, placed[t][k : k + 1], rows)
            out[layer, k, :, cut] = rows.astype(BF16)

    def settle_keys(src, from_x, from_y):
        def step(from_z, carry):
            settle(src.at[from_x * 4 + from_y, from_z], 0, from_x, from_y, from_z)
            return carry

        lax.fori_loop(0, 4, step, 0)

    def settle_values(src, from_x, low, from_z):
        def step(half, carry):
            from_low = owner_low(low)
            block = src.at[from_z, from_x * 4 + from_low * 2 + half]
            settle(block, 1, from_x, half * 2 + from_low, from_z)
            return carry

        lax.fori_loop(0, 2, step, 0)

    owners = [lax.div(slot, 16) for slot in slots]

    def assemble(l, carry):
        picked = []
        for k in range(4):
            part = slice((k % 2) * 8, (k % 2) * 8 + 8)
            first, second = (rows_land[l, n, k // 2].astype(F32)[part] for n in range(2))
            picked.append(jnp.where(owners[k] == 0, first, second))
        for t in range(2):
            attention[t, l] = jnp.concatenate(
                [
                    jnp.concatenate([rows[t * 4 + g : t * 4 + g + 1] for rows in picked], axis=0)
                    for g in range(4)
                ],
                axis=1,
            ).astype(BF16)
        return carry

    settle_keys(keys_packed, x, y)
    for low in (1, 0):
        for dx, _ in ARRIVALS[low]:
            settle_values(values_mid, away(dx, x, -sign), low, z)
    for low in (1, 0):
        if low == 0:
            wait_for(rows_land, rows_recv_sem)
            lax.fori_loop(0, 8, assemble, 0)
        for dx, _ in ARRIVALS[low]:
            group = group_of(dx, low)
            from_x = away(dx, x, -sign)
            chips = [dy for to_x, dy in PLANE[low] if to_x == dx]
            wait_for(keys_land.at[pl.ds(0, len(chips))], keys_recv.at[group])
            for dy in chips:
                settle_keys(keys_land, from_x, away(dy, y, -sign))
            wait_for(values_land.at[pl.ds(0, 3), pl.ds(0, 2)], values_recv.at[group])
            for dz in (1, 3, 2):
                settle_values(values_land, from_x, low, away(dz, z, -sign))

    wait_for(value_rows.at[pl.ds(0, 8)], chip_send)
    wait_for(value_rows.at[pl.ds(0, 14)], line_send)
    for n, part in enumerate((query_all, fresh_all.at[0], fresh_all.at[1])):
        wait_for(part.at[pl.ds(0, 7)], small_send.at[n])
    wait_for(values_packed.at[pl.ds(0, 15)], mid_send)
    wait_for(keys_packed.at[pl.ds(0, 15)], keys_send)
    wait_for(values_land.at[pl.ds(0, 3)], values_send)
    wait_for(rows_send.at[pl.ds(0, 7)], rows_send_sem)
    wait_for(rows_send.at[0, 0], rows_send_sem)


def hand_out(attention, keys, values, attention_out, keys_out, values_out, sem):
    copies = [pltpu.make_async_copy(attention, attention_out, sem.at[16])]
    for n, (src, dst) in enumerate(((keys, keys_out), (values, values_out))):
        copies += [pltpu.make_async_copy(src.at[l], dst.at[l], sem.at[n * 8 + l]) for l in range(8)]
    for copy in copies:
        copy.start()
    for copy in copies:
        copy.wait()


def body(keys_prefill, values_prefill, lengths, slot_order, queries, new_keys, new_values):
    keys = keys_prefill.reshape(16, 4, 2, 2, BLOCK, HD)
    values = values_prefill.reshape(16, 4, 2, 2, BLOCK, HD)
    flat = (keys_prefill.reshape(16, 512, HD), values_prefill.reshape(16, 512, HD))
    any_spec = pl.BlockSpec(memory_space=pl.ANY)
    hbm_spec = pl.BlockSpec(memory_space=pltpu.HBM)
    vmem_spec = pl.BlockSpec(memory_space=pltpu.VMEM)
    dma, vmem = pltpu.SemaphoreType.DMA, pltpu.VMEM
    rows_shape, cache_shape = (2, 8, 4, 4 * HD), (8, 4, BLOCK, KVH * HD)
    plane, line = vmem((16, 4, 4, BLOCK, HD), BF16), vmem((4, 16, 4, BLOCK, HD), BF16)

    def in_hbm(array):
        return pltpu.with_memory_space_constraint(array, pltpu.HBM)

    held = pl.pallas_call(
        relay,
        out_shape=(vmem(rows_shape, BF16), vmem(cache_shape, BF16), vmem(cache_shape, BF16)),
        in_specs=[hbm_spec] * 9,
        out_specs=(vmem_spec,) * 3,
        scratch_shapes=[
            vmem((512, 16 * HD), BF16), vmem((16, 512, HD), BF16),
            [vmem((4, 32, BLOCK, HD), BF16)] * 2, [vmem((32, 4, BLOCK, HD), BF16)] * 2,
            plane, plane, plane, line, line,
            vmem((2, 2, 8, 4, KVH * HD), BF16), vmem((8, 2, 4, GROUP * HD), BF16), vmem((32, 16, HD), F32),
            vmem((2, 8, 2, 4, HD), BF16), vmem((16, 16, HD), F32),
            vmem((8, 2, 2, 16, HD), BF16), vmem((8, 2, 2, 16, HD), BF16),
            pltpu.SMEM((32,), jnp.int32), pltpu.SMEM((32,), jnp.int32), pltpu.SMEM((16,), jnp.int32),
            dma((2,)), dma((2,)), dma((2,)), dma, dma((2,)), dma, dma((2,)),
            dma, dma((8,)), dma, dma((8,)), dma, dma((8,)),
            dma((3,)), dma((3,)), dma, dma,
        ],
        compiler_params=pltpu.CompilerParams(
            collective_id=0, has_side_effects=True, vmem_limit_bytes=48 * 2**20
        ),
        name="relay",
    )(*(in_hbm(x) for x in (slot_order, lengths, keys, values, *flat, queries, new_keys, new_values)))
    return pl.pallas_call(
        hand_out,
        out_shape=tuple(jax.ShapeDtypeStruct(shape, BF16) for shape in (rows_shape, cache_shape, cache_shape)),
        in_specs=[vmem_spec] * 3,
        out_specs=(any_spec,) * 3,
        scratch_shapes=[dma((17,))],
        compiler_params=pltpu.CompilerParams(vmem_limit_bytes=8 * 2**20),
        name="hand_out",
    )(*(pltpu.with_memory_space_constraint(x, pltpu.VMEM) for x in held))


def solution(mesh):
    in_specs = (
        P("section", "batch", None, "head"),
        P("section", "batch", None, "head"),
        P(),
        P(),
        P(None, None, "section", None),
        P(None, None, "section", None),
        P(None, None, "section", None),
    )
    out_specs = (
        P(None, None, "section", ("head", "batch")),
        P(None, "section", ("head", "batch"), None),
        P(None, "section", ("head", "batch"), None),
    )
    return jax.shard_map(body, mesh=mesh, in_specs=in_specs, out_specs=out_specs, check_vma=False)
```

```python
import jax
import jax.numpy as jnp
from jax import lax
from jax.experimental import pallas as pl
from jax.experimental.pallas import tpu as pltpu
from jax.sharding import PartitionSpec as P

KVH = 8
HD = 128
GROUP = 8
BLOCK = 32
MESH = pl.DeviceIdType.MESH
HIDDEN = -1e30
BF16, F32 = jnp.bfloat16, jnp.float32


PLANE = {
    1: ((1, 1), (3, 3), (1, 3), (3, 1), (2, 1), (0, 3), (2, 3), (0, 1)),
    0: ((1, 0), (0, 2), (3, 2), (1, 2), (3, 0), (2, 2), (2, 0)),
}
ARRIVALS = {low: tuple((dx, low) for dx in (1, 3, 2, 0)) for low in (1, 0)}


def group_of(dx, low):
    return low * 4 + dx


def relay(
    slot_order_hbm, lengths_hbm, keys, values, keys_flat, values_flat, queries, new_keys, new_values,
    attention, keys_cache, values_cache,
    key_columns, value_rows, keys_line, values_chip, keys_packed, values_packed, keys_land, values_mid, values_land,
    fresh_rows, query_all, query_rows, fresh_all, result, rows_send, rows_land,
    slot_order, lengths, slot_of,
    scalar_sem, full_sem, fresh_sem, line_send, line_recv, chip_send, chip_recv,
    keys_send, keys_recv, mid_send, mid_recv, values_send, values_recv,
    small_send, small_recv, rows_send_sem, rows_recv_sem,
):
    s, h, b = lax.axis_index("section"), lax.axis_index("head"), lax.axis_index("batch")
    x, z = lax.div(s, 2), lax.div(h, 2)
    y_low = lax.rem(h, 2)
    y = lax.rem(s, 2) * 2 + y_low
    other = 1 - b
    sign = 1 - 2 * b
    mine = pl.ds(b * 16, 16)
    here = x * 4 + y
    here_mid = x * 4 + y_low * 2 + lax.div(y, 2)

    def remote(src, dst, send_sem, recv_sem, to):
        return pltpu.make_async_remote_copy(
            src_ref=src, dst_ref=dst, send_sem=send_sem, recv_sem=recv_sem,
            device_id=to, device_id_type=MESH,
        )

    def wait_for(ref, sem):
        pltpu.make_async_copy(ref, ref, sem).wait()

    def away(d, at, way):
        return lax.rem(at + way * d + 4, 4)

    def in_plane(at_x, at_y):
        return at_x * 2 + lax.div(at_y, 2), z * 2 + lax.rem(at_y, 2)

    def in_line(at_z):
        return at_z * 2 + y_low

    def owner_low(low):
        return lax.rem(y_low + low, 2)

    barrier = pltpu.get_barrier_semaphore()

    def greet(to):
        pl.semaphore_signal(barrier, inc=1, device_id=to, device_id_type=MESH)

    for dz in range(4):
        at_h = in_line(away(dz, z, 1))
        greet((s, at_h, other))
        if dz:
            greet((s, at_h, b))
    for low in (1, 0):
        for dx, dy in PLANE[low]:
            at_s, at_h = in_plane(away(dx, x, 1), away(dy, y, 1))
            greet((at_s, at_h, b))
            if low == 0:
                greet((at_s, at_h, other))

    scalars = [
        pltpu.make_async_copy(slot_order_hbm, slot_order, scalar_sem.at[0]),
        pltpu.make_async_copy(lengths_hbm, lengths, scalar_sem.at[1]),
    ]
    whole = [
        pltpu.make_async_copy(keys_flat.at[at], key_columns.at[:, pl.ds(at * HD, HD)], full_sem.at[0])
        for at in range(16)
    ]
    whole.append(pltpu.make_async_copy(values_flat, value_rows, full_sem.at[1]))
    fresh = [
        pltpu.make_async_copy(src, fresh_rows.at[n], fresh_sem.at[n])
        for n, src in enumerate((new_keys, new_values))
    ]
    for copy in scalars:
        copy.start()
    for low in (1, 0):
        pltpu.make_async_copy(
            values.at[:, :, owner_low(low), b], values_chip[low].at[mine], chip_recv.at[low]
        ).start()
    for low in (1, 0):
        pltpu.make_async_copy(
            keys.at[:, z, owner_low(low), b], keys_line[low].at[z, mine], line_recv.at[low]
        ).start()
    for copy in whole + fresh:
        copy.start()
    pl.semaphore_wait(barrier, 29)

    for low in (1, 0):
        remote(
            values.at[:, :, owner_low(low), other], values_chip[low].at[mine],
            chip_send, chip_recv.at[low], (s, h, other),
        ).start()

    def send_line(low, dz, to_b):
        to_z = away(dz, z, sign)
        remote(
            keys.at[:, to_z, owner_low(low), to_b], keys_line[low].at[z, mine],
            line_send, line_recv.at[low], (s, in_line(to_z), to_b),
        ).start()

    lines = [
        (low, dz, to_b)
        for low in (1, 0)
        for dz, to_b in ((1, b), (3, other), (2, b), (1, other), (3, b), (2, other), (0, other))
    ]
    for line in lines[:3]:
        send_line(*line)

    head_rows = pl.ds(pl.multiple_of(h * GROUP * HD, GROUP * HD), GROUP * HD)
    head_cols = pl.ds(pl.multiple_of(h * HD, HD), HD)

    def small_pieces(to_s):
        return (
            (queries.at[:, to_s, :, head_rows], query_all.at[s]),
            (new_keys.at[:, to_s, :, head_cols], fresh_all.at[0, s]),
            (new_values.at[:, to_s, :, head_cols], fresh_all.at[1, s]),
        )

    def send_small(step, carry):
        to_s = lax.rem(s + step, 8)
        for n, (src, dst) in enumerate(small_pieces(to_s)):
            remote(src, dst, small_send.at[n], small_recv.at[n], (to_s, h, b)).start()
        return carry

    lax.fori_loop(1, 8, send_small, 0)
    for n, (src, dst) in enumerate(small_pieces(s)):
        pltpu.make_async_copy(src, dst, small_recv.at[n]).start()

    scalars[0].wait()
    scalars[1].wait()

    def pack_values(low):
        def step(at_s, carry):
            for k in range(4):
                values_packed[at_s * 2 + owner_low(low), :, k] = values_chip[low][slot_order[at_s * 4 + k]]
            return carry

        lax.fori_loop(0, 8, step, 0)

    def pack_keys(low):
        def step(at_s, carry):
            for k in range(4):
                slot = slot_order[at_s * 4 + k]
                for from_z in range(4):
                    keys_packed[at_s * 2 + owner_low(low), from_z, k] = keys_line[low][from_z, slot]
            return carry

        lax.fori_loop(0, 8, step, 0)

    def send_plane(packed, dx, dy, dst, send_sem, recv_sem):
        to_x, to_y = away(dx, x, sign), away(dy, y, sign)
        to_s, to_h = in_plane(to_x, to_y)
        remote(
            packed.at[to_x * 4 + to_y], dst, send_sem, recv_sem.at[group_of(dx, dy % 2)], (to_s, to_h, b)
        ).start()

    lines = lines[3:]
    for low in (1, 0):
        wait_for(values_chip[low], chip_recv.at[low])
        pack_values(low)
        for dx, dy in PLANE[low]:
            send_plane(values_packed, dx, dy, values_mid.at[:, here_mid], mid_send, mid_recv)
            if lines:
                send_line(*lines.pop(0))
    assert not lines
    pltpu.make_async_copy(
        values_packed.at[here], values_mid.at[:, here_mid], mid_recv.at[group_of(0, 0)]
    ).start()

    def start_of(dx, low):
        return away(dx, x, -sign) * 4 + owner_low(low) * 2

    def forward_values(dx, low):
        group = group_of(dx, low)
        wait_for(values_mid.at[:, pl.ds(0, 2)], mid_recv.at[group])
        pair = pl.ds(away(dx, x, -sign) * 4 + owner_low(low) * 2, 2)
        for dz in (1, 3, 2):
            to_z = away(dz, z, sign)
            remote(
                values_mid.at[to_z, pair], values_land.at[z, pair],
                values_send, values_recv.at[group], (s, in_line(to_z), b),
            ).start()

    def take_keys(low):
        wait_for(keys_line[low], line_recv.at[low])
        pack_keys(low)

    def send_keys(chips):
        for dx, dy in chips:
            send_plane(keys_packed, dx, dy, keys_land.at[here], keys_send, keys_recv)

    for n, part in enumerate((query_all, fresh_all.at[0], fresh_all.at[1])):
        wait_for(part, small_recv.at[n])
    wait_for(key_columns, full_sem.at[0])
    wait_for(value_rows, full_sem.at[1])

    def spread_queries(at_s, carry):
        for t in range(2):
            rows = query_all[at_s, t].astype(F32)
            for g in range(GROUP):
                row = (g // 4) * 8 + t * 4 + g % 4
                for k in range(4):
                    query_rows[at_s * 4 + k, row : row + 1, :] = rows[k : k + 1, g * HD : g * HD + HD]
        return carry

    lax.fori_loop(0, 8, spread_queries, 0)

    def find_slot(at, carry):
        found = jnp.int32(0)
        for slot in range(32):
            found = jnp.where(slot_order[slot] == b * 16 + at, slot, found)
        slot_of[at] = found
        return carry

    lax.fori_loop(0, 16, find_slot, 0)

    lane = lax.broadcasted_iota(jnp.int32, (1, HD), 1)
    lane_prompt = lax.div(lane, 16)
    lane_later = lax.rem(lax.div(lane, 4), 2) == 1
    block_lane = lax.div(lax.broadcasted_iota(jnp.int32, (HD, HD), 1), 16)
    row4 = lax.broadcasted_iota(jnp.int32, (4, HD), 0)
    row512 = lax.broadcasted_iota(jnp.int32, (512, HD), 0)
    scale = HD ** -0.5

    def attend(first):
        slots = [slot_of[first + p] for p in range(8)]
        live = jnp.zeros((1, HD), jnp.int32)
        for p in range(8):
            live = jnp.where(lane_prompt == p, lengths[first + p + b * 16], live)

        def fresh_row(n, t, slot):
            rows = fresh_all[n, lax.div(slot, 4), t].astype(F32)
            return jnp.sum(jnp.where(row4 == lax.rem(slot, 4), rows, 0.0), axis=0, keepdims=True)

        questions = jnp.concatenate([query_rows[slot] for slot in slots], axis=0).T
        diagonal = jnp.concatenate(
            [jnp.where(block_lane == p, questions, 0.0) for p in range(8)], axis=0
        ).astype(BF16)
        fresh_keys = jnp.concatenate(
            [
                jnp.concatenate([fresh_row(0, 0, slot), fresh_row(0, 1, slot), jnp.zeros((14, HD), F32)], axis=0)
                for slot in slots
            ],
            axis=1,
        ).astype(BF16)
        scores = jnp.dot(
            key_columns[:, first * HD : (first + 8) * HD], diagonal, preferred_element_type=F32
        ) * scale
        fresh_scores = jnp.dot(fresh_keys, diagonal, preferred_element_type=F32) * scale
        kept = row512 < live
        scores = jnp.where(kept, scores, HIDDEN)
        n0 = fresh_scores[0:1]
        n1 = jnp.where(lane_later, fresh_scores[1:2], HIDDEN)
        peak = jnp.maximum(jnp.max(scores, axis=0, keepdims=True), jnp.maximum(n0, n1))
        mass = jnp.where(kept, jnp.exp(scores - peak), 0.0)
        m0 = jnp.exp(n0 - peak)
        m1 = jnp.where(lane_later, jnp.exp(n1 - peak), 0.0)
        total = jnp.sum(mass, axis=0, keepdims=True) + m0 + m1
        weights = mass.T.astype(BF16)
        m0, m1 = (m.astype(BF16).astype(F32) for m in (m0, m1))
        sides = jnp.concatenate([total, m0, m1, jnp.zeros((HD - 3, HD), F32)], axis=0).T
        for p, slot in enumerate(slots):
            cut = slice(p * 16, p * 16 + 16)
            weighted = jnp.dot(weights[cut], value_rows[first + p], preferred_element_type=F32)
            weighted += sides[cut, 1:2] * fresh_row(1, 0, slot)
            weighted += sides[cut, 2:3] * fresh_row(1, 1, slot)
            result[first + p] = weighted / sides[cut, 0:1]

    attend(0)
    attend(8)

    def hand_rows(at_s, carry):
        for pair in range(2):
            first, second = (
                result[jnp.clip(slot_order[at_s * 4 + pair * 2 + n] - b * 16, 0, 15)] for n in range(2)
            )
            for to_b in range(2):
                cut = slice(to_b * 8, to_b * 8 + 8)
                rows_send[at_s, to_b, pair] = jnp.concatenate((first[cut], second[cut]), axis=0).astype(BF16)
        return carry

    lax.fori_loop(0, 8, hand_rows, 0)

    def send_rows(to_s, to_b):
        remote(
            rows_send.at[to_s, to_b], rows_land.at[s, b], rows_send_sem, rows_recv_sem, (to_s, h, to_b)
        ).start()

    def send_rows_step(step, carry):
        to_s = lax.rem(s + step, 8)
        send_rows(to_s, b)
        send_rows(to_s, other)
        return carry

    lax.fori_loop(1, 8, send_rows_step, 0)
    send_rows(s, other)
    pltpu.make_async_copy(rows_send.at[s, b], rows_land.at[s, b], rows_recv_sem).start()
    for group in ARRIVALS[1]:
        forward_values(*group)
    take_keys(1)
    for group in ARRIVALS[0][:3]:
        forward_values(*group)
    send_keys(PLANE[1][:4])
    forward_values(*ARRIVALS[0][3])
    send_keys(PLANE[1][4:])
    take_keys(0)
    send_keys(PLANE[0])

    slots = [slot_order[s * 4 + k] for k in range(4)]
    lives = [lengths[slot] for slot in slots]
    position = (h * 2 + b) * BLOCK + lax.broadcasted_iota(jnp.int32, (BLOCK, HD), 0)
    fresh[0].wait()
    fresh[1].wait()

    def settle(block, n, from_x, from_y, from_z):
        layer = from_x * 2 + lax.div(from_y, 2)
        cut = pl.ds(pl.multiple_of((from_z * 2 + lax.rem(from_y, 2)) * HD, HD), HD)
        out = (keys_cache, values_cache)[n]
        placed = [fresh_rows[n, t, layer, :, cut].astype(F32) for t in range(2)]
        for k in range(4):
            rows = jnp.where(position < lives[k], block[k].astype(F32), 0.0)
            for t in range(2):
                rows = jnp.where(position == lives[k] + t, placed[t][k : k + 1], rows)
            out[layer, k, :, cut] = rows.astype(BF16)

    def settle_keys(src, from_x, from_y):
        def step(from_z, carry):
            settle(src.at[from_x * 4 + from_y, from_z], 0, from_x, from_y, from_z)
            return carry

        lax.fori_loop(0, 4, step, 0)

    def settle_values(src, from_x, low, from_z):
        def step(half, carry):
            from_low = owner_low(low)
            block = src.at[from_z, from_x * 4 + from_low * 2 + half]
            settle(block, 1, from_x, half * 2 + from_low, from_z)
            return carry

        lax.fori_loop(0, 2, step, 0)

    owners = [lax.div(slot, 16) for slot in slots]

    def assemble(l, carry):
        picked = []
        for k in range(4):
            part = slice((k % 2) * 8, (k % 2) * 8 + 8)
            first, second = (rows_land[l, n, k // 2].astype(F32)[part] for n in range(2))
            picked.append(jnp.where(owners[k] == 0, first, second))
        for t in range(2):
            attention[t, l] = jnp.concatenate(
                [
                    jnp.concatenate([rows[t * 4 + g : t * 4 + g + 1] for rows in picked], axis=0)
                    for g in range(4)
                ],
                axis=1,
            ).astype(BF16)
        return carry

    settle_keys(keys_packed, x, y)
    for low in (1, 0):
        for dx, _ in ARRIVALS[low]:
            settle_values(values_mid, away(dx, x, -sign), low, z)
    for low in (1, 0):
        if low == 0:
            wait_for(rows_land, rows_recv_sem)
            lax.fori_loop(0, 8, assemble, 0)
        for dx, _ in ARRIVALS[low]:
            group = group_of(dx, low)
            from_x = away(dx, x, -sign)
            chips = [dy for to_x, dy in PLANE[low] if to_x == dx]
            wait_for(keys_land.at[pl.ds(0, len(chips))], keys_recv.at[group])
            for dy in chips:
                settle_keys(keys_land, from_x, away(dy, y, -sign))
            wait_for(values_land.at[pl.ds(0, 3), pl.ds(0, 2)], values_recv.at[group])
            for dz in (1, 3, 2):
                settle_values(values_land, from_x, low, away(dz, z, -sign))

    wait_for(value_rows.at[pl.ds(0, 8)], chip_send)
    wait_for(value_rows.at[pl.ds(0, 14)], line_send)
    for n, part in enumerate((query_all, fresh_all.at[0], fresh_all.at[1])):
        wait_for(part.at[pl.ds(0, 7)], small_send.at[n])
    wait_for(values_packed.at[pl.ds(0, 15)], mid_send)
    wait_for(keys_packed.at[pl.ds(0, 15)], keys_send)
    wait_for(values_land.at[pl.ds(0, 3)], values_send)
    wait_for(rows_send.at[pl.ds(0, 7)], rows_send_sem)
    wait_for(rows_send.at[0, 0], rows_send_sem)


def hand_out(attention, keys, values, attention_out, keys_out, values_out, sem):
    copies = [pltpu.make_async_copy(attention, attention_out, sem.at[16])]
    for n, (src, dst) in enumerate(((keys, keys_out), (values, values_out))):
        copies += [pltpu.make_async_copy(src.at[l], dst.at[l], sem.at[n * 8 + l]) for l in range(8)]
    for copy in copies:
        copy.start()
    for copy in copies:
        copy.wait()


def body(keys_prefill, values_prefill, lengths, slot_order, queries, new_keys, new_values):
    keys = keys_prefill.reshape(16, 4, 2, 2, BLOCK, HD)
    values = values_prefill.reshape(16, 4, 2, 2, BLOCK, HD)
    flat = (keys_prefill.reshape(16, 512, HD), values_prefill.reshape(16, 512, HD))
    any_spec = pl.BlockSpec(memory_space=pl.ANY)
    hbm_spec = pl.BlockSpec(memory_space=pltpu.HBM)
    vmem_spec = pl.BlockSpec(memory_space=pltpu.VMEM)
    dma, vmem = pltpu.SemaphoreType.DMA, pltpu.VMEM
    rows_shape, cache_shape = (2, 8, 4, 4 * HD), (8, 4, BLOCK, KVH * HD)
    plane, line = vmem((16, 4, 4, BLOCK, HD), BF16), vmem((4, 16, 4, BLOCK, HD), BF16)

    def in_hbm(array):
        return pltpu.with_memory_space_constraint(array, pltpu.HBM)

    held = pl.pallas_call(
        relay,
        out_shape=(vmem(rows_shape, BF16), vmem(cache_shape, BF16), vmem(cache_shape, BF16)),
        in_specs=[hbm_spec] * 9,
        out_specs=(vmem_spec,) * 3,
        scratch_shapes=[
            vmem((512, 16 * HD), BF16), vmem((16, 512, HD), BF16),
            [vmem((4, 32, BLOCK, HD), BF16)] * 2, [vmem((32, 4, BLOCK, HD), BF16)] * 2,
            plane, plane, plane, line, line,
            vmem((2, 2, 8, 4, KVH * HD), BF16), vmem((8, 2, 4, GROUP * HD), BF16), vmem((32, 16, HD), F32),
            vmem((2, 8, 2, 4, HD), BF16), vmem((16, 16, HD), F32),
            vmem((8, 2, 2, 16, HD), BF16), vmem((8, 2, 2, 16, HD), BF16),
            pltpu.SMEM((32,), jnp.int32), pltpu.SMEM((32,), jnp.int32), pltpu.SMEM((16,), jnp.int32),
            dma((2,)), dma((2,)), dma((2,)), dma, dma((2,)), dma, dma((2,)),
            dma, dma((8,)), dma, dma((8,)), dma, dma((8,)),
            dma((3,)), dma((3,)), dma, dma,
        ],
        compiler_params=pltpu.CompilerParams(
            collective_id=0, has_side_effects=True, vmem_limit_bytes=48 * 2**20
        ),
        name="relay",
    )(*(in_hbm(x) for x in (slot_order, lengths, keys, values, *flat, queries, new_keys, new_values)))
    return pl.pallas_call(
        hand_out,
        out_shape=tuple(jax.ShapeDtypeStruct(shape, BF16) for shape in (rows_shape, cache_shape, cache_shape)),
        in_specs=[vmem_spec] * 3,
        out_specs=(any_spec,) * 3,
        scratch_shapes=[dma((17,))],
        compiler_params=pltpu.CompilerParams(vmem_limit_bytes=8 * 2**20),
        name="hand_out",
    )(*(pltpu.with_memory_space_constraint(x, pltpu.VMEM) for x in held))


def solution(mesh):
    in_specs = (
        P("section", "batch", None, "head"),
        P("section", "batch", None, "head"),
        P(),
        P(),
        P(None, None, "section", None),
        P(None, None, "section", None),
        P(None, None, "section", None),
    )
    out_specs = (
        P(None, None, "section", ("head", "batch")),
        P(None, "section", ("head", "batch"), None),
        P(None, "section", ("head", "batch"), None),
    )
    return jax.shard_map(body, mesh=mesh, in_specs=in_specs, out_specs=out_specs, check_vma=False)
```

```python
import jax
import jax.numpy as jnp
from jax import lax
from jax.experimental import pallas as pl
from jax.experimental.pallas import tpu as pltpu
from jax.sharding import PartitionSpec as P

KVH = 8
HD = 128
GROUP = 8
BLOCK = 32
MESH = pl.DeviceIdType.MESH
HIDDEN = -1e30
BF16, F32 = jnp.bfloat16, jnp.float32


PIECES = ((2, 1), (2, 0), (1, 0), (3, 0), (1, 1), (3, 1), (0, 1), (0, 0))


def has_tie(offset):
    return 2 in offset


OFFSETS = [(dx, dy, dz) for dz, low in PIECES for dy in (low, low + 2) for dx in (1, 3, 2, 0)]
STOPS = [o for o in OFFSETS if has_tie(o)]
DIRECT = [o for o in OFFSETS if not has_tie(o) and any(o)]


def coordinates(offset, sign, s, h):
    dx, dy, dz = offset
    x = lax.rem(lax.div(s, 2) + sign * dx + 4, 4)
    y = lax.rem(lax.rem(s, 2) * 2 + lax.rem(h, 2) + sign * dy + 4, 4)
    z = lax.rem(lax.div(h, 2) + sign * dz + 4, 4)
    return x * 2 + lax.div(y, 2), z * 2 + lax.rem(y, 2)


def first_leg(offset):
    return tuple(d // 2 * (1 - d % 2) if isinstance(d, int) else lax.div(d, 2) * (1 - lax.rem(d, 2)) for d in offset)


def pack_word(offsets):
    return sum((dx + 4 * dy + 16 * dz) * 64**n for n, (dx, dy, dz) in enumerate(offsets))


def from_word(word):
    return lax.rem(word, 4), lax.rem(lax.div(word, 4), 4), lax.rem(lax.div(word, 16), 4)


def relay(
    slot_order_hbm, lengths_hbm, keys, values, keys_flat, values_flat, queries, new_keys, new_values,
    attention, keys_cache, values_cache,
    gathered, key_columns, value_rows, packed, landed, stopped,
    fresh_rows, query_all, query_rows, fresh_all, result, rows_send, rows_land,
    slot_order, lengths, slot_of,
    piece_sem, swap_send, full_sem, fresh_sem, small_send, small_recv,
    bulk_send, bulk_recv, stop_send, stop_recv, rows_send_sem, rows_recv_sem, scalar_sem,
):
    s, h, b = lax.axis_index("section"), lax.axis_index("head"), lax.axis_index("batch")
    other = 1 - b
    sign = 1 - 2 * b
    mine = pl.ds(b * 16, 16)
    caches = (keys, values)

    def remote(src, dst, send_sem, recv_sem, to):
        return pltpu.make_async_remote_copy(
            src_ref=src, dst_ref=dst, send_sem=send_sem, recv_sem=recv_sem,
            device_id=to, device_id_type=MESH,
        )

    def wait_for(ref, sem):
        pltpu.make_async_copy(ref, ref, sem).wait()

    def head_at(piece, sign):
        dz, dy = PIECES[piece]
        return coordinates((0, dy, dz), sign, s, h)[1]

    scalars = [
        pltpu.make_async_copy(slot_order_hbm, slot_order, scalar_sem.at[0]),
        pltpu.make_async_copy(lengths_hbm, lengths, scalar_sem.at[1]),
    ]
    for copy in scalars:
        copy.start()
    for piece in range(8):
        for n in range(2):
            pltpu.make_async_copy(
                caches[n].at[:, head_at(piece, sign), b], gathered[piece].at[n, mine], piece_sem.at[piece]
            ).start()
    whole = [
        pltpu.make_async_copy(keys_flat.at[at], key_columns.at[:, pl.ds(at * HD, HD)], full_sem.at[0])
        for at in range(16)
    ]
    whole.append(pltpu.make_async_copy(values_flat, value_rows, full_sem.at[1]))
    fresh = [
        pltpu.make_async_copy(src, fresh_rows.at[n], fresh_sem.at[n])
        for n, src in enumerate((new_keys, new_values))
    ]
    for copy in whole + fresh:
        copy.start()

    barrier = pltpu.get_barrier_semaphore()

    def greet_other(step, carry):
        pl.semaphore_signal(
            barrier, inc=1, device_id=(lax.rem(s + step, 8), h, other), device_id_type=MESH
        )
        return carry

    def greet(step, carry):
        to_s, to_h = lax.rem(s + lax.div(step, 8), 8), lax.rem(h + lax.rem(step, 8), 8)
        pl.semaphore_signal(barrier, inc=1, device_id=(to_s, to_h, b), device_id_type=MESH)
        return carry

    lax.fori_loop(0, 8, greet_other, 0)
    lax.fori_loop(1, 64, greet, 0)
    pl.semaphore_wait(barrier, 71)

    for piece in range(8):
        for n in range(2):
            remote(
                caches[n].at[:, head_at(piece, -sign), other], gathered[piece].at[n, mine],
                swap_send, piece_sem.at[piece], (s, h, other),
            ).start()

    head_rows = pl.ds(pl.multiple_of(h * GROUP * HD, GROUP * HD), GROUP * HD)
    head_cols = pl.ds(pl.multiple_of(h * HD, HD), HD)

    def small_pieces(to_s):
        return (
            (queries.at[:, to_s, :, head_rows], query_all.at[s]),
            (new_keys.at[:, to_s, :, head_cols], fresh_all.at[0, s]),
            (new_values.at[:, to_s, :, head_cols], fresh_all.at[1, s]),
        )

    def send_small(step, carry):
        to_s = lax.rem(s + step, 8)
        for n, (src, dst) in enumerate(small_pieces(to_s)):
            remote(src, dst, small_send.at[n], small_recv.at[n], (to_s, h, b)).start()
        return carry

    lax.fori_loop(1, 8, send_small, 0)
    for n, (src, dst) in enumerate(small_pieces(s)):
        pltpu.make_async_copy(src, dst, small_recv.at[n]).start()

    def deliver(src, offset, legs_left, send_sem, from_place):
        to_s, to_h = coordinates(legs_left, sign, s, h)
        _, dy, dz = offset
        remote(
            src(to_s * 8 + to_h), landed.at[from_place], send_sem,
            bulk_recv.at[dz * 2 + lax.rem(dy, 2)], (to_s, to_h, b),
        ).start()

    def send_direct(offset):
        offset = tuple(jnp.int32(d) if isinstance(d, int) else d for d in offset)
        deliver(lambda place: packed.at[place], offset, offset, bulk_send, s * 8 + h)

    scalars[0].wait()
    scalars[1].wait()
    for piece, (dz, low) in enumerate(PIECES):
        at_h = head_at(piece, sign)
        wait_for(gathered[piece], piece_sem.at[piece])

        def pack(at_s, carry):
            for k in range(4):
                slot = slot_order[at_s * 4 + k]
                for n in range(2):
                    packed[at_s * 8 + at_h, n, k] = gathered[piece][n, slot]
            return carry

        lax.fori_loop(0, 8, pack, 0)
        for at, offset in enumerate(STOPS):
            if offset[2] == dz and offset[1] % 2 == low:
                owner_s, owner_h = coordinates(offset, sign, s, h)
                to_s, to_h = coordinates(first_leg(offset), sign, s, h)
                remote(
                    packed.at[owner_s * 8 + owner_h], stopped.at[at], bulk_send, stop_recv.at[at],
                    (to_s, to_h, b),
                ).start()
        for offset in DIRECT:
            if offset[2] == dz and offset[1] % 2 == low:
                send_direct(offset)

    for n, part in enumerate((query_all, fresh_all.at[0], fresh_all.at[1])):
        wait_for(part, small_recv.at[n])
    wait_for(key_columns, full_sem.at[0])
    wait_for(value_rows, full_sem.at[1])

    def pass_on(at, word):
        offset = from_word(word)
        leg = first_leg(offset)
        rest = tuple(d - m for d, m in zip(offset, leg))
        from_s, from_h = coordinates(leg, -sign, s, h)
        wait_for(stopped.at[at], stop_recv.at[at])
        deliver(lambda _: stopped.at[at], offset, rest, stop_send, from_s * 8 + from_h)

    def pass_on_from(first, last):
        for start in range(first, last, 5):
            stops = STOPS[start : min(start + 5, last)]

            def step(n, word):
                pass_on(start + n, word)
                return lax.div(word, 64)

            lax.fori_loop(0, len(stops), step, jnp.int32(pack_word(stops)))

    def spread_queries(at_s, carry):
        for t in range(2):
            rows = query_all[at_s, t].astype(F32)
            for g in range(GROUP):
                row = (g // 4) * 8 + t * 4 + g % 4
                for k in range(4):
                    query_rows[at_s * 4 + k, row : row + 1, :] = rows[k : k + 1, g * HD : g * HD + HD]
        return carry

    lax.fori_loop(0, 8, spread_queries, 0)

    def find_slot(at, carry):
        found = jnp.int32(0)
        for slot in range(32):
            found = jnp.where(slot_order[slot] == b * 16 + at, slot, found)
        slot_of[at] = found
        return carry

    lax.fori_loop(0, 16, find_slot, 0)

    lane = lax.broadcasted_iota(jnp.int32, (1, HD), 1)
    lane_prompt = lax.div(lane, 16)
    lane_later = lax.rem(lax.div(lane, 4), 2) == 1
    block_lane = lax.div(lax.broadcasted_iota(jnp.int32, (HD, HD), 1), 16)
    row4 = lax.broadcasted_iota(jnp.int32, (4, HD), 0)
    row512 = lax.broadcasted_iota(jnp.int32, (512, HD), 0)
    scale = HD ** -0.5

    def attend(first):
        slots = [slot_of[first + p] for p in range(8)]
        live = jnp.zeros((1, HD), jnp.int32)
        for p in range(8):
            live = jnp.where(lane_prompt == p, lengths[first + p + b * 16], live)

        def fresh_row(n, t, slot):
            rows = fresh_all[n, lax.div(slot, 4), t].astype(F32)
            return jnp.sum(jnp.where(row4 == lax.rem(slot, 4), rows, 0.0), axis=0, keepdims=True)

        questions = jnp.concatenate([query_rows[slot] for slot in slots], axis=0).T
        diagonal = jnp.concatenate(
            [jnp.where(block_lane == p, questions, 0.0) for p in range(8)], axis=0
        ).astype(BF16)
        fresh_keys = jnp.concatenate(
            [
                jnp.concatenate([fresh_row(0, 0, slot), fresh_row(0, 1, slot), jnp.zeros((14, HD), F32)], axis=0)
                for slot in slots
            ],
            axis=1,
        ).astype(BF16)
        scores = jnp.dot(
            key_columns[:, first * HD : (first + 8) * HD], diagonal, preferred_element_type=F32
        ) * scale
        fresh_scores = jnp.dot(fresh_keys, diagonal, preferred_element_type=F32) * scale
        kept = row512 < live
        scores = jnp.where(kept, scores, HIDDEN)
        n0 = fresh_scores[0:1]
        n1 = jnp.where(lane_later, fresh_scores[1:2], HIDDEN)
        peak = jnp.maximum(jnp.max(scores, axis=0, keepdims=True), jnp.maximum(n0, n1))
        mass = jnp.where(kept, jnp.exp(scores - peak), 0.0)
        m0 = jnp.exp(n0 - peak)
        m1 = jnp.where(lane_later, jnp.exp(n1 - peak), 0.0)
        total = jnp.sum(mass, axis=0, keepdims=True) + m0 + m1
        weights = mass.T.astype(BF16)
        m0, m1 = (m.astype(BF16).astype(F32) for m in (m0, m1))
        sides = jnp.concatenate([total, m0, m1, jnp.zeros((HD - 3, HD), F32)], axis=0).T
        for p, slot in enumerate(slots):
            cut = slice(p * 16, p * 16 + 16)
            weighted = jnp.dot(weights[cut], value_rows[first + p], preferred_element_type=F32)
            weighted += sides[cut, 1:2] * fresh_row(1, 0, slot)
            weighted += sides[cut, 2:3] * fresh_row(1, 1, slot)
            result[first + p] = weighted / sides[cut, 0:1]

    pass_on_from(0, 10)
    attend(0)
    pass_on_from(10, 20)
    attend(8)

    def hand_rows(at_s, carry):
        for pair in range(2):
            first, second = (
                result[jnp.clip(slot_order[at_s * 4 + pair * 2 + n] - b * 16, 0, 15)] for n in range(2)
            )
            for to_b in range(2):
                cut = slice(to_b * 8, to_b * 8 + 8)
                rows_send[at_s, to_b, pair] = jnp.concatenate((first[cut], second[cut]), axis=0).astype(BF16)
        return carry

    lax.fori_loop(0, 8, hand_rows, 0)

    def send_rows(to_s, to_b):
        remote(
            rows_send.at[to_s, to_b], rows_land.at[s, b], rows_send_sem, rows_recv_sem, (to_s, h, to_b)
        ).start()

    def send_rows_step(step, carry):
        to_s = lax.rem(s + step, 8)
        send_rows(to_s, b)
        send_rows(to_s, other)
        return carry

    lax.fori_loop(1, 8, send_rows_step, 0)
    send_rows(s, other)
    pltpu.make_async_copy(rows_send.at[s, b], rows_land.at[s, b], rows_recv_sem).start()
    pass_on_from(20, len(STOPS))

    slots = [slot_order[s * 4 + k] for k in range(4)]
    lives = [lengths[slot] for slot in slots]
    position = (h * 2 + b) * BLOCK + lax.broadcasted_iota(jnp.int32, (BLOCK, HD), 0)
    fresh[0].wait()
    fresh[1].wait()

    def settle(block, from_s, from_h):
        cut = pl.ds(pl.multiple_of(from_h * HD, HD), HD)
        for n, out in enumerate((keys_cache, values_cache)):
            placed = [fresh_rows[n, t, from_s, :, cut].astype(F32) for t in range(2)]
            for k in range(4):
                rows = jnp.where(position < lives[k], block[n, k].astype(F32), 0.0)
                for t in range(2):
                    rows = jnp.where(position == lives[k] + t, placed[t][k : k + 1], rows)
                out[from_s, k, :, cut] = rows.astype(BF16)

    owners = [lax.div(slot, 16) for slot in slots]

    def assemble(l, carry):
        picked = []
        for k in range(4):
            part = slice((k % 2) * 8, (k % 2) * 8 + 8)
            first, second = (rows_land[l, n, k // 2].astype(F32)[part] for n in range(2))
            picked.append(jnp.where(owners[k] == 0, first, second))
        for t in range(2):
            attention[t, l] = jnp.concatenate(
                [
                    jnp.concatenate([rows[t * 4 + g : t * 4 + g + 1] for rows in picked], axis=0)
                    for g in range(4)
                ],
                axis=1,
            ).astype(BF16)
        return carry

    settle(packed.at[s * 8 + h], s, h)
    for piece, (dz, low) in enumerate(PIECES):
        if piece == 7:
            wait_for(rows_land, rows_recv_sem)
            lax.fori_loop(0, 8, assemble, 0)
        blocks = 7 if piece == 7 else 8
        wait_for(landed.at[pl.ds(0, blocks)], bulk_recv.at[dz * 2 + low])

        def settle_one(step, carry):
            offset = (lax.rem(step, 4), low + 2 * lax.div(step, 4), dz)
            from_s, from_h = coordinates(offset, -sign, s, h)
            settle(landed.at[from_s * 8 + from_h], from_s, from_h)
            return carry

        lax.fori_loop(8 - blocks, 8, settle_one, 0)

    wait_for(value_rows, swap_send)
    for n, part in enumerate((query_all, fresh_all.at[0], fresh_all.at[1])):
        wait_for(part.at[pl.ds(0, 7)], small_send.at[n])
    wait_for(packed.at[pl.ds(0, 63)], bulk_send)
    wait_for(stopped, stop_send)
    wait_for(rows_send.at[pl.ds(0, 7)], rows_send_sem)
    wait_for(rows_send.at[0, 0], rows_send_sem)


def hand_out(attention, keys, values, attention_out, keys_out, values_out, sem):
    copies = [pltpu.make_async_copy(attention, attention_out, sem.at[16])]
    for n, (src, dst) in enumerate(((keys, keys_out), (values, values_out))):
        copies += [pltpu.make_async_copy(src.at[l], dst.at[l], sem.at[n * 8 + l]) for l in range(8)]
    for copy in copies:
        copy.start()
    for copy in copies:
        copy.wait()


def body(keys_prefill, values_prefill, lengths, slot_order, queries, new_keys, new_values):
    keys = keys_prefill.reshape(16, 8, 2, BLOCK, HD)
    values = values_prefill.reshape(16, 8, 2, BLOCK, HD)
    flat = (keys_prefill.reshape(16, 512, HD), values_prefill.reshape(16, 512, HD))
    any_spec = pl.BlockSpec(memory_space=pl.ANY)
    hbm_spec = pl.BlockSpec(memory_space=pltpu.HBM)
    vmem_spec = pl.BlockSpec(memory_space=pltpu.VMEM)
    dma, vmem = pltpu.SemaphoreType.DMA, pltpu.VMEM
    rows_shape, cache_shape = (2, 8, 4, 4 * HD), (8, 4, BLOCK, KVH * HD)

    def in_hbm(array):
        return pltpu.with_memory_space_constraint(array, pltpu.HBM)

    held = pl.pallas_call(
        relay,
        out_shape=(vmem(rows_shape, BF16), vmem(cache_shape, BF16), vmem(cache_shape, BF16)),
        in_specs=[hbm_spec] * 9,
        out_specs=(vmem_spec,) * 3,
        scratch_shapes=[
            [vmem((2, 32, BLOCK, HD), BF16)] * 8, vmem((512, 16 * HD), BF16), vmem((16, 512, HD), BF16),
            vmem((64, 2, 4, BLOCK, HD), BF16), vmem((64, 2, 4, BLOCK, HD), BF16),
            vmem((len(STOPS), 2, 4, BLOCK, HD), BF16),
            vmem((2, 2, 8, 4, KVH * HD), BF16), vmem((8, 2, 4, GROUP * HD), BF16), vmem((32, 16, HD), F32),
            vmem((2, 8, 2, 4, HD), BF16), vmem((16, 16, HD), F32),
            vmem((8, 2, 2, 16, HD), BF16), vmem((8, 2, 2, 16, HD), BF16),
            pltpu.SMEM((32,), jnp.int32), pltpu.SMEM((32,), jnp.int32), pltpu.SMEM((16,), jnp.int32),
            dma((8,)), dma, dma((2,)), dma((2,)), dma((3,)), dma((3,)),
            dma, dma((8,)), dma, dma((len(STOPS),)), dma, dma, dma((2,)),
        ],
        compiler_params=pltpu.CompilerParams(
            collective_id=0, has_side_effects=True, vmem_limit_bytes=48 * 2**20
        ),
        name="relay",
    )(*(in_hbm(x) for x in (slot_order, lengths, keys, values, *flat, queries, new_keys, new_values)))
    return pl.pallas_call(
        hand_out,
        out_shape=tuple(jax.ShapeDtypeStruct(shape, BF16) for shape in (rows_shape, cache_shape, cache_shape)),
        in_specs=[vmem_spec] * 3,
        out_specs=(any_spec,) * 3,
        scratch_shapes=[dma((17,))],
        compiler_params=pltpu.CompilerParams(vmem_limit_bytes=8 * 2**20),
        name="hand_out",
    )(*(pltpu.with_memory_space_constraint(x, pltpu.VMEM) for x in held))


def solution(mesh):
    in_specs = (
        P("section", "batch", None, "head"),
        P("section", "batch", None, "head"),
        P(),
        P(),
        P(None, None, "section", None),
        P(None, None, "section", None),
        P(None, None, "section", None),
    )
    out_specs = (
        P(None, None, "section", ("head", "batch")),
        P(None, "section", ("head", "batch"), None),
        P(None, "section", ("head", "batch"), None),
    )
    return jax.shard_map(body, mesh=mesh, in_specs=in_specs, out_specs=out_specs, check_vma=False)
```

```python
import jax
import jax.numpy as jnp
from jax import lax
from jax.experimental import pallas as pl
from jax.experimental.pallas import tpu as pltpu
from jax.sharding import PartitionSpec as P

KVH = 8
HD = 128
GROUP = 8
BLOCK = 32
MESH = pl.DeviceIdType.MESH
HIDDEN = -1e30
BF16, F32 = jnp.bfloat16, jnp.float32


PLANE = {
    1: ((1, 1), (3, 3), (1, 3), (3, 1), (2, 1), (0, 3), (2, 3), (0, 1)),
    0: ((1, 0), (0, 2), (3, 2), (1, 2), (3, 0), (2, 2), (2, 0)),
}
def group_of(dx, low):
    return low * 4 + dx


def turn(offset):
    return lax.rem(offset * 4 - 1, 63) + 1


def static_turn(offset):
    return (offset * 4 - 1) % 63 + 1


def digits(offset):
    return offset % 4, offset // 4 % 4, offset // 16


def hops(offset):
    return sum(min(d, 4 - d) for d in digits(offset))


def orbits():
    seen, out, fixed = set(), [], []
    for offset in range(1, 64):
        if offset not in seen:
            ring = {offset, static_turn(offset), static_turn(static_turn(offset))}
            seen |= ring
            (out if len(ring) == 3 else fixed).append(offset)
    return out, fixed


def grouped():
    reps, fixed = orbits()
    odd = [o for o in reps if all(d % 2 for d in digits(o))]
    rest = sorted((o for o in reps if o not in odd), key=lambda o: -hops(o))
    groups = [(odd, [o for o in fixed if all(d % 2 for d in digits(o))])]
    groups += [([rest[g], rest[11 - g], rest[12 + g]], []) for g in range(6)]
    groups[3][1].append(42)
    return groups


GROUPS = grouped()
SIZES = [3 * len(reps) + len(lone) for reps, lone in GROUPS]
PIECES = ((1, 1), (3, 1), (2, 1), (0, 1), (1, 0), (3, 0), (2, 0), (0, 0))


def coordinates(offset, sign, s, h):
    dx, dy, dz = lax.rem(offset, 4), lax.rem(lax.div(offset, 4), 4), lax.div(offset, 16)
    x = lax.rem(lax.div(s, 2) + sign * dx + 4, 4)
    y = lax.rem(lax.rem(s, 2) * 2 + lax.rem(h, 2) + sign * dy + 4, 4)
    z = lax.rem(lax.div(h, 2) + sign * dz + 4, 4)
    return x * 2 + lax.div(y, 2), z * 2 + lax.rem(y, 2)


def each_of(group, do):
    reps, lone = GROUPS[group]
    for offset in lone:
        do(jnp.int32(offset))

    def rep_step(_, word):
        def turn_step(_, offset):
            do(offset)
            return turn(offset)

        lax.fori_loop(0, 3, turn_step, lax.rem(word, 64))
        return lax.div(word, 64)

    lax.fori_loop(0, len(reps), rep_step, jnp.int32(sum(rep * 64**n for n, rep in enumerate(reps))))


def relay(
    slot_order_hbm, lengths_hbm, keys, values, keys_flat, values_flat, queries, new_keys, new_values,
    attention, keys_cache, values_cache,
    key_columns, value_rows, keys_line, values_chip, keys_packed, values_packed, keys_land, values_land,
    fresh_rows, query_all, query_rows, fresh_all, result, rows_send, rows_land,
    slot_order, lengths, slot_of,
    scalar_sem, full_sem, fresh_sem, line_send, line_recv, chip_send, chip_recv,
    keys_send, keys_recv, values_send, values_recv,
    small_send, small_recv, rows_send_sem, rows_recv_sem,
):
    s, h, b = lax.axis_index("section"), lax.axis_index("head"), lax.axis_index("batch")
    x, z = lax.div(s, 2), lax.div(h, 2)
    y_low = lax.rem(h, 2)
    y = lax.rem(s, 2) * 2 + y_low
    other = 1 - b
    sign = 1 - 2 * b
    mine = pl.ds(b * 16, 16)
    here = x * 4 + y

    def remote(src, dst, send_sem, recv_sem, to):
        return pltpu.make_async_remote_copy(
            src_ref=src, dst_ref=dst, send_sem=send_sem, recv_sem=recv_sem,
            device_id=to, device_id_type=MESH,
        )

    def wait_for(ref, sem):
        pltpu.make_async_copy(ref, ref, sem).wait()

    def away(d, at, way):
        return lax.rem(at + way * d + 4, 4)

    def in_plane(at_x, at_y):
        return at_x * 2 + lax.div(at_y, 2), z * 2 + lax.rem(at_y, 2)

    def in_line(at_z):
        return at_z * 2 + y_low

    def owner_low(low):
        return lax.rem(y_low + low, 2)

    barrier = pltpu.get_barrier_semaphore()

    def greet(to):
        pl.semaphore_signal(barrier, inc=1, device_id=to, device_id_type=MESH)

    def greet_section(step, carry):
        to_s = lax.rem(s + step, 8)
        greet((to_s, h, other))
        for at in range(8):
            greet((to_s, lax.rem(h + at, 8), b))
        return carry

    for dz in range(1, 4):
        greet((s, in_line(away(dz, z, 1)), other))
    greet((s, h, other))
    for at in range(1, 8):
        greet((s, lax.rem(h + at, 8), b))
    lax.fori_loop(1, 8, greet_section, 0)

    scalars = [
        pltpu.make_async_copy(slot_order_hbm, slot_order, scalar_sem.at[0]),
        pltpu.make_async_copy(lengths_hbm, lengths, scalar_sem.at[1]),
    ]
    whole = [
        pltpu.make_async_copy(keys_flat.at[at], key_columns.at[:, pl.ds(at * HD, HD)], full_sem.at[0])
        for at in range(16)
    ]
    whole.append(pltpu.make_async_copy(values_flat, value_rows, full_sem.at[1]))
    fresh = [
        pltpu.make_async_copy(src, fresh_rows.at[n], fresh_sem.at[n])
        for n, src in enumerate((new_keys, new_values))
    ]
    for copy in scalars:
        copy.start()
    def piece_of(piece, way):
        dz, low = PIECES[piece]
        return away(dz, z, way), owner_low(low)

    for piece in range(8):
        at_z, at_low = piece_of(piece, sign)
        pltpu.make_async_copy(
            values.at[:, at_z, at_low, b], values_chip[piece].at[mine], chip_recv.at[piece]
        ).start()
    for low in (1, 0):
        pltpu.make_async_copy(
            keys.at[:, z, owner_low(low), b], keys_line[low].at[z, mine], line_recv.at[low]
        ).start()
    for copy in whole + fresh:
        copy.start()
    pl.semaphore_wait(barrier, 74)

    def swap(piece):
        at_z, at_low = piece_of(piece, -sign)
        remote(
            values.at[:, at_z, at_low, other], values_chip[piece].at[mine],
            chip_send, chip_recv.at[piece], (s, h, other),
        ).start()

    swap(0)
    swap(1)

    def send_line(low, dz, to_b):
        to_z = away(dz, z, sign)
        remote(
            keys.at[:, to_z, owner_low(low), to_b], keys_line[low].at[z, mine],
            line_send, line_recv.at[low], (s, in_line(to_z), to_b),
        ).start()

    lines = [
        (low, dz, to_b)
        for low in (1, 0)
        for dz, to_b in ((1, b), (3, other), (2, b), (1, other), (3, b), (2, other), (0, other))
    ]
    for line in lines[:3]:
        send_line(*line)
    for piece in range(2, 8):
        swap(piece)

    head_rows = pl.ds(pl.multiple_of(h * GROUP * HD, GROUP * HD), GROUP * HD)
    head_cols = pl.ds(pl.multiple_of(h * HD, HD), HD)

    def small_pieces(to_s):
        return (
            (queries.at[:, to_s, :, head_rows], query_all.at[s]),
            (new_keys.at[:, to_s, :, head_cols], fresh_all.at[0, s]),
            (new_values.at[:, to_s, :, head_cols], fresh_all.at[1, s]),
        )

    def send_small(step, carry):
        to_s = lax.rem(s + step, 8)
        for n, (src, dst) in enumerate(small_pieces(to_s)):
            remote(src, dst, small_send.at[n], small_recv.at[n], (to_s, h, b)).start()
        return carry

    lax.fori_loop(1, 8, send_small, 0)
    for n, (src, dst) in enumerate(small_pieces(s)):
        pltpu.make_async_copy(src, dst, small_recv.at[n]).start()

    scalars[0].wait()
    scalars[1].wait()

    def pack_values(piece):
        at_z, at_low = piece_of(piece, sign)
        at_h = at_z * 2 + at_low

        def step(at_s, carry):
            for k in range(4):
                values_packed[at_s * 8 + at_h, k] = values_chip[piece][slot_order[at_s * 4 + k]]
            return carry

        lax.fori_loop(0, 8, step, 0)

    def send_values(group):
        def send_one(offset):
            to_s, to_h = coordinates(offset, sign, s, h)
            remote(
                values_packed.at[to_s * 8 + to_h], values_land.at[s * 8 + h],
                values_send, values_recv.at[group], (to_s, to_h, b),
            ).start()

        each_of(group, send_one)

    def pack_keys(low):
        def step(at_s, carry):
            for k in range(4):
                slot = slot_order[at_s * 4 + k]
                for from_z in range(4):
                    keys_packed[at_s * 2 + owner_low(low), from_z, k] = keys_line[low][from_z, slot]
            return carry

        lax.fori_loop(0, 8, step, 0)

    def send_plane(packed, dx, dy, dst, send_sem, recv_sem):
        to_x, to_y = away(dx, x, sign), away(dy, y, sign)
        to_s, to_h = in_plane(to_x, to_y)
        remote(
            packed.at[to_x * 4 + to_y], dst, send_sem, recv_sem.at[group_of(dx, dy % 2)], (to_s, to_h, b)
        ).start()

    lines = lines[3:]
    for piece in range(8):
        wait_for(values_chip[piece], chip_recv.at[piece])
        pack_values(piece)
        if piece == 1:
            send_values(0)
        if lines:
            send_line(*lines.pop(0))
    for group in range(1, 7):
        send_values(group)
        if lines:
            send_line(*lines.pop(0))
    assert not lines

    def turn_keys(low):
        wait_for(keys_line[low], line_recv.at[low])
        pack_keys(low)
        for dx, dy in PLANE[low]:
            send_plane(keys_packed, dx, dy, keys_land.at[here], keys_send, keys_recv)

    for n, part in enumerate((query_all, fresh_all.at[0], fresh_all.at[1])):
        wait_for(part, small_recv.at[n])
    wait_for(key_columns, full_sem.at[0])
    wait_for(value_rows, full_sem.at[1])

    def spread_queries(at_s, carry):
        for t in range(2):
            rows = query_all[at_s, t].astype(F32)
            for g in range(GROUP):
                row = (g // 4) * 8 + t * 4 + g % 4
                for k in range(4):
                    query_rows[at_s * 4 + k, row : row + 1, :] = rows[k : k + 1, g * HD : g * HD + HD]
        return carry

    lax.fori_loop(0, 8, spread_queries, 0)

    def find_slot(at, carry):
        found = jnp.int32(0)
        for slot in range(32):
            found = jnp.where(slot_order[slot] == b * 16 + at, slot, found)
        slot_of[at] = found
        return carry

    lax.fori_loop(0, 16, find_slot, 0)

    lane = lax.broadcasted_iota(jnp.int32, (1, HD), 1)
    lane_prompt = lax.div(lane, 16)
    lane_later = lax.rem(lax.div(lane, 4), 2) == 1
    block_lane = lax.div(lax.broadcasted_iota(jnp.int32, (HD, HD), 1), 16)
    row4 = lax.broadcasted_iota(jnp.int32, (4, HD), 0)
    row512 = lax.broadcasted_iota(jnp.int32, (512, HD), 0)
    scale = HD ** -0.5

    def attend(first):
        slots = [slot_of[first + p] for p in range(8)]
        live = jnp.zeros((1, HD), jnp.int32)
        for p in range(8):
            live = jnp.where(lane_prompt == p, lengths[first + p + b * 16], live)

        def fresh_row(n, t, slot):
            rows = fresh_all[n, lax.div(slot, 4), t].astype(F32)
            return jnp.sum(jnp.where(row4 == lax.rem(slot, 4), rows, 0.0), axis=0, keepdims=True)

        questions = jnp.concatenate([query_rows[slot] for slot in slots], axis=0).T
        diagonal = jnp.concatenate(
            [jnp.where(block_lane == p, questions, 0.0) for p in range(8)], axis=0
        ).astype(BF16)
        fresh_keys = jnp.concatenate(
            [
                jnp.concatenate([fresh_row(0, 0, slot), fresh_row(0, 1, slot), jnp.zeros((14, HD), F32)], axis=0)
                for slot in slots
            ],
            axis=1,
        ).astype(BF16)
        scores = jnp.dot(
            key_columns[:, first * HD : (first + 8) * HD], diagonal, preferred_element_type=F32
        ) * scale
        fresh_scores = jnp.dot(fresh_keys, diagonal, preferred_element_type=F32) * scale
        kept = row512 < live
        scores = jnp.where(kept, scores, HIDDEN)
        n0 = fresh_scores[0:1]
        n1 = jnp.where(lane_later, fresh_scores[1:2], HIDDEN)
        peak = jnp.maximum(jnp.max(scores, axis=0, keepdims=True), jnp.maximum(n0, n1))
        mass = jnp.where(kept, jnp.exp(scores - peak), 0.0)
        m0 = jnp.exp(n0 - peak)
        m1 = jnp.where(lane_later, jnp.exp(n1 - peak), 0.0)
        total = jnp.sum(mass, axis=0, keepdims=True) + m0 + m1
        weights = mass.T.astype(BF16)
        m0, m1 = (m.astype(BF16).astype(F32) for m in (m0, m1))
        sides = jnp.concatenate([total, m0, m1, jnp.zeros((HD - 3, HD), F32)], axis=0).T
        for p, slot in enumerate(slots):
            cut = slice(p * 16, p * 16 + 16)
            weighted = jnp.dot(weights[cut], value_rows[first + p], preferred_element_type=F32)
            weighted += sides[cut, 1:2] * fresh_row(1, 0, slot)
            weighted += sides[cut, 2:3] * fresh_row(1, 1, slot)
            result[first + p] = weighted / sides[cut, 0:1]

    attend(0)
    attend(8)

    def hand_rows(at_s, carry):
        for pair in range(2):
            first, second = (
                result[jnp.clip(slot_order[at_s * 4 + pair * 2 + n] - b * 16, 0, 15)] for n in range(2)
            )
            for to_b in range(2):
                cut = slice(to_b * 8, to_b * 8 + 8)
                rows_send[at_s, to_b, pair] = jnp.concatenate((first[cut], second[cut]), axis=0).astype(BF16)
        return carry

    lax.fori_loop(0, 8, hand_rows, 0)

    def send_rows(to_s, to_b):
        remote(
            rows_send.at[to_s, to_b], rows_land.at[s, b], rows_send_sem, rows_recv_sem, (to_s, h, to_b)
        ).start()

    def send_rows_step(step, carry):
        to_s = lax.rem(s + step, 8)
        send_rows(to_s, b)
        send_rows(to_s, other)
        return carry

    lax.fori_loop(1, 8, send_rows_step, 0)
    send_rows(s, other)
    pltpu.make_async_copy(rows_send.at[s, b], rows_land.at[s, b], rows_recv_sem).start()
    turn_keys(1)
    turn_keys(0)

    slots = [slot_order[s * 4 + k] for k in range(4)]
    lives = [lengths[slot] for slot in slots]
    position = (h * 2 + b) * BLOCK + lax.broadcasted_iota(jnp.int32, (BLOCK, HD), 0)
    fresh[0].wait()
    fresh[1].wait()

    def settle(block, n, from_x, from_y, from_z):
        layer = from_x * 2 + lax.div(from_y, 2)
        cut = pl.ds(pl.multiple_of((from_z * 2 + lax.rem(from_y, 2)) * HD, HD), HD)
        out = (keys_cache, values_cache)[n]
        placed = [fresh_rows[n, t, layer, :, cut].astype(F32) for t in range(2)]
        for k in range(4):
            rows = jnp.where(position < lives[k], block[k].astype(F32), 0.0)
            for t in range(2):
                rows = jnp.where(position == lives[k] + t, placed[t][k : k + 1], rows)
            out[layer, k, :, cut] = rows.astype(BF16)

    def settle_keys(src, from_x, from_y):
        def step(from_z, carry):
            settle(src.at[from_x * 4 + from_y, from_z], 0, from_x, from_y, from_z)
            return carry

        lax.fori_loop(0, 4, step, 0)

    def settle_values(src, from_s, from_h):
        from_y = lax.rem(from_s, 2) * 2 + lax.rem(from_h, 2)
        settle(src.at[from_s * 8 + from_h], 1, lax.div(from_s, 2), from_y, lax.div(from_h, 2))

    owners = [lax.div(slot, 16) for slot in slots]

    def assemble(l, carry):
        picked = []
        for k in range(4):
            part = slice((k % 2) * 8, (k % 2) * 8 + 8)
            first, second = (rows_land[l, n, k // 2].astype(F32)[part] for n in range(2))
            picked.append(jnp.where(owners[k] == 0, first, second))
        for t in range(2):
            attention[t, l] = jnp.concatenate(
                [
                    jnp.concatenate([rows[t * 4 + g : t * 4 + g + 1] for rows in picked], axis=0)
                    for g in range(4)
                ],
                axis=1,
            ).astype(BF16)
        return carry

    settle_keys(keys_packed, x, y)
    settle_values(values_packed, s, h)
    for group in range(7):
        wait_for(values_land.at[pl.ds(0, SIZES[group])], values_recv.at[group])

        def settle_one(offset):
            settle_values(values_land, *coordinates(offset, -sign, s, h))

        each_of(group, settle_one)
        if group == 3:
            wait_for(rows_land, rows_recv_sem)
            lax.fori_loop(0, 8, assemble, 0)
    for low in (1, 0):
        for dx in (1, 3, 2, 0):
            chips = [dy for to_x, dy in PLANE[low] if to_x == dx]
            wait_for(keys_land.at[pl.ds(0, len(chips))], keys_recv.at[group_of(dx, low)])
            for dy in chips:
                settle_keys(keys_land, away(dx, x, -sign), away(dy, y, -sign))

    wait_for(value_rows.at[pl.ds(0, 8)], chip_send)
    wait_for(value_rows.at[pl.ds(0, 14)], line_send)
    for n, part in enumerate((query_all, fresh_all.at[0], fresh_all.at[1])):
        wait_for(part.at[pl.ds(0, 7)], small_send.at[n])
    wait_for(keys_packed.at[pl.ds(0, 15)], keys_send)
    wait_for(values_packed.at[pl.ds(0, 63)], values_send)
    wait_for(rows_send.at[pl.ds(0, 7)], rows_send_sem)
    wait_for(rows_send.at[0, 0], rows_send_sem)


def hand_out(attention, keys, values, attention_out, keys_out, values_out, sem):
    copies = [pltpu.make_async_copy(attention, attention_out, sem.at[16])]
    for n, (src, dst) in enumerate(((keys, keys_out), (values, values_out))):
        copies += [pltpu.make_async_copy(src.at[l], dst.at[l], sem.at[n * 8 + l]) for l in range(8)]
    for copy in copies:
        copy.start()
    for copy in copies:
        copy.wait()


def body(keys_prefill, values_prefill, lengths, slot_order, queries, new_keys, new_values):
    keys = keys_prefill.reshape(16, 4, 2, 2, BLOCK, HD)
    values = values_prefill.reshape(16, 4, 2, 2, BLOCK, HD)
    flat = (keys_prefill.reshape(16, 512, HD), values_prefill.reshape(16, 512, HD))
    any_spec = pl.BlockSpec(memory_space=pl.ANY)
    hbm_spec = pl.BlockSpec(memory_space=pltpu.HBM)
    vmem_spec = pl.BlockSpec(memory_space=pltpu.VMEM)
    dma, vmem = pltpu.SemaphoreType.DMA, pltpu.VMEM
    rows_shape, cache_shape = (2, 8, 4, 4 * HD), (8, 4, BLOCK, KVH * HD)
    plane, straight = vmem((16, 4, 4, BLOCK, HD), BF16), vmem((64, 4, BLOCK, HD), BF16)

    def in_hbm(array):
        return pltpu.with_memory_space_constraint(array, pltpu.HBM)

    held = pl.pallas_call(
        relay,
        out_shape=(vmem(rows_shape, BF16), vmem(cache_shape, BF16), vmem(cache_shape, BF16)),
        in_specs=[hbm_spec] * 9,
        out_specs=(vmem_spec,) * 3,
        scratch_shapes=[
            vmem((512, 16 * HD), BF16), vmem((16, 512, HD), BF16),
            [vmem((4, 32, BLOCK, HD), BF16)] * 2, [vmem((32, BLOCK, HD), BF16)] * 8,
            plane, straight, plane, straight,
            vmem((2, 2, 8, 4, KVH * HD), BF16), vmem((8, 2, 4, GROUP * HD), BF16), vmem((32, 16, HD), F32),
            vmem((2, 8, 2, 4, HD), BF16), vmem((16, 16, HD), F32),
            vmem((8, 2, 2, 16, HD), BF16), vmem((8, 2, 2, 16, HD), BF16),
            pltpu.SMEM((32,), jnp.int32), pltpu.SMEM((32,), jnp.int32), pltpu.SMEM((16,), jnp.int32),
            dma((2,)), dma((2,)), dma((2,)), dma, dma((2,)), dma, dma((8,)),
            dma, dma((8,)), dma, dma((7,)),
            dma((3,)), dma((3,)), dma, dma,
        ],
        compiler_params=pltpu.CompilerParams(
            collective_id=0, has_side_effects=True, vmem_limit_bytes=48 * 2**20
        ),
        name="relay",
    )(*(in_hbm(x) for x in (slot_order, lengths, keys, values, *flat, queries, new_keys, new_values)))
    return pl.pallas_call(
        hand_out,
        out_shape=tuple(jax.ShapeDtypeStruct(shape, BF16) for shape in (rows_shape, cache_shape, cache_shape)),
        in_specs=[vmem_spec] * 3,
        out_specs=(any_spec,) * 3,
        scratch_shapes=[dma((17,))],
        compiler_params=pltpu.CompilerParams(vmem_limit_bytes=8 * 2**20),
        name="hand_out",
    )(*(pltpu.with_memory_space_constraint(x, pltpu.VMEM) for x in held))


def solution(mesh):
    in_specs = (
        P("section", "batch", None, "head"),
        P("section", "batch", None, "head"),
        P(),
        P(),
        P(None, None, "section", None),
        P(None, None, "section", None),
        P(None, None, "section", None),
    )
    out_specs = (
        P(None, None, "section", ("head", "batch")),
        P(None, "section", ("head", "batch"), None),
        P(None, "section", ("head", "batch"), None),
    )
    return jax.shard_map(body, mesh=mesh, in_specs=in_specs, out_specs=out_specs, check_vma=False)
```

```python
import jax
import jax.numpy as jnp
from jax import lax
from jax.experimental import pallas as pl
from jax.experimental.pallas import tpu as pltpu
from jax.sharding import PartitionSpec as P

KVH = 8
HD = 128
GROUP = 8
BLOCK = 32
MESH = pl.DeviceIdType.MESH
HIDDEN = -1e30
BF16, F32 = jnp.bfloat16, jnp.float32


PLANE = {
    1: ((1, 1), (3, 3), (1, 3), (3, 1), (2, 1), (0, 3), (2, 3), (0, 1)),
    0: ((1, 0), (0, 2), (3, 2), (1, 2), (3, 0), (2, 2), (2, 0)),
}
def group_of(dx, low):
    return low * 4 + dx


def relay(
    slot_order_hbm, lengths_hbm, keys, values, keys_flat, values_flat, queries, new_keys, new_values,
    attention, values_cache, keys_land, keys_fresh, keep,
    key_columns, value_rows, keys_line, values_chip, keys_packed, values_packed, values_mid, values_land,
    fresh_rows, query_all, query_rows, fresh_all, result, rows_send, rows_land,
    slot_order, lengths, slot_of,
    scalar_sem, full_sem, fresh_sem, line_send, line_recv, chip_send, chip_recv,
    keys_send, keys_recv, mid_first, mid_send, mid_recv, values_send, values_recv,
    small_send, small_recv, rows_send_sem, rows_recv_sem,
):
    s, h, b = lax.axis_index("section"), lax.axis_index("head"), lax.axis_index("batch")
    x, z = lax.div(s, 2), lax.div(h, 2)
    y_low = lax.rem(h, 2)
    y = lax.rem(s, 2) * 2 + y_low
    other = 1 - b
    sign = 1 - 2 * b
    mine = pl.ds(b * 16, 16)
    here = x * 4 + y
    here_mid = x * 4 + y_low * 2 + lax.div(y, 2)

    def remote(src, dst, send_sem, recv_sem, to):
        return pltpu.make_async_remote_copy(
            src_ref=src, dst_ref=dst, send_sem=send_sem, recv_sem=recv_sem,
            device_id=to, device_id_type=MESH,
        )

    def wait_for(ref, sem):
        pltpu.make_async_copy(ref, ref, sem).wait()

    def away(d, at, way):
        return lax.rem(at + way * d + 4, 4)

    def in_plane(at_x, at_y):
        return at_x * 2 + lax.div(at_y, 2), z * 2 + lax.rem(at_y, 2)

    def in_line(at_z):
        return at_z * 2 + y_low

    def owner_low(low):
        return lax.rem(y_low + low, 2)

    barrier = pltpu.get_barrier_semaphore()

    def greet(to):
        pl.semaphore_signal(barrier, inc=1, device_id=to, device_id_type=MESH)

    for dz in range(4):
        at_h = in_line(away(dz, z, 1))
        greet((s, at_h, other))
        if dz:
            greet((s, at_h, b))
    for low in (1, 0):
        for dx, dy in PLANE[low]:
            at_s, at_h = in_plane(away(dx, x, 1), away(dy, y, 1))
            greet((at_s, at_h, b))
            if low == 0:
                greet((at_s, at_h, other))

    scalars = [
        pltpu.make_async_copy(slot_order_hbm, slot_order, scalar_sem.at[0]),
        pltpu.make_async_copy(lengths_hbm, lengths, scalar_sem.at[1]),
    ]
    whole = [
        pltpu.make_async_copy(keys_flat.at[at], key_columns.at[:, pl.ds(at * HD, HD)], full_sem.at[0])
        for at in range(16)
    ]
    whole.append(pltpu.make_async_copy(values_flat, value_rows, full_sem.at[1]))
    fresh = [
        pltpu.make_async_copy(src, fresh_rows.at[n], fresh_sem.at[n])
        for n, src in enumerate((new_keys, new_values))
    ]
    for copy in scalars:
        copy.start()
    for low in (1, 0):
        pltpu.make_async_copy(
            values.at[:, :, owner_low(low), b], values_chip[low].at[mine], chip_recv.at[low]
        ).start()
    for low in (1, 0):
        pltpu.make_async_copy(
            keys.at[:, z, owner_low(low), b], keys_line[low].at[z, mine], line_recv.at[low]
        ).start()
    for copy in whole + fresh:
        copy.start()
    pl.semaphore_wait(barrier, 29)

    def swap(low):
        remote(
            values.at[:, :, owner_low(low), other], values_chip[low].at[mine],
            chip_send, chip_recv.at[low], (s, h, other),
        ).start()

    swap(1)

    def send_line(low, dz, to_b):
        to_z = away(dz, z, sign)
        remote(
            keys.at[:, to_z, owner_low(low), to_b], keys_line[low].at[z, mine],
            line_send, line_recv.at[low], (s, in_line(to_z), to_b),
        ).start()

    for low in (1, 0):
        for dz, to_b in ((1, b), (3, other), (2, b), (1, other), (3, b), (2, other), (0, other)):
            send_line(low, dz, to_b)

    head_rows = pl.ds(pl.multiple_of(h * GROUP * HD, GROUP * HD), GROUP * HD)
    head_cols = pl.ds(pl.multiple_of(h * HD, HD), HD)

    def small_pieces(to_s):
        return (
            (queries.at[:, to_s, :, head_rows], query_all.at[s]),
            (new_keys.at[:, to_s, :, head_cols], fresh_all.at[0, s]),
            (new_values.at[:, to_s, :, head_cols], fresh_all.at[1, s]),
        )

    def send_small(step, carry):
        to_s = lax.rem(s + step, 8)
        for n, (src, dst) in enumerate(small_pieces(to_s)):
            remote(src, dst, small_send.at[n], small_recv.at[n], (to_s, h, b)).start()
        return carry

    def pack_values(low):
        def step(at_s, carry):
            for k in range(4):
                values_packed[at_s * 2 + owner_low(low), :, k] = values_chip[low][slot_order[at_s * 4 + k]]
            return carry

        lax.fori_loop(0, 8, step, 0)

    def pack_keys(low):
        def step(at_s, carry):
            for k in range(4):
                slot = slot_order[at_s * 4 + k]
                for from_z in range(4):
                    keys_packed[at_s * 2 + owner_low(low), from_z, k] = keys_line[low][from_z, slot]
            return carry

        lax.fori_loop(0, 8, step, 0)

    def send_plane(packed, dx, dy, dst, send_sem, recv_sem):
        to_x, to_y = away(dx, x, sign), away(dy, y, sign)
        to_s, to_h = in_plane(to_x, to_y)
        remote(
            packed.at[to_x * 4 + to_y], dst, send_sem, recv_sem.at[group_of(dx, dy % 2)], (to_s, to_h, b)
        ).start()

    def take_values(low):
        wait_for(values_chip[low], chip_recv.at[low])
        if low == 1:
            swap(0)
        pack_values(low)

    def send_values(low):
        for at, (dx, dy) in enumerate(PLANE[low]):
            sem = mid_first.at[at] if low == 1 else mid_send
            send_plane(values_packed, dx, dy, values_mid.at[:, here_mid], sem, mid_recv)

    def forward_values(dx, low):
        group = group_of(dx, low)
        wait_for(values_mid.at[:, pl.ds(0, 2)], mid_recv.at[group])
        pair = pl.ds(away(dx, x, -sign) * 4 + owner_low(low) * 2, 2)
        for dz in (1, 3, 2):
            to_z = away(dz, z, sign)
            remote(
                values_mid.at[to_z, pair], values_land.at[z, pair],
                values_send, values_recv.at[group], (s, in_line(to_z), b),
            ).start()

    def turn_keys(low):
        wait_for(keys_line[low], line_recv.at[low])
        pack_keys(low)
        for dx, dy in PLANE[low]:
            send_plane(keys_packed, dx, dy, keys_land.at[here], keys_send, keys_recv)

    scalars[0].wait()
    scalars[1].wait()
    take_values(1)
    send_values(1)
    lax.fori_loop(1, 8, send_small, 0)
    for n, (src, dst) in enumerate(small_pieces(s)):
        pltpu.make_async_copy(src, dst, small_recv.at[n]).start()
    take_values(0)
    pltpu.make_async_copy(
        values_packed.at[here], values_mid.at[:, here_mid], mid_recv.at[group_of(0, 0)]
    ).start()

    owned = [slot_order[s * 4 + k] for k in range(4)]
    lives = [lengths[slot] for slot in owned]
    first_position = (h * 2 + b) * BLOCK
    position = first_position + lax.broadcasted_iota(jnp.int32, (BLOCK, HD), 0)
    for k in range(4):
        keep[k] = jnp.where(position < lives[k], 1.0, 0.0).astype(BF16)
    fresh[0].wait()
    fresh[1].wait()

    def place_fresh(layer, carry):
        wide = first_position + lax.broadcasted_iota(jnp.int32, (BLOCK, KVH * HD), 0)
        for n, out in enumerate((keys_fresh, values_cache)):
            new = [fresh_rows[n, t, layer].astype(F32) for t in range(2)]
            for k in range(4):
                rows = jnp.zeros((BLOCK, KVH * HD), F32)
                for t in range(2):
                    rows = jnp.where(wide == lives[k] + t, new[t][k : k + 1], rows)
                out[layer, k] = rows.astype(BF16)
        return carry

    lax.fori_loop(0, 8, place_fresh, 0)
    for n, part in enumerate((query_all, fresh_all.at[0], fresh_all.at[1])):
        wait_for(part, small_recv.at[n])
    for at in range(5):
        wait_for(values_packed.at[0], mid_first.at[at])
    send_values(0)
    wait_for(key_columns, full_sem.at[0])
    wait_for(value_rows, full_sem.at[1])

    def spread_queries(at_s, carry):
        for t in range(2):
            rows = query_all[at_s, t].astype(F32)
            for g in range(GROUP):
                row = (g // 4) * 8 + t * 4 + g % 4
                for k in range(4):
                    query_rows[at_s * 4 + k, row : row + 1, :] = rows[k : k + 1, g * HD : g * HD + HD]
        return carry

    lax.fori_loop(0, 8, spread_queries, 0)

    def find_slot(at, carry):
        found = jnp.int32(0)
        for slot in range(32):
            found = jnp.where(slot_order[slot] == b * 16 + at, slot, found)
        slot_of[at] = found
        return carry

    lax.fori_loop(0, 16, find_slot, 0)

    lane = lax.broadcasted_iota(jnp.int32, (1, HD), 1)
    lane_prompt = lax.div(lane, 16)
    lane_later = lax.rem(lax.div(lane, 4), 2) == 1
    block_lane = lax.div(lax.broadcasted_iota(jnp.int32, (HD, HD), 1), 16)
    row4 = lax.broadcasted_iota(jnp.int32, (4, HD), 0)
    row512 = lax.broadcasted_iota(jnp.int32, (512, HD), 0)
    scale = HD ** -0.5

    def attend(first):
        slots = [slot_of[first + p] for p in range(8)]
        live = jnp.zeros((1, HD), jnp.int32)
        for p in range(8):
            live = jnp.where(lane_prompt == p, lengths[first + p + b * 16], live)

        def fresh_row(n, t, slot):
            rows = fresh_all[n, lax.div(slot, 4), t].astype(F32)
            return jnp.sum(jnp.where(row4 == lax.rem(slot, 4), rows, 0.0), axis=0, keepdims=True)

        questions = jnp.concatenate([query_rows[slot] for slot in slots], axis=0).T
        diagonal = jnp.concatenate(
            [jnp.where(block_lane == p, questions, 0.0) for p in range(8)], axis=0
        ).astype(BF16)
        fresh_keys = jnp.concatenate(
            [
                jnp.concatenate([fresh_row(0, 0, slot), fresh_row(0, 1, slot), jnp.zeros((14, HD), F32)], axis=0)
                for slot in slots
            ],
            axis=1,
        ).astype(BF16)
        scores = jnp.dot(
            key_columns[:, first * HD : (first + 8) * HD], diagonal, preferred_element_type=F32
        ) * scale
        fresh_scores = jnp.dot(fresh_keys, diagonal, preferred_element_type=F32) * scale
        kept = row512 < live
        scores = jnp.where(kept, scores, HIDDEN)
        n0 = fresh_scores[0:1]
        n1 = jnp.where(lane_later, fresh_scores[1:2], HIDDEN)
        peak = jnp.maximum(jnp.max(scores, axis=0, keepdims=True), jnp.maximum(n0, n1))
        mass = jnp.where(kept, jnp.exp(scores - peak), 0.0)
        m0 = jnp.exp(n0 - peak)
        m1 = jnp.where(lane_later, jnp.exp(n1 - peak), 0.0)
        total = jnp.sum(mass, axis=0, keepdims=True) + m0 + m1
        weights = mass.T.astype(BF16)
        m0, m1 = (m.astype(BF16).astype(F32) for m in (m0, m1))
        sides = jnp.concatenate([total, m0, m1, jnp.zeros((HD - 3, HD), F32)], axis=0).T
        for p, slot in enumerate(slots):
            cut = slice(p * 16, p * 16 + 16)
            weighted = jnp.dot(weights[cut], value_rows[first + p], preferred_element_type=F32)
            weighted += sides[cut, 1:2] * fresh_row(1, 0, slot)
            weighted += sides[cut, 2:3] * fresh_row(1, 1, slot)
            result[first + p] = weighted / sides[cut, 0:1]

    attend(0)
    for dx in (1, 3, 2, 0):
        forward_values(dx, 1)
    attend(8)

    def hand_rows(at_s, carry):
        for pair in range(2):
            first, second = (
                result[jnp.clip(slot_order[at_s * 4 + pair * 2 + n] - b * 16, 0, 15)] for n in range(2)
            )
            for to_b in range(2):
                cut = slice(to_b * 8, to_b * 8 + 8)
                rows_send[at_s, to_b, pair] = jnp.concatenate((first[cut], second[cut]), axis=0).astype(BF16)
        return carry

    lax.fori_loop(0, 8, hand_rows, 0)

    def send_rows(to_s, to_b):
        remote(
            rows_send.at[to_s, to_b], rows_land.at[s, b], rows_send_sem, rows_recv_sem, (to_s, h, to_b)
        ).start()

    def send_rows_step(step, carry):
        to_s = lax.rem(s + step, 8)
        send_rows(to_s, b)
        send_rows(to_s, other)
        return carry

    lax.fori_loop(1, 8, send_rows_step, 0)
    send_rows(s, other)
    pltpu.make_async_copy(rows_send.at[s, b], rows_land.at[s, b], rows_recv_sem).start()
    turn_keys(1)
    turn_keys(0)
    pltpu.make_async_copy(keys_packed.at[here], keys_land.at[here], keys_recv.at[group_of(0, 0)]).start()
    for dx in (1, 3, 2, 0):
        forward_values(dx, 0)

    def settle_values(src, from_x, low, from_z):
        def step(half, carry):
            from_low = owner_low(low)
            block = src.at[from_z, from_x * 4 + from_low * 2 + half]
            layer = from_x * 2 + half
            cut = pl.ds(pl.multiple_of((from_z * 2 + from_low) * HD, HD), HD)
            for k in range(4):
                values_cache[layer, k, :, cut] = jnp.where(keep[k] > 0, block[k], values_cache[layer, k, :, cut])
            return carry

        lax.fori_loop(0, 2, step, 0)

    owners = [lax.div(slot, 16) for slot in owned]

    def assemble(l, carry):
        picked = []
        for k in range(4):
            part = slice((k % 2) * 8, (k % 2) * 8 + 8)
            first, second = (rows_land[l, n, k // 2].astype(F32)[part] for n in range(2))
            picked.append(jnp.where(owners[k] == 0, first, second))
        for t in range(2):
            attention[t, l] = jnp.concatenate(
                [
                    jnp.concatenate([rows[t * 4 + g : t * 4 + g + 1] for rows in picked], axis=0)
                    for g in range(4)
                ],
                axis=1,
            ).astype(BF16)
        return carry

    for low in (1, 0):
        for dx in (1, 3, 2, 0):
            settle_values(values_mid, away(dx, x, -sign), low, z)
    wait_for(rows_land, rows_recv_sem)
    lax.fori_loop(0, 8, assemble, 0)
    for low in (1, 0):
        for dx in (1, 3, 2, 0):
            wait_for(values_land.at[pl.ds(0, 3), pl.ds(0, 2)], values_recv.at[group_of(dx, low)])
            for dz in (1, 3, 2):
                settle_values(values_land, away(dx, x, -sign), low, away(dz, z, -sign))
    for group in range(8):
        wait_for(keys_land.at[pl.ds(0, 2)], keys_recv.at[group])

    wait_for(value_rows.at[pl.ds(0, 8)], chip_send)
    wait_for(value_rows.at[pl.ds(0, 14)], line_send)
    for n, part in enumerate((query_all, fresh_all.at[0], fresh_all.at[1])):
        wait_for(part.at[pl.ds(0, 7)], small_send.at[n])
    for at in range(5, 8):
        wait_for(values_packed.at[0], mid_first.at[at])
    wait_for(values_packed.at[pl.ds(0, 7)], mid_send)
    wait_for(keys_packed.at[pl.ds(0, 15)], keys_send)
    wait_for(values_land.at[pl.ds(0, 3)], values_send)
    wait_for(rows_send.at[pl.ds(0, 7)], rows_send_sem)
    wait_for(rows_send.at[0, 0], rows_send_sem)


def hand_out(
    attention, values, keys_land, keys_fresh, keep, attention_out, values_out, keys_out, keys, sem
):
    copies = [pltpu.make_async_copy(values.at[l], values_out.at[l], sem.at[l]) for l in range(8)]
    copies.append(pltpu.make_async_copy(attention, attention_out, sem.at[16]))
    for copy in copies:
        copy.start()
    kept = [keep[k] > 0 for k in range(4)]
    for l in range(8):
        for h in range(KVH):
            cut = slice(h * HD, h * HD + HD)
            for k in range(4):
                landed = keys_land[l // 2 * 4 + l % 2 * 2 + h % 2, h // 2, k]
                keys[l, k, :, cut] = jnp.where(kept[k], landed, keys_fresh[l, k, :, cut])
        copies.append(pltpu.make_async_copy(keys.at[l], keys_out.at[l], sem.at[8 + l]))
        copies[-1].start()
    for copy in copies:
        copy.wait()


def body(keys_prefill, values_prefill, lengths, slot_order, queries, new_keys, new_values):
    keys = keys_prefill.reshape(16, 4, 2, 2, BLOCK, HD)
    values = values_prefill.reshape(16, 4, 2, 2, BLOCK, HD)
    flat = (keys_prefill.reshape(16, 512, HD), values_prefill.reshape(16, 512, HD))
    any_spec = pl.BlockSpec(memory_space=pl.ANY)
    hbm_spec = pl.BlockSpec(memory_space=pltpu.HBM)
    vmem_spec = pl.BlockSpec(memory_space=pltpu.VMEM)
    dma, vmem = pltpu.SemaphoreType.DMA, pltpu.VMEM
    rows_shape, cache_shape = (2, 8, 4, 4 * HD), (8, 4, BLOCK, KVH * HD)
    plane_shape = (16, 4, 4, BLOCK, HD)
    plane, line = vmem(plane_shape, BF16), vmem((4, 16, 4, BLOCK, HD), BF16)

    def in_hbm(array):
        return pltpu.with_memory_space_constraint(array, pltpu.HBM)

    held = pl.pallas_call(
        relay,
        out_shape=tuple(
            vmem(shape, BF16) for shape in (rows_shape, cache_shape, plane_shape, cache_shape, (4, BLOCK, HD))
        ),
        in_specs=[hbm_spec] * 9,
        out_specs=(vmem_spec,) * 5,
        scratch_shapes=[
            vmem((512, 16 * HD), BF16), vmem((16, 512, HD), BF16),
            [vmem((4, 32, BLOCK, HD), BF16)] * 2, [vmem((32, 4, BLOCK, HD), BF16)] * 2,
            plane, plane, line, line,
            vmem((2, 2, 8, 4, KVH * HD), BF16), vmem((8, 2, 4, GROUP * HD), BF16), vmem((32, 16, HD), F32),
            vmem((2, 8, 2, 4, HD), BF16), vmem((16, 16, HD), F32),
            vmem((8, 2, 2, 16, HD), BF16), vmem((8, 2, 2, 16, HD), BF16),
            pltpu.SMEM((32,), jnp.int32), pltpu.SMEM((32,), jnp.int32), pltpu.SMEM((16,), jnp.int32),
            dma((2,)), dma((2,)), dma((2,)), dma, dma((2,)), dma, dma((2,)),
            dma, dma((8,)), dma((8,)), dma, dma((8,)), dma, dma((8,)),
            dma((3,)), dma((3,)), dma, dma,
        ],
        compiler_params=pltpu.CompilerParams(
            collective_id=0, has_side_effects=True, vmem_limit_bytes=48 * 2**20
        ),
        name="relay",
    )(*(in_hbm(x) for x in (slot_order, lengths, keys, values, *flat, queries, new_keys, new_values)))
    attention, values_cache, keys_cache = pl.pallas_call(
        hand_out,
        out_shape=tuple(jax.ShapeDtypeStruct(shape, BF16) for shape in (rows_shape, cache_shape, cache_shape)),
        in_specs=[vmem_spec] * 5,
        out_specs=(any_spec,) * 3,
        scratch_shapes=[vmem(cache_shape, BF16), dma((17,))],
        compiler_params=pltpu.CompilerParams(vmem_limit_bytes=8 * 2**20),
        name="hand_out",
    )(*(pltpu.with_memory_space_constraint(x, pltpu.VMEM) for x in held))
    return attention, keys_cache, values_cache


def solution(mesh):
    in_specs = (
        P("section", "batch", None, "head"),
        P("section", "batch", None, "head"),
        P(),
        P(),
        P(None, None, "section", None),
        P(None, None, "section", None),
        P(None, None, "section", None),
    )
    out_specs = (
        P(None, None, "section", ("head", "batch")),
        P(None, "section", ("head", "batch"), None),
        P(None, "section", ("head", "batch"), None),
    )
    return jax.shard_map(body, mesh=mesh, in_specs=in_specs, out_specs=out_specs, check_vma=False)
```

```python
import jax
import jax.numpy as jnp
from jax import lax
from jax.experimental import pallas as pl
from jax.experimental.pallas import tpu as pltpu
from jax.sharding import PartitionSpec as P

KVH = 8
HD = 128
GROUP = 8
BLOCK = 32
MESH = pl.DeviceIdType.MESH
HIDDEN = -1e30
BF16, F32 = jnp.bfloat16, jnp.float32


PLANE = {
    1: ((1, 1), (3, 3), (1, 3), (3, 1), (2, 1), (0, 3), (2, 3), (0, 1)),
    0: ((1, 0), (0, 2), (3, 2), (1, 2), (3, 0), (2, 2), (2, 0)),
}
def group_of(dx, low):
    return low * 4 + dx


def relay(
    slot_order_hbm, lengths_hbm, keys, values, keys_flat, values_flat, queries, new_keys, new_values,
    attention, values_cache, keys_land, keys_fresh, keep,
    key_columns, value_rows, keys_line, values_chip, keys_packed, values_packed, values_mid, values_land,
    fresh_rows, query_all, query_rows, fresh_all, result, rows_send, rows_land,
    slot_order, lengths, slot_of,
    scalar_sem, full_sem, fresh_sem, line_send, line_recv, chip_send, chip_recv,
    keys_send, keys_recv, mid_send, mid_recv, values_send, values_recv,
    small_send, small_recv, rows_send_sem, rows_recv_sem,
):
    s, h, b = lax.axis_index("section"), lax.axis_index("head"), lax.axis_index("batch")
    x, z = lax.div(s, 2), lax.div(h, 2)
    y_low = lax.rem(h, 2)
    y = lax.rem(s, 2) * 2 + y_low
    other = 1 - b
    sign = 1 - 2 * b
    mine = pl.ds(b * 16, 16)
    here = x * 4 + y
    here_mid = x * 4 + y_low * 2 + lax.div(y, 2)

    def remote(src, dst, send_sem, recv_sem, to):
        return pltpu.make_async_remote_copy(
            src_ref=src, dst_ref=dst, send_sem=send_sem, recv_sem=recv_sem,
            device_id=to, device_id_type=MESH,
        )

    def wait_for(ref, sem):
        pltpu.make_async_copy(ref, ref, sem).wait()

    def away(d, at, way):
        return lax.rem(at + way * d + 4, 4)

    def in_plane(at_x, at_y):
        return at_x * 2 + lax.div(at_y, 2), z * 2 + lax.rem(at_y, 2)

    def in_line(at_z):
        return at_z * 2 + y_low

    def owner_low(low):
        return lax.rem(y_low + low, 2)

    barrier = pltpu.get_barrier_semaphore()

    def greet(to):
        pl.semaphore_signal(barrier, inc=1, device_id=to, device_id_type=MESH)

    for dz in range(4):
        at_h = in_line(away(dz, z, 1))
        greet((s, at_h, other))
        if dz:
            greet((s, at_h, b))
    for low in (1, 0):
        for dx, dy in PLANE[low]:
            at_s, at_h = in_plane(away(dx, x, 1), away(dy, y, 1))
            greet((at_s, at_h, b))
            if low == 0:
                greet((at_s, at_h, other))

    scalars = [
        pltpu.make_async_copy(slot_order_hbm, slot_order, scalar_sem.at[0]),
        pltpu.make_async_copy(lengths_hbm, lengths, scalar_sem.at[1]),
    ]
    whole = [
        pltpu.make_async_copy(keys_flat.at[at], key_columns.at[:, pl.ds(at * HD, HD)], full_sem.at[0])
        for at in range(16)
    ]
    whole.append(pltpu.make_async_copy(values_flat, value_rows, full_sem.at[1]))
    fresh = [
        pltpu.make_async_copy(src, fresh_rows.at[n], fresh_sem.at[n])
        for n, src in enumerate((new_keys, new_values))
    ]
    for copy in scalars:
        copy.start()
    for low in (1, 0):
        pltpu.make_async_copy(
            values.at[:, :, owner_low(low), b], values_chip[low].at[mine], chip_recv.at[low]
        ).start()
    for low in (1, 0):
        pltpu.make_async_copy(
            keys.at[:, z, owner_low(low), b], keys_line[low].at[z, mine], line_recv.at[low]
        ).start()
    for copy in whole + fresh:
        copy.start()
    pl.semaphore_wait(barrier, 29)

    def swap(low):
        remote(
            values.at[:, :, owner_low(low), other], values_chip[low].at[mine],
            chip_send, chip_recv.at[low], (s, h, other),
        ).start()

    swap(1)

    def send_line(low, dz, to_b):
        to_z = away(dz, z, sign)
        remote(
            keys.at[:, to_z, owner_low(low), to_b], keys_line[low].at[z, mine],
            line_send, line_recv.at[low], (s, in_line(to_z), to_b),
        ).start()

    for low in (1, 0):
        for dz, to_b in ((1, b), (3, other), (2, b), (1, other), (3, b), (2, other), (0, other)):
            send_line(low, dz, to_b)

    head_rows = pl.ds(pl.multiple_of(h * GROUP * HD, GROUP * HD), GROUP * HD)
    head_cols = pl.ds(pl.multiple_of(h * HD, HD), HD)

    def small_pieces(to_s):
        return (
            (queries.at[:, to_s, :, head_rows], query_all.at[s]),
            (new_keys.at[:, to_s, :, head_cols], fresh_all.at[0, s]),
            (new_values.at[:, to_s, :, head_cols], fresh_all.at[1, s]),
        )

    def send_small(step, carry):
        to_s = lax.rem(s + step, 8)
        for n, (src, dst) in enumerate(small_pieces(to_s)):
            remote(src, dst, small_send.at[n], small_recv.at[n], (to_s, h, b)).start()
        return carry

    def pack_values(low):
        def step(at_s, carry):
            for k in range(4):
                values_packed[at_s * 2 + owner_low(low), :, k] = values_chip[low][slot_order[at_s * 4 + k]]
            return carry

        lax.fori_loop(0, 8, step, 0)

    def pack_keys(low):
        def step(at_s, carry):
            for k in range(4):
                slot = slot_order[at_s * 4 + k]
                for from_z in range(4):
                    keys_packed[at_s * 2 + owner_low(low), from_z, k] = keys_line[low][from_z, slot]
            return carry

        lax.fori_loop(0, 8, step, 0)

    def send_plane(packed, dx, dy, dst, send_sem, recv_sem):
        to_x, to_y = away(dx, x, sign), away(dy, y, sign)
        to_s, to_h = in_plane(to_x, to_y)
        remote(
            packed.at[to_x * 4 + to_y], dst, send_sem, recv_sem.at[group_of(dx, dy % 2)], (to_s, to_h, b)
        ).start()

    def take_values(low):
        wait_for(values_chip[low], chip_recv.at[low])
        if low == 1:
            swap(0)
        pack_values(low)

    def send_values(low):
        for dx, dy in PLANE[low]:
            send_plane(values_packed, dx, dy, values_mid.at[:, here_mid], mid_send, mid_recv)

    def forward_values(dx, low):
        group = group_of(dx, low)
        wait_for(values_mid.at[:, pl.ds(0, 2)], mid_recv.at[group])
        pair = pl.ds(away(dx, x, -sign) * 4 + owner_low(low) * 2, 2)
        for dz in (1, 3, 2):
            to_z = away(dz, z, sign)
            remote(
                values_mid.at[to_z, pair], values_land.at[z, pair],
                values_send, values_recv.at[group], (s, in_line(to_z), b),
            ).start()

    def turn_keys(low):
        wait_for(keys_line[low], line_recv.at[low])
        pack_keys(low)
        for dx, dy in PLANE[low]:
            send_plane(keys_packed, dx, dy, keys_land.at[here], keys_send, keys_recv)

    scalars[0].wait()
    scalars[1].wait()
    lax.fori_loop(1, 8, send_small, 0)
    for n, (src, dst) in enumerate(small_pieces(s)):
        pltpu.make_async_copy(src, dst, small_recv.at[n]).start()
    take_values(1)
    send_values(1)
    take_values(0)
    send_values(0)
    pltpu.make_async_copy(
        values_packed.at[here], values_mid.at[:, here_mid], mid_recv.at[group_of(0, 0)]
    ).start()

    for n, part in enumerate((query_all, fresh_all.at[0], fresh_all.at[1])):
        wait_for(part, small_recv.at[n])
    wait_for(key_columns, full_sem.at[0])
    wait_for(value_rows, full_sem.at[1])

    def spread_queries(at_s, carry):
        for t in range(2):
            rows = query_all[at_s, t].astype(F32)
            for g in range(GROUP):
                row = (g // 4) * 8 + t * 4 + g % 4
                for k in range(4):
                    query_rows[at_s * 4 + k, row : row + 1, :] = rows[k : k + 1, g * HD : g * HD + HD]
        return carry

    lax.fori_loop(0, 8, spread_queries, 0)

    def find_slot(at, carry):
        found = jnp.int32(0)
        for slot in range(32):
            found = jnp.where(slot_order[slot] == b * 16 + at, slot, found)
        slot_of[at] = found
        return carry

    lax.fori_loop(0, 16, find_slot, 0)

    lane = lax.broadcasted_iota(jnp.int32, (1, HD), 1)
    lane_prompt = lax.div(lane, 16)
    lane_later = lax.rem(lax.div(lane, 4), 2) == 1
    block_lane = lax.div(lax.broadcasted_iota(jnp.int32, (HD, HD), 1), 16)
    row4 = lax.broadcasted_iota(jnp.int32, (4, HD), 0)
    row512 = lax.broadcasted_iota(jnp.int32, (512, HD), 0)
    scale = HD ** -0.5

    def attend(first):
        slots = [slot_of[first + p] for p in range(8)]
        live = jnp.zeros((1, HD), jnp.int32)
        for p in range(8):
            live = jnp.where(lane_prompt == p, lengths[first + p + b * 16], live)

        def fresh_row(n, t, slot):
            rows = fresh_all[n, lax.div(slot, 4), t].astype(F32)
            return jnp.sum(jnp.where(row4 == lax.rem(slot, 4), rows, 0.0), axis=0, keepdims=True)

        questions = jnp.concatenate([query_rows[slot] for slot in slots], axis=0).T
        diagonal = jnp.concatenate(
            [jnp.where(block_lane == p, questions, 0.0) for p in range(8)], axis=0
        ).astype(BF16)
        fresh_keys = jnp.concatenate(
            [
                jnp.concatenate([fresh_row(0, 0, slot), fresh_row(0, 1, slot), jnp.zeros((14, HD), F32)], axis=0)
                for slot in slots
            ],
            axis=1,
        ).astype(BF16)
        scores = jnp.dot(
            key_columns[:, first * HD : (first + 8) * HD], diagonal, preferred_element_type=F32
        ) * scale
        fresh_scores = jnp.dot(fresh_keys, diagonal, preferred_element_type=F32) * scale
        kept = row512 < live
        scores = jnp.where(kept, scores, HIDDEN)
        n0 = fresh_scores[0:1]
        n1 = jnp.where(lane_later, fresh_scores[1:2], HIDDEN)
        peak = jnp.maximum(jnp.max(scores, axis=0, keepdims=True), jnp.maximum(n0, n1))
        mass = jnp.where(kept, jnp.exp(scores - peak), 0.0)
        m0 = jnp.exp(n0 - peak)
        m1 = jnp.where(lane_later, jnp.exp(n1 - peak), 0.0)
        total = jnp.sum(mass, axis=0, keepdims=True) + m0 + m1
        weights = mass.T.astype(BF16)
        m0, m1 = (m.astype(BF16).astype(F32) for m in (m0, m1))
        sides = jnp.concatenate([total, m0, m1, jnp.zeros((HD - 3, HD), F32)], axis=0).T
        for p, slot in enumerate(slots):
            cut = slice(p * 16, p * 16 + 16)
            weighted = jnp.dot(weights[cut], value_rows[first + p], preferred_element_type=F32)
            weighted += sides[cut, 1:2] * fresh_row(1, 0, slot)
            weighted += sides[cut, 2:3] * fresh_row(1, 1, slot)
            result[first + p] = weighted / sides[cut, 0:1]

    attend(0)
    attend(8)

    def hand_rows(at_s, carry):
        for pair in range(2):
            first, second = (
                result[jnp.clip(slot_order[at_s * 4 + pair * 2 + n] - b * 16, 0, 15)] for n in range(2)
            )
            for to_b in range(2):
                cut = slice(to_b * 8, to_b * 8 + 8)
                rows_send[at_s, to_b, pair] = jnp.concatenate((first[cut], second[cut]), axis=0).astype(BF16)
        return carry

    lax.fori_loop(0, 8, hand_rows, 0)

    def send_rows(to_s, to_b):
        remote(
            rows_send.at[to_s, to_b], rows_land.at[s, b], rows_send_sem, rows_recv_sem, (to_s, h, to_b)
        ).start()

    def send_rows_step(step, carry):
        to_s = lax.rem(s + step, 8)
        send_rows(to_s, b)
        send_rows(to_s, other)
        return carry

    lax.fori_loop(1, 8, send_rows_step, 0)
    send_rows(s, other)
    pltpu.make_async_copy(rows_send.at[s, b], rows_land.at[s, b], rows_recv_sem).start()
    owned = [slot_order[s * 4 + k] for k in range(4)]
    lives = [lengths[slot] for slot in owned]
    first_position = (h * 2 + b) * BLOCK
    position = first_position + lax.broadcasted_iota(jnp.int32, (BLOCK, HD), 0)
    for k in range(4):
        keep[k] = jnp.where(position < lives[k], 1.0, 0.0).astype(BF16)
    fresh[0].wait()
    fresh[1].wait()

    def place_fresh(layer, carry):
        wide = first_position + lax.broadcasted_iota(jnp.int32, (BLOCK, KVH * HD), 0)
        for n, out in enumerate((keys_fresh, values_cache)):
            new = [fresh_rows[n, t, layer].astype(F32) for t in range(2)]
            for k in range(4):
                rows = jnp.zeros((BLOCK, KVH * HD), F32)
                for t in range(2):
                    rows = jnp.where(wide == lives[k] + t, new[t][k : k + 1], rows)
                out[layer, k] = rows.astype(BF16)
        return carry

    lax.fori_loop(0, 8, place_fresh, 0)
    turn_keys(1)
    turn_keys(0)
    pltpu.make_async_copy(keys_packed.at[here], keys_land.at[here], keys_recv.at[group_of(0, 0)]).start()
    for low in (1, 0):
        for dx in (1, 3, 2, 0):
            forward_values(dx, low)

    def settle_values(src, from_x, low, from_z):
        def step(half, carry):
            from_low = owner_low(low)
            block = src.at[from_z, from_x * 4 + from_low * 2 + half]
            layer = from_x * 2 + half
            cut = pl.ds(pl.multiple_of((from_z * 2 + from_low) * HD, HD), HD)
            for k in range(4):
                values_cache[layer, k, :, cut] = jnp.where(keep[k] > 0, block[k], values_cache[layer, k, :, cut])
            return carry

        lax.fori_loop(0, 2, step, 0)

    owners = [lax.div(slot, 16) for slot in owned]

    def assemble(l, carry):
        picked = []
        for k in range(4):
            part = slice((k % 2) * 8, (k % 2) * 8 + 8)
            first, second = (rows_land[l, n, k // 2].astype(F32)[part] for n in range(2))
            picked.append(jnp.where(owners[k] == 0, first, second))
        for t in range(2):
            attention[t, l] = jnp.concatenate(
                [
                    jnp.concatenate([rows[t * 4 + g : t * 4 + g + 1] for rows in picked], axis=0)
                    for g in range(4)
                ],
                axis=1,
            ).astype(BF16)
        return carry

    for low in (1, 0):
        for dx in (1, 3, 2, 0):
            settle_values(values_mid, away(dx, x, -sign), low, z)
    wait_for(rows_land, rows_recv_sem)
    lax.fori_loop(0, 8, assemble, 0)
    for low in (1, 0):
        for dx in (1, 3, 2, 0):
            wait_for(values_land.at[pl.ds(0, 3), pl.ds(0, 2)], values_recv.at[group_of(dx, low)])
            for dz in (1, 3, 2):
                settle_values(values_land, away(dx, x, -sign), low, away(dz, z, -sign))
    for group in range(8):
        wait_for(keys_land.at[pl.ds(0, 2)], keys_recv.at[group])

    wait_for(value_rows.at[pl.ds(0, 8)], chip_send)
    wait_for(value_rows.at[pl.ds(0, 14)], line_send)
    for n, part in enumerate((query_all, fresh_all.at[0], fresh_all.at[1])):
        wait_for(part.at[pl.ds(0, 7)], small_send.at[n])
    wait_for(values_packed.at[pl.ds(0, 15)], mid_send)
    wait_for(keys_packed.at[pl.ds(0, 15)], keys_send)
    wait_for(values_land.at[pl.ds(0, 3)], values_send)
    wait_for(rows_send.at[pl.ds(0, 7)], rows_send_sem)
    wait_for(rows_send.at[0, 0], rows_send_sem)


def hand_out(
    attention, values, keys_land, keys_fresh, keep, attention_out, values_out, keys_out, keys, sem
):
    copies = [pltpu.make_async_copy(values.at[l], values_out.at[l], sem.at[l]) for l in range(8)]
    copies.append(pltpu.make_async_copy(attention, attention_out, sem.at[16]))
    for copy in copies:
        copy.start()
    kept = [keep[k] > 0 for k in range(4)]
    for l in range(8):
        for h in range(KVH):
            cut = slice(h * HD, h * HD + HD)
            for k in range(4):
                landed = keys_land[l // 2 * 4 + l % 2 * 2 + h % 2, h // 2, k]
                keys[l, k, :, cut] = jnp.where(kept[k], landed, keys_fresh[l, k, :, cut])
        copies.append(pltpu.make_async_copy(keys.at[l], keys_out.at[l], sem.at[8 + l]))
        copies[-1].start()
    for copy in copies:
        copy.wait()


def body(keys_prefill, values_prefill, lengths, slot_order, queries, new_keys, new_values):
    keys = keys_prefill.reshape(16, 4, 2, 2, BLOCK, HD)
    values = values_prefill.reshape(16, 4, 2, 2, BLOCK, HD)
    flat = (keys_prefill.reshape(16, 512, HD), values_prefill.reshape(16, 512, HD))
    any_spec = pl.BlockSpec(memory_space=pl.ANY)
    hbm_spec = pl.BlockSpec(memory_space=pltpu.HBM)
    vmem_spec = pl.BlockSpec(memory_space=pltpu.VMEM)
    dma, vmem = pltpu.SemaphoreType.DMA, pltpu.VMEM
    rows_shape, cache_shape = (2, 8, 4, 4 * HD), (8, 4, BLOCK, KVH * HD)
    plane_shape = (16, 4, 4, BLOCK, HD)
    plane, line = vmem(plane_shape, BF16), vmem((4, 16, 4, BLOCK, HD), BF16)

    def in_hbm(array):
        return pltpu.with_memory_space_constraint(array, pltpu.HBM)

    held = pl.pallas_call(
        relay,
        out_shape=tuple(
            vmem(shape, BF16) for shape in (rows_shape, cache_shape, plane_shape, cache_shape, (4, BLOCK, HD))
        ),
        in_specs=[hbm_spec] * 9,
        out_specs=(vmem_spec,) * 5,
        scratch_shapes=[
            vmem((512, 16 * HD), BF16), vmem((16, 512, HD), BF16),
            [vmem((4, 32, BLOCK, HD), BF16)] * 2, [vmem((32, 4, BLOCK, HD), BF16)] * 2,
            plane, plane, line, line,
            vmem((2, 2, 8, 4, KVH * HD), BF16), vmem((8, 2, 4, GROUP * HD), BF16), vmem((32, 16, HD), F32),
            vmem((2, 8, 2, 4, HD), BF16), vmem((16, 16, HD), F32),
            vmem((8, 2, 2, 16, HD), BF16), vmem((8, 2, 2, 16, HD), BF16),
            pltpu.SMEM((32,), jnp.int32), pltpu.SMEM((32,), jnp.int32), pltpu.SMEM((16,), jnp.int32),
            dma((2,)), dma((2,)), dma((2,)), dma, dma((2,)), dma, dma((2,)),
            dma, dma((8,)), dma, dma((8,)), dma, dma((8,)),
            dma((3,)), dma((3,)), dma, dma,
        ],
        compiler_params=pltpu.CompilerParams(
            collective_id=0, has_side_effects=True, vmem_limit_bytes=48 * 2**20
        ),
        name="relay",
    )(*(in_hbm(x) for x in (slot_order, lengths, keys, values, *flat, queries, new_keys, new_values)))
    attention, values_cache, keys_cache = pl.pallas_call(
        hand_out,
        out_shape=tuple(jax.ShapeDtypeStruct(shape, BF16) for shape in (rows_shape, cache_shape, cache_shape)),
        in_specs=[vmem_spec] * 5,
        out_specs=(any_spec,) * 3,
        scratch_shapes=[vmem(cache_shape, BF16), dma((17,))],
        compiler_params=pltpu.CompilerParams(vmem_limit_bytes=8 * 2**20),
        name="hand_out",
    )(*(pltpu.with_memory_space_constraint(x, pltpu.VMEM) for x in held))
    return attention, keys_cache, values_cache


def solution(mesh):
    in_specs = (
        P("section", "batch", None, "head"),
        P("section", "batch", None, "head"),
        P(),
        P(),
        P(None, None, "section", None),
        P(None, None, "section", None),
        P(None, None, "section", None),
    )
    out_specs = (
        P(None, None, "section", ("head", "batch")),
        P(None, "section", ("head", "batch"), None),
        P(None, "section", ("head", "batch"), None),
    )
    return jax.shard_map(body, mesh=mesh, in_specs=in_specs, out_specs=out_specs, check_vma=False)
```

```python
import jax
import jax.numpy as jnp
from jax import lax
from jax.experimental import pallas as pl
from jax.experimental.pallas import tpu as pltpu
from jax.sharding import PartitionSpec as P

KVH = 8
HD = 128
GROUP = 8
BLOCK = 32
MESH = pl.DeviceIdType.MESH
HIDDEN = -1e30
BF16, F32 = jnp.bfloat16, jnp.float32


PLANE = {
    1: ((1, 1), (3, 3), (1, 3), (3, 1), (2, 1), (0, 3), (2, 3), (0, 1)),
    0: ((1, 0), (0, 2), (3, 2), (1, 2), (3, 0), (2, 2), (2, 0)),
}
PIECES = ((1, 1), (1, 3), (1, 2), (0, 1), (0, 3), (0, 2), (1, 0), (0, 0))


def group_of(dx, low):
    return low * 4 + dx


def relay(
    slot_order_hbm, lengths_hbm, keys, values, keys_flat, values_flat, queries, new_keys, new_values,
    attention, values_cache, keys_land, keys_fresh, keep,
    key_columns, value_rows, keys_line, keys_near, values_chip, keys_packed, values_packed, values_mid, values_land,
    fresh_rows, query_all, query_rows, fresh_all, result, rows_send, rows_land,
    slot_order, lengths, slot_of,
    scalar_sem, full_sem, fresh_sem, line_send, line_recv, near_recv, chip_send, chip_recv,
    keys_send, keys_recv, mid_first, mid_send, mid_recv, mid_near, mid_near_recv, values_send, values_recv,
    small_send, small_recv, rows_send_sem, rows_recv_sem,
):
    s, h, b = lax.axis_index("section"), lax.axis_index("head"), lax.axis_index("batch")
    x, z = lax.div(s, 2), lax.div(h, 2)
    y_low = lax.rem(h, 2)
    y = lax.rem(s, 2) * 2 + y_low
    other = 1 - b
    sign = 1 - 2 * b
    mine = pl.ds(b * 16, 16)
    here = x * 4 + y
    here_mid = x * 4 + y_low * 2 + lax.div(y, 2)

    def remote(src, dst, send_sem, recv_sem, to):
        return pltpu.make_async_remote_copy(
            src_ref=src, dst_ref=dst, send_sem=send_sem, recv_sem=recv_sem,
            device_id=to, device_id_type=MESH,
        )

    def wait_for(ref, sem):
        pltpu.make_async_copy(ref, ref, sem).wait()

    def away(d, at, way):
        return lax.rem(at + way * d + 4, 4)

    def in_plane(at_x, at_y):
        return at_x * 2 + lax.div(at_y, 2), z * 2 + lax.rem(at_y, 2)

    def in_line(at_z):
        return at_z * 2 + y_low

    def owner_low(low):
        return lax.rem(y_low + low, 2)

    barrier = pltpu.get_barrier_semaphore()

    def greet(to):
        pl.semaphore_signal(barrier, inc=1, device_id=to, device_id_type=MESH)

    for dz in range(4):
        at_h = in_line(away(dz, z, 1))
        greet((s, at_h, other))
        if dz:
            greet((s, at_h, b))
    for low in (1, 0):
        for dx, dy in PLANE[low]:
            at_s, at_h = in_plane(away(dx, x, 1), away(dy, y, 1))
            greet((at_s, at_h, b))
            if low == 0:
                greet((at_s, at_h, other))

    scalars = [
        pltpu.make_async_copy(slot_order_hbm, slot_order, scalar_sem.at[0]),
        pltpu.make_async_copy(lengths_hbm, lengths, scalar_sem.at[1]),
    ]
    whole = [
        pltpu.make_async_copy(keys_flat.at[at], key_columns.at[:, pl.ds(at * HD, HD)], full_sem.at[0])
        for at in range(16)
    ]
    whole.append(pltpu.make_async_copy(values_flat, value_rows, full_sem.at[1]))
    fresh = [
        pltpu.make_async_copy(src, fresh_rows.at[n], fresh_sem.at[n])
        for n, src in enumerate((new_keys, new_values))
    ]
    for copy in scalars:
        copy.start()
    for piece, (low, dz) in enumerate(PIECES):
        pltpu.make_async_copy(
            values.at[:, away(dz, z, sign), owner_low(low), b], values_chip[piece].at[mine], chip_recv.at[piece]
        ).start()
    for low in (1, 0):
        pltpu.make_async_copy(
            keys.at[:, z, owner_low(low), b], keys_near[low].at[mine], near_recv.at[low]
        ).start()
    for copy in whole + fresh:
        copy.start()
    pl.semaphore_wait(barrier, 29)

    def swap(piece):
        low, dz = PIECES[piece]
        remote(
            values.at[:, away(dz, z, -sign), owner_low(low), other], values_chip[piece].at[mine],
            chip_send, chip_recv.at[piece], (s, h, other),
        ).start()

    swap(0)
    swap(1)

    def send_line(low, dz, to_b):
        to_z = away(dz, z, sign)
        d = away(dz, 0, sign)
        remote(
            keys.at[:, to_z, owner_low(low), to_b], keys_line[low].at[3 - d, mine],
            line_send, line_recv.at[low], (s, in_line(to_z), to_b),
        ).start()

    for low in (1, 0):
        for dz, to_b in ((1, b), (3, other), (2, b), (1, other), (3, b), (2, other)):
            send_line(low, dz, to_b)
    for low in (1, 0):
        remote(
            keys.at[:, z, owner_low(low), other], keys_near[low].at[mine],
            line_send, near_recv.at[low], (s, h, other),
        ).start()

    head_rows = pl.ds(pl.multiple_of(h * GROUP * HD, GROUP * HD), GROUP * HD)
    head_cols = pl.ds(pl.multiple_of(h * HD, HD), HD)

    def small_pieces(to_s):
        return (
            (queries.at[:, to_s, :, head_rows], query_all.at[s]),
            (new_keys.at[:, to_s, :, head_cols], fresh_all.at[0, s]),
            (new_values.at[:, to_s, :, head_cols], fresh_all.at[1, s]),
        )

    def send_small(step, carry):
        to_s = lax.rem(s + step, 8)
        for n, (src, dst) in enumerate(small_pieces(to_s)):
            remote(src, dst, small_send.at[n], small_recv.at[n], (to_s, h, b)).start()
        return carry

    def each_slot(do):
        def step(at_s, carry):
            for k in range(4):
                do(at_s, k, slot_order[at_s * 4 + k])
            return carry

        lax.fori_loop(0, 8, step, 0)

    def send_plane(src, dx, dy, dst, send_sem, recv_sem):
        to_x, to_y = away(dx, x, sign), away(dy, y, sign)
        to_s, to_h = in_plane(to_x, to_y)
        remote(src(to_x * 4 + to_y), dst, send_sem, recv_sem, (to_s, to_h, b)).start()

    def take_values(piece):
        low, dz = PIECES[piece]
        at_z = away(dz, 0, sign)
        wait_for(values_chip[piece], chip_recv.at[piece])
        if piece + 2 < len(PIECES):
            swap(piece + 2)

        def pack(at_s, k, slot):
            values_packed[at_s * 2 + owner_low(low), at_z, k] = values_chip[piece][slot]

        each_slot(pack)
        if dz:
            for dx, dy in PLANE[low]:
                send_plane(
                    lambda to: values_packed.at[to, at_z], dx, dy, values_mid.at[at_z, here_mid],
                    mid_first if low else mid_send, mid_recv.at[group_of(dx, low)],
                )

    far = pl.ds(1, 3)

    def forward_values(dx, low):
        group = group_of(dx, low)
        wait_for(values_mid.at[far, pl.ds(0, 2)], mid_recv.at[group])
        pair = pl.ds(away(dx, x, -sign) * 4 + owner_low(low) * 2, 2)
        for dz in (1, 3, 2):
            remote(
                values_mid.at[dz, pair], values_land.at[dz - 1, pair],
                values_send, values_recv.at[group], (s, in_line(away(dz, z, 1)), b),
            ).start()

    def take_near_keys(low):
        wait_for(keys_near[low], near_recv.at[low])

        def pack(at_s, k, slot):
            keys_packed[at_s * 2 + owner_low(low), 0, k] = keys_near[low][slot]

        each_slot(pack)

    def send_near(low):
        for dx, dy in PLANE[low]:
            send_plane(
                lambda to: values_packed.at[to, 0], dx, dy, values_mid.at[0, here_mid], mid_near, mid_near_recv
            )
            send_plane(lambda to: keys_packed.at[to, 0], dx, dy, keys_land.at[here, 0], keys_send, keys_recv)

    def turn_keys(low):
        wait_for(keys_line[low], line_recv.at[low])

        def pack(at_s, k, slot):
            for dz in range(1, 4):
                keys_packed[at_s * 2 + owner_low(low), dz, k] = keys_line[low][dz - 1, slot]

        each_slot(pack)
        for dx, dy in PLANE[low]:
            send_plane(lambda to: keys_packed.at[to, far], dx, dy, keys_land.at[here, far], keys_send, keys_recv)

    scalars[0].wait()
    scalars[1].wait()
    lax.fori_loop(1, 8, send_small, 0)
    for n, (src, dst) in enumerate(small_pieces(s)):
        pltpu.make_async_copy(src, dst, small_recv.at[n]).start()
    for piece in range(len(PIECES)):
        take_values(piece)
    pltpu.make_async_copy(
        values_packed.at[here, far], values_mid.at[far, here_mid], mid_recv.at[group_of(0, 0)]
    ).start()
    pltpu.make_async_copy(values_packed.at[here, 0], values_mid.at[0, here_mid], mid_near_recv).start()

    for n, part in enumerate((query_all, fresh_all.at[0], fresh_all.at[1])):
        wait_for(part, small_recv.at[n])
    wait_for(key_columns, full_sem.at[0])
    wait_for(value_rows, full_sem.at[1])

    def spread_queries(at_s, carry):
        for t in range(2):
            rows = query_all[at_s, t].astype(F32)
            for g in range(GROUP):
                row = (g // 4) * 8 + t * 4 + g % 4
                for k in range(4):
                    query_rows[at_s * 4 + k, row : row + 1, :] = rows[k : k + 1, g * HD : g * HD + HD]
        return carry

    lax.fori_loop(0, 8, spread_queries, 0)

    def find_slot(at, carry):
        found = jnp.int32(0)
        for slot in range(32):
            found = jnp.where(slot_order[slot] == b * 16 + at, slot, found)
        slot_of[at] = found
        return carry

    lax.fori_loop(0, 16, find_slot, 0)

    lane = lax.broadcasted_iota(jnp.int32, (1, HD), 1)
    lane_prompt = lax.div(lane, 16)
    lane_later = lax.rem(lax.div(lane, 4), 2) == 1
    block_lane = lax.div(lax.broadcasted_iota(jnp.int32, (HD, HD), 1), 16)
    row4 = lax.broadcasted_iota(jnp.int32, (4, HD), 0)
    row512 = lax.broadcasted_iota(jnp.int32, (512, HD), 0)
    scale = HD ** -0.5

    def attend(first):
        slots = [slot_of[first + p] for p in range(8)]
        live = jnp.zeros((1, HD), jnp.int32)
        for p in range(8):
            live = jnp.where(lane_prompt == p, lengths[first + p + b * 16], live)

        def fresh_row(n, t, slot):
            rows = fresh_all[n, lax.div(slot, 4), t].astype(F32)
            return jnp.sum(jnp.where(row4 == lax.rem(slot, 4), rows, 0.0), axis=0, keepdims=True)

        questions = jnp.concatenate([query_rows[slot] for slot in slots], axis=0).T
        diagonal = jnp.concatenate(
            [jnp.where(block_lane == p, questions, 0.0) for p in range(8)], axis=0
        ).astype(BF16)
        fresh_keys = jnp.concatenate(
            [
                jnp.concatenate([fresh_row(0, 0, slot), fresh_row(0, 1, slot), jnp.zeros((14, HD), F32)], axis=0)
                for slot in slots
            ],
            axis=1,
        ).astype(BF16)
        scores = jnp.dot(
            key_columns[:, first * HD : (first + 8) * HD], diagonal, preferred_element_type=F32
        ) * scale
        fresh_scores = jnp.dot(fresh_keys, diagonal, preferred_element_type=F32) * scale
        kept = row512 < live
        scores = jnp.where(kept, scores, HIDDEN)
        n0 = fresh_scores[0:1]
        n1 = jnp.where(lane_later, fresh_scores[1:2], HIDDEN)
        peak = jnp.maximum(jnp.max(scores, axis=0, keepdims=True), jnp.maximum(n0, n1))
        mass = jnp.where(kept, jnp.exp(scores - peak), 0.0)
        m0 = jnp.exp(n0 - peak)
        m1 = jnp.where(lane_later, jnp.exp(n1 - peak), 0.0)
        total = jnp.sum(mass, axis=0, keepdims=True) + m0 + m1
        weights = mass.T.astype(BF16)
        m0, m1 = (m.astype(BF16).astype(F32) for m in (m0, m1))
        sides = jnp.concatenate([total, m0, m1, jnp.zeros((HD - 3, HD), F32)], axis=0).T
        for p, slot in enumerate(slots):
            cut = slice(p * 16, p * 16 + 16)
            weighted = jnp.dot(weights[cut], value_rows[first + p], preferred_element_type=F32)
            weighted += sides[cut, 1:2] * fresh_row(1, 0, slot)
            weighted += sides[cut, 2:3] * fresh_row(1, 1, slot)
            result[first + p] = weighted / sides[cut, 0:1]

    attend(0)
    attend(8)

    def hand_rows(at_s, carry):
        for pair in range(2):
            first, second = (
                result[jnp.clip(slot_order[at_s * 4 + pair * 2 + n] - b * 16, 0, 15)] for n in range(2)
            )
            for to_b in range(2):
                cut = slice(to_b * 8, to_b * 8 + 8)
                rows_send[at_s, to_b, pair] = jnp.concatenate((first[cut], second[cut]), axis=0).astype(BF16)
        return carry

    lax.fori_loop(0, 8, hand_rows, 0)

    def send_rows(to_s, to_b):
        remote(
            rows_send.at[to_s, to_b], rows_land.at[s, b], rows_send_sem, rows_recv_sem, (to_s, h, to_b)
        ).start()

    def send_rows_step(step, carry):
        to_s = lax.rem(s + step, 8)
        send_rows(to_s, b)
        send_rows(to_s, other)
        return carry

    lax.fori_loop(1, 8, send_rows_step, 0)
    send_rows(s, other)
    pltpu.make_async_copy(rows_send.at[s, b], rows_land.at[s, b], rows_recv_sem).start()
    owned = [slot_order[s * 4 + k] for k in range(4)]
    lives = [lengths[slot] for slot in owned]
    first_position = (h * 2 + b) * BLOCK
    position = first_position + lax.broadcasted_iota(jnp.int32, (BLOCK, HD), 0)
    for k in range(4):
        keep[k] = jnp.where(position < lives[k], 1.0, 0.0).astype(BF16)
    fresh[0].wait()
    fresh[1].wait()

    def place_fresh(layer, carry):
        wide = first_position + lax.broadcasted_iota(jnp.int32, (BLOCK, KVH * HD), 0)
        for n, out in enumerate((keys_fresh, values_cache)):
            new = [fresh_rows[n, t, layer].astype(F32) for t in range(2)]
            for k in range(4):
                rows = jnp.zeros((BLOCK, KVH * HD), F32)
                for t in range(2):
                    rows = jnp.where(wide == lives[k] + t, new[t][k : k + 1], rows)
                out[layer, k] = rows.astype(BF16)
        return carry

    lax.fori_loop(0, 8, place_fresh, 0)
    take_near_keys(1)
    take_near_keys(0)
    wait_for(values_packed.at[pl.ds(0, 8), far], mid_first)
    send_near(1)
    send_near(0)
    for low in (1, 0):
        for dx in (1, 3, 2, 0):
            forward_values(dx, low)
    turn_keys(1)
    turn_keys(0)
    pltpu.make_async_copy(keys_packed.at[here], keys_land.at[here], keys_recv).start()

    def settle_values(src, at, from_x, low, from_z):
        def step(half, carry):
            from_low = owner_low(low)
            block = src.at[at, from_x * 4 + from_low * 2 + half]
            layer = from_x * 2 + half
            cut = pl.ds(pl.multiple_of((from_z * 2 + from_low) * HD, HD), HD)
            for k in range(4):
                values_cache[layer, k, :, cut] = jnp.where(keep[k] > 0, block[k], values_cache[layer, k, :, cut])
            return carry

        lax.fori_loop(0, 2, step, 0)

    owners = [lax.div(slot, 16) for slot in owned]

    def assemble(l, carry):
        picked = []
        for k in range(4):
            part = slice((k % 2) * 8, (k % 2) * 8 + 8)
            first, second = (rows_land[l, n, k // 2].astype(F32)[part] for n in range(2))
            picked.append(jnp.where(owners[k] == 0, first, second))
        for t in range(2):
            attention[t, l] = jnp.concatenate(
                [
                    jnp.concatenate([rows[t * 4 + g : t * 4 + g + 1] for rows in picked], axis=0)
                    for g in range(4)
                ],
                axis=1,
            ).astype(BF16)
        return carry

    wait_for(rows_land, rows_recv_sem)
    lax.fori_loop(0, 8, assemble, 0)
    wait_for(values_mid.at[0], mid_near_recv)
    for low in (1, 0):
        for dx in (1, 3, 2, 0):
            settle_values(values_mid, 0, away(dx, x, -sign), low, z)
    for low in (1, 0):
        for dx in (1, 3, 2, 0):
            wait_for(values_land.at[:, pl.ds(0, 2)], values_recv.at[group_of(dx, low)])
            for dz in (1, 3, 2):
                settle_values(values_land, dz - 1, away(dx, x, -sign), low, away(dz, z, -1))
    wait_for(keys_land, keys_recv)

    wait_for(value_rows.at[pl.ds(0, 8)], chip_send)
    wait_for(value_rows.at[pl.ds(0, 14)], line_send)
    for n, part in enumerate((query_all, fresh_all.at[0], fresh_all.at[1])):
        wait_for(part.at[pl.ds(0, 7)], small_send.at[n])
    wait_for(values_packed.at[pl.ds(0, 7), far], mid_send)
    wait_for(values_packed.at[pl.ds(0, 15), 0], mid_near)
    wait_for(keys_packed.at[pl.ds(0, 15)], keys_send)
    wait_for(values_land, values_send)
    wait_for(rows_send.at[pl.ds(0, 7)], rows_send_sem)
    wait_for(rows_send.at[0, 0], rows_send_sem)


def hand_out(
    attention, values, keys_land, keys_fresh, keep, attention_out, values_out, keys_out, keys, sem
):
    copies = [pltpu.make_async_copy(values.at[l], values_out.at[l], sem.at[l]) for l in range(8)]
    copies.append(pltpu.make_async_copy(attention, attention_out, sem.at[16]))
    for copy in copies:
        copy.start()
    kept = [keep[k] > 0 for k in range(4)]
    z = lax.div(lax.axis_index("head"), 2)
    for l in range(8):
        for h in range(KVH):
            cut = slice(h * HD, h * HD + HD)
            for k in range(4):
                landed = keys_land[l // 2 * 4 + l % 2 * 2 + h % 2, lax.rem(h // 2 - z + 4, 4), k]
                keys[l, k, :, cut] = jnp.where(kept[k], landed, keys_fresh[l, k, :, cut])
        copies.append(pltpu.make_async_copy(keys.at[l], keys_out.at[l], sem.at[8 + l]))
        copies[-1].start()
    for copy in copies:
        copy.wait()


def body(keys_prefill, values_prefill, lengths, slot_order, queries, new_keys, new_values):
    keys = keys_prefill.reshape(16, 4, 2, 2, BLOCK, HD)
    values = values_prefill.reshape(16, 4, 2, 2, BLOCK, HD)
    flat = (keys_prefill.reshape(16, 512, HD), values_prefill.reshape(16, 512, HD))
    any_spec = pl.BlockSpec(memory_space=pl.ANY)
    hbm_spec = pl.BlockSpec(memory_space=pltpu.HBM)
    vmem_spec = pl.BlockSpec(memory_space=pltpu.VMEM)
    dma, vmem = pltpu.SemaphoreType.DMA, pltpu.VMEM
    rows_shape, cache_shape = (2, 8, 4, 4 * HD), (8, 4, BLOCK, KVH * HD)
    plane_shape = (16, 4, 4, BLOCK, HD)

    def in_hbm(array):
        return pltpu.with_memory_space_constraint(array, pltpu.HBM)

    held = pl.pallas_call(
        relay,
        out_shape=tuple(
            vmem(shape, BF16) for shape in (rows_shape, cache_shape, plane_shape, cache_shape, (4, BLOCK, HD))
        ),
        in_specs=[hbm_spec] * 9,
        out_specs=(vmem_spec,) * 5,
        scratch_shapes=[
            vmem((512, 16 * HD), BF16), vmem((16, 512, HD), BF16),
            [vmem((3, 32, BLOCK, HD), BF16)] * 2, [vmem((32, BLOCK, HD), BF16)] * 2,
            [vmem((32, BLOCK, HD), BF16)] * len(PIECES),
            vmem(plane_shape, BF16), vmem(plane_shape, BF16),
            vmem((4, 16, 4, BLOCK, HD), BF16), vmem((3, 16, 4, BLOCK, HD), BF16),
            vmem((2, 2, 8, 4, KVH * HD), BF16), vmem((8, 2, 4, GROUP * HD), BF16), vmem((32, 16, HD), F32),
            vmem((2, 8, 2, 4, HD), BF16), vmem((16, 16, HD), F32),
            vmem((8, 2, 2, 16, HD), BF16), vmem((8, 2, 2, 16, HD), BF16),
            pltpu.SMEM((32,), jnp.int32), pltpu.SMEM((32,), jnp.int32), pltpu.SMEM((16,), jnp.int32),
            dma((2,)), dma((2,)), dma((2,)), dma, dma((2,)), dma((2,)), dma, dma((len(PIECES),)),
            dma, dma, dma, dma, dma((8,)), dma, dma, dma, dma((8,)),
            dma((3,)), dma((3,)), dma, dma,
        ],
        compiler_params=pltpu.CompilerParams(
            collective_id=0, has_side_effects=True, vmem_limit_bytes=48 * 2**20
        ),
        name="relay",
    )(*(in_hbm(x) for x in (slot_order, lengths, keys, values, *flat, queries, new_keys, new_values)))
    attention, values_cache, keys_cache = pl.pallas_call(
        hand_out,
        out_shape=tuple(jax.ShapeDtypeStruct(shape, BF16) for shape in (rows_shape, cache_shape, cache_shape)),
        in_specs=[vmem_spec] * 5,
        out_specs=(any_spec,) * 3,
        scratch_shapes=[vmem(cache_shape, BF16), dma((17,))],
        compiler_params=pltpu.CompilerParams(vmem_limit_bytes=8 * 2**20),
        name="hand_out",
    )(*(pltpu.with_memory_space_constraint(x, pltpu.VMEM) for x in held))
    return attention, keys_cache, values_cache


def solution(mesh):
    in_specs = (
        P("section", "batch", None, "head"),
        P("section", "batch", None, "head"),
        P(),
        P(),
        P(None, None, "section", None),
        P(None, None, "section", None),
        P(None, None, "section", None),
    )
    out_specs = (
        P(None, None, "section", ("head", "batch")),
        P(None, "section", ("head", "batch"), None),
        P(None, "section", ("head", "batch"), None),
    )
    return jax.shard_map(body, mesh=mesh, in_specs=in_specs, out_specs=out_specs, check_vma=False)
```

```python
import jax
import jax.numpy as jnp
from jax import lax
from jax.experimental import pallas as pl
from jax.experimental.pallas import tpu as pltpu
from jax.sharding import PartitionSpec as P

KVH = 8
HD = 128
GROUP = 8
BLOCK = 32
MESH = pl.DeviceIdType.MESH
HIDDEN = -1e30
BF16, F32 = jnp.bfloat16, jnp.float32


PLANE = {
    1: ((1, 1), (3, 3), (1, 3), (3, 1), (2, 1), (0, 3), (2, 3), (0, 1)),
    0: ((1, 0), (0, 2), (3, 2), (1, 2), (3, 0), (2, 2), (2, 0)),
}
PIECES = ((1, 1), (1, 3), (1, 2), (0, 1), (0, 3), (0, 2), (1, 0), (0, 0))


def group_of(dx, low):
    return low * 4 + dx


def relay(
    slot_order_hbm, lengths_hbm, keys, values, keys_flat, values_flat, queries, new_keys, new_values,
    attention, values_cache, keys_land, keys_fresh, keep,
    key_columns, value_rows, keys_line, keys_near, values_chip, keys_packed, values_packed, values_mid, values_land,
    fresh_rows, query_all, query_rows, fresh_all, result, rows_send, rows_land,
    slot_order, lengths, slot_of,
    scalar_sem, full_sem, fresh_sem, line_send, line_recv, near_recv, chip_send, chip_recv,
    keys_send, keys_recv, mid_send, mid_recv, mid_near, mid_near_recv, values_send, values_recv,
    small_send, small_recv, rows_send_sem, rows_recv_sem,
):
    s, h, b = lax.axis_index("section"), lax.axis_index("head"), lax.axis_index("batch")
    x, z = lax.div(s, 2), lax.div(h, 2)
    y_low = lax.rem(h, 2)
    y = lax.rem(s, 2) * 2 + y_low
    other = 1 - b
    sign = 1 - 2 * b
    mine = pl.ds(b * 16, 16)
    here = x * 4 + y
    here_mid = x * 4 + y_low * 2 + lax.div(y, 2)

    def remote(src, dst, send_sem, recv_sem, to):
        return pltpu.make_async_remote_copy(
            src_ref=src, dst_ref=dst, send_sem=send_sem, recv_sem=recv_sem,
            device_id=to, device_id_type=MESH,
        )

    def wait_for(ref, sem):
        pltpu.make_async_copy(ref, ref, sem).wait()

    def away(d, at, way):
        return lax.rem(at + way * d + 4, 4)

    def in_plane(at_x, at_y):
        return at_x * 2 + lax.div(at_y, 2), z * 2 + lax.rem(at_y, 2)

    def in_line(at_z):
        return at_z * 2 + y_low

    def owner_low(low):
        return lax.rem(y_low + low, 2)

    barrier = pltpu.get_barrier_semaphore()

    def greet(to):
        pl.semaphore_signal(barrier, inc=1, device_id=to, device_id_type=MESH)

    for dz in range(4):
        at_h = in_line(away(dz, z, 1))
        greet((s, at_h, other))
        if dz:
            greet((s, at_h, b))
    for low in (1, 0):
        for dx, dy in PLANE[low]:
            at_s, at_h = in_plane(away(dx, x, 1), away(dy, y, 1))
            greet((at_s, at_h, b))
            if low == 0:
                greet((at_s, at_h, other))

    scalars = [
        pltpu.make_async_copy(slot_order_hbm, slot_order, scalar_sem.at[0]),
        pltpu.make_async_copy(lengths_hbm, lengths, scalar_sem.at[1]),
    ]
    whole = [
        pltpu.make_async_copy(keys_flat.at[at], key_columns.at[:, pl.ds(at * HD, HD)], full_sem.at[0])
        for at in range(16)
    ]
    whole.append(pltpu.make_async_copy(values_flat, value_rows, full_sem.at[1]))
    fresh = [
        pltpu.make_async_copy(src, fresh_rows.at[n], fresh_sem.at[n])
        for n, src in enumerate((new_keys, new_values))
    ]
    for copy in scalars:
        copy.start()
    for piece, (low, dz) in enumerate(PIECES):
        pltpu.make_async_copy(
            values.at[:, away(dz, z, sign), owner_low(low), b], values_chip[piece].at[mine], chip_recv.at[piece]
        ).start()
    for low in (1, 0):
        pltpu.make_async_copy(
            keys.at[:, z, owner_low(low), b], keys_near[low].at[mine], near_recv.at[low]
        ).start()
    for copy in whole + fresh:
        copy.start()
    pl.semaphore_wait(barrier, 29)

    def swap(piece):
        low, dz = PIECES[piece]
        remote(
            values.at[:, away(dz, z, -sign), owner_low(low), other], values_chip[piece].at[mine],
            chip_send, chip_recv.at[piece], (s, h, other),
        ).start()

    swap(0)
    swap(1)

    def send_line(low, dz, to_b):
        to_z = away(dz, z, sign)
        d = away(dz, 0, sign)
        remote(
            keys.at[:, to_z, owner_low(low), to_b], keys_line[low].at[3 - d, mine],
            line_send, line_recv.at[low], (s, in_line(to_z), to_b),
        ).start()

    for low in (1, 0):
        for dz, to_b in ((1, b), (3, other), (2, b), (1, other), (3, b), (2, other)):
            send_line(low, dz, to_b)
    for low in (1, 0):
        remote(
            keys.at[:, z, owner_low(low), other], keys_near[low].at[mine],
            line_send, near_recv.at[low], (s, h, other),
        ).start()

    head_rows = pl.ds(pl.multiple_of(h * GROUP * HD, GROUP * HD), GROUP * HD)
    head_cols = pl.ds(pl.multiple_of(h * HD, HD), HD)

    def small_pieces(to_s):
        return (
            (queries.at[:, to_s, :, head_rows], query_all.at[s]),
            (new_keys.at[:, to_s, :, head_cols], fresh_all.at[0, s]),
            (new_values.at[:, to_s, :, head_cols], fresh_all.at[1, s]),
        )

    def send_small(step, carry):
        to_s = lax.rem(s + step, 8)
        for n, (src, dst) in enumerate(small_pieces(to_s)):
            remote(src, dst, small_send.at[n], small_recv.at[n], (to_s, h, b)).start()
        return carry

    def each_slot(do):
        def step(at_s, carry):
            for k in range(4):
                do(at_s, k, slot_order[at_s * 4 + k])
            return carry

        lax.fori_loop(0, 8, step, 0)

    def send_plane(src, dx, dy, dst, send_sem, recv_sem):
        to_x, to_y = away(dx, x, sign), away(dy, y, sign)
        to_s, to_h = in_plane(to_x, to_y)
        remote(src(to_x * 4 + to_y), dst, send_sem, recv_sem, (to_s, to_h, b)).start()

    def take_values(piece):
        low, dz = PIECES[piece]
        at_z = away(dz, 0, sign)
        wait_for(values_chip[piece], chip_recv.at[piece])
        if piece + 2 < len(PIECES):
            swap(piece + 2)

        def pack(at_s, k, slot):
            values_packed[at_s * 2 + owner_low(low), at_z, k] = values_chip[piece][slot]

        each_slot(pack)
        if dz:
            for dx, dy in PLANE[low]:
                send_plane(
                    lambda to: values_packed.at[to, at_z], dx, dy, values_mid.at[at_z, here_mid],
                    mid_send, mid_recv.at[group_of(dx, low)],
                )

    far = pl.ds(1, 3)

    def forward_values(dx, low):
        group = group_of(dx, low)
        wait_for(values_mid.at[far, pl.ds(0, 2)], mid_recv.at[group])
        pair = pl.ds(away(dx, x, -sign) * 4 + owner_low(low) * 2, 2)
        for dz in (1, 3, 2):
            remote(
                values_mid.at[dz, pair], values_land.at[dz - 1, pair],
                values_send, values_recv.at[group], (s, in_line(away(dz, z, 1)), b),
            ).start()

    def take_near_keys(low):
        wait_for(keys_near[low], near_recv.at[low])

        def pack(at_s, k, slot):
            keys_packed[at_s * 2 + owner_low(low), 0, k] = keys_near[low][slot]

        each_slot(pack)

    def send_near_values():
        for dx, dy in PLANE[1] + PLANE[0]:
            send_plane(
                lambda to: values_packed.at[to, 0], dx, dy, values_mid.at[0, here_mid], mid_near, mid_near_recv
            )

    def send_near_keys():
        for dx, dy in PLANE[1] + PLANE[0]:
            send_plane(lambda to: keys_packed.at[to, 0], dx, dy, keys_land.at[here, 0], keys_send, keys_recv)

    def turn_keys(low):
        wait_for(keys_line[low], line_recv.at[low])

        def pack(at_s, k, slot):
            for dz in range(1, 4):
                keys_packed[at_s * 2 + owner_low(low), dz, k] = keys_line[low][dz - 1, slot]

        each_slot(pack)
        for dx, dy in PLANE[low]:
            send_plane(lambda to: keys_packed.at[to, far], dx, dy, keys_land.at[here, far], keys_send, keys_recv)

    scalars[0].wait()
    scalars[1].wait()
    lax.fori_loop(1, 8, send_small, 0)
    for n, (src, dst) in enumerate(small_pieces(s)):
        pltpu.make_async_copy(src, dst, small_recv.at[n]).start()
    for piece in range(len(PIECES)):
        take_values(piece)
    pltpu.make_async_copy(
        values_packed.at[here, far], values_mid.at[far, here_mid], mid_recv.at[group_of(0, 0)]
    ).start()
    pltpu.make_async_copy(values_packed.at[here, 0], values_mid.at[0, here_mid], mid_near_recv).start()

    for n, part in enumerate((query_all, fresh_all.at[0], fresh_all.at[1])):
        wait_for(part, small_recv.at[n])
    wait_for(key_columns, full_sem.at[0])
    wait_for(value_rows, full_sem.at[1])

    def spread_queries(at_s, carry):
        for t in range(2):
            rows = query_all[at_s, t].astype(F32)
            for g in range(GROUP):
                row = (g // 4) * 8 + t * 4 + g % 4
                for k in range(4):
                    query_rows[at_s * 4 + k, row : row + 1, :] = rows[k : k + 1, g * HD : g * HD + HD]
        return carry

    lax.fori_loop(0, 8, spread_queries, 0)

    def find_slot(at, carry):
        found = jnp.int32(0)
        for slot in range(32):
            found = jnp.where(slot_order[slot] == b * 16 + at, slot, found)
        slot_of[at] = found
        return carry

    lax.fori_loop(0, 16, find_slot, 0)

    lane = lax.broadcasted_iota(jnp.int32, (1, HD), 1)
    lane_prompt = lax.div(lane, 16)
    lane_later = lax.rem(lax.div(lane, 4), 2) == 1
    block_lane = lax.div(lax.broadcasted_iota(jnp.int32, (HD, HD), 1), 16)
    row4 = lax.broadcasted_iota(jnp.int32, (4, HD), 0)
    row512 = lax.broadcasted_iota(jnp.int32, (512, HD), 0)
    scale = HD ** -0.5

    def attend(first):
        slots = [slot_of[first + p] for p in range(8)]
        live = jnp.zeros((1, HD), jnp.int32)
        for p in range(8):
            live = jnp.where(lane_prompt == p, lengths[first + p + b * 16], live)

        def fresh_row(n, t, slot):
            rows = fresh_all[n, lax.div(slot, 4), t].astype(F32)
            return jnp.sum(jnp.where(row4 == lax.rem(slot, 4), rows, 0.0), axis=0, keepdims=True)

        questions = jnp.concatenate([query_rows[slot] for slot in slots], axis=0).T
        diagonal = jnp.concatenate(
            [jnp.where(block_lane == p, questions, 0.0) for p in range(8)], axis=0
        ).astype(BF16)
        fresh_keys = jnp.concatenate(
            [
                jnp.concatenate([fresh_row(0, 0, slot), fresh_row(0, 1, slot), jnp.zeros((14, HD), F32)], axis=0)
                for slot in slots
            ],
            axis=1,
        ).astype(BF16)
        scores = jnp.dot(
            key_columns[:, first * HD : (first + 8) * HD], diagonal, preferred_element_type=F32
        ) * scale
        fresh_scores = jnp.dot(fresh_keys, diagonal, preferred_element_type=F32) * scale
        kept = row512 < live
        scores = jnp.where(kept, scores, HIDDEN)
        n0 = fresh_scores[0:1]
        n1 = jnp.where(lane_later, fresh_scores[1:2], HIDDEN)
        peak = jnp.maximum(jnp.max(scores, axis=0, keepdims=True), jnp.maximum(n0, n1))
        mass = jnp.where(kept, jnp.exp(scores - peak), 0.0)
        m0 = jnp.exp(n0 - peak)
        m1 = jnp.where(lane_later, jnp.exp(n1 - peak), 0.0)
        total = jnp.sum(mass, axis=0, keepdims=True) + m0 + m1
        weights = mass.T.astype(BF16)
        m0, m1 = (m.astype(BF16).astype(F32) for m in (m0, m1))
        sides = jnp.concatenate([total, m0, m1, jnp.zeros((HD - 3, HD), F32)], axis=0).T
        for p, slot in enumerate(slots):
            cut = slice(p * 16, p * 16 + 16)
            weighted = jnp.dot(weights[cut], value_rows[first + p], preferred_element_type=F32)
            weighted += sides[cut, 1:2] * fresh_row(1, 0, slot)
            weighted += sides[cut, 2:3] * fresh_row(1, 1, slot)
            result[first + p] = weighted / sides[cut, 0:1]

    attend(0)
    attend(8)

    def hand_rows(at_s, carry):
        for pair in range(2):
            first, second = (
                result[jnp.clip(slot_order[at_s * 4 + pair * 2 + n] - b * 16, 0, 15)] for n in range(2)
            )
            for to_b in range(2):
                cut = slice(to_b * 8, to_b * 8 + 8)
                rows_send[at_s, to_b, pair] = jnp.concatenate((first[cut], second[cut]), axis=0).astype(BF16)
        return carry

    lax.fori_loop(0, 8, hand_rows, 0)

    def send_rows(to_s, to_b):
        remote(
            rows_send.at[to_s, to_b], rows_land.at[s, b], rows_send_sem, rows_recv_sem, (to_s, h, to_b)
        ).start()

    def send_rows_step(step, carry):
        to_s = lax.rem(s + step, 8)
        send_rows(to_s, b)
        send_rows(to_s, other)
        return carry

    lax.fori_loop(1, 8, send_rows_step, 0)
    send_rows(s, other)
    pltpu.make_async_copy(rows_send.at[s, b], rows_land.at[s, b], rows_recv_sem).start()
    owned = [slot_order[s * 4 + k] for k in range(4)]
    lives = [lengths[slot] for slot in owned]
    first_position = (h * 2 + b) * BLOCK
    position = first_position + lax.broadcasted_iota(jnp.int32, (BLOCK, HD), 0)
    for k in range(4):
        keep[k] = jnp.where(position < lives[k], 1.0, 0.0).astype(BF16)
    fresh[0].wait()
    fresh[1].wait()

    def place_fresh(layer, carry):
        wide = first_position + lax.broadcasted_iota(jnp.int32, (BLOCK, KVH * HD), 0)
        for n, out in enumerate((keys_fresh, values_cache)):
            new = [fresh_rows[n, t, layer].astype(F32) for t in range(2)]
            for k in range(4):
                rows = jnp.zeros((BLOCK, KVH * HD), F32)
                for t in range(2):
                    rows = jnp.where(wide == lives[k] + t, new[t][k : k + 1], rows)
                out[layer, k] = rows.astype(BF16)
        return carry

    lax.fori_loop(0, 8, place_fresh, 0)
    take_near_keys(1)
    take_near_keys(0)
    for dx in (1, 3, 2, 0):
        forward_values(dx, 1)
    send_near_values()
    for dx in (1, 3, 2, 0):
        forward_values(dx, 0)
    send_near_keys()
    turn_keys(1)
    turn_keys(0)
    pltpu.make_async_copy(keys_packed.at[here], keys_land.at[here], keys_recv).start()

    def settle_values(src, at, from_x, low, from_z):
        def step(half, carry):
            from_low = owner_low(low)
            block = src.at[at, from_x * 4 + from_low * 2 + half]
            layer = from_x * 2 + half
            cut = pl.ds(pl.multiple_of((from_z * 2 + from_low) * HD, HD), HD)
            for k in range(4):
                values_cache[layer, k, :, cut] = jnp.where(keep[k] > 0, block[k], values_cache[layer, k, :, cut])
            return carry

        lax.fori_loop(0, 2, step, 0)

    owners = [lax.div(slot, 16) for slot in owned]

    def assemble(l, carry):
        picked = []
        for k in range(4):
            part = slice((k % 2) * 8, (k % 2) * 8 + 8)
            first, second = (rows_land[l, n, k // 2].astype(F32)[part] for n in range(2))
            picked.append(jnp.where(owners[k] == 0, first, second))
        for t in range(2):
            attention[t, l] = jnp.concatenate(
                [
                    jnp.concatenate([rows[t * 4 + g : t * 4 + g + 1] for rows in picked], axis=0)
                    for g in range(4)
                ],
                axis=1,
            ).astype(BF16)
        return carry

    wait_for(rows_land, rows_recv_sem)
    lax.fori_loop(0, 8, assemble, 0)
    wait_for(values_mid.at[0], mid_near_recv)
    for low in (1, 0):
        for dx in (1, 3, 2, 0):
            settle_values(values_mid, 0, away(dx, x, -sign), low, z)
    for low in (1, 0):
        for dx in (1, 3, 2, 0):
            wait_for(values_land.at[:, pl.ds(0, 2)], values_recv.at[group_of(dx, low)])
            for dz in (1, 3, 2):
                settle_values(values_land, dz - 1, away(dx, x, -sign), low, away(dz, z, -1))
    wait_for(keys_land, keys_recv)

    wait_for(value_rows.at[pl.ds(0, 8)], chip_send)
    wait_for(value_rows.at[pl.ds(0, 14)], line_send)
    for n, part in enumerate((query_all, fresh_all.at[0], fresh_all.at[1])):
        wait_for(part.at[pl.ds(0, 7)], small_send.at[n])
    wait_for(values_packed.at[pl.ds(0, 15), far], mid_send)
    wait_for(values_packed.at[pl.ds(0, 15), 0], mid_near)
    wait_for(keys_packed.at[pl.ds(0, 15)], keys_send)
    wait_for(values_land, values_send)
    wait_for(rows_send.at[pl.ds(0, 7)], rows_send_sem)
    wait_for(rows_send.at[0, 0], rows_send_sem)


def hand_out(
    attention, values, keys_land, keys_fresh, keep, attention_out, values_out, keys_out, keys, sem
):
    copies = [pltpu.make_async_copy(values.at[l], values_out.at[l], sem.at[l]) for l in range(8)]
    copies.append(pltpu.make_async_copy(attention, attention_out, sem.at[16]))
    for copy in copies:
        copy.start()
    kept = [keep[k] > 0 for k in range(4)]
    z = lax.div(lax.axis_index("head"), 2)
    for l in range(8):
        for h in range(KVH):
            cut = slice(h * HD, h * HD + HD)
            for k in range(4):
                landed = keys_land[l // 2 * 4 + l % 2 * 2 + h % 2, lax.rem(h // 2 - z + 4, 4), k]
                keys[l, k, :, cut] = jnp.where(kept[k], landed, keys_fresh[l, k, :, cut])
        copies.append(pltpu.make_async_copy(keys.at[l], keys_out.at[l], sem.at[8 + l]))
        copies[-1].start()
    for copy in copies:
        copy.wait()


def body(keys_prefill, values_prefill, lengths, slot_order, queries, new_keys, new_values):
    keys = keys_prefill.reshape(16, 4, 2, 2, BLOCK, HD)
    values = values_prefill.reshape(16, 4, 2, 2, BLOCK, HD)
    flat = (keys_prefill.reshape(16, 512, HD), values_prefill.reshape(16, 512, HD))
    any_spec = pl.BlockSpec(memory_space=pl.ANY)
    hbm_spec = pl.BlockSpec(memory_space=pltpu.HBM)
    vmem_spec = pl.BlockSpec(memory_space=pltpu.VMEM)
    dma, vmem = pltpu.SemaphoreType.DMA, pltpu.VMEM
    rows_shape, cache_shape = (2, 8, 4, 4 * HD), (8, 4, BLOCK, KVH * HD)
    plane_shape = (16, 4, 4, BLOCK, HD)

    def in_hbm(array):
        return pltpu.with_memory_space_constraint(array, pltpu.HBM)

    held = pl.pallas_call(
        relay,
        out_shape=tuple(
            vmem(shape, BF16) for shape in (rows_shape, cache_shape, plane_shape, cache_shape, (4, BLOCK, HD))
        ),
        in_specs=[hbm_spec] * 9,
        out_specs=(vmem_spec,) * 5,
        scratch_shapes=[
            vmem((512, 16 * HD), BF16), vmem((16, 512, HD), BF16),
            [vmem((3, 32, BLOCK, HD), BF16)] * 2, [vmem((32, BLOCK, HD), BF16)] * 2,
            [vmem((32, BLOCK, HD), BF16)] * len(PIECES),
            vmem(plane_shape, BF16), vmem(plane_shape, BF16),
            vmem((4, 16, 4, BLOCK, HD), BF16), vmem((3, 16, 4, BLOCK, HD), BF16),
            vmem((2, 2, 8, 4, KVH * HD), BF16), vmem((8, 2, 4, GROUP * HD), BF16), vmem((32, 16, HD), F32),
            vmem((2, 8, 2, 4, HD), BF16), vmem((16, 16, HD), F32),
            vmem((8, 2, 2, 16, HD), BF16), vmem((8, 2, 2, 16, HD), BF16),
            pltpu.SMEM((32,), jnp.int32), pltpu.SMEM((32,), jnp.int32), pltpu.SMEM((16,), jnp.int32),
            dma((2,)), dma((2,)), dma((2,)), dma, dma((2,)), dma((2,)), dma, dma((len(PIECES),)),
            dma, dma, dma, dma((8,)), dma, dma, dma, dma((8,)),
            dma((3,)), dma((3,)), dma, dma,
        ],
        compiler_params=pltpu.CompilerParams(
            collective_id=0, has_side_effects=True, vmem_limit_bytes=48 * 2**20
        ),
        name="relay",
    )(*(in_hbm(x) for x in (slot_order, lengths, keys, values, *flat, queries, new_keys, new_values)))
    attention, values_cache, keys_cache = pl.pallas_call(
        hand_out,
        out_shape=tuple(jax.ShapeDtypeStruct(shape, BF16) for shape in (rows_shape, cache_shape, cache_shape)),
        in_specs=[vmem_spec] * 5,
        out_specs=(any_spec,) * 3,
        scratch_shapes=[vmem(cache_shape, BF16), dma((17,))],
        compiler_params=pltpu.CompilerParams(vmem_limit_bytes=8 * 2**20),
        name="hand_out",
    )(*(pltpu.with_memory_space_constraint(x, pltpu.VMEM) for x in held))
    return attention, keys_cache, values_cache


def solution(mesh):
    in_specs = (
        P("section", "batch", None, "head"),
        P("section", "batch", None, "head"),
        P(),
        P(),
        P(None, None, "section", None),
        P(None, None, "section", None),
        P(None, None, "section", None),
    )
    out_specs = (
        P(None, None, "section", ("head", "batch")),
        P(None, "section", ("head", "batch"), None),
        P(None, "section", ("head", "batch"), None),
    )
    return jax.shard_map(body, mesh=mesh, in_specs=in_specs, out_specs=out_specs, check_vma=False)
```

```python
import jax
import jax.numpy as jnp
from jax import lax
from jax.experimental import pallas as pl
from jax.experimental.pallas import tpu as pltpu
from jax.sharding import PartitionSpec as P

KVH = 8
HD = 128
GROUP = 8
BLOCK = 32
MESH = pl.DeviceIdType.MESH
HIDDEN = -1e30
BF16, F32 = jnp.bfloat16, jnp.float32


PLANE = {
    1: ((1, 1), (3, 3), (1, 3), (3, 1), (2, 1), (0, 3), (2, 3), (0, 1)),
    0: ((1, 0), (0, 2), (3, 2), (1, 2), (3, 0), (2, 2), (2, 0)),
}
PIECES = ((1, 1), (1, 3), (1, 2), (0, 1), (0, 3), (0, 2), (1, 0), (0, 0))


def group_of(dx, low):
    return low * 4 + dx


def relay(
    slot_order_hbm, lengths_hbm, keys, values, keys_flat, values_flat, queries, new_keys, new_values,
    attention, values_cache, keys_land, keys_fresh, keep,
    key_columns, value_rows, keys_line, keys_near, values_chip, keys_packed, values_packed, values_mid, values_land,
    fresh_rows, query_all, query_rows, fresh_all, result, rows_send, rows_land,
    slot_order, lengths, slot_of,
    scalar_sem, full_sem, fresh_sem, line_send, line_recv, near_recv, chip_send, chip_recv,
    keys_send, keys_recv, mid_send, mid_recv, mid_near, mid_near_recv, values_send, values_recv,
    small_send, small_recv, rows_send_sem, rows_recv_sem,
):
    s, h, b = lax.axis_index("section"), lax.axis_index("head"), lax.axis_index("batch")
    x, z = lax.div(s, 2), lax.div(h, 2)
    y_low = lax.rem(h, 2)
    y = lax.rem(s, 2) * 2 + y_low
    other = 1 - b
    sign = 1 - 2 * b
    mine = pl.ds(b * 16, 16)
    here = x * 4 + y
    here_mid = x * 4 + y_low * 2 + lax.div(y, 2)

    def remote(src, dst, send_sem, recv_sem, to):
        return pltpu.make_async_remote_copy(
            src_ref=src, dst_ref=dst, send_sem=send_sem, recv_sem=recv_sem,
            device_id=to, device_id_type=MESH,
        )

    def wait_for(ref, sem):
        pltpu.make_async_copy(ref, ref, sem).wait()

    def away(d, at, way):
        return lax.rem(at + way * d + 4, 4)

    def in_plane(at_x, at_y):
        return at_x * 2 + lax.div(at_y, 2), z * 2 + lax.rem(at_y, 2)

    def in_line(at_z):
        return at_z * 2 + y_low

    def owner_low(low):
        return lax.rem(y_low + low, 2)

    barrier = pltpu.get_barrier_semaphore()

    def greet(to):
        pl.semaphore_signal(barrier, inc=1, device_id=to, device_id_type=MESH)

    for dz in range(4):
        at_h = in_line(away(dz, z, 1))
        greet((s, at_h, other))
        if dz:
            greet((s, at_h, b))
    for low in (1, 0):
        for dx, dy in PLANE[low]:
            at_s, at_h = in_plane(away(dx, x, 1), away(dy, y, 1))
            greet((at_s, at_h, b))
            if low == 0:
                greet((at_s, at_h, other))

    scalars = [
        pltpu.make_async_copy(slot_order_hbm, slot_order, scalar_sem.at[0]),
        pltpu.make_async_copy(lengths_hbm, lengths, scalar_sem.at[1]),
    ]
    whole = [
        pltpu.make_async_copy(keys_flat.at[at], key_columns.at[:, pl.ds(at * HD, HD)], full_sem.at[0])
        for at in range(16)
    ]
    whole.append(pltpu.make_async_copy(values_flat, value_rows, full_sem.at[1]))
    fresh = [
        pltpu.make_async_copy(src, fresh_rows.at[n], fresh_sem.at[n])
        for n, src in enumerate((new_keys, new_values))
    ]
    for copy in scalars:
        copy.start()
    for piece, (low, dz) in enumerate(PIECES):
        pltpu.make_async_copy(
            values.at[:, away(dz, z, sign), owner_low(low), b], values_chip[piece].at[mine], chip_recv.at[piece]
        ).start()
    for low in (1, 0):
        pltpu.make_async_copy(
            keys.at[:, z, owner_low(low), b], keys_near[low].at[mine], near_recv.at[low]
        ).start()
    for copy in whole + fresh:
        copy.start()
    pl.semaphore_wait(barrier, 29)

    def swap(piece):
        low, dz = PIECES[piece]
        remote(
            values.at[:, away(dz, z, -sign), owner_low(low), other], values_chip[piece].at[mine],
            chip_send, chip_recv.at[piece], (s, h, other),
        ).start()

    swap(0)
    swap(1)

    def send_line(low, dz, to_b):
        to_z = away(dz, z, sign)
        d = away(dz, 0, sign)
        for half in range(2):
            remote(
                keys.at[pl.ds(half * 8, 8), to_z, owner_low(low), to_b],
                keys_line[low].at[3 - d, pl.ds(b * 16 + half * 8, 8)],
                line_send, line_recv.at[low], (s, in_line(to_z), to_b),
            ).start()

    for low in (1, 0):
        for dz, to_b in ((1, b), (3, other), (2, b), (1, other), (3, b), (2, other)):
            send_line(low, dz, to_b)
    for low in (1, 0):
        remote(
            keys.at[:, z, owner_low(low), other], keys_near[low].at[mine],
            line_send, near_recv.at[low], (s, h, other),
        ).start()

    head_rows = pl.ds(pl.multiple_of(h * GROUP * HD, GROUP * HD), GROUP * HD)
    head_cols = pl.ds(pl.multiple_of(h * HD, HD), HD)

    def small_pieces(to_s):
        return (
            (queries.at[:, to_s, :, head_rows], query_all.at[s]),
            (new_keys.at[:, to_s, :, head_cols], fresh_all.at[0, s]),
            (new_values.at[:, to_s, :, head_cols], fresh_all.at[1, s]),
        )

    def send_small(step, carry):
        to_s = lax.rem(s + step, 8)
        for n, (src, dst) in enumerate(small_pieces(to_s)):
            remote(src, dst, small_send.at[n], small_recv.at[n], (to_s, h, b)).start()
        return carry

    def each_slot(do):
        def step(at_s, carry):
            for k in range(4):
                do(at_s, k, slot_order[at_s * 4 + k])
            return carry

        lax.fori_loop(0, 8, step, 0)

    def send_plane(src, dx, dy, dst, send_sem, recv_sem):
        to_x, to_y = away(dx, x, sign), away(dy, y, sign)
        to_s, to_h = in_plane(to_x, to_y)
        remote(src(to_x * 4 + to_y), dst, send_sem, recv_sem, (to_s, to_h, b)).start()

    def take_values(piece):
        low, dz = PIECES[piece]
        at_z = away(dz, 0, sign)
        wait_for(values_chip[piece], chip_recv.at[piece])
        if piece + 2 < len(PIECES):
            swap(piece + 2)

        def pack(at_s, k, slot):
            values_packed[at_s * 2 + owner_low(low), at_z, k] = values_chip[piece][slot]

        each_slot(pack)
        if dz:
            for dx, dy in PLANE[low]:
                send_plane(
                    lambda to: values_packed.at[to, at_z], dx, dy, values_mid.at[at_z, here_mid],
                    mid_send, mid_recv.at[group_of(dx, low)],
                )

    far = pl.ds(1, 3)

    def forward_values(dx, low):
        group = group_of(dx, low)
        wait_for(values_mid.at[far, pl.ds(0, 2)], mid_recv.at[group])
        first = away(dx, x, -sign) * 4 + owner_low(low) * 2
        for at in range(2):
            for dz in (1, 3, 2):
                remote(
                    values_mid.at[dz, first + at], values_land.at[dz - 1, first + at],
                    values_send, values_recv.at[group], (s, in_line(away(dz, z, 1)), b),
                ).start()

    def take_near_keys(low):
        wait_for(keys_near[low], near_recv.at[low])

        def pack(at_s, k, slot):
            keys_packed[at_s * 2 + owner_low(low), 0, k] = keys_near[low][slot]

        each_slot(pack)

    def send_near_values():
        for dx, dy in PLANE[1] + PLANE[0]:
            send_plane(
                lambda to: values_packed.at[to, 0], dx, dy, values_mid.at[0, here_mid], mid_near, mid_near_recv
            )

    def send_near_keys():
        for dx, dy in PLANE[1] + PLANE[0]:
            send_plane(lambda to: keys_packed.at[to, 0], dx, dy, keys_land.at[here, 0], keys_send, keys_recv)

    def turn_keys(low):
        wait_for(keys_line[low], line_recv.at[low])

        def pack(at_s, k, slot):
            for dz in range(1, 4):
                keys_packed[at_s * 2 + owner_low(low), dz, k] = keys_line[low][dz - 1, slot]

        each_slot(pack)
        for dx, dy in PLANE[low]:
            for dz in range(1, 4):
                send_plane(lambda to: keys_packed.at[to, dz], dx, dy, keys_land.at[here, dz], keys_send, keys_recv)

    scalars[0].wait()
    scalars[1].wait()
    lax.fori_loop(1, 8, send_small, 0)
    for n, (src, dst) in enumerate(small_pieces(s)):
        pltpu.make_async_copy(src, dst, small_recv.at[n]).start()
    for piece in range(len(PIECES)):
        take_values(piece)
    pltpu.make_async_copy(
        values_packed.at[here, far], values_mid.at[far, here_mid], mid_recv.at[group_of(0, 0)]
    ).start()
    pltpu.make_async_copy(values_packed.at[here, 0], values_mid.at[0, here_mid], mid_near_recv).start()

    for n, part in enumerate((query_all, fresh_all.at[0], fresh_all.at[1])):
        wait_for(part, small_recv.at[n])
    wait_for(key_columns, full_sem.at[0])
    wait_for(value_rows, full_sem.at[1])

    def spread_queries(at_s, carry):
        for t in range(2):
            rows = query_all[at_s, t].astype(F32)
            for g in range(GROUP):
                row = (g // 4) * 8 + t * 4 + g % 4
                for k in range(4):
                    query_rows[at_s * 4 + k, row : row + 1, :] = rows[k : k + 1, g * HD : g * HD + HD]
        return carry

    lax.fori_loop(0, 8, spread_queries, 0)

    def find_slot(at, carry):
        found = jnp.int32(0)
        for slot in range(32):
            found = jnp.where(slot_order[slot] == b * 16 + at, slot, found)
        slot_of[at] = found
        return carry

    lax.fori_loop(0, 16, find_slot, 0)

    lane = lax.broadcasted_iota(jnp.int32, (1, HD), 1)
    lane_prompt = lax.div(lane, 16)
    lane_later = lax.rem(lax.div(lane, 4), 2) == 1
    block_lane = lax.div(lax.broadcasted_iota(jnp.int32, (HD, HD), 1), 16)
    row4 = lax.broadcasted_iota(jnp.int32, (4, HD), 0)
    row512 = lax.broadcasted_iota(jnp.int32, (512, HD), 0)
    scale = HD ** -0.5

    def attend(first):
        slots = [slot_of[first + p] for p in range(8)]
        live = jnp.zeros((1, HD), jnp.int32)
        for p in range(8):
            live = jnp.where(lane_prompt == p, lengths[first + p + b * 16], live)

        def fresh_row(n, t, slot):
            rows = fresh_all[n, lax.div(slot, 4), t].astype(F32)
            return jnp.sum(jnp.where(row4 == lax.rem(slot, 4), rows, 0.0), axis=0, keepdims=True)

        questions = jnp.concatenate([query_rows[slot] for slot in slots], axis=0).T
        diagonal = jnp.concatenate(
            [jnp.where(block_lane == p, questions, 0.0) for p in range(8)], axis=0
        ).astype(BF16)
        fresh_keys = jnp.concatenate(
            [
                jnp.concatenate([fresh_row(0, 0, slot), fresh_row(0, 1, slot), jnp.zeros((14, HD), F32)], axis=0)
                for slot in slots
            ],
            axis=1,
        ).astype(BF16)
        scores = jnp.dot(
            key_columns[:, first * HD : (first + 8) * HD], diagonal, preferred_element_type=F32
        ) * scale
        fresh_scores = jnp.dot(fresh_keys, diagonal, preferred_element_type=F32) * scale
        kept = row512 < live
        scores = jnp.where(kept, scores, HIDDEN)
        n0 = fresh_scores[0:1]
        n1 = jnp.where(lane_later, fresh_scores[1:2], HIDDEN)
        peak = jnp.maximum(jnp.max(scores, axis=0, keepdims=True), jnp.maximum(n0, n1))
        mass = jnp.where(kept, jnp.exp(scores - peak), 0.0)
        m0 = jnp.exp(n0 - peak)
        m1 = jnp.where(lane_later, jnp.exp(n1 - peak), 0.0)
        total = jnp.sum(mass, axis=0, keepdims=True) + m0 + m1
        weights = mass.T.astype(BF16)
        m0, m1 = (m.astype(BF16).astype(F32) for m in (m0, m1))
        sides = jnp.concatenate([total, m0, m1, jnp.zeros((HD - 3, HD), F32)], axis=0).T
        for p, slot in enumerate(slots):
            cut = slice(p * 16, p * 16 + 16)
            weighted = jnp.dot(weights[cut], value_rows[first + p], preferred_element_type=F32)
            weighted += sides[cut, 1:2] * fresh_row(1, 0, slot)
            weighted += sides[cut, 2:3] * fresh_row(1, 1, slot)
            result[first + p] = weighted / sides[cut, 0:1]

    attend(0)
    attend(8)

    def hand_rows(at_s, carry):
        for pair in range(2):
            first, second = (
                result[jnp.clip(slot_order[at_s * 4 + pair * 2 + n] - b * 16, 0, 15)] for n in range(2)
            )
            for to_b in range(2):
                cut = slice(to_b * 8, to_b * 8 + 8)
                rows_send[at_s, to_b, pair] = jnp.concatenate((first[cut], second[cut]), axis=0).astype(BF16)
        return carry

    lax.fori_loop(0, 8, hand_rows, 0)

    def send_rows(to_s, to_b):
        remote(
            rows_send.at[to_s, to_b], rows_land.at[s, b], rows_send_sem, rows_recv_sem, (to_s, h, to_b)
        ).start()

    def send_rows_step(step, carry):
        to_s = lax.rem(s + step, 8)
        send_rows(to_s, b)
        send_rows(to_s, other)
        return carry

    lax.fori_loop(1, 8, send_rows_step, 0)
    send_rows(s, other)
    pltpu.make_async_copy(rows_send.at[s, b], rows_land.at[s, b], rows_recv_sem).start()
    owned = [slot_order[s * 4 + k] for k in range(4)]
    lives = [lengths[slot] for slot in owned]
    first_position = (h * 2 + b) * BLOCK
    position = first_position + lax.broadcasted_iota(jnp.int32, (BLOCK, HD), 0)
    for k in range(4):
        keep[k] = jnp.where(position < lives[k], 1.0, 0.0).astype(BF16)
    fresh[0].wait()
    fresh[1].wait()

    def place_fresh(layer, carry):
        wide = first_position + lax.broadcasted_iota(jnp.int32, (BLOCK, KVH * HD), 0)
        for n, out in enumerate((keys_fresh, values_cache)):
            new = [fresh_rows[n, t, layer].astype(F32) for t in range(2)]
            for k in range(4):
                rows = jnp.zeros((BLOCK, KVH * HD), F32)
                for t in range(2):
                    rows = jnp.where(wide == lives[k] + t, new[t][k : k + 1], rows)
                out[layer, k] = rows.astype(BF16)
        return carry

    lax.fori_loop(0, 8, place_fresh, 0)
    take_near_keys(1)
    take_near_keys(0)
    for dx in (1, 3, 2, 0):
        forward_values(dx, 1)
    send_near_values()
    for dx in (1, 3, 2, 0):
        forward_values(dx, 0)
    send_near_keys()
    turn_keys(1)
    turn_keys(0)
    pltpu.make_async_copy(keys_packed.at[here], keys_land.at[here], keys_recv).start()

    def settle_values(src, at, from_x, low, from_z):
        def step(half, carry):
            from_low = owner_low(low)
            block = src.at[at, from_x * 4 + from_low * 2 + half]
            layer = from_x * 2 + half
            cut = pl.ds(pl.multiple_of((from_z * 2 + from_low) * HD, HD), HD)
            for k in range(4):
                values_cache[layer, k, :, cut] = jnp.where(keep[k] > 0, block[k], values_cache[layer, k, :, cut])
            return carry

        lax.fori_loop(0, 2, step, 0)

    owners = [lax.div(slot, 16) for slot in owned]

    def assemble(l, carry):
        picked = []
        for k in range(4):
            part = slice((k % 2) * 8, (k % 2) * 8 + 8)
            first, second = (rows_land[l, n, k // 2].astype(F32)[part] for n in range(2))
            picked.append(jnp.where(owners[k] == 0, first, second))
        for t in range(2):
            attention[t, l] = jnp.concatenate(
                [
                    jnp.concatenate([rows[t * 4 + g : t * 4 + g + 1] for rows in picked], axis=0)
                    for g in range(4)
                ],
                axis=1,
            ).astype(BF16)
        return carry

    wait_for(rows_land, rows_recv_sem)
    lax.fori_loop(0, 8, assemble, 0)
    wait_for(values_mid.at[0], mid_near_recv)
    for low in (1, 0):
        for dx in (1, 3, 2, 0):
            settle_values(values_mid, 0, away(dx, x, -sign), low, z)
    for low in (1, 0):
        for dx in (1, 3, 2, 0):
            wait_for(values_land.at[:, pl.ds(0, 2)], values_recv.at[group_of(dx, low)])
            for dz in (1, 3, 2):
                settle_values(values_land, dz - 1, away(dx, x, -sign), low, away(dz, z, -1))
    wait_for(keys_land, keys_recv)

    wait_for(value_rows.at[pl.ds(0, 8)], chip_send)
    wait_for(value_rows.at[pl.ds(0, 14)], line_send)
    for n, part in enumerate((query_all, fresh_all.at[0], fresh_all.at[1])):
        wait_for(part.at[pl.ds(0, 7)], small_send.at[n])
    wait_for(values_packed.at[pl.ds(0, 15), far], mid_send)
    wait_for(values_packed.at[pl.ds(0, 15), 0], mid_near)
    wait_for(keys_packed.at[pl.ds(0, 15)], keys_send)
    wait_for(values_land, values_send)
    wait_for(rows_send.at[pl.ds(0, 7)], rows_send_sem)
    wait_for(rows_send.at[0, 0], rows_send_sem)


def hand_out(
    attention, values, keys_land, keys_fresh, keep, attention_out, values_out, keys_out, keys, sem
):
    copies = [pltpu.make_async_copy(values.at[l], values_out.at[l], sem.at[l]) for l in range(8)]
    copies.append(pltpu.make_async_copy(attention, attention_out, sem.at[16]))
    for copy in copies:
        copy.start()
    kept = [keep[k] > 0 for k in range(4)]
    z = lax.div(lax.axis_index("head"), 2)
    for l in range(8):
        for h in range(KVH):
            cut = slice(h * HD, h * HD + HD)
            for k in range(4):
                landed = keys_land[l // 2 * 4 + l % 2 * 2 + h % 2, lax.rem(h // 2 - z + 4, 4), k]
                keys[l, k, :, cut] = jnp.where(kept[k], landed, keys_fresh[l, k, :, cut])
        copies.append(pltpu.make_async_copy(keys.at[l], keys_out.at[l], sem.at[8 + l]))
        copies[-1].start()
    for copy in copies:
        copy.wait()


def body(keys_prefill, values_prefill, lengths, slot_order, queries, new_keys, new_values):
    keys = keys_prefill.reshape(16, 4, 2, 2, BLOCK, HD)
    values = values_prefill.reshape(16, 4, 2, 2, BLOCK, HD)
    flat = (keys_prefill.reshape(16, 512, HD), values_prefill.reshape(16, 512, HD))
    any_spec = pl.BlockSpec(memory_space=pl.ANY)
    hbm_spec = pl.BlockSpec(memory_space=pltpu.HBM)
    vmem_spec = pl.BlockSpec(memory_space=pltpu.VMEM)
    dma, vmem = pltpu.SemaphoreType.DMA, pltpu.VMEM
    rows_shape, cache_shape = (2, 8, 4, 4 * HD), (8, 4, BLOCK, KVH * HD)
    plane_shape = (16, 4, 4, BLOCK, HD)

    def in_hbm(array):
        return pltpu.with_memory_space_constraint(array, pltpu.HBM)

    held = pl.pallas_call(
        relay,
        out_shape=tuple(
            vmem(shape, BF16) for shape in (rows_shape, cache_shape, plane_shape, cache_shape, (4, BLOCK, HD))
        ),
        in_specs=[hbm_spec] * 9,
        out_specs=(vmem_spec,) * 5,
        scratch_shapes=[
            vmem((512, 16 * HD), BF16), vmem((16, 512, HD), BF16),
            [vmem((3, 32, BLOCK, HD), BF16)] * 2, [vmem((32, BLOCK, HD), BF16)] * 2,
            [vmem((32, BLOCK, HD), BF16)] * len(PIECES),
            vmem(plane_shape, BF16), vmem(plane_shape, BF16),
            vmem((4, 16, 4, BLOCK, HD), BF16), vmem((3, 16, 4, BLOCK, HD), BF16),
            vmem((2, 2, 8, 4, KVH * HD), BF16), vmem((8, 2, 4, GROUP * HD), BF16), vmem((32, 16, HD), F32),
            vmem((2, 8, 2, 4, HD), BF16), vmem((16, 16, HD), F32),
            vmem((8, 2, 2, 16, HD), BF16), vmem((8, 2, 2, 16, HD), BF16),
            pltpu.SMEM((32,), jnp.int32), pltpu.SMEM((32,), jnp.int32), pltpu.SMEM((16,), jnp.int32),
            dma((2,)), dma((2,)), dma((2,)), dma, dma((2,)), dma((2,)), dma, dma((len(PIECES),)),
            dma, dma, dma, dma((8,)), dma, dma, dma, dma((8,)),
            dma((3,)), dma((3,)), dma, dma,
        ],
        compiler_params=pltpu.CompilerParams(
            collective_id=0, has_side_effects=True, vmem_limit_bytes=48 * 2**20
        ),
        name="relay",
    )(*(in_hbm(x) for x in (slot_order, lengths, keys, values, *flat, queries, new_keys, new_values)))
    attention, values_cache, keys_cache = pl.pallas_call(
        hand_out,
        out_shape=tuple(jax.ShapeDtypeStruct(shape, BF16) for shape in (rows_shape, cache_shape, cache_shape)),
        in_specs=[vmem_spec] * 5,
        out_specs=(any_spec,) * 3,
        scratch_shapes=[vmem(cache_shape, BF16), dma((17,))],
        compiler_params=pltpu.CompilerParams(vmem_limit_bytes=8 * 2**20),
        name="hand_out",
    )(*(pltpu.with_memory_space_constraint(x, pltpu.VMEM) for x in held))
    return attention, keys_cache, values_cache


def solution(mesh):
    in_specs = (
        P("section", "batch", None, "head"),
        P("section", "batch", None, "head"),
        P(),
        P(),
        P(None, None, "section", None),
        P(None, None, "section", None),
        P(None, None, "section", None),
    )
    out_specs = (
        P(None, None, "section", ("head", "batch")),
        P(None, "section", ("head", "batch"), None),
        P(None, "section", ("head", "batch"), None),
    )
    return jax.shard_map(body, mesh=mesh, in_specs=in_specs, out_specs=out_specs, check_vma=False)
```

```python
import jax
import jax.numpy as jnp
from jax import lax
from jax.experimental import pallas as pl
from jax.experimental.pallas import tpu as pltpu
from jax.sharding import PartitionSpec as P

KVH = 8
HD = 128
GROUP = 8
BLOCK = 32
MESH = pl.DeviceIdType.MESH
HIDDEN = -1e30
BF16, F32 = jnp.bfloat16, jnp.float32


PLANE = {
    1: ((1, 1), (3, 3), (1, 3), (3, 1), (2, 1), (0, 3), (2, 3), (0, 1)),
    0: ((1, 0), (0, 2), (3, 2), (1, 2), (3, 0), (2, 2), (2, 0)),
}
PIECES = ((1, 1), (1, 3), (1, 2), (0, 1), (0, 3), (0, 2), (1, 0), (0, 0))


def group_of(dx, low):
    return low * 4 + dx


def relay(
    slot_order_hbm, lengths_hbm, keys, values, keys_flat, values_flat, queries, new_keys, new_values,
    attention, keys_land, values_land, keys_fresh, values_fresh, keep,
    key_columns, value_rows, keys_line, keys_near, values_chip, keys_packed, values_packed, values_mid,
    fresh_rows, query_all, query_rows, fresh_all, result, rows_send, rows_land,
    slot_order, lengths, slot_of,
    scalar_sem, full_sem, fresh_sem, line_send, line_recv, near_recv, chip_send, chip_recv,
    keys_send, keys_recv, mid_send, mid_recv, mid_near, mid_near_recv, values_send, values_recv,
    small_send, small_recv, rows_send_sem, rows_recv_sem,
):
    s, h, b = lax.axis_index("section"), lax.axis_index("head"), lax.axis_index("batch")
    x, z = lax.div(s, 2), lax.div(h, 2)
    y_low = lax.rem(h, 2)
    y = lax.rem(s, 2) * 2 + y_low
    other = 1 - b
    sign = 1 - 2 * b
    mine = pl.ds(b * 16, 16)
    here = x * 4 + y
    here_mid = x * 4 + y_low * 2 + lax.div(y, 2)

    def remote(src, dst, send_sem, recv_sem, to):
        return pltpu.make_async_remote_copy(
            src_ref=src, dst_ref=dst, send_sem=send_sem, recv_sem=recv_sem,
            device_id=to, device_id_type=MESH,
        )

    def wait_for(ref, sem):
        pltpu.make_async_copy(ref, ref, sem).wait()

    def away(d, at, way):
        return lax.rem(at + way * d + 4, 4)

    def in_plane(at_x, at_y):
        return at_x * 2 + lax.div(at_y, 2), z * 2 + lax.rem(at_y, 2)

    def in_line(at_z):
        return at_z * 2 + y_low

    def owner_low(low):
        return lax.rem(y_low + low, 2)

    barrier = pltpu.get_barrier_semaphore()

    def greet(to):
        pl.semaphore_signal(barrier, inc=1, device_id=to, device_id_type=MESH)

    for dz in range(4):
        at_h = in_line(away(dz, z, 1))
        greet((s, at_h, other))
        if dz:
            greet((s, at_h, b))
    for low in (1, 0):
        for dx, dy in PLANE[low]:
            at_s, at_h = in_plane(away(dx, x, 1), away(dy, y, 1))
            greet((at_s, at_h, b))
            if low == 0:
                greet((at_s, at_h, other))

    scalars = [
        pltpu.make_async_copy(slot_order_hbm, slot_order, scalar_sem.at[0]),
        pltpu.make_async_copy(lengths_hbm, lengths, scalar_sem.at[1]),
    ]
    whole = [
        pltpu.make_async_copy(keys_flat.at[at], key_columns.at[:, pl.ds(at * HD, HD)], full_sem.at[0])
        for at in range(16)
    ]
    whole.append(pltpu.make_async_copy(values_flat, value_rows, full_sem.at[1]))
    fresh = [
        pltpu.make_async_copy(src, fresh_rows.at[n], fresh_sem.at[n])
        for n, src in enumerate((new_keys, new_values))
    ]
    for copy in scalars:
        copy.start()
    for piece, (low, dz) in enumerate(PIECES):
        pltpu.make_async_copy(
            values.at[:, away(dz, z, sign), owner_low(low), b], values_chip[piece].at[mine], chip_recv.at[piece]
        ).start()
    for low in (1, 0):
        pltpu.make_async_copy(
            keys.at[:, z, owner_low(low), b], keys_near[low].at[mine], near_recv.at[low]
        ).start()
    for copy in whole + fresh:
        copy.start()
    pl.semaphore_wait(barrier, 29)

    def swap(piece):
        low, dz = PIECES[piece]
        remote(
            values.at[:, away(dz, z, -sign), owner_low(low), other], values_chip[piece].at[mine],
            chip_send, chip_recv.at[piece], (s, h, other),
        ).start()

    swap(0)
    swap(1)

    def send_line(low, dz, to_b):
        to_z = away(dz, z, sign)
        d = away(dz, 0, sign)
        remote(
            keys.at[:, to_z, owner_low(low), to_b], keys_line[low].at[3 - d, mine],
            line_send, line_recv.at[low], (s, in_line(to_z), to_b),
        ).start()

    for low in (1, 0):
        for dz, to_b in ((1, b), (3, other), (2, b), (1, other), (3, b), (2, other)):
            send_line(low, dz, to_b)
    for low in (1, 0):
        remote(
            keys.at[:, z, owner_low(low), other], keys_near[low].at[mine],
            line_send, near_recv.at[low], (s, h, other),
        ).start()

    head_rows = pl.ds(pl.multiple_of(h * GROUP * HD, GROUP * HD), GROUP * HD)
    head_cols = pl.ds(pl.multiple_of(h * HD, HD), HD)

    def small_pieces(to_s):
        return (
            (queries.at[:, to_s, :, head_rows], query_all.at[s]),
            (new_keys.at[:, to_s, :, head_cols], fresh_all.at[0, s]),
            (new_values.at[:, to_s, :, head_cols], fresh_all.at[1, s]),
        )

    def send_small(step, carry):
        to_s = lax.rem(s + step, 8)
        for n, (src, dst) in enumerate(small_pieces(to_s)):
            remote(src, dst, small_send.at[n], small_recv.at[n], (to_s, h, b)).start()
        return carry

    def each_slot(do):
        def step(at_s, carry):
            for k in range(4):
                do(at_s, k, slot_order[at_s * 4 + k])
            return carry

        lax.fori_loop(0, 8, step, 0)

    def send_plane(src, dx, dy, dst, send_sem, recv_sem):
        to_x, to_y = away(dx, x, sign), away(dy, y, sign)
        to_s, to_h = in_plane(to_x, to_y)
        remote(src(to_x * 4 + to_y), dst, send_sem, recv_sem, (to_s, to_h, b)).start()

    def take_values(piece):
        low, dz = PIECES[piece]
        at_z = away(dz, 0, sign)
        wait_for(values_chip[piece], chip_recv.at[piece])
        if piece + 2 < len(PIECES):
            swap(piece + 2)

        def pack(at_s, k, slot):
            values_packed[at_s * 2 + owner_low(low), at_z, k] = values_chip[piece][slot]

        each_slot(pack)
        if dz:
            for dx, dy in PLANE[low]:
                send_plane(
                    lambda to: values_packed.at[to, at_z], dx, dy, values_mid.at[at_z - 1, here_mid],
                    mid_send, mid_recv.at[group_of(dx, low)],
                )

    far = pl.ds(1, 3)

    def forward_values(dx, low):
        group = group_of(dx, low)
        wait_for(values_mid.at[:, pl.ds(0, 2)], mid_recv.at[group])
        pair = pl.ds(away(dx, x, -sign) * 4 + owner_low(low) * 2, 2)
        for dz in (1, 3, 2):
            remote(
                values_mid.at[dz - 1, pair], values_land.at[dz, pair],
                values_send, values_recv, (s, in_line(away(dz, z, 1)), b),
            ).start()

    def take_near_keys(low):
        wait_for(keys_near[low], near_recv.at[low])

        def pack(at_s, k, slot):
            keys_packed[at_s * 2 + owner_low(low), 0, k] = keys_near[low][slot]

        each_slot(pack)

    def send_near_values():
        for dx, dy in PLANE[1] + PLANE[0]:
            send_plane(
                lambda to: values_packed.at[to, 0], dx, dy, values_land.at[0, here_mid], mid_near, mid_near_recv
            )

    def send_near_keys():
        for dx, dy in PLANE[1] + PLANE[0]:
            send_plane(lambda to: keys_packed.at[to, 0], dx, dy, keys_land.at[here, 0], keys_send, keys_recv)

    def turn_keys(low):
        wait_for(keys_line[low], line_recv.at[low])

        def pack(at_s, k, slot):
            for dz in range(1, 4):
                keys_packed[at_s * 2 + owner_low(low), dz, k] = keys_line[low][dz - 1, slot]

        each_slot(pack)
        for dx, dy in PLANE[low]:
            send_plane(lambda to: keys_packed.at[to, far], dx, dy, keys_land.at[here, far], keys_send, keys_recv)

    scalars[0].wait()
    scalars[1].wait()
    lax.fori_loop(1, 8, send_small, 0)
    for n, (src, dst) in enumerate(small_pieces(s)):
        pltpu.make_async_copy(src, dst, small_recv.at[n]).start()
    for piece in range(len(PIECES)):
        take_values(piece)
    pltpu.make_async_copy(
        values_packed.at[here, far], values_mid.at[:, here_mid], mid_recv.at[group_of(0, 0)]
    ).start()
    pltpu.make_async_copy(values_packed.at[here, 0], values_land.at[0, here_mid], mid_near_recv).start()

    for n, part in enumerate((query_all, fresh_all.at[0], fresh_all.at[1])):
        wait_for(part, small_recv.at[n])
    wait_for(key_columns, full_sem.at[0])
    wait_for(value_rows, full_sem.at[1])

    def spread_queries(at_s, carry):
        for t in range(2):
            rows = query_all[at_s, t].astype(F32)
            for g in range(GROUP):
                row = (g // 4) * 8 + t * 4 + g % 4
                for k in range(4):
                    query_rows[at_s * 4 + k, row : row + 1, :] = rows[k : k + 1, g * HD : g * HD + HD]
        return carry

    lax.fori_loop(0, 8, spread_queries, 0)

    def find_slot(at, carry):
        found = jnp.int32(0)
        for slot in range(32):
            found = jnp.where(slot_order[slot] == b * 16 + at, slot, found)
        slot_of[at] = found
        return carry

    lax.fori_loop(0, 16, find_slot, 0)

    lane = lax.broadcasted_iota(jnp.int32, (1, HD), 1)
    lane_prompt = lax.div(lane, 16)
    lane_later = lax.rem(lax.div(lane, 4), 2) == 1
    block_lane = lax.div(lax.broadcasted_iota(jnp.int32, (HD, HD), 1), 16)
    row4 = lax.broadcasted_iota(jnp.int32, (4, HD), 0)
    row512 = lax.broadcasted_iota(jnp.int32, (512, HD), 0)
    scale = HD ** -0.5

    def attend(first):
        slots = [slot_of[first + p] for p in range(8)]
        live = jnp.zeros((1, HD), jnp.int32)
        for p in range(8):
            live = jnp.where(lane_prompt == p, lengths[first + p + b * 16], live)

        def fresh_row(n, t, slot):
            rows = fresh_all[n, lax.div(slot, 4), t].astype(F32)
            return jnp.sum(jnp.where(row4 == lax.rem(slot, 4), rows, 0.0), axis=0, keepdims=True)

        questions = jnp.concatenate([query_rows[slot] for slot in slots], axis=0).T
        diagonal = jnp.concatenate(
            [jnp.where(block_lane == p, questions, 0.0) for p in range(8)], axis=0
        ).astype(BF16)
        fresh_keys = jnp.concatenate(
            [
                jnp.concatenate([fresh_row(0, 0, slot), fresh_row(0, 1, slot), jnp.zeros((14, HD), F32)], axis=0)
                for slot in slots
            ],
            axis=1,
        ).astype(BF16)
        scores = jnp.dot(
            key_columns[:, first * HD : (first + 8) * HD], diagonal, preferred_element_type=F32
        ) * scale
        fresh_scores = jnp.dot(fresh_keys, diagonal, preferred_element_type=F32) * scale
        kept = row512 < live
        scores = jnp.where(kept, scores, HIDDEN)
        n0 = fresh_scores[0:1]
        n1 = jnp.where(lane_later, fresh_scores[1:2], HIDDEN)
        peak = jnp.maximum(jnp.max(scores, axis=0, keepdims=True), jnp.maximum(n0, n1))
        mass = jnp.where(kept, jnp.exp(scores - peak), 0.0)
        m0 = jnp.exp(n0 - peak)
        m1 = jnp.where(lane_later, jnp.exp(n1 - peak), 0.0)
        total = jnp.sum(mass, axis=0, keepdims=True) + m0 + m1
        weights = mass.T.astype(BF16)
        m0, m1 = (m.astype(BF16).astype(F32) for m in (m0, m1))
        sides = jnp.concatenate([total, m0, m1, jnp.zeros((HD - 3, HD), F32)], axis=0).T
        for p, slot in enumerate(slots):
            cut = slice(p * 16, p * 16 + 16)
            weighted = jnp.dot(weights[cut], value_rows[first + p], preferred_element_type=F32)
            weighted += sides[cut, 1:2] * fresh_row(1, 0, slot)
            weighted += sides[cut, 2:3] * fresh_row(1, 1, slot)
            result[first + p] = weighted / sides[cut, 0:1]

    attend(0)
    attend(8)

    def hand_rows(at_s, carry):
        for pair in range(2):
            first, second = (
                result[jnp.clip(slot_order[at_s * 4 + pair * 2 + n] - b * 16, 0, 15)] for n in range(2)
            )
            for to_b in range(2):
                cut = slice(to_b * 8, to_b * 8 + 8)
                rows_send[at_s, to_b, pair] = jnp.concatenate((first[cut], second[cut]), axis=0).astype(BF16)
        return carry

    lax.fori_loop(0, 8, hand_rows, 0)

    def send_rows(to_s, to_b):
        remote(
            rows_send.at[to_s, to_b], rows_land.at[s, b], rows_send_sem, rows_recv_sem, (to_s, h, to_b)
        ).start()

    def send_rows_step(step, carry):
        to_s = lax.rem(s + step, 8)
        send_rows(to_s, b)
        send_rows(to_s, other)
        return carry

    lax.fori_loop(1, 8, send_rows_step, 0)
    send_rows(s, other)
    pltpu.make_async_copy(rows_send.at[s, b], rows_land.at[s, b], rows_recv_sem).start()
    owned = [slot_order[s * 4 + k] for k in range(4)]
    lives = [lengths[slot] for slot in owned]
    first_position = (h * 2 + b) * BLOCK
    position = first_position + lax.broadcasted_iota(jnp.int32, (BLOCK, HD), 0)
    for k in range(4):
        keep[k] = jnp.where(position < lives[k], 1.0, 0.0).astype(BF16)
    fresh[0].wait()
    fresh[1].wait()

    def place_fresh(layer, carry):
        wide = first_position + lax.broadcasted_iota(jnp.int32, (BLOCK, KVH * HD), 0)
        for n, out in enumerate((keys_fresh, values_fresh)):
            new = [fresh_rows[n, t, layer].astype(F32) for t in range(2)]
            for k in range(4):
                rows = jnp.zeros((BLOCK, KVH * HD), F32)
                for t in range(2):
                    rows = jnp.where(wide == lives[k] + t, new[t][k : k + 1], rows)
                out[layer, k] = rows.astype(BF16)
        return carry

    lax.fori_loop(0, 8, place_fresh, 0)
    take_near_keys(1)
    take_near_keys(0)
    for dx in (1, 3, 2, 0):
        forward_values(dx, 1)
    send_near_values()
    for dx in (1, 3, 2, 0):
        forward_values(dx, 0)
    send_near_keys()
    turn_keys(1)
    turn_keys(0)
    pltpu.make_async_copy(keys_packed.at[here], keys_land.at[here], keys_recv).start()

    owners = [lax.div(slot, 16) for slot in owned]

    def assemble(l, carry):
        picked = []
        for k in range(4):
            part = slice((k % 2) * 8, (k % 2) * 8 + 8)
            first, second = (rows_land[l, n, k // 2].astype(F32)[part] for n in range(2))
            picked.append(jnp.where(owners[k] == 0, first, second))
        for t in range(2):
            attention[t, l] = jnp.concatenate(
                [
                    jnp.concatenate([rows[t * 4 + g : t * 4 + g + 1] for rows in picked], axis=0)
                    for g in range(4)
                ],
                axis=1,
            ).astype(BF16)
        return carry

    wait_for(rows_land, rows_recv_sem)
    lax.fori_loop(0, 8, assemble, 0)
    wait_for(values_land.at[0], mid_near_recv)
    wait_for(values_land.at[far], values_recv)
    wait_for(keys_land, keys_recv)

    wait_for(value_rows.at[pl.ds(0, 8)], chip_send)
    wait_for(value_rows.at[pl.ds(0, 14)], line_send)
    for n, part in enumerate((query_all, fresh_all.at[0], fresh_all.at[1])):
        wait_for(part.at[pl.ds(0, 7)], small_send.at[n])
    wait_for(values_packed.at[pl.ds(0, 15), far], mid_send)
    wait_for(values_packed.at[pl.ds(0, 15), 0], mid_near)
    wait_for(keys_packed.at[pl.ds(0, 15)], keys_send)
    wait_for(values_mid, values_send)
    wait_for(rows_send.at[pl.ds(0, 7)], rows_send_sem)
    wait_for(rows_send.at[0, 0], rows_send_sem)


def hand_out(
    attention, keys_land, values_land, keys_fresh, values_fresh, keep,
    attention_out, keys_out, values_out, keys, values, sem,
):
    copies = [pltpu.make_async_copy(attention, attention_out, sem.at[16])]
    copies[0].start()
    kept = [keep[k] > 0 for k in range(4)]
    z = lax.div(lax.axis_index("head"), 2)
    for l in range(8):
        x, y_high = l // 2, l % 2
        for h in range(KVH):
            cut = slice(h * HD, h * HD + HD)
            from_z, y_low = h // 2, h % 2
            for k in range(4):
                landed = keys_land[x * 4 + y_high * 2 + y_low, lax.rem(from_z - z + 4, 4), k]
                keys[l, k, :, cut] = jnp.where(kept[k], landed, keys_fresh[l, k, :, cut])
                landed = values_land[lax.rem(z - from_z + 4, 4), x * 4 + y_low * 2 + y_high, k]
                values[l, k, :, cut] = jnp.where(kept[k], landed, values_fresh[l, k, :, cut])
        for n, (src, dst) in enumerate(((keys, keys_out), (values, values_out))):
            copies.append(pltpu.make_async_copy(src.at[l], dst.at[l], sem.at[n * 8 + l]))
            copies[-1].start()
    for copy in copies:
        copy.wait()


def body(keys_prefill, values_prefill, lengths, slot_order, queries, new_keys, new_values):
    keys = keys_prefill.reshape(16, 4, 2, 2, BLOCK, HD)
    values = values_prefill.reshape(16, 4, 2, 2, BLOCK, HD)
    flat = (keys_prefill.reshape(16, 512, HD), values_prefill.reshape(16, 512, HD))
    any_spec = pl.BlockSpec(memory_space=pl.ANY)
    hbm_spec = pl.BlockSpec(memory_space=pltpu.HBM)
    vmem_spec = pl.BlockSpec(memory_space=pltpu.VMEM)
    dma, vmem = pltpu.SemaphoreType.DMA, pltpu.VMEM
    rows_shape, cache_shape = (2, 8, 4, 4 * HD), (8, 4, BLOCK, KVH * HD)
    plane_shape, line_shape = (16, 4, 4, BLOCK, HD), (4, 16, 4, BLOCK, HD)

    def in_hbm(array):
        return pltpu.with_memory_space_constraint(array, pltpu.HBM)

    held = pl.pallas_call(
        relay,
        out_shape=tuple(
            vmem(shape, BF16) for shape in (rows_shape, plane_shape, line_shape, cache_shape, cache_shape, (4, BLOCK, HD))
        ),
        in_specs=[hbm_spec] * 9,
        out_specs=(vmem_spec,) * 6,
        scratch_shapes=[
            vmem((512, 16 * HD), BF16), vmem((16, 512, HD), BF16),
            [vmem((3, 32, BLOCK, HD), BF16)] * 2, [vmem((32, BLOCK, HD), BF16)] * 2,
            [vmem((32, BLOCK, HD), BF16)] * len(PIECES),
            vmem(plane_shape, BF16), vmem(plane_shape, BF16),
            vmem((3, 16, 4, BLOCK, HD), BF16),
            vmem((2, 2, 8, 4, KVH * HD), BF16), vmem((8, 2, 4, GROUP * HD), BF16), vmem((32, 16, HD), F32),
            vmem((2, 8, 2, 4, HD), BF16), vmem((16, 16, HD), F32),
            vmem((8, 2, 2, 16, HD), BF16), vmem((8, 2, 2, 16, HD), BF16),
            pltpu.SMEM((32,), jnp.int32), pltpu.SMEM((32,), jnp.int32), pltpu.SMEM((16,), jnp.int32),
            dma((2,)), dma((2,)), dma((2,)), dma, dma((2,)), dma((2,)), dma, dma((len(PIECES),)),
            dma, dma, dma, dma((8,)), dma, dma, dma, dma,
            dma((3,)), dma((3,)), dma, dma,
        ],
        compiler_params=pltpu.CompilerParams(
            collective_id=0, has_side_effects=True, vmem_limit_bytes=48 * 2**20
        ),
        name="relay",
    )(*(in_hbm(x) for x in (slot_order, lengths, keys, values, *flat, queries, new_keys, new_values)))
    return pl.pallas_call(
        hand_out,
        out_shape=tuple(jax.ShapeDtypeStruct(shape, BF16) for shape in (rows_shape, cache_shape, cache_shape)),
        in_specs=[vmem_spec] * 6,
        out_specs=(any_spec,) * 3,
        scratch_shapes=[vmem(cache_shape, BF16), vmem(cache_shape, BF16), dma((17,))],
        compiler_params=pltpu.CompilerParams(vmem_limit_bytes=8 * 2**20),
        name="hand_out",
    )(*(pltpu.with_memory_space_constraint(x, pltpu.VMEM) for x in held))


def solution(mesh):
    in_specs = (
        P("section", "batch", None, "head"),
        P("section", "batch", None, "head"),
        P(),
        P(),
        P(None, None, "section", None),
        P(None, None, "section", None),
        P(None, None, "section", None),
    )
    out_specs = (
        P(None, None, "section", ("head", "batch")),
        P(None, "section", ("head", "batch"), None),
        P(None, "section", ("head", "batch"), None),
    )
    return jax.shard_map(body, mesh=mesh, in_specs=in_specs, out_specs=out_specs, check_vma=False)
```

```python
import jax
import jax.numpy as jnp
from jax import lax
from jax.experimental import pallas as pl
from jax.experimental.pallas import tpu as pltpu
from jax.sharding import PartitionSpec as P

KVH = 8
HD = 128
GROUP = 8
BLOCK = 32
MESH = pl.DeviceIdType.MESH
HIDDEN = -1e30
BF16, F32 = jnp.bfloat16, jnp.float32


PLANE = {
    1: ((1, 1), (3, 3), (1, 3), (3, 1), (2, 1), (0, 3), (2, 3), (0, 1)),
    0: ((1, 0), (0, 2), (3, 2), (1, 2), (3, 0), (2, 2), (2, 0)),
}
PIECES = ((1, 1), (1, 3), (1, 2), (0, 1), (0, 3), (0, 2), (1, 0), (0, 0))


def group_of(dx, low):
    return low * 4 + dx


def relay(
    slot_order_hbm, lengths_hbm, keys, values, keys_flat, values_flat, queries, new_keys, new_values,
    attention, keys_land, values_land, keys_fresh, values_fresh, keep,
    key_columns, value_rows, keys_line, keys_near, values_chip, keys_packed, values_packed, values_mid,
    fresh_rows, query_all, query_rows, fresh_all, result, rows_mine, rows_swap, rows_send, rows_land,
    slot_order, lengths, slot_of,
    scalar_sem, full_sem, fresh_sem, line_send, line_recv, near_recv, chip_send, chip_recv,
    keys_send, keys_recv, mid_send, mid_recv, mid_near, mid_near_recv, values_send, values_recv,
    small_send, small_recv, share_send, share_recv, rows_swap_send, rows_swap_recv, rows_send_sem, rows_recv_sem,
):
    s, h, b = lax.axis_index("section"), lax.axis_index("head"), lax.axis_index("batch")
    x, z = lax.div(s, 2), lax.div(h, 2)
    y_low = lax.rem(h, 2)
    y = lax.rem(s, 2) * 2 + y_low
    other = 1 - b
    sign = 1 - 2 * b
    mine = pl.ds(b * 16, 16)
    here = x * 4 + y
    here_mid = x * 4 + y_low * 2 + lax.div(y, 2)

    def remote(src, dst, send_sem, recv_sem, to):
        return pltpu.make_async_remote_copy(
            src_ref=src, dst_ref=dst, send_sem=send_sem, recv_sem=recv_sem,
            device_id=to, device_id_type=MESH,
        )

    def wait_for(ref, sem):
        pltpu.make_async_copy(ref, ref, sem).wait()

    def away(d, at, way):
        return lax.rem(at + way * d + 4, 4)

    def in_plane(at_x, at_y):
        return at_x * 2 + lax.div(at_y, 2), z * 2 + lax.rem(at_y, 2)

    def in_line(at_z):
        return at_z * 2 + y_low

    def owner_low(low):
        return lax.rem(y_low + low, 2)

    barrier = pltpu.get_barrier_semaphore()

    def greet(to):
        pl.semaphore_signal(barrier, inc=1, device_id=to, device_id_type=MESH)

    for dz in range(4):
        at_h = in_line(away(dz, z, 1))
        greet((s, at_h, other))
        if dz:
            greet((s, at_h, b))
    for low in (1, 0):
        for dx, dy in PLANE[low]:
            at_s, at_h = in_plane(away(dx, x, 1), away(dy, y, 1))
            greet((at_s, at_h, b))

    scalars = [
        pltpu.make_async_copy(slot_order_hbm, slot_order, scalar_sem.at[0]),
        pltpu.make_async_copy(lengths_hbm, lengths, scalar_sem.at[1]),
    ]
    whole = [
        pltpu.make_async_copy(keys_flat.at[at], key_columns.at[:, pl.ds(at * HD, HD)], full_sem.at[0])
        for at in range(16)
    ]
    whole.append(pltpu.make_async_copy(values_flat, value_rows, full_sem.at[1]))
    fresh = [
        pltpu.make_async_copy(src, fresh_rows.at[n], fresh_sem.at[n])
        for n, src in enumerate((new_keys, new_values))
    ]
    for copy in scalars:
        copy.start()
    for piece, (low, dz) in enumerate(PIECES):
        pltpu.make_async_copy(
            values.at[:, away(dz, z, sign), owner_low(low), b], values_chip[piece].at[mine], chip_recv.at[piece]
        ).start()
    for low in (1, 0):
        pltpu.make_async_copy(
            keys.at[:, z, owner_low(low), b], keys_near[low].at[mine], near_recv.at[low]
        ).start()
    for copy in whole + fresh:
        copy.start()
    pl.semaphore_wait(barrier, 22)

    def swap(piece):
        low, dz = PIECES[piece]
        remote(
            values.at[:, away(dz, z, -sign), owner_low(low), other], values_chip[piece].at[mine],
            chip_send, chip_recv.at[piece], (s, h, other),
        ).start()

    swap(0)
    swap(1)

    def send_line(low, dz, to_b):
        to_z = away(dz, z, sign)
        d = away(dz, 0, sign)
        remote(
            keys.at[:, to_z, owner_low(low), to_b], keys_line[low].at[3 - d, mine],
            line_send, line_recv.at[low], (s, in_line(to_z), to_b),
        ).start()

    for low in (1, 0):
        for dz, to_b in ((1, b), (3, other), (2, b), (1, other), (3, b), (2, other)):
            send_line(low, dz, to_b)
    for low in (1, 0):
        remote(
            keys.at[:, z, owner_low(low), other], keys_near[low].at[mine],
            line_send, near_recv.at[low], (s, h, other),
        ).start()

    head_rows = pl.ds(pl.multiple_of(h * GROUP * HD, GROUP * HD), GROUP * HD)
    head_cols = pl.ds(pl.multiple_of(h * HD, HD), HD)

    def small_pieces(to_s):
        return (
            (queries.at[b, to_s, :, head_rows], query_all.at[b, s]),
            (new_keys.at[b, to_s, :, head_cols], fresh_all.at[0, b, s]),
            (new_values.at[b, to_s, :, head_cols], fresh_all.at[1, b, s]),
        )

    small_parts = (query_all, fresh_all.at[0], fresh_all.at[1])

    def send_small(step, carry):
        to_s = lax.rem(s + step, 8)
        for n, (src, dst) in enumerate(small_pieces(to_s)):
            remote(src, dst, small_send.at[n], small_recv.at[n], (to_s, h, b)).start()
        return carry

    def each_slot(do):
        def step(at_s, carry):
            for k in range(4):
                do(at_s, k, slot_order[at_s * 4 + k])
            return carry

        lax.fori_loop(0, 8, step, 0)

    def send_plane(src, dx, dy, dst, send_sem, recv_sem):
        to_x, to_y = away(dx, x, sign), away(dy, y, sign)
        to_s, to_h = in_plane(to_x, to_y)
        remote(src(to_x * 4 + to_y), dst, send_sem, recv_sem, (to_s, to_h, b)).start()

    def take_values(piece):
        low, dz = PIECES[piece]
        at_z = away(dz, 0, sign)
        wait_for(values_chip[piece], chip_recv.at[piece])
        if piece + 2 < len(PIECES):
            swap(piece + 2)

        def pack(at_s, k, slot):
            values_packed[at_s * 2 + owner_low(low), at_z, k] = values_chip[piece][slot]

        each_slot(pack)
        if dz:
            for dx, dy in PLANE[low]:
                send_plane(
                    lambda to: values_packed.at[to, at_z], dx, dy, values_mid.at[at_z - 1, here_mid],
                    mid_send, mid_recv.at[group_of(dx, low)],
                )

    far = pl.ds(1, 3)

    def forward_values(dx, low):
        group = group_of(dx, low)
        wait_for(values_mid.at[:, pl.ds(0, 2)], mid_recv.at[group])
        pair = pl.ds(away(dx, x, -sign) * 4 + owner_low(low) * 2, 2)
        for dz in (1, 3, 2):
            remote(
                values_mid.at[dz - 1, pair], values_land.at[dz, pair],
                values_send, values_recv, (s, in_line(away(dz, z, 1)), b),
            ).start()

    def take_near_keys(low):
        wait_for(keys_near[low], near_recv.at[low])

        def pack(at_s, k, slot):
            keys_packed[at_s * 2 + owner_low(low), 0, k] = keys_near[low][slot]

        each_slot(pack)

    def send_near_values():
        for dx, dy in PLANE[1] + PLANE[0]:
            send_plane(
                lambda to: values_packed.at[to, 0], dx, dy, values_land.at[0, here_mid], mid_near, mid_near_recv
            )

    def send_near_keys():
        for dx, dy in PLANE[1] + PLANE[0]:
            send_plane(lambda to: keys_packed.at[to, 0], dx, dy, keys_land.at[here, 0], keys_send, keys_recv)

    def turn_keys(low):
        wait_for(keys_line[low], line_recv.at[low])

        def pack(at_s, k, slot):
            for dz in range(1, 4):
                keys_packed[at_s * 2 + owner_low(low), dz, k] = keys_line[low][dz - 1, slot]

        each_slot(pack)
        for dx, dy in PLANE[low]:
            send_plane(lambda to: keys_packed.at[to, far], dx, dy, keys_land.at[here, far], keys_send, keys_recv)

    scalars[0].wait()
    scalars[1].wait()
    lax.fori_loop(1, 8, send_small, 0)
    for n, (src, dst) in enumerate(small_pieces(s)):
        pltpu.make_async_copy(src, dst, small_recv.at[n]).start()
    for piece in range(len(PIECES)):
        take_values(piece)
    pltpu.make_async_copy(
        values_packed.at[here, far], values_mid.at[:, here_mid], mid_recv.at[group_of(0, 0)]
    ).start()
    pltpu.make_async_copy(values_packed.at[here, 0], values_land.at[0, here_mid], mid_near_recv).start()

    for n, part in enumerate(small_parts):
        wait_for(part.at[b], small_recv.at[n])
        remote(part.at[b], part.at[b], share_send.at[n], share_recv.at[n], (s, h, other)).start()
    for n, part in enumerate(small_parts):
        wait_for(part.at[other], share_recv.at[n])
    wait_for(key_columns, full_sem.at[0])
    wait_for(value_rows, full_sem.at[1])

    def spread_queries(at_s, carry):
        for t in range(2):
            rows = query_all[t, at_s].astype(F32)
            for g in range(GROUP):
                row = (g // 4) * 8 + t * 4 + g % 4
                for k in range(4):
                    query_rows[at_s * 4 + k, row : row + 1, :] = rows[k : k + 1, g * HD : g * HD + HD]
        return carry

    lax.fori_loop(0, 8, spread_queries, 0)

    def find_slot(at, carry):
        found = jnp.int32(0)
        for slot in range(32):
            found = jnp.where(slot_order[slot] == b * 16 + at, slot, found)
        slot_of[at] = found
        return carry

    lax.fori_loop(0, 16, find_slot, 0)

    lane = lax.broadcasted_iota(jnp.int32, (1, HD), 1)
    lane_prompt = lax.div(lane, 16)
    lane_later = lax.rem(lax.div(lane, 4), 2) == 1
    block_lane = lax.div(lax.broadcasted_iota(jnp.int32, (HD, HD), 1), 16)
    row4 = lax.broadcasted_iota(jnp.int32, (4, HD), 0)
    row512 = lax.broadcasted_iota(jnp.int32, (512, HD), 0)
    scale = HD ** -0.5

    def attend(first):
        slots = [slot_of[first + p] for p in range(8)]
        live = jnp.zeros((1, HD), jnp.int32)
        for p in range(8):
            live = jnp.where(lane_prompt == p, lengths[first + p + b * 16], live)

        def fresh_row(n, t, slot):
            rows = fresh_all[n, t, lax.div(slot, 4)].astype(F32)
            return jnp.sum(jnp.where(row4 == lax.rem(slot, 4), rows, 0.0), axis=0, keepdims=True)

        questions = jnp.concatenate([query_rows[slot] for slot in slots], axis=0).T
        diagonal = jnp.concatenate(
            [jnp.where(block_lane == p, questions, 0.0) for p in range(8)], axis=0
        ).astype(BF16)
        fresh_keys = jnp.concatenate(
            [
                jnp.concatenate([fresh_row(0, 0, slot), fresh_row(0, 1, slot), jnp.zeros((14, HD), F32)], axis=0)
                for slot in slots
            ],
            axis=1,
        ).astype(BF16)
        scores = jnp.dot(
            key_columns[:, first * HD : (first + 8) * HD], diagonal, preferred_element_type=F32
        ) * scale
        fresh_scores = jnp.dot(fresh_keys, diagonal, preferred_element_type=F32) * scale
        kept = row512 < live
        scores = jnp.where(kept, scores, HIDDEN)
        n0 = fresh_scores[0:1]
        n1 = jnp.where(lane_later, fresh_scores[1:2], HIDDEN)
        peak = jnp.maximum(jnp.max(scores, axis=0, keepdims=True), jnp.maximum(n0, n1))
        mass = jnp.where(kept, jnp.exp(scores - peak), 0.0)
        m0 = jnp.exp(n0 - peak)
        m1 = jnp.where(lane_later, jnp.exp(n1 - peak), 0.0)
        total = jnp.sum(mass, axis=0, keepdims=True) + m0 + m1
        weights = mass.T.astype(BF16)
        m0, m1 = (m.astype(BF16).astype(F32) for m in (m0, m1))
        sides = jnp.concatenate([total, m0, m1, jnp.zeros((HD - 3, HD), F32)], axis=0).T
        for p, slot in enumerate(slots):
            cut = slice(p * 16, p * 16 + 16)
            weighted = jnp.dot(weights[cut], value_rows[first + p], preferred_element_type=F32)
            weighted += sides[cut, 1:2] * fresh_row(1, 0, slot)
            weighted += sides[cut, 2:3] * fresh_row(1, 1, slot)
            result[first + p] = weighted / sides[cut, 0:1]

    attend(0)
    attend(8)

    def hand_rows(at_s, carry):
        for pair in range(2):
            first, second = (
                result[jnp.clip(slot_order[at_s * 4 + pair * 2 + n] - b * 16, 0, 15)] for n in range(2)
            )
            for to_b in range(2):
                cut = slice(to_b * 8, to_b * 8 + 8)
                rows_mine[to_b, at_s, pair] = jnp.concatenate((first[cut], second[cut]), axis=0).astype(BF16)
        return carry

    lax.fori_loop(0, 8, hand_rows, 0)

    swap_rows = remote(
        rows_mine.at[other], rows_swap, rows_swap_send, rows_swap_recv, (s, h, other)
    )
    swap_rows.start()
    upper = lax.broadcasted_iota(jnp.int32, (16, HD), 0) < 8

    def merge_rows(at_s, carry):
        for pair in range(2):
            first, second = (lax.div(slot_order[at_s * 4 + pair * 2 + n], 16) == b for n in range(2))
            ours = jnp.where(upper, jnp.where(first, 1.0, 0.0), jnp.where(second, 1.0, 0.0)) > 0.5
            rows_send[at_s, pair] = jnp.where(
                ours, rows_mine[b, at_s, pair].astype(F32), rows_swap[at_s, pair].astype(F32)
            ).astype(BF16)
        return carry

    swap_rows.wait_recv()
    lax.fori_loop(0, 8, merge_rows, 0)

    def send_rows(step, carry):
        to_s = lax.rem(s + step, 8)
        remote(rows_send.at[to_s], rows_land.at[s], rows_send_sem, rows_recv_sem, (to_s, h, b)).start()
        return carry

    lax.fori_loop(1, 8, send_rows, 0)
    pltpu.make_async_copy(rows_send.at[s], rows_land.at[s], rows_recv_sem).start()
    owned = [slot_order[s * 4 + k] for k in range(4)]
    lives = [lengths[slot] for slot in owned]
    first_position = (h * 2 + b) * BLOCK
    position = first_position + lax.broadcasted_iota(jnp.int32, (BLOCK, HD), 0)
    for k in range(4):
        keep[k] = jnp.where(position < lives[k], 1.0, 0.0).astype(BF16)
    fresh[0].wait()
    fresh[1].wait()

    def place_fresh(layer, carry):
        wide = first_position + lax.broadcasted_iota(jnp.int32, (BLOCK, KVH * HD), 0)
        for n, out in enumerate((keys_fresh, values_fresh)):
            new = [fresh_rows[n, t, layer].astype(F32) for t in range(2)]
            for k in range(4):
                rows = jnp.zeros((BLOCK, KVH * HD), F32)
                for t in range(2):
                    rows = jnp.where(wide == lives[k] + t, new[t][k : k + 1], rows)
                out[layer, k] = rows.astype(BF16)
        return carry

    lax.fori_loop(0, 8, place_fresh, 0)
    take_near_keys(1)
    take_near_keys(0)
    for dx in (1, 3, 2, 0):
        forward_values(dx, 1)
    send_near_values()
    for dx in (1, 3, 2, 0):
        forward_values(dx, 0)
    send_near_keys()
    turn_keys(1)
    turn_keys(0)
    pltpu.make_async_copy(keys_packed.at[here], keys_land.at[here], keys_recv).start()

    def assemble(l, carry):
        picked = []
        for k in range(4):
            part = slice((k % 2) * 8, (k % 2) * 8 + 8)
            picked.append(rows_land[l, k // 2].astype(F32)[part])
        for t in range(2):
            attention[t, l] = jnp.concatenate(
                [
                    jnp.concatenate([rows[t * 4 + g : t * 4 + g + 1] for rows in picked], axis=0)
                    for g in range(4)
                ],
                axis=1,
            ).astype(BF16)
        return carry

    wait_for(rows_land, rows_recv_sem)
    lax.fori_loop(0, 8, assemble, 0)
    wait_for(values_land.at[0], mid_near_recv)
    wait_for(values_land.at[far], values_recv)
    wait_for(keys_land, keys_recv)

    wait_for(value_rows.at[pl.ds(0, 8)], chip_send)
    wait_for(value_rows.at[pl.ds(0, 14)], line_send)
    for n, part in enumerate(small_parts):
        wait_for(part.at[b, pl.ds(0, 7)], small_send.at[n])
        wait_for(part.at[b], share_send.at[n])
    swap_rows.wait_send()
    wait_for(values_packed.at[pl.ds(0, 15), far], mid_send)
    wait_for(values_packed.at[pl.ds(0, 15), 0], mid_near)
    wait_for(keys_packed.at[pl.ds(0, 15)], keys_send)
    wait_for(values_mid, values_send)
    wait_for(rows_send.at[pl.ds(0, 7)], rows_send_sem)


def hand_out(
    attention, keys_land, values_land, keys_fresh, values_fresh, keep,
    attention_out, keys_out, values_out, keys, values, sem,
):
    copies = [pltpu.make_async_copy(attention, attention_out, sem.at[16])]
    copies[0].start()
    kept = [keep[k] > 0 for k in range(4)]
    z = lax.div(lax.axis_index("head"), 2)
    for l in range(8):
        x, y_high = l // 2, l % 2
        for h in range(KVH):
            cut = slice(h * HD, h * HD + HD)
            from_z, y_low = h // 2, h % 2
            for k in range(4):
                landed = keys_land[x * 4 + y_high * 2 + y_low, lax.rem(from_z - z + 4, 4), k]
                keys[l, k, :, cut] = jnp.where(kept[k], landed, keys_fresh[l, k, :, cut])
                landed = values_land[lax.rem(z - from_z + 4, 4), x * 4 + y_low * 2 + y_high, k]
                values[l, k, :, cut] = jnp.where(kept[k], landed, values_fresh[l, k, :, cut])
        for n, (src, dst) in enumerate(((keys, keys_out), (values, values_out))):
            copies.append(pltpu.make_async_copy(src.at[l], dst.at[l], sem.at[n * 8 + l]))
            copies[-1].start()
    for copy in copies:
        copy.wait()


def body(keys_prefill, values_prefill, lengths, slot_order, queries, new_keys, new_values):
    keys = keys_prefill.reshape(16, 4, 2, 2, BLOCK, HD)
    values = values_prefill.reshape(16, 4, 2, 2, BLOCK, HD)
    flat = (keys_prefill.reshape(16, 512, HD), values_prefill.reshape(16, 512, HD))
    any_spec = pl.BlockSpec(memory_space=pl.ANY)
    hbm_spec = pl.BlockSpec(memory_space=pltpu.HBM)
    vmem_spec = pl.BlockSpec(memory_space=pltpu.VMEM)
    dma, vmem = pltpu.SemaphoreType.DMA, pltpu.VMEM
    rows_shape, cache_shape = (2, 8, 4, 4 * HD), (8, 4, BLOCK, KVH * HD)
    plane_shape, line_shape = (16, 4, 4, BLOCK, HD), (4, 16, 4, BLOCK, HD)

    def in_hbm(array):
        return pltpu.with_memory_space_constraint(array, pltpu.HBM)

    held = pl.pallas_call(
        relay,
        out_shape=tuple(
            vmem(shape, BF16) for shape in (rows_shape, plane_shape, line_shape, cache_shape, cache_shape, (4, BLOCK, HD))
        ),
        in_specs=[hbm_spec] * 9,
        out_specs=(vmem_spec,) * 6,
        scratch_shapes=[
            vmem((512, 16 * HD), BF16), vmem((16, 512, HD), BF16),
            [vmem((3, 32, BLOCK, HD), BF16)] * 2, [vmem((32, BLOCK, HD), BF16)] * 2,
            [vmem((32, BLOCK, HD), BF16)] * len(PIECES),
            vmem(plane_shape, BF16), vmem(plane_shape, BF16),
            vmem((3, 16, 4, BLOCK, HD), BF16),
            vmem((2, 2, 8, 4, KVH * HD), BF16), vmem((2, 8, 4, GROUP * HD), BF16), vmem((32, 16, HD), F32),
            vmem((2, 2, 8, 4, HD), BF16), vmem((16, 16, HD), F32),
            vmem((2, 8, 2, 16, HD), BF16), vmem((8, 2, 16, HD), BF16),
            vmem((8, 2, 16, HD), BF16), vmem((8, 2, 16, HD), BF16),
            pltpu.SMEM((32,), jnp.int32), pltpu.SMEM((32,), jnp.int32), pltpu.SMEM((16,), jnp.int32),
            dma((2,)), dma((2,)), dma((2,)), dma, dma((2,)), dma((2,)), dma, dma((len(PIECES),)),
            dma, dma, dma, dma((8,)), dma, dma, dma, dma,
            dma((3,)), dma((3,)), dma((3,)), dma((3,)), dma, dma, dma, dma,
        ],
        compiler_params=pltpu.CompilerParams(
            collective_id=0, has_side_effects=True, vmem_limit_bytes=48 * 2**20
        ),
        name="relay",
    )(*(in_hbm(x) for x in (slot_order, lengths, keys, values, *flat, queries, new_keys, new_values)))
    return pl.pallas_call(
        hand_out,
        out_shape=tuple(jax.ShapeDtypeStruct(shape, BF16) for shape in (rows_shape, cache_shape, cache_shape)),
        in_specs=[vmem_spec] * 6,
        out_specs=(any_spec,) * 3,
        scratch_shapes=[vmem(cache_shape, BF16), vmem(cache_shape, BF16), dma((17,))],
        compiler_params=pltpu.CompilerParams(vmem_limit_bytes=8 * 2**20),
        name="hand_out",
    )(*(pltpu.with_memory_space_constraint(x, pltpu.VMEM) for x in held))


def solution(mesh):
    in_specs = (
        P("section", "batch", None, "head"),
        P("section", "batch", None, "head"),
        P(),
        P(),
        P(None, None, "section", None),
        P(None, None, "section", None),
        P(None, None, "section", None),
    )
    out_specs = (
        P(None, None, "section", ("head", "batch")),
        P(None, "section", ("head", "batch"), None),
        P(None, "section", ("head", "batch"), None),
    )
    return jax.shard_map(body, mesh=mesh, in_specs=in_specs, out_specs=out_specs, check_vma=False)
```

```python
import jax
import jax.numpy as jnp
from jax import lax
from jax.experimental import pallas as pl
from jax.experimental.pallas import tpu as pltpu
from jax.sharding import PartitionSpec as P

KVH = 8
HD = 128
GROUP = 8
BLOCK = 32
MESH = pl.DeviceIdType.MESH
HIDDEN = -1e30
BF16, F32 = jnp.bfloat16, jnp.float32


PLANE = {
    1: ((1, 1), (3, 3), (1, 3), (3, 1), (2, 1), (0, 3), (2, 3), (0, 1)),
    0: ((1, 0), (0, 2), (3, 2), (1, 2), (3, 0), (2, 2), (2, 0)),
}
PIECES = ((1, 1), (1, 3), (1, 2), (0, 1), (0, 3), (0, 2), (1, 0), (0, 0))


def group_of(dx, low):
    return low * 4 + dx


def relay(
    slot_order_hbm, lengths_hbm, keys, values, keys_flat, values_flat, queries, new_keys, new_values,
    attention, keys_land, values_land, keys_fresh, values_fresh, keep,
    key_columns, value_rows, keys_line, keys_near, values_chip, keys_packed, values_packed, values_mid,
    fresh_rows, query_all, query_rows, fresh_all, result, rows_mine, rows_swap, rows_send, rows_land,
    slot_order, lengths, slot_of,
    scalar_sem, full_sem, fresh_sem, line_send, line_recv, near_recv, chip_send, chip_recv,
    keys_send, keys_recv, mid_send, mid_recv, mid_near, mid_near_recv, values_send, values_recv,
    small_send, small_recv, share_send, share_recv, rows_swap_send, rows_swap_recv, rows_send_sem, rows_recv_sem,
):
    s, h, b = lax.axis_index("section"), lax.axis_index("head"), lax.axis_index("batch")
    x, z = lax.div(s, 2), lax.div(h, 2)
    y_low = lax.rem(h, 2)
    y = lax.rem(s, 2) * 2 + y_low
    other = 1 - b
    sign = 1 - 2 * b
    mine = pl.ds(b * 16, 16)
    here = x * 4 + y
    here_mid = x * 4 + y_low * 2 + lax.div(y, 2)

    def remote(src, dst, send_sem, recv_sem, to):
        return pltpu.make_async_remote_copy(
            src_ref=src, dst_ref=dst, send_sem=send_sem, recv_sem=recv_sem,
            device_id=to, device_id_type=MESH,
        )

    def wait_for(ref, sem):
        pltpu.make_async_copy(ref, ref, sem).wait()

    def away(d, at, way):
        return lax.rem(at + way * d + 4, 4)

    def in_plane(at_x, at_y):
        return at_x * 2 + lax.div(at_y, 2), z * 2 + lax.rem(at_y, 2)

    def in_line(at_z):
        return at_z * 2 + y_low

    def owner_low(low):
        return lax.rem(y_low + low, 2)

    barrier = pltpu.get_barrier_semaphore()

    def greet(to):
        pl.semaphore_signal(barrier, inc=1, device_id=to, device_id_type=MESH)

    for dz in range(4):
        at_h = in_line(away(dz, z, 1))
        greet((s, at_h, other))
        if dz:
            greet((s, at_h, b))
    for low in (1, 0):
        for dx, dy in PLANE[low]:
            at_s, at_h = in_plane(away(dx, x, 1), away(dy, y, 1))
            greet((at_s, at_h, b))

    scalars = [
        pltpu.make_async_copy(slot_order_hbm, slot_order, scalar_sem.at[0]),
        pltpu.make_async_copy(lengths_hbm, lengths, scalar_sem.at[1]),
    ]
    whole = [
        pltpu.make_async_copy(keys_flat.at[at], key_columns.at[:, pl.ds(at * HD, HD)], full_sem.at[0])
        for at in range(16)
    ]
    whole.append(pltpu.make_async_copy(values_flat, value_rows, full_sem.at[1]))
    fresh = [
        pltpu.make_async_copy(src, fresh_rows.at[n], fresh_sem.at[n])
        for n, src in enumerate((new_keys, new_values))
    ]
    for copy in scalars:
        copy.start()
    for piece, (low, dz) in enumerate(PIECES):
        pltpu.make_async_copy(
            values.at[:, away(dz, z, sign), owner_low(low), b], values_chip[piece].at[mine], chip_recv.at[piece]
        ).start()
    for low in (1, 0):
        pltpu.make_async_copy(
            keys.at[:, z, owner_low(low), b], keys_near[low].at[mine], near_recv.at[low]
        ).start()
    for copy in whole + fresh:
        copy.start()
    pl.semaphore_wait(barrier, 22)

    def swap(piece):
        low, dz = PIECES[piece]
        remote(
            values.at[:, away(dz, z, -sign), owner_low(low), other], values_chip[piece].at[mine],
            chip_send, chip_recv.at[piece], (s, h, other),
        ).start()

    swap(0)
    swap(1)

    def send_line(low, dz, to_b):
        to_z = away(dz, z, sign)
        d = away(dz, 0, sign)
        remote(
            keys.at[:, to_z, owner_low(low), to_b], keys_line[low].at[3 - d, mine],
            line_send, line_recv.at[low], (s, in_line(to_z), to_b),
        ).start()

    def send_lines(low):
        for dz, to_b in ((1, b), (3, other), (2, b), (1, other), (3, b), (2, other)):
            send_line(low, dz, to_b)

    send_lines(1)

    head_rows = pl.ds(pl.multiple_of(h * GROUP * HD, GROUP * HD), GROUP * HD)
    head_cols = pl.ds(pl.multiple_of(h * HD, HD), HD)

    def small_pieces(to_s):
        return (
            (queries.at[b, to_s, :, head_rows], query_all.at[b, s]),
            (new_keys.at[b, to_s, :, head_cols], fresh_all.at[0, b, s]),
            (new_values.at[b, to_s, :, head_cols], fresh_all.at[1, b, s]),
        )

    small_parts = (query_all, fresh_all.at[0], fresh_all.at[1])

    def send_small(step, carry):
        to_s = lax.rem(s + step, 8)
        for n, (src, dst) in enumerate(small_pieces(to_s)):
            remote(src, dst, small_send.at[n], small_recv.at[n], (to_s, h, b)).start()
        return carry

    def each_slot(do):
        def step(at_s, carry):
            for k in range(4):
                do(at_s, k, slot_order[at_s * 4 + k])
            return carry

        lax.fori_loop(0, 8, step, 0)

    def send_plane(src, dx, dy, dst, send_sem, recv_sem):
        to_x, to_y = away(dx, x, sign), away(dy, y, sign)
        to_s, to_h = in_plane(to_x, to_y)
        remote(src(to_x * 4 + to_y), dst, send_sem, recv_sem, (to_s, to_h, b)).start()

    def take_values(piece):
        low, dz = PIECES[piece]
        at_z = away(dz, 0, sign)
        wait_for(values_chip[piece], chip_recv.at[piece])
        if piece + 2 < len(PIECES):
            swap(piece + 2)

        def pack(at_s, k, slot):
            values_packed[at_s * 2 + owner_low(low), at_z, k] = values_chip[piece][slot]

        each_slot(pack)
        if dz:
            for dx, dy in PLANE[low]:
                send_plane(
                    lambda to: values_packed.at[to, at_z], dx, dy, values_mid.at[at_z - 1, here_mid],
                    mid_send, mid_recv.at[group_of(dx, low)],
                )

    far = pl.ds(1, 3)

    def forward_values(dx, low):
        group = group_of(dx, low)
        wait_for(values_mid.at[:, pl.ds(0, 2)], mid_recv.at[group])
        pair = pl.ds(away(dx, x, -sign) * 4 + owner_low(low) * 2, 2)
        for dz in (1, 3, 2):
            remote(
                values_mid.at[dz - 1, pair], values_land.at[dz, pair],
                values_send, values_recv, (s, in_line(away(dz, z, 1)), b),
            ).start()

    def take_near_keys(low):
        wait_for(keys_near[low], near_recv.at[low])

        def pack(at_s, k, slot):
            keys_packed[at_s * 2 + owner_low(low), 0, k] = keys_near[low][slot]

        each_slot(pack)

    def send_near_values():
        for dx, dy in PLANE[1] + PLANE[0]:
            send_plane(
                lambda to: values_packed.at[to, 0], dx, dy, values_land.at[0, here_mid], mid_near, mid_near_recv
            )

    def send_near_keys():
        for dx, dy in PLANE[1] + PLANE[0]:
            send_plane(lambda to: keys_packed.at[to, 0], dx, dy, keys_land.at[here, 0], keys_send, keys_recv)

    def turn_keys(low):
        wait_for(keys_line[low], line_recv.at[low])

        def pack(at_s, k, slot):
            for dz in range(1, 4):
                keys_packed[at_s * 2 + owner_low(low), dz, k] = keys_line[low][dz - 1, slot]

        each_slot(pack)
        for dx, dy in PLANE[low]:
            send_plane(lambda to: keys_packed.at[to, far], dx, dy, keys_land.at[here, far], keys_send, keys_recv)

    scalars[0].wait()
    scalars[1].wait()
    for piece in range(2):
        take_values(piece)
    send_lines(0)
    lax.fori_loop(1, 8, send_small, 0)
    for n, (src, dst) in enumerate(small_pieces(s)):
        pltpu.make_async_copy(src, dst, small_recv.at[n]).start()
    for piece in range(2, len(PIECES)):
        take_values(piece)
    for low in (1, 0):
        remote(
            keys.at[:, z, owner_low(low), other], keys_near[low].at[mine],
            line_send, near_recv.at[low], (s, h, other),
        ).start()
    pltpu.make_async_copy(
        values_packed.at[here, far], values_mid.at[:, here_mid], mid_recv.at[group_of(0, 0)]
    ).start()
    pltpu.make_async_copy(values_packed.at[here, 0], values_land.at[0, here_mid], mid_near_recv).start()

    for n, part in enumerate(small_parts):
        wait_for(part.at[b], small_recv.at[n])
        remote(part.at[b], part.at[b], share_send.at[n], share_recv.at[n], (s, h, other)).start()
    for n, part in enumerate(small_parts):
        wait_for(part.at[other], share_recv.at[n])
    wait_for(key_columns, full_sem.at[0])
    wait_for(value_rows, full_sem.at[1])

    def spread_queries(at_s, carry):
        for t in range(2):
            rows = query_all[t, at_s].astype(F32)
            for g in range(GROUP):
                row = (g // 4) * 8 + t * 4 + g % 4
                for k in range(4):
                    query_rows[at_s * 4 + k, row : row + 1, :] = rows[k : k + 1, g * HD : g * HD + HD]
        return carry

    lax.fori_loop(0, 8, spread_queries, 0)

    def find_slot(at, carry):
        found = jnp.int32(0)
        for slot in range(32):
            found = jnp.where(slot_order[slot] == b * 16 + at, slot, found)
        slot_of[at] = found
        return carry

    lax.fori_loop(0, 16, find_slot, 0)

    lane = lax.broadcasted_iota(jnp.int32, (1, HD), 1)
    lane_prompt = lax.div(lane, 16)
    lane_later = lax.rem(lax.div(lane, 4), 2) == 1
    block_lane = lax.div(lax.broadcasted_iota(jnp.int32, (HD, HD), 1), 16)
    row4 = lax.broadcasted_iota(jnp.int32, (4, HD), 0)
    row512 = lax.broadcasted_iota(jnp.int32, (512, HD), 0)
    scale = HD ** -0.5

    def attend(first):
        slots = [slot_of[first + p] for p in range(8)]
        live = jnp.zeros((1, HD), jnp.int32)
        for p in range(8):
            live = jnp.where(lane_prompt == p, lengths[first + p + b * 16], live)

        def fresh_row(n, t, slot):
            rows = fresh_all[n, t, lax.div(slot, 4)].astype(F32)
            return jnp.sum(jnp.where(row4 == lax.rem(slot, 4), rows, 0.0), axis=0, keepdims=True)

        questions = jnp.concatenate([query_rows[slot] for slot in slots], axis=0).T
        diagonal = jnp.concatenate(
            [jnp.where(block_lane == p, questions, 0.0) for p in range(8)], axis=0
        ).astype(BF16)
        fresh_keys = jnp.concatenate(
            [
                jnp.concatenate([fresh_row(0, 0, slot), fresh_row(0, 1, slot), jnp.zeros((14, HD), F32)], axis=0)
                for slot in slots
            ],
            axis=1,
        ).astype(BF16)
        scores = jnp.dot(
            key_columns[:, first * HD : (first + 8) * HD], diagonal, preferred_element_type=F32
        ) * scale
        fresh_scores = jnp.dot(fresh_keys, diagonal, preferred_element_type=F32) * scale
        kept = row512 < live
        scores = jnp.where(kept, scores, HIDDEN)
        n0 = fresh_scores[0:1]
        n1 = jnp.where(lane_later, fresh_scores[1:2], HIDDEN)
        peak = jnp.maximum(jnp.max(scores, axis=0, keepdims=True), jnp.maximum(n0, n1))
        mass = jnp.where(kept, jnp.exp(scores - peak), 0.0)
        m0 = jnp.exp(n0 - peak)
        m1 = jnp.where(lane_later, jnp.exp(n1 - peak), 0.0)
        total = jnp.sum(mass, axis=0, keepdims=True) + m0 + m1
        weights = mass.T.astype(BF16)
        m0, m1 = (m.astype(BF16).astype(F32) for m in (m0, m1))
        sides = jnp.concatenate([total, m0, m1, jnp.zeros((HD - 3, HD), F32)], axis=0).T
        for p, slot in enumerate(slots):
            cut = slice(p * 16, p * 16 + 16)
            weighted = jnp.dot(weights[cut], value_rows[first + p], preferred_element_type=F32)
            weighted += sides[cut, 1:2] * fresh_row(1, 0, slot)
            weighted += sides[cut, 2:3] * fresh_row(1, 1, slot)
            result[first + p] = weighted / sides[cut, 0:1]

    attend(0)
    attend(8)

    def hand_rows(at_s, carry):
        for pair in range(2):
            first, second = (
                result[jnp.clip(slot_order[at_s * 4 + pair * 2 + n] - b * 16, 0, 15)] for n in range(2)
            )
            for to_b in range(2):
                cut = slice(to_b * 8, to_b * 8 + 8)
                rows_mine[to_b, at_s, pair] = jnp.concatenate((first[cut], second[cut]), axis=0).astype(BF16)
        return carry

    lax.fori_loop(0, 8, hand_rows, 0)

    swap_rows = remote(
        rows_mine.at[other], rows_swap, rows_swap_send, rows_swap_recv, (s, h, other)
    )
    swap_rows.start()
    upper = lax.broadcasted_iota(jnp.int32, (16, HD), 0) < 8

    def merge_rows(at_s, carry):
        for pair in range(2):
            first, second = (lax.div(slot_order[at_s * 4 + pair * 2 + n], 16) == b for n in range(2))
            ours = jnp.where(upper, jnp.where(first, 1.0, 0.0), jnp.where(second, 1.0, 0.0)) > 0.5
            rows_send[at_s, pair] = jnp.where(
                ours, rows_mine[b, at_s, pair].astype(F32), rows_swap[at_s, pair].astype(F32)
            ).astype(BF16)
        return carry

    swap_rows.wait_recv()
    lax.fori_loop(0, 8, merge_rows, 0)

    def send_rows(step, carry):
        to_s = lax.rem(s + step, 8)
        remote(rows_send.at[to_s], rows_land.at[s], rows_send_sem, rows_recv_sem, (to_s, h, b)).start()
        return carry

    lax.fori_loop(1, 8, send_rows, 0)
    pltpu.make_async_copy(rows_send.at[s], rows_land.at[s], rows_recv_sem).start()
    owned = [slot_order[s * 4 + k] for k in range(4)]
    lives = [lengths[slot] for slot in owned]
    first_position = (h * 2 + b) * BLOCK
    position = first_position + lax.broadcasted_iota(jnp.int32, (BLOCK, HD), 0)
    for k in range(4):
        keep[k] = jnp.where(position < lives[k], 1.0, 0.0).astype(BF16)
    fresh[0].wait()
    fresh[1].wait()

    def place_fresh(layer, carry):
        wide = first_position + lax.broadcasted_iota(jnp.int32, (BLOCK, KVH * HD), 0)
        for n, out in enumerate((keys_fresh, values_fresh)):
            new = [fresh_rows[n, t, layer].astype(F32) for t in range(2)]
            for k in range(4):
                rows = jnp.zeros((BLOCK, KVH * HD), F32)
                for t in range(2):
                    rows = jnp.where(wide == lives[k] + t, new[t][k : k + 1], rows)
                out[layer, k] = rows.astype(BF16)
        return carry

    lax.fori_loop(0, 8, place_fresh, 0)
    take_near_keys(1)
    take_near_keys(0)
    for dx in (1, 3, 2, 0):
        forward_values(dx, 1)
    send_near_values()
    for dx in (1, 3, 2, 0):
        forward_values(dx, 0)
    send_near_keys()
    turn_keys(1)
    turn_keys(0)
    pltpu.make_async_copy(keys_packed.at[here], keys_land.at[here], keys_recv).start()

    def assemble(l, carry):
        picked = []
        for k in range(4):
            part = slice((k % 2) * 8, (k % 2) * 8 + 8)
            picked.append(rows_land[l, k // 2].astype(F32)[part])
        for t in range(2):
            attention[t, l] = jnp.concatenate(
                [
                    jnp.concatenate([rows[t * 4 + g : t * 4 + g + 1] for rows in picked], axis=0)
                    for g in range(4)
                ],
                axis=1,
            ).astype(BF16)
        return carry

    wait_for(rows_land, rows_recv_sem)
    lax.fori_loop(0, 8, assemble, 0)
    wait_for(values_land.at[0], mid_near_recv)
    wait_for(values_land.at[far], values_recv)
    wait_for(keys_land, keys_recv)

    wait_for(value_rows.at[pl.ds(0, 8)], chip_send)
    wait_for(value_rows.at[pl.ds(0, 14)], line_send)
    for n, part in enumerate(small_parts):
        wait_for(part.at[b, pl.ds(0, 7)], small_send.at[n])
        wait_for(part.at[b], share_send.at[n])
    swap_rows.wait_send()
    wait_for(values_packed.at[pl.ds(0, 15), far], mid_send)
    wait_for(values_packed.at[pl.ds(0, 15), 0], mid_near)
    wait_for(keys_packed.at[pl.ds(0, 15)], keys_send)
    wait_for(values_mid, values_send)
    wait_for(rows_send.at[pl.ds(0, 7)], rows_send_sem)


def hand_out(
    attention, keys_land, values_land, keys_fresh, values_fresh, keep,
    attention_out, keys_out, values_out, keys, values, sem,
):
    copies = [pltpu.make_async_copy(attention, attention_out, sem.at[16])]
    copies[0].start()
    kept = [keep[k] > 0 for k in range(4)]
    z = lax.div(lax.axis_index("head"), 2)
    for l in range(8):
        x, y_high = l // 2, l % 2
        for h in range(KVH):
            cut = slice(h * HD, h * HD + HD)
            from_z, y_low = h // 2, h % 2
            for k in range(4):
                landed = keys_land[x * 4 + y_high * 2 + y_low, lax.rem(from_z - z + 4, 4), k]
                keys[l, k, :, cut] = jnp.where(kept[k], landed, keys_fresh[l, k, :, cut])
                landed = values_land[lax.rem(z - from_z + 4, 4), x * 4 + y_low * 2 + y_high, k]
                values[l, k, :, cut] = jnp.where(kept[k], landed, values_fresh[l, k, :, cut])
        for n, (src, dst) in enumerate(((keys, keys_out), (values, values_out))):
            copies.append(pltpu.make_async_copy(src.at[l], dst.at[l], sem.at[n * 8 + l]))
            copies[-1].start()
    for copy in copies:
        copy.wait()


def body(keys_prefill, values_prefill, lengths, slot_order, queries, new_keys, new_values):
    keys = keys_prefill.reshape(16, 4, 2, 2, BLOCK, HD)
    values = values_prefill.reshape(16, 4, 2, 2, BLOCK, HD)
    flat = (keys_prefill.reshape(16, 512, HD), values_prefill.reshape(16, 512, HD))
    any_spec = pl.BlockSpec(memory_space=pl.ANY)
    hbm_spec = pl.BlockSpec(memory_space=pltpu.HBM)
    vmem_spec = pl.BlockSpec(memory_space=pltpu.VMEM)
    dma, vmem = pltpu.SemaphoreType.DMA, pltpu.VMEM
    rows_shape, cache_shape = (2, 8, 4, 4 * HD), (8, 4, BLOCK, KVH * HD)
    plane_shape, line_shape = (16, 4, 4, BLOCK, HD), (4, 16, 4, BLOCK, HD)

    def in_hbm(array):
        return pltpu.with_memory_space_constraint(array, pltpu.HBM)

    held = pl.pallas_call(
        relay,
        out_shape=tuple(
            vmem(shape, BF16) for shape in (rows_shape, plane_shape, line_shape, cache_shape, cache_shape, (4, BLOCK, HD))
        ),
        in_specs=[hbm_spec] * 9,
        out_specs=(vmem_spec,) * 6,
        scratch_shapes=[
            vmem((512, 16 * HD), BF16), vmem((16, 512, HD), BF16),
            [vmem((3, 32, BLOCK, HD), BF16)] * 2, [vmem((32, BLOCK, HD), BF16)] * 2,
            [vmem((32, BLOCK, HD), BF16)] * len(PIECES),
            vmem(plane_shape, BF16), vmem(plane_shape, BF16),
            vmem((3, 16, 4, BLOCK, HD), BF16),
            vmem((2, 2, 8, 4, KVH * HD), BF16), vmem((2, 8, 4, GROUP * HD), BF16), vmem((32, 16, HD), F32),
            vmem((2, 2, 8, 4, HD), BF16), vmem((16, 16, HD), F32),
            vmem((2, 8, 2, 16, HD), BF16), vmem((8, 2, 16, HD), BF16),
            vmem((8, 2, 16, HD), BF16), vmem((8, 2, 16, HD), BF16),
            pltpu.SMEM((32,), jnp.int32), pltpu.SMEM((32,), jnp.int32), pltpu.SMEM((16,), jnp.int32),
            dma((2,)), dma((2,)), dma((2,)), dma, dma((2,)), dma((2,)), dma, dma((len(PIECES),)),
            dma, dma, dma, dma((8,)), dma, dma, dma, dma,
            dma((3,)), dma((3,)), dma((3,)), dma((3,)), dma, dma, dma, dma,
        ],
        compiler_params=pltpu.CompilerParams(
            collective_id=0, has_side_effects=True, vmem_limit_bytes=48 * 2**20
        ),
        name="relay",
    )(*(in_hbm(x) for x in (slot_order, lengths, keys, values, *flat, queries, new_keys, new_values)))
    return pl.pallas_call(
        hand_out,
        out_shape=tuple(jax.ShapeDtypeStruct(shape, BF16) for shape in (rows_shape, cache_shape, cache_shape)),
        in_specs=[vmem_spec] * 6,
        out_specs=(any_spec,) * 3,
        scratch_shapes=[vmem(cache_shape, BF16), vmem(cache_shape, BF16), dma((17,))],
        compiler_params=pltpu.CompilerParams(vmem_limit_bytes=8 * 2**20),
        name="hand_out",
    )(*(pltpu.with_memory_space_constraint(x, pltpu.VMEM) for x in held))


def solution(mesh):
    in_specs = (
        P("section", "batch", None, "head"),
        P("section", "batch", None, "head"),
        P(),
        P(),
        P(None, None, "section", None),
        P(None, None, "section", None),
        P(None, None, "section", None),
    )
    out_specs = (
        P(None, None, "section", ("head", "batch")),
        P(None, "section", ("head", "batch"), None),
        P(None, "section", ("head", "batch"), None),
    )
    return jax.shard_map(body, mesh=mesh, in_specs=in_specs, out_specs=out_specs, check_vma=False)
```

```python
import jax
import jax.numpy as jnp
from jax import lax
from jax.experimental import pallas as pl
from jax.experimental.pallas import tpu as pltpu
from jax.sharding import PartitionSpec as P

KVH = 8
HD = 128
GROUP = 8
BLOCK = 32
MESH = pl.DeviceIdType.MESH
HIDDEN = -1e30
BF16, F32 = jnp.bfloat16, jnp.float32


PLANE = {
    1: ((1, 1), (3, 3), (1, 3), (3, 1), (2, 1), (0, 3), (2, 3), (0, 1)),
    0: ((1, 0), (0, 2), (3, 2), (1, 2), (3, 0), (2, 2), (2, 0)),
}
PIECES = ((1, 1), (1, 3), (1, 2), (0, 1), (0, 3), (0, 2), (1, 0), (0, 0))


def relay(
    slot_order_hbm, lengths_hbm, keys, values, keys_flat, values_flat, queries, new_keys, new_values,
    attention, keys_land, values_land, keys_fresh, values_fresh, keep,
    key_columns, value_rows, keys_line, keys_near, values_chip, keys_packed, values_packed, values_mid,
    fresh_rows, query_all, query_rows, fresh_all, result, rows_mine, rows_swap, rows_send, rows_land,
    slot_order, lengths, slot_of,
    scalar_sem, full_sem, fresh_sem, line_send, line_recv, near_recv, chip_send, chip_recv,
    keys_send, keys_recv, mid_send, mid_recv, mid_near, mid_near_recv, values_send, values_recv,
    small_send, small_recv, share_send, share_recv, rows_swap_send, rows_swap_recv, rows_send_sem, rows_recv_sem,
):
    s, h, b = lax.axis_index("section"), lax.axis_index("head"), lax.axis_index("batch")
    x, z = lax.div(s, 2), lax.div(h, 2)
    y_low = lax.rem(h, 2)
    y = lax.rem(s, 2) * 2 + y_low
    other = 1 - b
    sign = 1 - 2 * b
    mine = pl.ds(b * 16, 16)
    here = x * 4 + y
    here_mid = (x, y_low, lax.div(y, 2))

    def remote(src, dst, send_sem, recv_sem, to):
        return pltpu.make_async_remote_copy(
            src_ref=src, dst_ref=dst, send_sem=send_sem, recv_sem=recv_sem,
            device_id=to, device_id_type=MESH,
        )

    def wait_for(ref, sem):
        pltpu.make_async_copy(ref, ref, sem).wait()

    def away(d, at, way):
        return lax.rem(at + way * d + 4, 4)

    def in_plane(at_x, at_y):
        return at_x * 2 + lax.div(at_y, 2), z * 2 + lax.rem(at_y, 2)

    def in_line(at_z):
        return at_z * 2 + y_low

    def owner_low(low):
        return lax.rem(y_low + low, 2)

    barrier = pltpu.get_barrier_semaphore()

    def greet(to):
        pl.semaphore_signal(barrier, inc=1, device_id=to, device_id_type=MESH)

    for dz in range(4):
        at_h = in_line(away(dz, z, 1))
        greet((s, at_h, other))
        if dz:
            greet((s, at_h, b))
    for low in (1, 0):
        for dx, dy in PLANE[low]:
            at_s, at_h = in_plane(away(dx, x, 1), away(dy, y, 1))
            greet((at_s, at_h, b))

    scalars = [
        pltpu.make_async_copy(slot_order_hbm, slot_order, scalar_sem.at[0]),
        pltpu.make_async_copy(lengths_hbm, lengths, scalar_sem.at[1]),
    ]
    whole = [
        pltpu.make_async_copy(keys_flat.at[at], key_columns.at[:, pl.ds(at * HD, HD)], full_sem.at[0])
        for at in range(16)
    ]
    whole.append(pltpu.make_async_copy(values_flat, value_rows, full_sem.at[1]))
    fresh = [
        pltpu.make_async_copy(src, fresh_rows.at[n], fresh_sem.at[n])
        for n, src in enumerate((new_keys, new_values))
    ]
    for copy in scalars:
        copy.start()
    for piece, (low, dz) in enumerate(PIECES):
        pltpu.make_async_copy(
            values.at[:, away(dz, z, sign), owner_low(low), b], values_chip[piece].at[mine], chip_recv.at[piece]
        ).start()
    for low in (1, 0):
        pltpu.make_async_copy(
            keys.at[:, z, owner_low(low), b], keys_near[low].at[mine], near_recv.at[low]
        ).start()
    for copy in whole + fresh:
        copy.start()
    pl.semaphore_wait(barrier, 22)

    def swap(piece):
        low, dz = PIECES[piece]
        remote(
            values.at[:, away(dz, z, -sign), owner_low(low), other], values_chip[piece].at[mine],
            chip_send, chip_recv.at[piece], (s, h, other),
        ).start()

    swap(0)
    swap(1)

    def send_line(low, dz, to_b):
        to_z = away(dz, z, sign)
        d = away(dz, 0, sign)
        remote(
            keys.at[:, to_z, owner_low(low), to_b], keys_line[low].at[3 - d, mine],
            line_send, line_recv.at[low], (s, in_line(to_z), to_b),
        ).start()

    for low in (1, 0):
        for dz, to_b in ((1, b), (3, other), (2, b), (1, other), (3, b), (2, other)):
            send_line(low, dz, to_b)
    for low in (1, 0):
        remote(
            keys.at[:, z, owner_low(low), other], keys_near[low].at[mine],
            line_send, near_recv.at[low], (s, h, other),
        ).start()

    head_rows = pl.ds(pl.multiple_of(h * GROUP * HD, GROUP * HD), GROUP * HD)
    head_cols = pl.ds(pl.multiple_of(h * HD, HD), HD)

    def small_pieces(to_s):
        return (
            (queries.at[b, to_s, :, head_rows], query_all.at[b, s]),
            (new_keys.at[b, to_s, :, head_cols], fresh_all.at[0, b, s]),
            (new_values.at[b, to_s, :, head_cols], fresh_all.at[1, b, s]),
        )

    small_parts = (query_all, fresh_all.at[0], fresh_all.at[1])

    def send_small(step, carry):
        to_s = lax.rem(s + step, 8)
        for n, (src, dst) in enumerate(small_pieces(to_s)):
            remote(src, dst, small_send.at[n], small_recv.at[n], (to_s, h, b)).start()
        return carry

    def each_slot(do):
        def step(at_s, carry):
            for k in range(4):
                do(at_s, k, slot_order[at_s * 4 + k])
            return carry

        lax.fori_loop(0, 8, step, 0)

    def send_plane(src, dx, dy, dst, send_sem, recv_sem):
        to_x, to_y = away(dx, x, sign), away(dy, y, sign)
        to_s, to_h = in_plane(to_x, to_y)
        remote(src(to_x * 4 + to_y), dst, send_sem, recv_sem, (to_s, to_h, b)).start()

    def take_values(piece):
        low, dz = PIECES[piece]
        at_z = away(dz, 0, sign)
        wait_for(values_chip[piece], chip_recv.at[piece])
        if piece + 2 < len(PIECES):
            swap(piece + 2)

        def pack(at_s, k, slot):
            values_packed[at_s * 2 + owner_low(low), at_z, k] = values_chip[piece][slot]

        each_slot(pack)
        if dz:
            for dx, dy in PLANE[low]:
                send_plane(
                    lambda to: values_packed.at[to, at_z], dx, dy, values_mid.at[at_z - 1, *here_mid],
                    mid_send, mid_recv.at[piece],
                )
            if low == 0:
                pltpu.make_async_copy(
                    values_packed.at[here, at_z], values_mid.at[at_z - 1, *here_mid], mid_recv.at[piece]
                ).start()

    far = pl.ds(1, 3)

    def forward_values(piece):
        low, dz = PIECES[piece]
        at_z = away(dz, 0, sign)
        wait_for(values_mid.at[0, :, 0], mid_recv.at[piece])
        for at_x in range(4):
            remote(
                values_mid.at[at_z - 1, at_x, owner_low(low)], values_land.at[at_z, at_x, owner_low(low)],
                values_send, values_recv, (s, in_line(away(dz, z, sign)), b),
            ).start()

    def take_near_keys(low):
        wait_for(keys_near[low], near_recv.at[low])

        def pack(at_s, k, slot):
            keys_packed[at_s * 2 + owner_low(low), 0, k] = keys_near[low][slot]

        each_slot(pack)

    def send_near_values():
        for dx, dy in PLANE[1] + PLANE[0]:
            send_plane(
                lambda to: values_packed.at[to, 0], dx, dy, values_land.at[0, *here_mid], mid_near, mid_near_recv
            )

    def send_near_keys():
        for dx, dy in PLANE[1] + PLANE[0]:
            send_plane(lambda to: keys_packed.at[to, 0], dx, dy, keys_land.at[here, 0], keys_send, keys_recv)

    def turn_keys(low):
        wait_for(keys_line[low], line_recv.at[low])

        def pack(at_s, k, slot):
            for dz in range(1, 4):
                keys_packed[at_s * 2 + owner_low(low), dz, k] = keys_line[low][dz - 1, slot]

        each_slot(pack)
        for dx, dy in PLANE[low]:
            send_plane(lambda to: keys_packed.at[to, far], dx, dy, keys_land.at[here, far], keys_send, keys_recv)

    scalars[0].wait()
    scalars[1].wait()
    lax.fori_loop(1, 8, send_small, 0)
    for n, (src, dst) in enumerate(small_pieces(s)):
        pltpu.make_async_copy(src, dst, small_recv.at[n]).start()
    for piece in range(len(PIECES)):
        take_values(piece)
    pltpu.make_async_copy(values_packed.at[here, 0], values_land.at[0, *here_mid], mid_near_recv).start()

    for n, part in enumerate(small_parts):
        wait_for(part.at[b], small_recv.at[n])
        remote(part.at[b], part.at[b], share_send.at[n], share_recv.at[n], (s, h, other)).start()
    for n, part in enumerate(small_parts):
        wait_for(part.at[other], share_recv.at[n])
    wait_for(key_columns, full_sem.at[0])
    wait_for(value_rows, full_sem.at[1])

    def spread_queries(at_s, carry):
        for t in range(2):
            rows = query_all[t, at_s].astype(F32)
            for g in range(GROUP):
                row = (g // 4) * 8 + t * 4 + g % 4
                for k in range(4):
                    query_rows[at_s * 4 + k, row : row + 1, :] = rows[k : k + 1, g * HD : g * HD + HD]
        return carry

    lax.fori_loop(0, 8, spread_queries, 0)

    def find_slot(at, carry):
        found = jnp.int32(0)
        for slot in range(32):
            found = jnp.where(slot_order[slot] == b * 16 + at, slot, found)
        slot_of[at] = found
        return carry

    lax.fori_loop(0, 16, find_slot, 0)

    lane = lax.broadcasted_iota(jnp.int32, (1, HD), 1)
    lane_prompt = lax.div(lane, 16)
    lane_later = lax.rem(lax.div(lane, 4), 2) == 1
    block_lane = lax.div(lax.broadcasted_iota(jnp.int32, (HD, HD), 1), 16)
    row4 = lax.broadcasted_iota(jnp.int32, (4, HD), 0)
    row512 = lax.broadcasted_iota(jnp.int32, (512, HD), 0)
    scale = HD ** -0.5

    def attend(first):
        slots = [slot_of[first + p] for p in range(8)]
        live = jnp.zeros((1, HD), jnp.int32)
        for p in range(8):
            live = jnp.where(lane_prompt == p, lengths[first + p + b * 16], live)

        def fresh_row(n, t, slot):
            rows = fresh_all[n, t, lax.div(slot, 4)].astype(F32)
            return jnp.sum(jnp.where(row4 == lax.rem(slot, 4), rows, 0.0), axis=0, keepdims=True)

        questions = jnp.concatenate([query_rows[slot] for slot in slots], axis=0).T
        diagonal = jnp.concatenate(
            [jnp.where(block_lane == p, questions, 0.0) for p in range(8)], axis=0
        ).astype(BF16)
        fresh_keys = jnp.concatenate(
            [
                jnp.concatenate([fresh_row(0, 0, slot), fresh_row(0, 1, slot), jnp.zeros((14, HD), F32)], axis=0)
                for slot in slots
            ],
            axis=1,
        ).astype(BF16)
        scores = jnp.dot(
            key_columns[:, first * HD : (first + 8) * HD], diagonal, preferred_element_type=F32
        ) * scale
        fresh_scores = jnp.dot(fresh_keys, diagonal, preferred_element_type=F32) * scale
        kept = row512 < live
        scores = jnp.where(kept, scores, HIDDEN)
        n0 = fresh_scores[0:1]
        n1 = jnp.where(lane_later, fresh_scores[1:2], HIDDEN)
        peak = jnp.maximum(jnp.max(scores, axis=0, keepdims=True), jnp.maximum(n0, n1))
        mass = jnp.where(kept, jnp.exp(scores - peak), 0.0)
        m0 = jnp.exp(n0 - peak)
        m1 = jnp.where(lane_later, jnp.exp(n1 - peak), 0.0)
        total = jnp.sum(mass, axis=0, keepdims=True) + m0 + m1
        weights = mass.T.astype(BF16)
        m0, m1 = (m.astype(BF16).astype(F32) for m in (m0, m1))
        sides = jnp.concatenate([total, m0, m1, jnp.zeros((HD - 3, HD), F32)], axis=0).T
        for p, slot in enumerate(slots):
            cut = slice(p * 16, p * 16 + 16)
            weighted = jnp.dot(weights[cut], value_rows[first + p], preferred_element_type=F32)
            weighted += sides[cut, 1:2] * fresh_row(1, 0, slot)
            weighted += sides[cut, 2:3] * fresh_row(1, 1, slot)
            result[first + p] = weighted / sides[cut, 0:1]

    attend(0)
    attend(8)

    def hand_rows(at_s, carry):
        for pair in range(2):
            first, second = (
                result[jnp.clip(slot_order[at_s * 4 + pair * 2 + n] - b * 16, 0, 15)] for n in range(2)
            )
            for to_b in range(2):
                cut = slice(to_b * 8, to_b * 8 + 8)
                rows_mine[to_b, at_s, pair] = jnp.concatenate((first[cut], second[cut]), axis=0).astype(BF16)
        return carry

    lax.fori_loop(0, 8, hand_rows, 0)

    swap_rows = remote(
        rows_mine.at[other], rows_swap, rows_swap_send, rows_swap_recv, (s, h, other)
    )
    swap_rows.start()
    upper = lax.broadcasted_iota(jnp.int32, (16, HD), 0) < 8

    def merge_rows(at_s, carry):
        for pair in range(2):
            first, second = (lax.div(slot_order[at_s * 4 + pair * 2 + n], 16) == b for n in range(2))
            ours = jnp.where(upper, jnp.where(first, 1.0, 0.0), jnp.where(second, 1.0, 0.0)) > 0.5
            rows_send[at_s, pair] = jnp.where(
                ours, rows_mine[b, at_s, pair].astype(F32), rows_swap[at_s, pair].astype(F32)
            ).astype(BF16)
        return carry

    swap_rows.wait_recv()
    lax.fori_loop(0, 8, merge_rows, 0)

    def send_rows(step, carry):
        to_s = lax.rem(s + step, 8)
        remote(rows_send.at[to_s], rows_land.at[s], rows_send_sem, rows_recv_sem, (to_s, h, b)).start()
        return carry

    lax.fori_loop(1, 8, send_rows, 0)
    pltpu.make_async_copy(rows_send.at[s], rows_land.at[s], rows_recv_sem).start()
    owned = [slot_order[s * 4 + k] for k in range(4)]
    lives = [lengths[slot] for slot in owned]
    first_position = (h * 2 + b) * BLOCK
    position = first_position + lax.broadcasted_iota(jnp.int32, (BLOCK, HD), 0)
    for k in range(4):
        keep[k] = jnp.where(position < lives[k], 1.0, 0.0).astype(BF16)
    fresh[0].wait()
    fresh[1].wait()

    def place_fresh(layer, carry):
        wide = first_position + lax.broadcasted_iota(jnp.int32, (BLOCK, KVH * HD), 0)
        for n, out in enumerate((keys_fresh, values_fresh)):
            new = [fresh_rows[n, t, layer].astype(F32) for t in range(2)]
            for k in range(4):
                rows = jnp.zeros((BLOCK, KVH * HD), F32)
                for t in range(2):
                    rows = jnp.where(wide == lives[k] + t, new[t][k : k + 1], rows)
                out[layer, k] = rows.astype(BF16)
        return carry

    lax.fori_loop(0, 8, place_fresh, 0)
    take_near_keys(1)
    take_near_keys(0)
    for piece in range(3):
        forward_values(piece)
    send_near_values()
    for piece in range(3, 6):
        forward_values(piece)
    send_near_keys()
    turn_keys(1)
    turn_keys(0)
    pltpu.make_async_copy(keys_packed.at[here], keys_land.at[here], keys_recv).start()

    def assemble(l, carry):
        picked = []
        for k in range(4):
            part = slice((k % 2) * 8, (k % 2) * 8 + 8)
            picked.append(rows_land[l, k // 2].astype(F32)[part])
        for t in range(2):
            attention[t, l] = jnp.concatenate(
                [
                    jnp.concatenate([rows[t * 4 + g : t * 4 + g + 1] for rows in picked], axis=0)
                    for g in range(4)
                ],
                axis=1,
            ).astype(BF16)
        return carry

    wait_for(rows_land, rows_recv_sem)
    lax.fori_loop(0, 8, assemble, 0)
    wait_for(values_land.at[0], mid_near_recv)
    wait_for(values_land.at[far], values_recv)
    wait_for(keys_land, keys_recv)

    wait_for(value_rows.at[pl.ds(0, 8)], chip_send)
    wait_for(value_rows.at[pl.ds(0, 14)], line_send)
    for n, part in enumerate(small_parts):
        wait_for(part.at[b, pl.ds(0, 7)], small_send.at[n])
        wait_for(part.at[b], share_send.at[n])
    swap_rows.wait_send()
    wait_for(values_packed.at[pl.ds(0, 15), far], mid_send)
    wait_for(values_packed.at[pl.ds(0, 15), 0], mid_near)
    wait_for(keys_packed.at[pl.ds(0, 15)], keys_send)
    wait_for(values_mid, values_send)
    wait_for(rows_send.at[pl.ds(0, 7)], rows_send_sem)


def hand_out(
    attention, keys_land, values_land, keys_fresh, values_fresh, keep,
    attention_out, keys_out, values_out, keys, values, sem,
):
    copies = [pltpu.make_async_copy(attention, attention_out, sem.at[16])]
    copies[0].start()
    kept = [keep[k] > 0 for k in range(4)]
    z = lax.div(lax.axis_index("head"), 2)
    for l in range(8):
        x, y_high = l // 2, l % 2
        for h in range(KVH):
            cut = slice(h * HD, h * HD + HD)
            from_z, y_low = h // 2, h % 2
            for k in range(4):
                landed = keys_land[x * 4 + y_high * 2 + y_low, lax.rem(from_z - z + 4, 4), k]
                keys[l, k, :, cut] = jnp.where(kept[k], landed, keys_fresh[l, k, :, cut])
                landed = values_land[lax.rem(z - from_z + 4, 4), x, y_low, y_high, k]
                values[l, k, :, cut] = jnp.where(kept[k], landed, values_fresh[l, k, :, cut])
        for n, (src, dst) in enumerate(((keys, keys_out), (values, values_out))):
            copies.append(pltpu.make_async_copy(src.at[l], dst.at[l], sem.at[n * 8 + l]))
            copies[-1].start()
    for copy in copies:
        copy.wait()


def body(keys_prefill, values_prefill, lengths, slot_order, queries, new_keys, new_values):
    keys = keys_prefill.reshape(16, 4, 2, 2, BLOCK, HD)
    values = values_prefill.reshape(16, 4, 2, 2, BLOCK, HD)
    flat = (keys_prefill.reshape(16, 512, HD), values_prefill.reshape(16, 512, HD))
    any_spec = pl.BlockSpec(memory_space=pl.ANY)
    hbm_spec = pl.BlockSpec(memory_space=pltpu.HBM)
    vmem_spec = pl.BlockSpec(memory_space=pltpu.VMEM)
    dma, vmem = pltpu.SemaphoreType.DMA, pltpu.VMEM
    rows_shape, cache_shape = (2, 8, 4, 4 * HD), (8, 4, BLOCK, KVH * HD)
    plane_shape, line_shape = (16, 4, 4, BLOCK, HD), (4, 4, 2, 2, 4, BLOCK, HD)

    def in_hbm(array):
        return pltpu.with_memory_space_constraint(array, pltpu.HBM)

    held = pl.pallas_call(
        relay,
        out_shape=tuple(
            vmem(shape, BF16) for shape in (rows_shape, plane_shape, line_shape, cache_shape, cache_shape, (4, BLOCK, HD))
        ),
        in_specs=[hbm_spec] * 9,
        out_specs=(vmem_spec,) * 6,
        scratch_shapes=[
            vmem((512, 16 * HD), BF16), vmem((16, 512, HD), BF16),
            [vmem((3, 32, BLOCK, HD), BF16)] * 2, [vmem((32, BLOCK, HD), BF16)] * 2,
            [vmem((32, BLOCK, HD), BF16)] * len(PIECES),
            vmem(plane_shape, BF16), vmem(plane_shape, BF16),
            vmem((3, *line_shape[1:]), BF16),
            vmem((2, 2, 8, 4, KVH * HD), BF16), vmem((2, 8, 4, GROUP * HD), BF16), vmem((32, 16, HD), F32),
            vmem((2, 2, 8, 4, HD), BF16), vmem((16, 16, HD), F32),
            vmem((2, 8, 2, 16, HD), BF16), vmem((8, 2, 16, HD), BF16),
            vmem((8, 2, 16, HD), BF16), vmem((8, 2, 16, HD), BF16),
            pltpu.SMEM((32,), jnp.int32), pltpu.SMEM((32,), jnp.int32), pltpu.SMEM((16,), jnp.int32),
            dma((2,)), dma((2,)), dma((2,)), dma, dma((2,)), dma((2,)), dma, dma((len(PIECES),)),
            dma, dma, dma, dma((6,)), dma, dma, dma, dma,
            dma((3,)), dma((3,)), dma((3,)), dma((3,)), dma, dma, dma, dma,
        ],
        compiler_params=pltpu.CompilerParams(
            collective_id=0, has_side_effects=True, vmem_limit_bytes=48 * 2**20
        ),
        name="relay",
    )(*(in_hbm(x) for x in (slot_order, lengths, keys, values, *flat, queries, new_keys, new_values)))
    return pl.pallas_call(
        hand_out,
        out_shape=tuple(jax.ShapeDtypeStruct(shape, BF16) for shape in (rows_shape, cache_shape, cache_shape)),
        in_specs=[vmem_spec] * 6,
        out_specs=(any_spec,) * 3,
        scratch_shapes=[vmem(cache_shape, BF16), vmem(cache_shape, BF16), dma((17,))],
        compiler_params=pltpu.CompilerParams(vmem_limit_bytes=8 * 2**20),
        name="hand_out",
    )(*(pltpu.with_memory_space_constraint(x, pltpu.VMEM) for x in held))


def solution(mesh):
    in_specs = (
        P("section", "batch", None, "head"),
        P("section", "batch", None, "head"),
        P(),
        P(),
        P(None, None, "section", None),
        P(None, None, "section", None),
        P(None, None, "section", None),
    )
    out_specs = (
        P(None, None, "section", ("head", "batch")),
        P(None, "section", ("head", "batch"), None),
        P(None, "section", ("head", "batch"), None),
    )
    return jax.shard_map(body, mesh=mesh, in_specs=in_specs, out_specs=out_specs, check_vma=False)
```

```python
import jax
import jax.numpy as jnp
from jax import lax
from jax.experimental import pallas as pl
from jax.experimental.pallas import tpu as pltpu
from jax.sharding import PartitionSpec as P

KVH = 8
HD = 128
GROUP = 8
BLOCK = 32
MESH = pl.DeviceIdType.MESH
HIDDEN = -1e30
BF16, F32 = jnp.bfloat16, jnp.float32


PLANE = {
    1: ((1, 1), (3, 3), (1, 3), (3, 1), (2, 1), (0, 3), (2, 3), (0, 1)),
    0: ((1, 0), (0, 2), (3, 2), (1, 2), (3, 0), (2, 2), (2, 0)),
}
PIECES = ((1, 1), (1, 3), (1, 2), (0, 1), (0, 3), (0, 2), (1, 0), (0, 0))


def relay(
    slot_order_hbm, lengths_hbm, keys, values, keys_flat, values_flat, queries, new_keys, new_values,
    attention, keys_land, values_land, keys_fresh, values_fresh, keep,
    key_columns, value_rows, keys_line, keys_near, values_chip, keys_packed, values_packed, values_mid,
    fresh_rows, query_all, query_rows, fresh_all, result, rows_mine, rows_swap, rows_send, rows_land,
    slot_order, lengths, slot_of,
    scalar_sem, full_sem, fresh_sem, line_send, line_recv, near_recv, chip_send, chip_recv,
    keys_send, keys_recv, mid_send, mid_recv, mid_near, mid_near_recv, values_send, values_recv,
    small_send, small_recv, share_send, share_recv, rows_swap_send, rows_swap_recv, rows_send_sem, rows_recv_sem,
):
    s, h, b = lax.axis_index("section"), lax.axis_index("head"), lax.axis_index("batch")
    x, z = lax.div(s, 2), lax.div(h, 2)
    y_low = lax.rem(h, 2)
    y = lax.rem(s, 2) * 2 + y_low
    other = 1 - b
    sign = 1 - 2 * b
    mine = pl.ds(b * 16, 16)
    here = x * 4 + y
    here_mid = (x, y_low, lax.div(y, 2))

    def remote(src, dst, send_sem, recv_sem, to):
        return pltpu.make_async_remote_copy(
            src_ref=src, dst_ref=dst, send_sem=send_sem, recv_sem=recv_sem,
            device_id=to, device_id_type=MESH,
        )

    def wait_for(ref, sem):
        pltpu.make_async_copy(ref, ref, sem).wait()

    def away(d, at, way):
        return lax.rem(at + way * d + 4, 4)

    def in_plane(at_x, at_y):
        return at_x * 2 + lax.div(at_y, 2), z * 2 + lax.rem(at_y, 2)

    def in_line(at_z):
        return at_z * 2 + y_low

    def owner_low(low):
        return lax.rem(y_low + low, 2)

    barrier = pltpu.get_barrier_semaphore()

    def greet(to):
        pl.semaphore_signal(barrier, inc=1, device_id=to, device_id_type=MESH)

    for dz in range(4):
        at_h = in_line(away(dz, z, 1))
        greet((s, at_h, other))
        if dz:
            greet((s, at_h, b))
    for low in (1, 0):
        for dx, dy in PLANE[low]:
            at_s, at_h = in_plane(away(dx, x, 1), away(dy, y, 1))
            greet((at_s, at_h, b))

    scalars = [
        pltpu.make_async_copy(slot_order_hbm, slot_order, scalar_sem.at[0]),
        pltpu.make_async_copy(lengths_hbm, lengths, scalar_sem.at[1]),
    ]
    whole = [
        pltpu.make_async_copy(keys_flat.at[at], key_columns.at[:, pl.ds(at * HD, HD)], full_sem.at[0])
        for at in range(16)
    ]
    whole.append(pltpu.make_async_copy(values_flat, value_rows, full_sem.at[1]))
    fresh = [
        pltpu.make_async_copy(src, fresh_rows.at[n], fresh_sem.at[n])
        for n, src in enumerate((new_keys, new_values))
    ]
    for copy in scalars:
        copy.start()
    def own_piece(piece):
        low, dz = PIECES[piece]
        pltpu.make_async_copy(
            values.at[:, away(dz, z, sign), owner_low(low), b], values_chip[piece].at[mine], chip_recv.at[piece]
        ).start()

    own_piece(0)
    own_piece(1)
    pl.semaphore_wait(barrier, 22)

    def swap(piece):
        low, dz = PIECES[piece]
        remote(
            values.at[:, away(dz, z, -sign), owner_low(low), other], values_chip[piece].at[mine],
            chip_send, chip_recv.at[piece], (s, h, other),
        ).start()

    swap(0)
    swap(1)

    def send_line(low, dz, to_b):
        to_z = away(dz, z, sign)
        d = away(dz, 0, sign)
        remote(
            keys.at[:, to_z, owner_low(low), to_b], keys_line[low].at[3 - d, mine],
            line_send, line_recv.at[low], (s, in_line(to_z), to_b),
        ).start()

    for low in (1, 0):
        for dz, to_b in ((1, b), (3, other), (2, b), (1, other), (3, b), (2, other)):
            send_line(low, dz, to_b)
    for low in (1, 0):
        remote(
            keys.at[:, z, owner_low(low), other], keys_near[low].at[mine],
            line_send, near_recv.at[low], (s, h, other),
        ).start()

    for piece in range(2, len(PIECES)):
        own_piece(piece)

    head_rows = pl.ds(pl.multiple_of(h * GROUP * HD, GROUP * HD), GROUP * HD)
    head_cols = pl.ds(pl.multiple_of(h * HD, HD), HD)

    def small_pieces(to_s):
        return (
            (queries.at[b, to_s, :, head_rows], query_all.at[b, s]),
            (new_keys.at[b, to_s, :, head_cols], fresh_all.at[0, b, s]),
            (new_values.at[b, to_s, :, head_cols], fresh_all.at[1, b, s]),
        )

    small_parts = (query_all, fresh_all.at[0], fresh_all.at[1])

    def send_small(step, carry):
        to_s = lax.rem(s + step, 8)
        for n, (src, dst) in enumerate(small_pieces(to_s)):
            remote(src, dst, small_send.at[n], small_recv.at[n], (to_s, h, b)).start()
        return carry

    def each_slot(do):
        def step(at_s, carry):
            for k in range(4):
                do(at_s, k, slot_order[at_s * 4 + k])
            return carry

        lax.fori_loop(0, 8, step, 0)

    def send_plane(src, dx, dy, dst, send_sem, recv_sem):
        to_x, to_y = away(dx, x, sign), away(dy, y, sign)
        to_s, to_h = in_plane(to_x, to_y)
        remote(src(to_x * 4 + to_y), dst, send_sem, recv_sem, (to_s, to_h, b)).start()

    def take_values(piece):
        low, dz = PIECES[piece]
        at_z = away(dz, 0, sign)
        wait_for(values_chip[piece], chip_recv.at[piece])
        if piece + 2 < len(PIECES):
            swap(piece + 2)

        def pack(at_s, k, slot):
            values_packed[at_s * 2 + owner_low(low), at_z, k] = values_chip[piece][slot]

        each_slot(pack)
        if dz:
            for dx, dy in PLANE[low]:
                send_plane(
                    lambda to: values_packed.at[to, at_z], dx, dy, values_mid.at[at_z - 1, *here_mid],
                    mid_send, mid_recv.at[piece],
                )
            if low == 0:
                pltpu.make_async_copy(
                    values_packed.at[here, at_z], values_mid.at[at_z - 1, *here_mid], mid_recv.at[piece]
                ).start()

    far = pl.ds(1, 3)

    def forward_values(piece):
        low, dz = PIECES[piece]
        at_z = away(dz, 0, sign)
        wait_for(values_mid.at[0, :, 0], mid_recv.at[piece])
        for at_x in range(4):
            remote(
                values_mid.at[at_z - 1, at_x, owner_low(low)], values_land.at[at_z, at_x, owner_low(low)],
                values_send, values_recv, (s, in_line(away(dz, z, sign)), b),
            ).start()

    def take_near_keys(low):
        wait_for(keys_near[low], near_recv.at[low])

        def pack(at_s, k, slot):
            keys_packed[at_s * 2 + owner_low(low), 0, k] = keys_near[low][slot]

        each_slot(pack)

    def send_near_values():
        for dx, dy in PLANE[1] + PLANE[0]:
            send_plane(
                lambda to: values_packed.at[to, 0], dx, dy, values_land.at[0, *here_mid], mid_near, mid_near_recv
            )

    def send_near_keys():
        for dx, dy in PLANE[1] + PLANE[0]:
            send_plane(lambda to: keys_packed.at[to, 0], dx, dy, keys_land.at[here, 0], keys_send, keys_recv)

    def turn_keys(low):
        wait_for(keys_line[low], line_recv.at[low])

        def pack(at_s, k, slot):
            for dz in range(1, 4):
                keys_packed[at_s * 2 + owner_low(low), dz, k] = keys_line[low][dz - 1, slot]

        each_slot(pack)
        for dx, dy in PLANE[low]:
            send_plane(lambda to: keys_packed.at[to, far], dx, dy, keys_land.at[here, far], keys_send, keys_recv)

    scalars[0].wait()
    scalars[1].wait()
    lax.fori_loop(1, 8, send_small, 0)
    for n, (src, dst) in enumerate(small_pieces(s)):
        pltpu.make_async_copy(src, dst, small_recv.at[n]).start()
    for piece in range(2):
        take_values(piece)
    for low in (1, 0):
        pltpu.make_async_copy(
            keys.at[:, z, owner_low(low), b], keys_near[low].at[mine], near_recv.at[low]
        ).start()
    for copy in whole + fresh:
        copy.start()
    for piece in range(2, len(PIECES)):
        take_values(piece)
    pltpu.make_async_copy(values_packed.at[here, 0], values_land.at[0, *here_mid], mid_near_recv).start()

    for n, part in enumerate(small_parts):
        wait_for(part.at[b], small_recv.at[n])
        remote(part.at[b], part.at[b], share_send.at[n], share_recv.at[n], (s, h, other)).start()
    for n, part in enumerate(small_parts):
        wait_for(part.at[other], share_recv.at[n])
    wait_for(key_columns, full_sem.at[0])
    wait_for(value_rows, full_sem.at[1])

    def spread_queries(at_s, carry):
        for t in range(2):
            rows = query_all[t, at_s].astype(F32)
            for g in range(GROUP):
                row = (g // 4) * 8 + t * 4 + g % 4
                for k in range(4):
                    query_rows[at_s * 4 + k, row : row + 1, :] = rows[k : k + 1, g * HD : g * HD + HD]
        return carry

    lax.fori_loop(0, 8, spread_queries, 0)

    def find_slot(at, carry):
        found = jnp.int32(0)
        for slot in range(32):
            found = jnp.where(slot_order[slot] == b * 16 + at, slot, found)
        slot_of[at] = found
        return carry

    lax.fori_loop(0, 16, find_slot, 0)

    lane = lax.broadcasted_iota(jnp.int32, (1, HD), 1)
    lane_prompt = lax.div(lane, 16)
    lane_later = lax.rem(lax.div(lane, 4), 2) == 1
    block_lane = lax.div(lax.broadcasted_iota(jnp.int32, (HD, HD), 1), 16)
    row4 = lax.broadcasted_iota(jnp.int32, (4, HD), 0)
    row512 = lax.broadcasted_iota(jnp.int32, (512, HD), 0)
    scale = HD ** -0.5

    def attend(first):
        slots = [slot_of[first + p] for p in range(8)]
        live = jnp.zeros((1, HD), jnp.int32)
        for p in range(8):
            live = jnp.where(lane_prompt == p, lengths[first + p + b * 16], live)

        def fresh_row(n, t, slot):
            rows = fresh_all[n, t, lax.div(slot, 4)].astype(F32)
            return jnp.sum(jnp.where(row4 == lax.rem(slot, 4), rows, 0.0), axis=0, keepdims=True)

        questions = jnp.concatenate([query_rows[slot] for slot in slots], axis=0).T
        diagonal = jnp.concatenate(
            [jnp.where(block_lane == p, questions, 0.0) for p in range(8)], axis=0
        ).astype(BF16)
        fresh_keys = jnp.concatenate(
            [
                jnp.concatenate([fresh_row(0, 0, slot), fresh_row(0, 1, slot), jnp.zeros((14, HD), F32)], axis=0)
                for slot in slots
            ],
            axis=1,
        ).astype(BF16)
        scores = jnp.dot(
            key_columns[:, first * HD : (first + 8) * HD], diagonal, preferred_element_type=F32
        ) * scale
        fresh_scores = jnp.dot(fresh_keys, diagonal, preferred_element_type=F32) * scale
        kept = row512 < live
        scores = jnp.where(kept, scores, HIDDEN)
        n0 = fresh_scores[0:1]
        n1 = jnp.where(lane_later, fresh_scores[1:2], HIDDEN)
        peak = jnp.maximum(jnp.max(scores, axis=0, keepdims=True), jnp.maximum(n0, n1))
        mass = jnp.where(kept, jnp.exp(scores - peak), 0.0)
        m0 = jnp.exp(n0 - peak)
        m1 = jnp.where(lane_later, jnp.exp(n1 - peak), 0.0)
        total = jnp.sum(mass, axis=0, keepdims=True) + m0 + m1
        weights = mass.T.astype(BF16)
        m0, m1 = (m.astype(BF16).astype(F32) for m in (m0, m1))
        sides = jnp.concatenate([total, m0, m1, jnp.zeros((HD - 3, HD), F32)], axis=0).T
        for p, slot in enumerate(slots):
            cut = slice(p * 16, p * 16 + 16)
            weighted = jnp.dot(weights[cut], value_rows[first + p], preferred_element_type=F32)
            weighted += sides[cut, 1:2] * fresh_row(1, 0, slot)
            weighted += sides[cut, 2:3] * fresh_row(1, 1, slot)
            result[first + p] = weighted / sides[cut, 0:1]

    attend(0)
    attend(8)

    def hand_rows(at_s, carry):
        for pair in range(2):
            first, second = (
                result[jnp.clip(slot_order[at_s * 4 + pair * 2 + n] - b * 16, 0, 15)] for n in range(2)
            )
            for to_b in range(2):
                cut = slice(to_b * 8, to_b * 8 + 8)
                rows_mine[to_b, at_s, pair] = jnp.concatenate((first[cut], second[cut]), axis=0).astype(BF16)
        return carry

    lax.fori_loop(0, 8, hand_rows, 0)

    swap_rows = remote(
        rows_mine.at[other], rows_swap, rows_swap_send, rows_swap_recv, (s, h, other)
    )
    swap_rows.start()
    upper = lax.broadcasted_iota(jnp.int32, (16, HD), 0) < 8

    def merge_rows(at_s, carry):
        for pair in range(2):
            first, second = (lax.div(slot_order[at_s * 4 + pair * 2 + n], 16) == b for n in range(2))
            ours = jnp.where(upper, jnp.where(first, 1.0, 0.0), jnp.where(second, 1.0, 0.0)) > 0.5
            rows_send[at_s, pair] = jnp.where(
                ours, rows_mine[b, at_s, pair].astype(F32), rows_swap[at_s, pair].astype(F32)
            ).astype(BF16)
        return carry

    swap_rows.wait_recv()
    lax.fori_loop(0, 8, merge_rows, 0)

    def send_rows(step, carry):
        to_s = lax.rem(s + step, 8)
        remote(rows_send.at[to_s], rows_land.at[s], rows_send_sem, rows_recv_sem, (to_s, h, b)).start()
        return carry

    lax.fori_loop(1, 8, send_rows, 0)
    pltpu.make_async_copy(rows_send.at[s], rows_land.at[s], rows_recv_sem).start()
    owned = [slot_order[s * 4 + k] for k in range(4)]
    lives = [lengths[slot] for slot in owned]
    first_position = (h * 2 + b) * BLOCK
    position = first_position + lax.broadcasted_iota(jnp.int32, (BLOCK, HD), 0)
    for k in range(4):
        keep[k] = jnp.where(position < lives[k], 1.0, 0.0).astype(BF16)
    fresh[0].wait()
    fresh[1].wait()

    def place_fresh(layer, carry):
        wide = first_position + lax.broadcasted_iota(jnp.int32, (BLOCK, KVH * HD), 0)
        for n, out in enumerate((keys_fresh, values_fresh)):
            new = [fresh_rows[n, t, layer].astype(F32) for t in range(2)]
            for k in range(4):
                rows = jnp.zeros((BLOCK, KVH * HD), F32)
                for t in range(2):
                    rows = jnp.where(wide == lives[k] + t, new[t][k : k + 1], rows)
                out[layer, k] = rows.astype(BF16)
        return carry

    lax.fori_loop(0, 8, place_fresh, 0)
    take_near_keys(1)
    take_near_keys(0)
    for piece in range(3):
        forward_values(piece)
    send_near_values()
    for piece in range(3, 6):
        forward_values(piece)
    send_near_keys()
    turn_keys(1)
    turn_keys(0)
    pltpu.make_async_copy(keys_packed.at[here], keys_land.at[here], keys_recv).start()

    def assemble(l, carry):
        picked = []
        for k in range(4):
            part = slice((k % 2) * 8, (k % 2) * 8 + 8)
            picked.append(rows_land[l, k // 2].astype(F32)[part])
        for t in range(2):
            attention[t, l] = jnp.concatenate(
                [
                    jnp.concatenate([rows[t * 4 + g : t * 4 + g + 1] for rows in picked], axis=0)
                    for g in range(4)
                ],
                axis=1,
            ).astype(BF16)
        return carry

    wait_for(rows_land, rows_recv_sem)
    lax.fori_loop(0, 8, assemble, 0)
    wait_for(values_land.at[0], mid_near_recv)
    wait_for(values_land.at[far], values_recv)
    wait_for(keys_land, keys_recv)

    wait_for(value_rows.at[pl.ds(0, 8)], chip_send)
    wait_for(value_rows.at[pl.ds(0, 14)], line_send)
    for n, part in enumerate(small_parts):
        wait_for(part.at[b, pl.ds(0, 7)], small_send.at[n])
        wait_for(part.at[b], share_send.at[n])
    swap_rows.wait_send()
    wait_for(values_packed.at[pl.ds(0, 15), far], mid_send)
    wait_for(values_packed.at[pl.ds(0, 15), 0], mid_near)
    wait_for(keys_packed.at[pl.ds(0, 15)], keys_send)
    wait_for(values_mid, values_send)
    wait_for(rows_send.at[pl.ds(0, 7)], rows_send_sem)


def hand_out(
    attention, keys_land, values_land, keys_fresh, values_fresh, keep,
    attention_out, keys_out, values_out, keys, values, sem,
):
    copies = [pltpu.make_async_copy(attention, attention_out, sem.at[16])]
    copies[0].start()
    kept = [keep[k] > 0 for k in range(4)]
    z = lax.div(lax.axis_index("head"), 2)
    for l in range(8):
        x, y_high = l // 2, l % 2
        for h in range(KVH):
            cut = slice(h * HD, h * HD + HD)
            from_z, y_low = h // 2, h % 2
            for k in range(4):
                landed = keys_land[x * 4 + y_high * 2 + y_low, lax.rem(from_z - z + 4, 4), k]
                keys[l, k, :, cut] = jnp.where(kept[k], landed, keys_fresh[l, k, :, cut])
                landed = values_land[lax.rem(z - from_z + 4, 4), x, y_low, y_high, k]
                values[l, k, :, cut] = jnp.where(kept[k], landed, values_fresh[l, k, :, cut])
        for n, (src, dst) in enumerate(((keys, keys_out), (values, values_out))):
            copies.append(pltpu.make_async_copy(src.at[l], dst.at[l], sem.at[n * 8 + l]))
            copies[-1].start()
    for copy in copies:
        copy.wait()


def body(keys_prefill, values_prefill, lengths, slot_order, queries, new_keys, new_values):
    keys = keys_prefill.reshape(16, 4, 2, 2, BLOCK, HD)
    values = values_prefill.reshape(16, 4, 2, 2, BLOCK, HD)
    flat = (keys_prefill.reshape(16, 512, HD), values_prefill.reshape(16, 512, HD))
    any_spec = pl.BlockSpec(memory_space=pl.ANY)
    hbm_spec = pl.BlockSpec(memory_space=pltpu.HBM)
    vmem_spec = pl.BlockSpec(memory_space=pltpu.VMEM)
    dma, vmem = pltpu.SemaphoreType.DMA, pltpu.VMEM
    rows_shape, cache_shape = (2, 8, 4, 4 * HD), (8, 4, BLOCK, KVH * HD)
    plane_shape, line_shape = (16, 4, 4, BLOCK, HD), (4, 4, 2, 2, 4, BLOCK, HD)

    def in_hbm(array):
        return pltpu.with_memory_space_constraint(array, pltpu.HBM)

    held = pl.pallas_call(
        relay,
        out_shape=tuple(
            vmem(shape, BF16) for shape in (rows_shape, plane_shape, line_shape, cache_shape, cache_shape, (4, BLOCK, HD))
        ),
        in_specs=[hbm_spec] * 9,
        out_specs=(vmem_spec,) * 6,
        scratch_shapes=[
            vmem((512, 16 * HD), BF16), vmem((16, 512, HD), BF16),
            [vmem((3, 32, BLOCK, HD), BF16)] * 2, [vmem((32, BLOCK, HD), BF16)] * 2,
            [vmem((32, BLOCK, HD), BF16)] * len(PIECES),
            vmem(plane_shape, BF16), vmem(plane_shape, BF16),
            vmem((3, *line_shape[1:]), BF16),
            vmem((2, 2, 8, 4, KVH * HD), BF16), vmem((2, 8, 4, GROUP * HD), BF16), vmem((32, 16, HD), F32),
            vmem((2, 2, 8, 4, HD), BF16), vmem((16, 16, HD), F32),
            vmem((2, 8, 2, 16, HD), BF16), vmem((8, 2, 16, HD), BF16),
            vmem((8, 2, 16, HD), BF16), vmem((8, 2, 16, HD), BF16),
            pltpu.SMEM((32,), jnp.int32), pltpu.SMEM((32,), jnp.int32), pltpu.SMEM((16,), jnp.int32),
            dma((2,)), dma((2,)), dma((2,)), dma, dma((2,)), dma((2,)), dma, dma((len(PIECES),)),
            dma, dma, dma, dma((6,)), dma, dma, dma, dma,
            dma((3,)), dma((3,)), dma((3,)), dma((3,)), dma, dma, dma, dma,
        ],
        compiler_params=pltpu.CompilerParams(
            collective_id=0, has_side_effects=True, vmem_limit_bytes=48 * 2**20
        ),
        name="relay",
    )(*(in_hbm(x) for x in (slot_order, lengths, keys, values, *flat, queries, new_keys, new_values)))
    return pl.pallas_call(
        hand_out,
        out_shape=tuple(jax.ShapeDtypeStruct(shape, BF16) for shape in (rows_shape, cache_shape, cache_shape)),
        in_specs=[vmem_spec] * 6,
        out_specs=(any_spec,) * 3,
        scratch_shapes=[vmem(cache_shape, BF16), vmem(cache_shape, BF16), dma((17,))],
        compiler_params=pltpu.CompilerParams(vmem_limit_bytes=8 * 2**20),
        name="hand_out",
    )(*(pltpu.with_memory_space_constraint(x, pltpu.VMEM) for x in held))


def solution(mesh):
    in_specs = (
        P("section", "batch", None, "head"),
        P("section", "batch", None, "head"),
        P(),
        P(),
        P(None, None, "section", None),
        P(None, None, "section", None),
        P(None, None, "section", None),
    )
    out_specs = (
        P(None, None, "section", ("head", "batch")),
        P(None, "section", ("head", "batch"), None),
        P(None, "section", ("head", "batch"), None),
    )
    return jax.shard_map(body, mesh=mesh, in_specs=in_specs, out_specs=out_specs, check_vma=False)
```

```python
import jax
import jax.numpy as jnp
from jax import lax
from jax.experimental import pallas as pl
from jax.experimental.pallas import tpu as pltpu
from jax.sharding import PartitionSpec as P

KVH = 8
HD = 128
GROUP = 8
BLOCK = 32
MESH = pl.DeviceIdType.MESH
HIDDEN = -1e30
BF16, F32 = jnp.bfloat16, jnp.float32


PLANE = {
    1: ((1, 1), (3, 3), (1, 3), (3, 1), (2, 1), (0, 3), (2, 3), (0, 1)),
    0: ((1, 0), (0, 2), (3, 2), (1, 2), (3, 0), (2, 2), (2, 0)),
}
PIECES = ((1, 1), (1, 3), (1, 2), (0, 1), (0, 3), (0, 2), (1, 0), (0, 0))


def relay(
    slot_order_hbm, lengths_hbm, keys, values, keys_flat, values_flat, queries, new_keys, new_values,
    attention, keys_land, values_land, keys_fresh, values_fresh, keep,
    key_columns, value_rows, keys_line, keys_near, values_chip, keys_packed, values_packed, values_mid,
    fresh_rows, query_all, query_rows, fresh_all, result, rows_mine, rows_swap, rows_send, rows_land,
    slot_order, lengths, slot_of,
    scalar_sem, full_sem, fresh_sem, line_send, line_recv, near_recv, chip_send, chip_recv,
    keys_send, keys_recv, mid_send, mid_recv, mid_near, mid_near_recv, values_send, values_recv,
    small_send, small_recv, share_send, share_recv, rows_swap_send, rows_swap_recv, rows_send_sem, rows_recv_sem,
):
    s, h, b = lax.axis_index("section"), lax.axis_index("head"), lax.axis_index("batch")
    x, z = lax.div(s, 2), lax.div(h, 2)
    y_low = lax.rem(h, 2)
    y = lax.rem(s, 2) * 2 + y_low
    other = 1 - b
    sign = 1 - 2 * b
    mine = pl.ds(b * 16, 16)
    here = x * 4 + y
    here_mid = (x, y_low, lax.div(y, 2))

    def remote(src, dst, send_sem, recv_sem, to):
        return pltpu.make_async_remote_copy(
            src_ref=src, dst_ref=dst, send_sem=send_sem, recv_sem=recv_sem,
            device_id=to, device_id_type=MESH,
        )

    def wait_for(ref, sem):
        pltpu.make_async_copy(ref, ref, sem).wait()

    def away(d, at, way):
        return lax.rem(at + way * d + 4, 4)

    def in_plane(at_x, at_y):
        return at_x * 2 + lax.div(at_y, 2), z * 2 + lax.rem(at_y, 2)

    def in_line(at_z):
        return at_z * 2 + y_low

    def owner_low(low):
        return lax.rem(y_low + low, 2)

    barrier = pltpu.get_barrier_semaphore()

    def greet(to):
        pl.semaphore_signal(barrier, inc=1, device_id=to, device_id_type=MESH)

    for dz in range(4):
        at_h = in_line(away(dz, z, 1))
        greet((s, at_h, other))
        if dz:
            greet((s, at_h, b))
    for low in (1, 0):
        for dx, dy in PLANE[low]:
            at_s, at_h = in_plane(away(dx, x, 1), away(dy, y, 1))
            greet((at_s, at_h, b))

    scalars = [
        pltpu.make_async_copy(slot_order_hbm, slot_order, scalar_sem.at[0]),
        pltpu.make_async_copy(lengths_hbm, lengths, scalar_sem.at[1]),
    ]
    whole = [
        pltpu.make_async_copy(keys_flat.at[at], key_columns.at[:, pl.ds(at * HD, HD)], full_sem.at[0])
        for at in range(16)
    ]
    whole.append(pltpu.make_async_copy(values_flat, value_rows, full_sem.at[1]))
    fresh = [
        pltpu.make_async_copy(src, fresh_rows.at[n], fresh_sem.at[n])
        for n, src in enumerate((new_keys, new_values))
    ]
    for copy in scalars:
        copy.start()
    for piece, (low, dz) in enumerate(PIECES):
        pltpu.make_async_copy(
            values.at[:, away(dz, z, sign), owner_low(low), b], values_chip[piece].at[mine], chip_recv.at[piece]
        ).start()
    for low in (1, 0):
        pltpu.make_async_copy(
            keys.at[:, z, owner_low(low), b], keys_near[low].at[mine], near_recv.at[low]
        ).start()
    for copy in whole + fresh:
        copy.start()
    pl.semaphore_wait(barrier, 22)

    def swap(piece):
        low, dz = PIECES[piece]
        remote(
            values.at[:, away(dz, z, -sign), owner_low(low), other], values_chip[piece].at[mine],
            chip_send, chip_recv.at[piece], (s, h, other),
        ).start()

    swap(0)
    swap(1)

    def send_line(low, dz, to_b):
        to_z = away(dz, z, sign)
        d = away(dz, 0, sign)
        remote(
            keys.at[:, to_z, owner_low(low), to_b], keys_line[low].at[3 - d, mine],
            line_send, line_recv.at[low], (s, in_line(to_z), to_b),
        ).start()

    for low in (1, 0):
        for dz, to_b in ((1, b), (3, other), (2, b), (1, other), (3, b), (2, other)):
            send_line(low, dz, to_b)
    for low in (1, 0):
        remote(
            keys.at[:, z, owner_low(low), other], keys_near[low].at[mine],
            line_send, near_recv.at[low], (s, h, other),
        ).start()

    head_rows = pl.ds(pl.multiple_of(h * GROUP * HD, GROUP * HD), GROUP * HD)
    head_cols = pl.ds(pl.multiple_of(h * HD, HD), HD)

    def small_pieces(to_s):
        return (
            (queries.at[b, to_s, :, head_rows], query_all.at[b, s]),
            (new_keys.at[b, to_s, :, head_cols], fresh_all.at[0, b, s]),
            (new_values.at[b, to_s, :, head_cols], fresh_all.at[1, b, s]),
        )

    small_parts = (query_all, fresh_all.at[0], fresh_all.at[1])

    def send_small(step, carry):
        to_s = lax.rem(s + step, 8)
        for n, (src, dst) in enumerate(small_pieces(to_s)):
            remote(src, dst, small_send.at[n], small_recv.at[n], (to_s, h, b)).start()
        return carry

    def each_slot(do):
        def step(at_s, carry):
            for k in range(4):
                do(at_s, k, slot_order[at_s * 4 + k])
            return carry

        lax.fori_loop(0, 8, step, 0)

    def send_plane(src, dx, dy, dst, send_sem, recv_sem):
        to_x, to_y = away(dx, x, sign), away(dy, y, sign)
        to_s, to_h = in_plane(to_x, to_y)
        remote(src(to_x * 4 + to_y), dst, send_sem, recv_sem, (to_s, to_h, b)).start()

    def take_values(piece):
        low, dz = PIECES[piece]
        at_z = away(dz, 0, sign)
        wait_for(values_chip[piece], chip_recv.at[piece])
        if piece + 2 < len(PIECES):
            swap(piece + 2)

        def pack(at_s, k, slot):
            values_packed[at_s * 2 + owner_low(low), at_z, k] = values_chip[piece][slot]

        each_slot(pack)
        if dz:
            for dx, dy in PLANE[low]:
                send_plane(
                    lambda to: values_packed.at[to, at_z], dx, dy, values_mid.at[at_z - 1, *here_mid],
                    mid_send, mid_recv.at[piece],
                )
            if low == 0:
                pltpu.make_async_copy(
                    values_packed.at[here, at_z], values_mid.at[at_z - 1, *here_mid], mid_recv.at[piece]
                ).start()

    far = pl.ds(1, 3)

    def forward_values(piece):
        low, dz = PIECES[piece]
        at_z = away(dz, 0, sign)
        wait_for(values_mid.at[0, :, 0], mid_recv.at[piece])
        for at_x in range(4):
            remote(
                values_mid.at[at_z - 1, at_x, owner_low(low)], values_land.at[at_z, at_x, owner_low(low)],
                values_send, values_recv, (s, in_line(away(dz, z, sign)), b),
            ).start()

    def take_near_keys(low):
        wait_for(keys_near[low], near_recv.at[low])

        def pack(at_s, k, slot):
            keys_packed[at_s * 2 + owner_low(low), 0, k] = keys_near[low][slot]

        each_slot(pack)

    def send_near_values():
        for dx, dy in PLANE[1] + PLANE[0]:
            send_plane(
                lambda to: values_packed.at[to, 0], dx, dy, values_land.at[0, *here_mid], mid_near, mid_near_recv
            )

    def send_near_keys():
        for dx, dy in PLANE[1] + PLANE[0]:
            send_plane(lambda to: keys_packed.at[to, 0], dx, dy, keys_land.at[here, 0], keys_send, keys_recv)

    def turn_keys(low):
        wait_for(keys_line[low], line_recv.at[low])

        def pack(at_s, k, slot):
            for dz in range(1, 4):
                keys_packed[at_s * 2 + owner_low(low), dz, k] = keys_line[low][dz - 1, slot]

        each_slot(pack)
        for dx, dy in PLANE[low]:
            send_plane(lambda to: keys_packed.at[to, far], dx, dy, keys_land.at[here, far], keys_send, keys_recv)

    scalars[0].wait()
    scalars[1].wait()
    lax.fori_loop(1, 8, send_small, 0)
    for n, (src, dst) in enumerate(small_pieces(s)):
        pltpu.make_async_copy(src, dst, small_recv.at[n]).start()
    for piece in range(len(PIECES)):
        take_values(piece)
    pltpu.make_async_copy(values_packed.at[here, 0], values_land.at[0, *here_mid], mid_near_recv).start()

    for n, part in enumerate(small_parts):
        wait_for(part.at[b], small_recv.at[n])
        remote(part.at[b], part.at[b], share_send.at[n], share_recv.at[n], (s, h, other)).start()
    for n, part in enumerate(small_parts):
        wait_for(part.at[other], share_recv.at[n])
    wait_for(key_columns, full_sem.at[0])
    wait_for(value_rows, full_sem.at[1])

    def spread_queries(at_s, carry):
        for t in range(2):
            rows = query_all[t, at_s].astype(F32)
            for g in range(GROUP):
                row = (g // 4) * 8 + t * 4 + g % 4
                for k in range(4):
                    query_rows[at_s * 4 + k, row : row + 1, :] = rows[k : k + 1, g * HD : g * HD + HD]
        return carry

    lax.fori_loop(0, 8, spread_queries, 0)

    def find_slot(at, carry):
        found = jnp.int32(0)
        for slot in range(32):
            found = jnp.where(slot_order[slot] == b * 16 + at, slot, found)
        slot_of[at] = found
        return carry

    lax.fori_loop(0, 16, find_slot, 0)

    lane = lax.broadcasted_iota(jnp.int32, (1, HD), 1)
    lane_prompt = lax.div(lane, 16)
    lane_later = lax.rem(lax.div(lane, 4), 2) == 1
    block_lane = lax.div(lax.broadcasted_iota(jnp.int32, (HD, HD), 1), 16)
    row4 = lax.broadcasted_iota(jnp.int32, (4, HD), 0)
    row512 = lax.broadcasted_iota(jnp.int32, (512, HD), 0)
    scale = HD ** -0.5

    def attend(first):
        slots = [slot_of[first + p] for p in range(8)]
        live = jnp.zeros((1, HD), jnp.int32)
        for p in range(8):
            live = jnp.where(lane_prompt == p, lengths[first + p + b * 16], live)

        def fresh_row(n, t, slot):
            rows = fresh_all[n, t, lax.div(slot, 4)].astype(F32)
            return jnp.sum(jnp.where(row4 == lax.rem(slot, 4), rows, 0.0), axis=0, keepdims=True)

        questions = jnp.concatenate([query_rows[slot] for slot in slots], axis=0).T
        diagonal = jnp.concatenate(
            [jnp.where(block_lane == p, questions, 0.0) for p in range(8)], axis=0
        ).astype(BF16)
        fresh_keys = jnp.concatenate(
            [
                jnp.concatenate([fresh_row(0, 0, slot), fresh_row(0, 1, slot), jnp.zeros((14, HD), F32)], axis=0)
                for slot in slots
            ],
            axis=1,
        ).astype(BF16)
        scores = jnp.dot(
            key_columns[:, first * HD : (first + 8) * HD], diagonal, preferred_element_type=F32
        ) * scale
        fresh_scores = jnp.dot(fresh_keys, diagonal, preferred_element_type=F32) * scale
        kept = row512 < live
        scores = jnp.where(kept, scores, HIDDEN)
        n0 = fresh_scores[0:1]
        n1 = jnp.where(lane_later, fresh_scores[1:2], HIDDEN)
        peak = jnp.maximum(jnp.max(scores, axis=0, keepdims=True), jnp.maximum(n0, n1))
        mass = jnp.where(kept, jnp.exp(scores - peak), 0.0)
        m0 = jnp.exp(n0 - peak)
        m1 = jnp.where(lane_later, jnp.exp(n1 - peak), 0.0)
        total = jnp.sum(mass, axis=0, keepdims=True) + m0 + m1
        weights = mass.T.astype(BF16)
        m0, m1 = (m.astype(BF16).astype(F32) for m in (m0, m1))
        sides = jnp.concatenate([total, m0, m1, jnp.zeros((HD - 3, HD), F32)], axis=0).T
        for p, slot in enumerate(slots):
            cut = slice(p * 16, p * 16 + 16)
            weighted = jnp.dot(weights[cut], value_rows[first + p], preferred_element_type=F32)
            weighted += sides[cut, 1:2] * fresh_row(1, 0, slot)
            weighted += sides[cut, 2:3] * fresh_row(1, 1, slot)
            result[first + p] = weighted / sides[cut, 0:1]

    attend(0)
    attend(8)

    def hand_rows(at_s, carry):
        for pair in range(2):
            first, second = (
                result[jnp.clip(slot_order[at_s * 4 + pair * 2 + n] - b * 16, 0, 15)] for n in range(2)
            )
            for to_b in range(2):
                cut = slice(to_b * 8, to_b * 8 + 8)
                rows_mine[to_b, at_s, pair] = jnp.concatenate((first[cut], second[cut]), axis=0).astype(BF16)
        return carry

    lax.fori_loop(0, 8, hand_rows, 0)

    swap_rows = remote(
        rows_mine.at[other], rows_swap, rows_swap_send, rows_swap_recv, (s, h, other)
    )
    swap_rows.start()
    upper = lax.broadcasted_iota(jnp.int32, (16, HD), 0) < 8

    def merge_rows(at_s, carry):
        for pair in range(2):
            first, second = (lax.div(slot_order[at_s * 4 + pair * 2 + n], 16) == b for n in range(2))
            ours = jnp.where(upper, jnp.where(first, 1.0, 0.0), jnp.where(second, 1.0, 0.0)) > 0.5
            rows_send[at_s, pair] = jnp.where(
                ours, rows_mine[b, at_s, pair].astype(F32), rows_swap[at_s, pair].astype(F32)
            ).astype(BF16)
        return carry

    swap_rows.wait_recv()
    lax.fori_loop(0, 8, merge_rows, 0)

    def send_rows(step, carry):
        to_s = lax.rem(s + step, 8)
        remote(rows_send.at[to_s], rows_land.at[s], rows_send_sem, rows_recv_sem, (to_s, h, b)).start()
        return carry

    lax.fori_loop(1, 8, send_rows, 0)
    pltpu.make_async_copy(rows_send.at[s], rows_land.at[s], rows_recv_sem).start()
    owned = [slot_order[s * 4 + k] for k in range(4)]
    lives = [lengths[slot] for slot in owned]
    first_position = (h * 2 + b) * BLOCK
    position = first_position + lax.broadcasted_iota(jnp.int32, (BLOCK, HD), 0)
    for k in range(4):
        keep[k] = jnp.where(position < lives[k], 1.0, 0.0).astype(BF16)
    fresh[0].wait()
    fresh[1].wait()

    def place_fresh(layer, carry):
        wide = first_position + lax.broadcasted_iota(jnp.int32, (BLOCK, KVH * HD), 0)
        for n, out in enumerate((keys_fresh, values_fresh)):
            new = [fresh_rows[n, t, layer].astype(F32) for t in range(2)]
            for k in range(4):
                rows = jnp.zeros((BLOCK, KVH * HD), F32)
                for t in range(2):
                    rows = jnp.where(wide == lives[k] + t, new[t][k : k + 1], rows)
                out[layer, k] = rows.astype(BF16)
        return carry

    lax.fori_loop(0, 8, place_fresh, 0)
    take_near_keys(1)
    take_near_keys(0)
    for piece in range(6):
        forward_values(piece)
    send_near_values()
    send_near_keys()
    turn_keys(1)
    turn_keys(0)
    pltpu.make_async_copy(keys_packed.at[here], keys_land.at[here], keys_recv).start()

    def assemble(l, carry):
        picked = []
        for k in range(4):
            part = slice((k % 2) * 8, (k % 2) * 8 + 8)
            picked.append(rows_land[l, k // 2].astype(F32)[part])
        for t in range(2):
            attention[t, l] = jnp.concatenate(
                [
                    jnp.concatenate([rows[t * 4 + g : t * 4 + g + 1] for rows in picked], axis=0)
                    for g in range(4)
                ],
                axis=1,
            ).astype(BF16)
        return carry

    wait_for(rows_land, rows_recv_sem)
    lax.fori_loop(0, 8, assemble, 0)
    wait_for(values_land.at[0], mid_near_recv)
    wait_for(values_land.at[far], values_recv)
    wait_for(keys_land, keys_recv)

    wait_for(value_rows.at[pl.ds(0, 8)], chip_send)
    wait_for(value_rows.at[pl.ds(0, 14)], line_send)
    for n, part in enumerate(small_parts):
        wait_for(part.at[b, pl.ds(0, 7)], small_send.at[n])
        wait_for(part.at[b], share_send.at[n])
    swap_rows.wait_send()
    wait_for(values_packed.at[pl.ds(0, 15), far], mid_send)
    wait_for(values_packed.at[pl.ds(0, 15), 0], mid_near)
    wait_for(keys_packed.at[pl.ds(0, 15)], keys_send)
    wait_for(values_mid, values_send)
    wait_for(rows_send.at[pl.ds(0, 7)], rows_send_sem)


def hand_out(
    attention, keys_land, values_land, keys_fresh, values_fresh, keep,
    attention_out, keys_out, values_out, keys, values, sem,
):
    copies = [pltpu.make_async_copy(attention, attention_out, sem.at[16])]
    copies[0].start()
    kept = [keep[k] > 0 for k in range(4)]
    z = lax.div(lax.axis_index("head"), 2)
    for l in range(8):
        x, y_high = l // 2, l % 2
        for h in range(KVH):
            cut = slice(h * HD, h * HD + HD)
            from_z, y_low = h // 2, h % 2
            for k in range(4):
                landed = keys_land[x * 4 + y_high * 2 + y_low, lax.rem(from_z - z + 4, 4), k]
                keys[l, k, :, cut] = jnp.where(kept[k], landed, keys_fresh[l, k, :, cut])
                landed = values_land[lax.rem(z - from_z + 4, 4), x, y_low, y_high, k]
                values[l, k, :, cut] = jnp.where(kept[k], landed, values_fresh[l, k, :, cut])
        for n, (src, dst) in enumerate(((keys, keys_out), (values, values_out))):
            copies.append(pltpu.make_async_copy(src.at[l], dst.at[l], sem.at[n * 8 + l]))
            copies[-1].start()
    for copy in copies:
        copy.wait()


def body(keys_prefill, values_prefill, lengths, slot_order, queries, new_keys, new_values):
    keys = keys_prefill.reshape(16, 4, 2, 2, BLOCK, HD)
    values = values_prefill.reshape(16, 4, 2, 2, BLOCK, HD)
    flat = (keys_prefill.reshape(16, 512, HD), values_prefill.reshape(16, 512, HD))
    any_spec = pl.BlockSpec(memory_space=pl.ANY)
    hbm_spec = pl.BlockSpec(memory_space=pltpu.HBM)
    vmem_spec = pl.BlockSpec(memory_space=pltpu.VMEM)
    dma, vmem = pltpu.SemaphoreType.DMA, pltpu.VMEM
    rows_shape, cache_shape = (2, 8, 4, 4 * HD), (8, 4, BLOCK, KVH * HD)
    plane_shape, line_shape = (16, 4, 4, BLOCK, HD), (4, 4, 2, 2, 4, BLOCK, HD)

    def in_hbm(array):
        return pltpu.with_memory_space_constraint(array, pltpu.HBM)

    held = pl.pallas_call(
        relay,
        out_shape=tuple(
            vmem(shape, BF16) for shape in (rows_shape, plane_shape, line_shape, cache_shape, cache_shape, (4, BLOCK, HD))
        ),
        in_specs=[hbm_spec] * 9,
        out_specs=(vmem_spec,) * 6,
        scratch_shapes=[
            vmem((512, 16 * HD), BF16), vmem((16, 512, HD), BF16),
            [vmem((3, 32, BLOCK, HD), BF16)] * 2, [vmem((32, BLOCK, HD), BF16)] * 2,
            [vmem((32, BLOCK, HD), BF16)] * len(PIECES),
            vmem(plane_shape, BF16), vmem(plane_shape, BF16),
            vmem((3, *line_shape[1:]), BF16),
            vmem((2, 2, 8, 4, KVH * HD), BF16), vmem((2, 8, 4, GROUP * HD), BF16), vmem((32, 16, HD), F32),
            vmem((2, 2, 8, 4, HD), BF16), vmem((16, 16, HD), F32),
            vmem((2, 8, 2, 16, HD), BF16), vmem((8, 2, 16, HD), BF16),
            vmem((8, 2, 16, HD), BF16), vmem((8, 2, 16, HD), BF16),
            pltpu.SMEM((32,), jnp.int32), pltpu.SMEM((32,), jnp.int32), pltpu.SMEM((16,), jnp.int32),
            dma((2,)), dma((2,)), dma((2,)), dma, dma((2,)), dma((2,)), dma, dma((len(PIECES),)),
            dma, dma, dma, dma((6,)), dma, dma, dma, dma,
            dma((3,)), dma((3,)), dma((3,)), dma((3,)), dma, dma, dma, dma,
        ],
        compiler_params=pltpu.CompilerParams(
            collective_id=0, has_side_effects=True, vmem_limit_bytes=48 * 2**20
        ),
        name="relay",
    )(*(in_hbm(x) for x in (slot_order, lengths, keys, values, *flat, queries, new_keys, new_values)))
    return pl.pallas_call(
        hand_out,
        out_shape=tuple(jax.ShapeDtypeStruct(shape, BF16) for shape in (rows_shape, cache_shape, cache_shape)),
        in_specs=[vmem_spec] * 6,
        out_specs=(any_spec,) * 3,
        scratch_shapes=[vmem(cache_shape, BF16), vmem(cache_shape, BF16), dma((17,))],
        compiler_params=pltpu.CompilerParams(vmem_limit_bytes=8 * 2**20),
        name="hand_out",
    )(*(pltpu.with_memory_space_constraint(x, pltpu.VMEM) for x in held))


def solution(mesh):
    in_specs = (
        P("section", "batch", None, "head"),
        P("section", "batch", None, "head"),
        P(),
        P(),
        P(None, None, "section", None),
        P(None, None, "section", None),
        P(None, None, "section", None),
    )
    out_specs = (
        P(None, None, "section", ("head", "batch")),
        P(None, "section", ("head", "batch"), None),
        P(None, "section", ("head", "batch"), None),
    )
    return jax.shard_map(body, mesh=mesh, in_specs=in_specs, out_specs=out_specs, check_vma=False)
```

```python
import jax
import jax.numpy as jnp
from jax import lax
from jax.experimental import pallas as pl
from jax.experimental.pallas import tpu as pltpu
from jax.sharding import PartitionSpec as P

KVH = 8
HD = 128
GROUP = 8
BLOCK = 32
MESH = pl.DeviceIdType.MESH
HIDDEN = -1e30
BF16, F32 = jnp.bfloat16, jnp.float32


PLANE = {
    1: ((1, 1), (3, 3), (1, 3), (3, 1), (2, 1), (0, 3), (2, 3), (0, 1)),
    0: ((1, 0), (0, 2), (3, 2), (1, 2), (3, 0), (2, 2), (2, 0)),
}
PIECES = ((1, 1), (1, 3), (1, 2), (0, 1), (0, 3), (0, 2), (1, 0), (0, 0))


def relay(
    slot_order_hbm, lengths_hbm, keys, values, keys_flat, values_flat, queries, new_keys, new_values,
    attention, keys_land, values_land, keys_fresh, values_fresh, keep,
    key_columns, value_rows, keys_line, keys_near, values_chip, keys_packed, values_packed, values_mid,
    fresh_rows, query_all, query_rows, fresh_all, result, rows_mine, rows_swap, rows_send, rows_land,
    slot_order, lengths, slot_of,
    scalar_sem, full_sem, fresh_sem, line_send, line_recv, near_recv, chip_send, chip_recv,
    keys_send, keys_recv, mid_send, mid_recv, mid_near, mid_near_recv, values_send, values_recv,
    small_send, small_recv, share_send, share_recv, rows_swap_send, rows_swap_recv, rows_send_sem, rows_recv_sem,
):
    s, h, b = lax.axis_index("section"), lax.axis_index("head"), lax.axis_index("batch")
    x, z = lax.div(s, 2), lax.div(h, 2)
    y_low = lax.rem(h, 2)
    y = lax.rem(s, 2) * 2 + y_low
    other = 1 - b
    sign = 1 - 2 * b
    mine = pl.ds(b * 16, 16)
    here = x * 4 + y
    here_mid = (x, y_low, lax.div(y, 2))

    def remote(src, dst, send_sem, recv_sem, to):
        return pltpu.make_async_remote_copy(
            src_ref=src, dst_ref=dst, send_sem=send_sem, recv_sem=recv_sem,
            device_id=to, device_id_type=MESH,
        )

    def wait_for(ref, sem):
        pltpu.make_async_copy(ref, ref, sem).wait()

    def away(d, at, way):
        return lax.rem(at + way * d + 4, 4)

    def in_plane(at_x, at_y):
        return at_x * 2 + lax.div(at_y, 2), z * 2 + lax.rem(at_y, 2)

    def in_line(at_z):
        return at_z * 2 + y_low

    def owner_low(low):
        return lax.rem(y_low + low, 2)

    barrier = pltpu.get_barrier_semaphore()

    def greet(to):
        pl.semaphore_signal(barrier, inc=1, device_id=to, device_id_type=MESH)

    for dz in range(4):
        at_h = in_line(away(dz, z, 1))
        greet((s, at_h, other))
        if dz:
            greet((s, at_h, b))
    for low in (1, 0):
        for dx, dy in PLANE[low]:
            at_s, at_h = in_plane(away(dx, x, 1), away(dy, y, 1))
            greet((at_s, at_h, b))

    scalars = [
        pltpu.make_async_copy(slot_order_hbm, slot_order, scalar_sem.at[0]),
        pltpu.make_async_copy(lengths_hbm, lengths, scalar_sem.at[1]),
    ]
    whole = [
        pltpu.make_async_copy(keys_flat.at[at], key_columns.at[:, pl.ds(at * HD, HD)], full_sem.at[0])
        for at in range(16)
    ]
    whole.append(pltpu.make_async_copy(values_flat, value_rows, full_sem.at[1]))
    fresh = [
        pltpu.make_async_copy(src, fresh_rows.at[n], fresh_sem.at[n])
        for n, src in enumerate((new_keys, new_values))
    ]
    for copy in scalars:
        copy.start()
    for piece, (low, dz) in enumerate(PIECES):
        pltpu.make_async_copy(
            values.at[:, away(dz, z, sign), owner_low(low), b], values_chip[piece].at[mine], chip_recv.at[piece]
        ).start()
    for low in (1, 0):
        pltpu.make_async_copy(
            keys.at[:, z, owner_low(low), b], keys_near[low].at[mine], near_recv.at[low]
        ).start()
    for copy in whole + fresh:
        copy.start()
    pl.semaphore_wait(barrier, 22)

    def swap(piece):
        low, dz = PIECES[piece]
        remote(
            values.at[:, away(dz, z, -sign), owner_low(low), other], values_chip[piece].at[mine],
            chip_send, chip_recv.at[piece], (s, h, other),
        ).start()

    swap(0)
    swap(1)

    def send_line(low, dz, to_b):
        to_z = away(dz, z, sign)
        d = away(dz, 0, sign)
        remote(
            keys.at[:, to_z, owner_low(low), to_b], keys_line[low].at[3 - d, mine],
            line_send, line_recv.at[low], (s, in_line(to_z), to_b),
        ).start()

    for low in (1, 0):
        for dz, to_b in ((1, b), (3, other), (2, b), (1, other), (3, b), (2, other)):
            send_line(low, dz, to_b)
    for low in (1, 0):
        remote(
            keys.at[:, z, owner_low(low), other], keys_near[low].at[mine],
            line_send, near_recv.at[low], (s, h, other),
        ).start()

    head_rows = pl.ds(pl.multiple_of(h * GROUP * HD, GROUP * HD), GROUP * HD)
    head_cols = pl.ds(pl.multiple_of(h * HD, HD), HD)

    def small_pieces(to_s):
        return (
            (queries.at[b, to_s, :, head_rows], query_all.at[b, s]),
            (new_keys.at[b, to_s, :, head_cols], fresh_all.at[0, b, s]),
            (new_values.at[b, to_s, :, head_cols], fresh_all.at[1, b, s]),
        )

    small_parts = (query_all, fresh_all.at[0], fresh_all.at[1])

    def send_small(step, carry):
        to_s = lax.rem(s + step, 8)
        for n, (src, dst) in enumerate(small_pieces(to_s)):
            remote(src, dst, small_send.at[n], small_recv.at[n], (to_s, h, b)).start()
        return carry

    def each_slot(do):
        def step(at_s, carry):
            for k in range(4):
                do(at_s, k, slot_order[at_s * 4 + k])
            return carry

        lax.fori_loop(0, 8, step, 0)

    def send_plane(src, dx, dy, dst, send_sem, recv_sem):
        to_x, to_y = away(dx, x, sign), away(dy, y, sign)
        to_s, to_h = in_plane(to_x, to_y)
        remote(src(to_x * 4 + to_y), dst, send_sem, recv_sem, (to_s, to_h, b)).start()

    def take_values(piece):
        low, dz = PIECES[piece]
        at_z = away(dz, 0, sign)
        wait_for(values_chip[piece], chip_recv.at[piece])
        if piece + 2 < len(PIECES):
            swap(piece + 2)

        def pack(at_s, k, slot):
            values_packed[at_s * 2 + owner_low(low), at_z, k] = values_chip[piece][slot]

        each_slot(pack)
        if dz:
            for dx, dy in PLANE[low]:
                send_plane(
                    lambda to: values_packed.at[to, at_z], dx, dy, values_mid.at[at_z - 1, *here_mid],
                    mid_send, mid_recv.at[piece],
                )
            if low == 0:
                pltpu.make_async_copy(
                    values_packed.at[here, at_z], values_mid.at[at_z - 1, *here_mid], mid_recv.at[piece]
                ).start()

    far = pl.ds(1, 3)

    def forward_values(piece):
        low, dz = PIECES[piece]
        at_z = away(dz, 0, sign)
        wait_for(values_mid.at[0, :, 0], mid_recv.at[piece])
        for at_x in range(4):
            remote(
                values_mid.at[at_z - 1, at_x, owner_low(low)], values_land.at[at_z, at_x, owner_low(low)],
                values_send, values_recv, (s, in_line(away(dz, z, sign)), b),
            ).start()

    def take_near_keys(low):
        wait_for(keys_near[low], near_recv.at[low])

        def pack(at_s, k, slot):
            keys_packed[at_s * 2 + owner_low(low), 0, k] = keys_near[low][slot]

        each_slot(pack)

    def send_near_values():
        for dx, dy in PLANE[1] + PLANE[0]:
            send_plane(
                lambda to: values_packed.at[to, 0], dx, dy, values_land.at[0, *here_mid], mid_near, mid_near_recv
            )

    def send_near_keys():
        for dx, dy in PLANE[1] + PLANE[0]:
            send_plane(lambda to: keys_packed.at[to, 0], dx, dy, keys_land.at[here, 0], keys_send, keys_recv)

    def turn_keys(low):
        wait_for(keys_line[low], line_recv.at[low])

        def pack(at_s, k, slot):
            for dz in range(1, 4):
                keys_packed[at_s * 2 + owner_low(low), dz, k] = keys_line[low][dz - 1, slot]

        each_slot(pack)
        for dx, dy in PLANE[low]:
            send_plane(lambda to: keys_packed.at[to, far], dx, dy, keys_land.at[here, far], keys_send, keys_recv)

    scalars[0].wait()
    scalars[1].wait()
    lax.fori_loop(1, 8, send_small, 0)
    for n, (src, dst) in enumerate(small_pieces(s)):
        pltpu.make_async_copy(src, dst, small_recv.at[n]).start()
    for piece in range(len(PIECES)):
        take_values(piece)
    pltpu.make_async_copy(values_packed.at[here, 0], values_land.at[0, *here_mid], mid_near_recv).start()

    for n, part in enumerate(small_parts):
        wait_for(part.at[b], small_recv.at[n])
        remote(part.at[b], part.at[b], share_send.at[n], share_recv.at[n], (s, h, other)).start()
    for n, part in enumerate(small_parts):
        wait_for(part.at[other], share_recv.at[n])
    wait_for(key_columns, full_sem.at[0])
    wait_for(value_rows, full_sem.at[1])

    def spread_queries(at_s, carry):
        for t in range(2):
            rows = query_all[t, at_s].astype(F32)
            for g in range(GROUP):
                row = (g // 4) * 8 + t * 4 + g % 4
                for k in range(4):
                    query_rows[at_s * 4 + k, row : row + 1, :] = rows[k : k + 1, g * HD : g * HD + HD]
        return carry

    lax.fori_loop(0, 8, spread_queries, 0)

    def find_slot(at, carry):
        found = jnp.int32(0)
        for slot in range(32):
            found = jnp.where(slot_order[slot] == b * 16 + at, slot, found)
        slot_of[at] = found
        return carry

    lax.fori_loop(0, 16, find_slot, 0)

    lane = lax.broadcasted_iota(jnp.int32, (1, HD), 1)
    lane_prompt = lax.div(lane, 16)
    lane_later = lax.rem(lax.div(lane, 4), 2) == 1
    block_lane = lax.div(lax.broadcasted_iota(jnp.int32, (HD, HD), 1), 16)
    row4 = lax.broadcasted_iota(jnp.int32, (4, HD), 0)
    row512 = lax.broadcasted_iota(jnp.int32, (512, HD), 0)
    scale = HD ** -0.5

    def attend(first):
        slots = [slot_of[first + p] for p in range(8)]
        live = jnp.zeros((1, HD), jnp.int32)
        for p in range(8):
            live = jnp.where(lane_prompt == p, lengths[first + p + b * 16], live)

        def fresh_row(n, t, slot):
            rows = fresh_all[n, t, lax.div(slot, 4)].astype(F32)
            return jnp.sum(jnp.where(row4 == lax.rem(slot, 4), rows, 0.0), axis=0, keepdims=True)

        questions = jnp.concatenate([query_rows[slot] for slot in slots], axis=0).T
        diagonal = jnp.concatenate(
            [jnp.where(block_lane == p, questions, 0.0) for p in range(8)], axis=0
        ).astype(BF16)
        fresh_keys = jnp.concatenate(
            [
                jnp.concatenate([fresh_row(0, 0, slot), fresh_row(0, 1, slot), jnp.zeros((14, HD), F32)], axis=0)
                for slot in slots
            ],
            axis=1,
        ).astype(BF16)
        scores = jnp.dot(
            key_columns[:, first * HD : (first + 8) * HD], diagonal, preferred_element_type=F32
        ) * scale
        fresh_scores = jnp.dot(fresh_keys, diagonal, preferred_element_type=F32) * scale
        kept = row512 < live
        scores = jnp.where(kept, scores, HIDDEN)
        n0 = fresh_scores[0:1]
        n1 = jnp.where(lane_later, fresh_scores[1:2], HIDDEN)
        peak = jnp.maximum(jnp.max(scores, axis=0, keepdims=True), jnp.maximum(n0, n1))
        mass = jnp.where(kept, jnp.exp(scores - peak), 0.0)
        m0 = jnp.exp(n0 - peak)
        m1 = jnp.where(lane_later, jnp.exp(n1 - peak), 0.0)
        total = jnp.sum(mass, axis=0, keepdims=True) + m0 + m1
        weights = mass.T.astype(BF16)
        m0, m1 = (m.astype(BF16).astype(F32) for m in (m0, m1))
        sides = jnp.concatenate([total, m0, m1, jnp.zeros((HD - 3, HD), F32)], axis=0).T
        for p, slot in enumerate(slots):
            cut = slice(p * 16, p * 16 + 16)
            weighted = jnp.dot(weights[cut], value_rows[first + p], preferred_element_type=F32)
            weighted += sides[cut, 1:2] * fresh_row(1, 0, slot)
            weighted += sides[cut, 2:3] * fresh_row(1, 1, slot)
            result[first + p] = weighted / sides[cut, 0:1]

    attend(0)
    attend(8)

    def hand_rows(at_s, carry):
        for pair in range(2):
            first, second = (
                result[jnp.clip(slot_order[at_s * 4 + pair * 2 + n] - b * 16, 0, 15)] for n in range(2)
            )
            for to_b in range(2):
                cut = slice(to_b * 8, to_b * 8 + 8)
                rows_mine[to_b, at_s, pair] = jnp.concatenate((first[cut], second[cut]), axis=0).astype(BF16)
        return carry

    lax.fori_loop(0, 8, hand_rows, 0)

    swap_rows = remote(
        rows_mine.at[other], rows_swap, rows_swap_send, rows_swap_recv, (s, h, other)
    )
    swap_rows.start()
    upper = lax.broadcasted_iota(jnp.int32, (16, HD), 0) < 8

    def merge_rows(at_s, carry):
        for pair in range(2):
            first, second = (lax.div(slot_order[at_s * 4 + pair * 2 + n], 16) == b for n in range(2))
            ours = jnp.where(upper, jnp.where(first, 1.0, 0.0), jnp.where(second, 1.0, 0.0)) > 0.5
            rows_send[at_s, pair] = jnp.where(
                ours, rows_mine[b, at_s, pair].astype(F32), rows_swap[at_s, pair].astype(F32)
            ).astype(BF16)
        return carry

    swap_rows.wait_recv()
    lax.fori_loop(0, 8, merge_rows, 0)

    def send_rows(step, carry):
        to_s = lax.rem(s + step, 8)
        remote(rows_send.at[to_s], rows_land.at[s], rows_send_sem, rows_recv_sem, (to_s, h, b)).start()
        return carry

    lax.fori_loop(1, 8, send_rows, 0)
    pltpu.make_async_copy(rows_send.at[s], rows_land.at[s], rows_recv_sem).start()
    owned = [slot_order[s * 4 + k] for k in range(4)]
    lives = [lengths[slot] for slot in owned]
    first_position = (h * 2 + b) * BLOCK
    position = first_position + lax.broadcasted_iota(jnp.int32, (BLOCK, HD), 0)
    for k in range(4):
        keep[k] = jnp.where(position < lives[k], 1.0, 0.0).astype(BF16)
    fresh[0].wait()
    fresh[1].wait()

    def place_fresh(layer, carry):
        wide = first_position + lax.broadcasted_iota(jnp.int32, (BLOCK, KVH * HD), 0)
        for n, out in enumerate((keys_fresh, values_fresh)):
            new = [fresh_rows[n, t, layer].astype(F32) for t in range(2)]
            for k in range(4):
                rows = jnp.zeros((BLOCK, KVH * HD), F32)
                for t in range(2):
                    rows = jnp.where(wide == lives[k] + t, new[t][k : k + 1], rows)
                out[layer, k] = rows.astype(BF16)
        return carry

    lax.fori_loop(0, 8, place_fresh, 0)
    take_near_keys(1)
    take_near_keys(0)
    for piece in range(6):
        forward_values(piece)
        if piece == 0:
            send_near_values()
        if piece == 2:
            send_near_keys()
    turn_keys(1)
    turn_keys(0)
    pltpu.make_async_copy(keys_packed.at[here], keys_land.at[here], keys_recv).start()

    def assemble(l, carry):
        picked = []
        for k in range(4):
            part = slice((k % 2) * 8, (k % 2) * 8 + 8)
            picked.append(rows_land[l, k // 2].astype(F32)[part])
        for t in range(2):
            attention[t, l] = jnp.concatenate(
                [
                    jnp.concatenate([rows[t * 4 + g : t * 4 + g + 1] for rows in picked], axis=0)
                    for g in range(4)
                ],
                axis=1,
            ).astype(BF16)
        return carry

    wait_for(rows_land, rows_recv_sem)
    lax.fori_loop(0, 8, assemble, 0)
    wait_for(values_land.at[0], mid_near_recv)
    wait_for(values_land.at[far], values_recv)
    wait_for(keys_land, keys_recv)

    wait_for(value_rows.at[pl.ds(0, 8)], chip_send)
    wait_for(value_rows.at[pl.ds(0, 14)], line_send)
    for n, part in enumerate(small_parts):
        wait_for(part.at[b, pl.ds(0, 7)], small_send.at[n])
        wait_for(part.at[b], share_send.at[n])
    swap_rows.wait_send()
    wait_for(values_packed.at[pl.ds(0, 15), far], mid_send)
    wait_for(values_packed.at[pl.ds(0, 15), 0], mid_near)
    wait_for(keys_packed.at[pl.ds(0, 15)], keys_send)
    wait_for(values_mid, values_send)
    wait_for(rows_send.at[pl.ds(0, 7)], rows_send_sem)


def hand_out(
    attention, keys_land, values_land, keys_fresh, values_fresh, keep,
    attention_out, keys_out, values_out, keys, values, sem,
):
    copies = [pltpu.make_async_copy(attention, attention_out, sem.at[16])]
    copies[0].start()
    kept = [keep[k] > 0 for k in range(4)]
    z = lax.div(lax.axis_index("head"), 2)
    for l in range(8):
        x, y_high = l // 2, l % 2
        for h in range(KVH):
            cut = slice(h * HD, h * HD + HD)
            from_z, y_low = h // 2, h % 2
            for k in range(4):
                landed = keys_land[x * 4 + y_high * 2 + y_low, lax.rem(from_z - z + 4, 4), k]
                keys[l, k, :, cut] = jnp.where(kept[k], landed, keys_fresh[l, k, :, cut])
                landed = values_land[lax.rem(z - from_z + 4, 4), x, y_low, y_high, k]
                values[l, k, :, cut] = jnp.where(kept[k], landed, values_fresh[l, k, :, cut])
        for n, (src, dst) in enumerate(((keys, keys_out), (values, values_out))):
            copies.append(pltpu.make_async_copy(src.at[l], dst.at[l], sem.at[n * 8 + l]))
            copies[-1].start()
    for copy in copies:
        copy.wait()


def body(keys_prefill, values_prefill, lengths, slot_order, queries, new_keys, new_values):
    keys = keys_prefill.reshape(16, 4, 2, 2, BLOCK, HD)
    values = values_prefill.reshape(16, 4, 2, 2, BLOCK, HD)
    flat = (keys_prefill.reshape(16, 512, HD), values_prefill.reshape(16, 512, HD))
    any_spec = pl.BlockSpec(memory_space=pl.ANY)
    hbm_spec = pl.BlockSpec(memory_space=pltpu.HBM)
    vmem_spec = pl.BlockSpec(memory_space=pltpu.VMEM)
    dma, vmem = pltpu.SemaphoreType.DMA, pltpu.VMEM
    rows_shape, cache_shape = (2, 8, 4, 4 * HD), (8, 4, BLOCK, KVH * HD)
    plane_shape, line_shape = (16, 4, 4, BLOCK, HD), (4, 4, 2, 2, 4, BLOCK, HD)

    def in_hbm(array):
        return pltpu.with_memory_space_constraint(array, pltpu.HBM)

    held = pl.pallas_call(
        relay,
        out_shape=tuple(
            vmem(shape, BF16) for shape in (rows_shape, plane_shape, line_shape, cache_shape, cache_shape, (4, BLOCK, HD))
        ),
        in_specs=[hbm_spec] * 9,
        out_specs=(vmem_spec,) * 6,
        scratch_shapes=[
            vmem((512, 16 * HD), BF16), vmem((16, 512, HD), BF16),
            [vmem((3, 32, BLOCK, HD), BF16)] * 2, [vmem((32, BLOCK, HD), BF16)] * 2,
            [vmem((32, BLOCK, HD), BF16)] * len(PIECES),
            vmem(plane_shape, BF16), vmem(plane_shape, BF16),
            vmem((3, *line_shape[1:]), BF16),
            vmem((2, 2, 8, 4, KVH * HD), BF16), vmem((2, 8, 4, GROUP * HD), BF16), vmem((32, 16, HD), F32),
            vmem((2, 2, 8, 4, HD), BF16), vmem((16, 16, HD), F32),
            vmem((2, 8, 2, 16, HD), BF16), vmem((8, 2, 16, HD), BF16),
            vmem((8, 2, 16, HD), BF16), vmem((8, 2, 16, HD), BF16),
            pltpu.SMEM((32,), jnp.int32), pltpu.SMEM((32,), jnp.int32), pltpu.SMEM((16,), jnp.int32),
            dma((2,)), dma((2,)), dma((2,)), dma, dma((2,)), dma((2,)), dma, dma((len(PIECES),)),
            dma, dma, dma, dma((6,)), dma, dma, dma, dma,
            dma((3,)), dma((3,)), dma((3,)), dma((3,)), dma, dma, dma, dma,
        ],
        compiler_params=pltpu.CompilerParams(
            collective_id=0, has_side_effects=True, vmem_limit_bytes=48 * 2**20
        ),
        name="relay",
    )(*(in_hbm(x) for x in (slot_order, lengths, keys, values, *flat, queries, new_keys, new_values)))
    return pl.pallas_call(
        hand_out,
        out_shape=tuple(jax.ShapeDtypeStruct(shape, BF16) for shape in (rows_shape, cache_shape, cache_shape)),
        in_specs=[vmem_spec] * 6,
        out_specs=(any_spec,) * 3,
        scratch_shapes=[vmem(cache_shape, BF16), vmem(cache_shape, BF16), dma((17,))],
        compiler_params=pltpu.CompilerParams(vmem_limit_bytes=8 * 2**20),
        name="hand_out",
    )(*(pltpu.with_memory_space_constraint(x, pltpu.VMEM) for x in held))


def solution(mesh):
    in_specs = (
        P("section", "batch", None, "head"),
        P("section", "batch", None, "head"),
        P(),
        P(),
        P(None, None, "section", None),
        P(None, None, "section", None),
        P(None, None, "section", None),
    )
    out_specs = (
        P(None, None, "section", ("head", "batch")),
        P(None, "section", ("head", "batch"), None),
        P(None, "section", ("head", "batch"), None),
    )
    return jax.shard_map(body, mesh=mesh, in_specs=in_specs, out_specs=out_specs, check_vma=False)
```
